128 devices in a mesh: rep: 8 (over x, y_hi), shard: 16 (over z, y_lo, core).
Axes of the slice: x: 4, y: 4 (y_hi: 2, y_lo: 2; y = y_hi * 2 + y_lo), z: 4, core: 2. Of those that a mesh axis runs over, the one named last changes fastest.
Arguments:
- layer_input: bfloat16 [24576, 1536], P(('rep', 'shard')), may hold values from -6 to 6
- grad_output: bfloat16 [24576, 1536], P(('rep', 'shard')), may hold values from -24 to 24
- routes: int32 [24576, 8], P(('rep', 'shard')), may hold values from 0 to 9, all different within a row
- route_logits: float32 [24576, 8], P(('rep', 'shard')), may hold values from -3 to 3
- norm_gains: bfloat16 [2, 1536], P(None, 'shard'), may hold values from 0.5 to 1.5
- inward: bfloat16 [1536, 2560], P('shard')
- outward: bfloat16 [1536, 1536], P('shard'), may hold values from -0.875 to 0.875
- lifting: bfloat16 [1536, 10, 1024], P('shard'), may hold values from -0.15625 to 0.15625
- lowering: bfloat16 [512, 10, 1536], P('shard'), may hold values from -1 to 1
- mean_gains: bfloat16 [2, 1536], P(None, 'shard')
- mean_inward: bfloat16 [1536, 2560], P('shard')
- mean_outward: bfloat16 [1536, 1536], P('shard')
- mean_lifting: bfloat16 [1536, 10, 1024], P('shard')
- mean_lowering: bfloat16 [512, 10, 1536], P('shard')
- square_gains: bfloat16 [2, 1536], P(None, 'shard'), as said below
- square_inward: bfloat16 [1536, 2560], P('shard'), as said below
- square_outward: bfloat16 [1536, 1536], P('shard'), as said below
- square_lifting: bfloat16 [1536, 10, 1024], P('shard'), as said below
- square_lowering: bfloat16 [512, 10, 1536], P('shard'), as said below
Outputs:
- layer_output: float32 [24576, 1536], P(('rep', 'shard'))
- input_grad: float32 [24576, 1536], P(('rep', 'shard'))
- moment_gains: float32 [2, 1536], P(None, 'shard')
- moment_inward: float32 [1536, 2560], P('shard')
- moment_outward: float32 [1536, 1536], P('shard')
- moment_lifting: float32 [1536, 10, 1024], P('shard')
- moment_lowering: float32 [512, 10, 1536], P('shard')
- variance_gains: float32 [2, 1536], P(None, 'shard')
- variance_inward: float32 [1536, 2560], P('shard')
- variance_outward: float32 [1536, 1536], P('shard')
- variance_lifting: float32 [1536, 10, 1024], P('shard')
- variance_lowering: float32 [512, 10, 1536], P('shard')
- updated_gains: float32 [2, 1536], P(None, 'shard')
- updated_inward: float32 [1536, 2560], P('shard')
- updated_outward: float32 [1536, 1536], P('shard')
- updated_lifting: float32 [1536, 10, 1024], P('shard')
- updated_lowering: float32 [512, 10, 1536], P('shard')
The draws below stay inside these ranges and needn't reach their ends.
Inputs may be any that keep to these rules, and one draw needn't show every extreme that they name: `routes`: each row names 8 different experts; every expert is named by some row. `square_gains`: Positive. `square_inward`: Positive. `square_outward`: Positive. `square_lifting`: Positive. `square_lowering`: Positive.
All inputs are finite; a program needn't handle non-finite values.
Results may differ from the reference program's by a relative error of at most 0.017.
Values may be sent and summed in bfloat16 or wider, within the bound.
A program may use at most 384 MiB of HBM per device.

```python
import math
import jax
import jax.numpy as jnp
from jax import lax

D = 1536
HEADS = 24
KV_HEADS = 8
HEAD = 64
FF_EXP = 512
EXPERTS = 10
TOP = 8
STEP = 10
ATT = 1536
QKV = 2560
SEQ = 3072
TOKENS = 24576


beta_one = 0.9


beta_two = 0.95


spread_gains = 1.0


spread_inward = 1.0


spread_outward = 0.2


spread_lifting = 0.4


spread_lowering = 0.06


def first_moment(key, shape, spread):
    grad_size = spread * float(TOKENS) ** 0.5
    return (1.0 - beta_one) / beta_one * grad_size * jax.random.truncated_normal(key, -3.0, 3.0, shape, jnp.float32)


def second_moment(key, shape, spread):
    grad_size = spread * float(TOKENS) ** 0.5
    factor = jnp.exp(jax.random.uniform(key, shape, jnp.float32, math.log(0.5), math.log(8.0)))
    return (1.0 - beta_two) / beta_two * grad_size * grad_size * factor


def draw_inward(key, part):
    key = jax.random.fold_in(key, 11)
    column = jnp.arange(QKV)
    factor = jnp.where(column < HEADS * HEAD, 2.0, 1.0) * D ** (-0.5)
    return (jax.random.normal(key, (D, QKV), jnp.float32) * factor[None, :]).astype(jnp.bfloat16)


def draw_mean_gains(key, part):
    key = jax.random.fold_in(key, 21)
    return first_moment(key, (2, D), spread_gains).astype(jnp.bfloat16)


def draw_mean_inward(key, part):
    key = jax.random.fold_in(key, 22)
    return first_moment(key, (D, QKV), spread_inward).astype(jnp.bfloat16)


def draw_mean_outward(key, part):
    key = jax.random.fold_in(key, 23)
    return first_moment(key, (HEADS * HEAD, D), spread_outward).astype(jnp.bfloat16)


def draw_mean_lifting(key, part):
    key = jax.random.fold_in(key, 24)
    return first_moment(key, (D, EXPERTS, 2 * FF_EXP), spread_lifting).astype(jnp.bfloat16)


def draw_mean_lowering(key, part):
    key = jax.random.fold_in(key, 25)
    return first_moment(key, (FF_EXP, EXPERTS, D), spread_lowering).astype(jnp.bfloat16)


def draw_square_gains(key, part):
    key = jax.random.fold_in(key, 31)
    return second_moment(key, (2, D), spread_gains).astype(jnp.bfloat16)


def draw_square_inward(key, part):
    key = jax.random.fold_in(key, 32)
    return second_moment(key, (D, QKV), spread_inward).astype(jnp.bfloat16)


def draw_square_outward(key, part):
    key = jax.random.fold_in(key, 33)
    return second_moment(key, (HEADS * HEAD, D), spread_outward).astype(jnp.bfloat16)


def draw_square_lifting(key, part):
    key = jax.random.fold_in(key, 34)
    return second_moment(key, (D, EXPERTS, 2 * FF_EXP), spread_lifting).astype(jnp.bfloat16)


def draw_square_lowering(key, part):
    key = jax.random.fold_in(key, 35)
    return second_moment(key, (FF_EXP, EXPERTS, D), spread_lowering).astype(jnp.bfloat16)


def spiked(values, stream_key, source, target, parts, factor):
    def block_of(axis_at):
        return (jnp.arange(values.shape[axis_at]) // (values.shape[axis_at] // parts)).reshape((-1,) + (1,) * (values.ndim - 1 - axis_at))

    first = jax.random.permutation(stream_key, parts)[block_of(target)]
    far = (block_of(target) + parts // 2) % parts
    return jnp.where((block_of(source) == first) | (block_of(source) == far), factor * values, values)


def shard_levels(rng, extent, pieces, low, largest):
    def one(dim, shards_of):
        draws = jax.random.uniform(jax.random.fold_in(jax.random.fold_in(rng, 6), dim), (shards_of,), jnp.float32, low / len(pieces), largest / len(pieces))
        return jnp.repeat(jnp.exp(draws), extent[dim] // shards_of).reshape((-1,) + (1,) * (len(extent) - dim - 1))

    loudness = one(*pieces[0])
    for cut in pieces[1:]:
        loudness = loudness * one(*cut)
    return loudness


def distinct(own_key, rows, number_of, top, lift):
    order = jax.random.permutation(jax.random.fold_in(own_key, 1), number_of)
    favour = order
    for power in range(3):
        favour = favour * favour // number_of
    favour = favour * lift // number_of
    lots = jax.random.randint(jax.random.fold_in(own_key, 2), (rows, number_of), 0, 4096) + favour
    holders = jax.random.permutation(jax.random.fold_in(own_key, 3), rows)[jnp.arange(number_of) % rows]
    lots = jnp.where(jnp.arange(rows)[:, None] == holders[None, :], 1 << 14, lots)
    merit = lots * number_of + jnp.arange(number_of)
    return lax.top_k(merit.astype(jnp.int32), top)[1].astype(jnp.int32)


def gaussian(rng, extent, deviation, most, cuts=(), kind=jnp.bfloat16):
    entries = deviation * jax.random.normal(rng, extent, jnp.float32)
    if cuts:
        entries = entries * shard_levels(rng, extent, cuts, -0.22, 0.18)
    return jnp.clip(entries, -most, most).astype(kind)


def heavy_noise(own_key, shape, width, reach, cuts, heavy, kind=jnp.bfloat16):
    entries = width * jax.random.normal(own_key, shape, jnp.float32)
    if cuts:
        entries = entries * shard_levels(own_key, shape, cuts, -0.22, 0.18)
    return jnp.clip(spiked(entries, jax.random.fold_in(own_key, 3), *heavy), -reach, reach).astype(kind)


def setup_inputs(seed: int = 0) -> dict:
    keys = jax.random.split(jax.random.key(seed), 20)
    layer_input = gaussian(keys[0], (TOKENS, D), 1.0, 6.0, ((0, 128),))
    grad_output = heavy_noise(keys[1], (TOKENS, D), 1.0, 24.0, ((0, 128),), (0, 1, 128, 5.5))
    routes = distinct(keys[2], TOKENS, EXPERTS, TOP, 6553)
    route_logits = gaussian(keys[3], (TOKENS, TOP), 0.5, 3.0, ((0, 128),), jnp.float32)
    norm_gains = jnp.clip(1.0 + 0.1 * jax.random.normal(keys[4], (2, D), jnp.float32), 0.5, 1.5).astype(jnp.bfloat16)
    inward = draw_inward(jax.random.fold_in(keys[19], 71), 0)
    outward = gaussian(keys[6], (ATT, D), (D // 32) ** -0.5, 0.875, ((0, 16),))
    lifting = gaussian(keys[7], (D, EXPERTS, 2 * FF_EXP), D ** -0.5, 0.15625, ((0, 16),))
    lowering = gaussian(keys[8], (FF_EXP, EXPERTS, D), (FF_EXP // 16) ** -0.5, 1.0, ((0, 16),))
    mean_gains = draw_mean_gains(jax.random.fold_in(keys[19], 71), 0)
    mean_inward = draw_mean_inward(jax.random.fold_in(keys[19], 71), 0)
    mean_outward = draw_mean_outward(jax.random.fold_in(keys[19], 71), 0)
    mean_lifting = draw_mean_lifting(jax.random.fold_in(keys[19], 71), 0)
    mean_lowering = draw_mean_lowering(jax.random.fold_in(keys[19], 71), 0)
    square_gains = draw_square_gains(jax.random.fold_in(keys[19], 71), 0)
    square_inward = draw_square_inward(jax.random.fold_in(keys[19], 71), 0)
    square_outward = draw_square_outward(jax.random.fold_in(keys[19], 71), 0)
    square_lifting = draw_square_lifting(jax.random.fold_in(keys[19], 71), 0)
    square_lowering = draw_square_lowering(jax.random.fold_in(keys[19], 71), 0)
    return dict(layer_input=layer_input, grad_output=grad_output, routes=routes, route_logits=route_logits, norm_gains=norm_gains, inward=inward, outward=outward, lifting=lifting, lowering=lowering, mean_gains=mean_gains, mean_inward=mean_inward, mean_outward=mean_outward, mean_lifting=mean_lifting, mean_lowering=mean_lowering, square_gains=square_gains, square_inward=square_inward, square_outward=square_outward, square_lifting=square_lifting, square_lowering=square_lowering)


norm_epsilon = 1e-06
beta_one = 0.9
beta_two = 0.95
adam_epsilon = 1e-08
weight_decay = 0.1
rate_gains = 0.5
rate_inward = 0.05
rate_outward = 0.3
rate_lifting = 0.05
rate_lowering = 0.3

@jax.custom_vjp
def low(v):
    return lax.optimization_barrier(v.astype(jnp.bfloat16)).astype(jnp.float32)

@jax.custom_vjp
def low_back(v):
    return v

def low_keep(v):
    return (low(v), None)

def low_pass(kept, grad):
    return (grad,)

def back_keep(v):
    return (v, None)

def back_low(kept, grad):
    return (low(grad),)
low.defvjp(low_keep, low_pass)
low_back.defvjp(back_keep, back_low)

def angles(position):
    half_width = HEAD // 2
    frequency = 10000.0 ** (-(2.0 * jnp.arange(half_width).astype(jnp.float32)) / HEAD)
    phases = position.astype(jnp.float32)[:, None] * frequency[None, :]
    return (jnp.cos(phases)[:, None, :], jnp.sin(phases)[:, None, :])

def rotate(heads, cosine, sine_table):
    half_width = HEAD // 2
    first = heads[..., :half_width]
    second = heads[..., half_width:]
    return jnp.concatenate([first * cosine - second * sine_table, second * cosine + first * sine_table], -1)

def normalize(stream, gain):
    inverse = lax.rsqrt(lax.optimization_barrier(jnp.mean(stream * stream, -1, keepdims=True)) + norm_epsilon)
    return stream * inverse * gain

def attend(query_all, key_all, value_all, position):
    length = query_all.shape[0]
    block_rows = min(512, length)
    blocks = length // block_rows
    factor = HEAD ** (-0.5)
    grouped = query_all.reshape(blocks, block_rows, KV_HEADS, HEADS // KV_HEADS, HEAD)
    offsets = jnp.arange(blocks, dtype=jnp.int32) * block_rows

    @jax.checkpoint
    def one_block(operands):
        query_block, offset = operands
        scores = low_back(jnp.einsum('bgrd,sgd->grbs', query_block, key_all, precision=lax.Precision.HIGHEST) * factor)
        rows_here = offset + jnp.arange(block_rows, dtype=jnp.int32)
        allowed = position[None, :] <= rows_here[:, None]
        weights = low(jax.nn.softmax(jnp.where(allowed, scores, -1e+30), axis=-1))
        return jnp.einsum('grbs,sgd->bgrd', weights, value_all, precision=lax.Precision.HIGHEST)
    result = lax.map(one_block, (grouped, offsets))
    return result.reshape(length, HEADS * HEAD)

def layer(params, stream, logits, chosen):
    gains, inward, outward, lifting, lowering = params
    length = stream.shape[0]
    attend_width = HEADS * HEAD
    key_width = KV_HEADS * HEAD
    position = jnp.arange(length, dtype=jnp.int32)
    cosine, sine_table = angles(position)
    low_one = low(normalize(stream, gains[0]))
    joined = jnp.dot(low_one, inward, precision=lax.Precision.HIGHEST)
    query_all = low(rotate(low_back(joined[:, :attend_width]).reshape(length, HEADS, HEAD), cosine, sine_table))
    key_all = low(rotate(low_back(joined[:, attend_width:attend_width + key_width]).reshape(length, KV_HEADS, HEAD), cosine, sine_table))
    value_all = low(low_back(joined[:, attend_width + key_width:])).reshape(length, KV_HEADS, HEAD)
    attended = low(low_back(attend(query_all, key_all, value_all, position)))
    mixed = stream + low_back(jnp.dot(attended, outward, precision=lax.Precision.HIGHEST))
    low_two = low(normalize(mixed, gains[1]))
    gate_weights = jax.nn.softmax(logits, axis=-1)
    picked = chosen[:, :, None] == jnp.arange(EXPERTS, dtype=jnp.int32)[None, None, :]
    combine = lax.optimization_barrier(jnp.sum(jnp.where(picked, gate_weights[:, :, None], 0.0), axis=1))
    lifted = low_back(jnp.einsum('td,def->tef', low_two, lifting, precision=lax.Precision.HIGHEST))
    gate_part = lifted[..., :FF_EXP]
    up_part = lifted[..., FF_EXP:]
    activation = low(gate_part * jax.nn.sigmoid(gate_part) * up_part)
    expert_out = low_back(jnp.einsum('tef,fed->ted', activation, lowering, precision=lax.Precision.HIGHEST))
    return mixed + lax.optimization_barrier(jnp.sum(combine[:, :, None] * expert_out, axis=1))

def adam(weight, old_mean, square, gradient, step_rate, decay_rate):
    values = weight.astype(jnp.float32)
    moment = beta_one * old_mean.astype(jnp.float32) + (1.0 - beta_one) * gradient
    variance = beta_two * square.astype(jnp.float32) + (1.0 - beta_two) * gradient * gradient
    normed_step = moment / (1.0 - beta_one ** STEP) / (jnp.sqrt(variance / (1.0 - beta_two ** STEP)) + adam_epsilon)
    return (moment, variance, values - step_rate * (normed_step + decay_rate * values))

def reference(layer_input, grad_output, routes, route_logits, norm_gains, inward, outward, lifting, lowering, mean_gains, mean_inward, mean_outward, mean_lifting, mean_lowering, square_gains, square_inward, square_outward, square_lifting, square_lowering):
    params = tuple((weight.astype(jnp.float32) for weight in (norm_gains, inward, outward, lifting, lowering)))
    sequences = layer_input.shape[0] // SEQ
    streams = layer_input.astype(jnp.float32).reshape(sequences, SEQ, D)
    cotangents = grad_output.astype(jnp.float32).reshape(sequences, SEQ, D)
    logit_rows = route_logits.reshape(sequences, SEQ, TOP)
    route_rows = routes.reshape(sequences, SEQ, TOP)

    def one_sequence(totals, operands):
        stream, cotangent, logits, chosen = operands

        def forward(weights, inputs):
            return layer(weights, inputs, logits, chosen)
        output, pullback = jax.vjp(forward, params, stream)
        weight_grads, stream_grad = pullback(cotangent)
        return (jax.tree.map(jnp.add, totals, weight_grads), (output, stream_grad))
    zeros = tuple((jnp.zeros_like(weight) for weight in params))
    totals, (outputs, stream_grads) = lax.scan(one_sequence, zeros, (streams, cotangents, logit_rows, route_rows))
    new_gains = adam(norm_gains, mean_gains, square_gains, totals[0], rate_gains, 0.0)
    new_inward = adam(inward, mean_inward, square_inward, totals[1], rate_inward, weight_decay)
    new_outward = adam(outward, mean_outward, square_outward, totals[2], rate_outward, weight_decay)
    new_lifting = adam(lifting, mean_lifting, square_lifting, totals[3], rate_lifting, weight_decay)
    new_lowering = adam(lowering, mean_lowering, square_lowering, totals[4], rate_lowering, weight_decay)
    return (outputs.reshape(-1, D), stream_grads.reshape(-1, D), new_gains[0], new_inward[0], new_outward[0], new_lifting[0], new_lowering[0], new_gains[1], new_inward[1], new_outward[1], new_lifting[1], new_lowering[1], new_gains[2], new_inward[2], new_outward[2], new_lifting[2], new_lowering[2])
```

```python
import functools

import jax
import jax.numpy as jnp
import numpy as np
from jax import lax
from jax.experimental import pallas as pl
from jax.experimental.pallas import tpu as pltpu
from jax.sharding import PartitionSpec as P

HEADS = 24
KV_HEADS = 8
HEAD = 64
GROUP = HEADS // KV_HEADS
FF_EXP = 512
EXPERTS = 10
STEP = 10

norm_epsilon = 1e-06
beta_one = 0.9
beta_two = 0.95
adam_epsilon = 1e-08
weight_decay = 0.1
rate_gains = 0.5
rate_inward = 0.05
rate_outward = 0.3
rate_lifting = 0.05
rate_lowering = 0.3

SHARDS = 16
CHIPS = 8
REPS = 8
OWN = 192
SEQ = OWN * SHARDS
D = 1536
HID = 320
PAD = 384
BLOCKS = 8
ROWS = GROUP * OWN
KEYS = 2 * OWN

MESH = pl.DeviceIdType.MESH
bf16 = jnp.bfloat16
f32 = jnp.float32


def place():
    rep = lax.axis_index("rep")
    shard = lax.axis_index("shard")
    return rep, shard


def greet(devices):
    barrier = pltpu.get_barrier_semaphore()
    for device in devices:
        pl.semaphore_signal(barrier, inc=1, device_id=device, device_id_type=MESH)
    pl.semaphore_wait(barrier, len(devices))


def send(src, dst, send_sem, recv_sem, device):
    copy = pltpu.make_async_remote_copy(
        src_ref=src,
        dst_ref=dst,
        send_sem=send_sem,
        recv_sem=recv_sem,
        device_id=device,
        device_id_type=MESH,
    )
    copy.start()
    return copy


def params(collective, vmem=None):
    return pltpu.CompilerParams(
        collective_id=collective, has_side_effects=True, vmem_limit_bytes=vmem
    )


ANY = pl.BlockSpec(memory_space=pl.ANY)
VMEM = pl.BlockSpec(memory_space=pltpu.VMEM)


def gather_kernel(x_ref, o_ref, local_sem, send_sem, recv_sem):
    rep, shard = place()
    half = x_ref.shape[0] // 2
    core = lax.rem(shard, 2)
    y = lax.rem(shard // 2, 2)
    sib = shard + 1 - 2 * core
    pair = shard + 2 - 4 * y
    up = lax.rem(shard + 4, 16)
    down = lax.rem(shard + 12, 16)
    far = lax.rem(shard + 8, 16)

    def other(block):
        return block + 2 - 4 * y

    greet([(rep, sib), (rep, pair), (rep, up), (rep, down)])
    own = pltpu.make_async_copy(x_ref, o_ref.at[shard], local_sem)
    own.start()
    sent = []

    def put(src, dst, slot, device):
        sent.append(send(src, dst, send_sem.at[len(sent)], recv_sem.at[slot], (rep, device)))

    def forward(block, slot, device, rows=None):
        ref = o_ref.at[block] if rows is None else o_ref.at[block, rows]
        put(ref, ref, slot, device)

    def arrived(block, slot, rows=None):
        ref = o_ref.at[block] if rows is None else o_ref.at[block, rows]
        pltpu.make_async_remote_copy(
            src_ref=ref,
            dst_ref=ref,
            send_sem=send_sem.at[0],
            recv_sem=recv_sem.at[slot],
            device_id=(rep, sib),
            device_id_type=MESH,
        ).wait_recv()

    top, bottom = pl.ds(0, half), pl.ds(half, half)
    put(x_ref, o_ref.at[shard], 0, pair)
    put(x_ref, o_ref.at[shard], 1, up)
    put(x_ref, o_ref.at[shard], 5, down)
    put(x_ref, o_ref.at[shard], 9, sib)
    arrived(pair, 0)
    forward(pair, 2, up)
    forward(pair, 6, down)
    forward(pair, 10, sib)
    arrived(down, 1)
    forward(down, 3, up, top)
    forward(down, 11, sib)
    arrived(up, 5)
    forward(up, 7, down, bottom)
    forward(up, 12, sib)
    arrived(other(down), 2)
    forward(other(down), 4, up, top)
    forward(other(down), 13, sib)
    arrived(other(up), 6)
    forward(other(up), 8, down, bottom)
    forward(other(up), 14, sib)
    arrived(far, 3, top)
    forward(far, 15, sib, top)
    arrived(far, 7, bottom)
    forward(far, 16, sib, bottom)
    arrived(other(far), 4, top)
    forward(other(far), 17, sib, top)
    arrived(other(far), 8, bottom)
    forward(other(far), 18, sib, bottom)

    def twin(block):
        return block + 1 - 2 * core

    arrived(twin(shard), 9)
    arrived(twin(pair), 10)
    arrived(twin(down), 11)
    arrived(twin(up), 12)
    arrived(twin(other(down)), 13)
    arrived(twin(other(up)), 14)
    arrived(twin(far), 15, top)
    arrived(twin(far), 16, bottom)
    arrived(twin(other(far)), 17, top)
    arrived(twin(other(far)), 18, bottom)
    for copy in sent:
        copy.wait_send()
    own.wait()


def gather(x, collective):
    rows, columns = x.shape
    out = pl.pallas_call(
        gather_kernel,
        out_shape=jax.ShapeDtypeStruct((SHARDS, rows, columns), x.dtype),
        in_specs=[ANY],
        out_specs=ANY,
        scratch_shapes=[
            pltpu.SemaphoreType.DMA,
            pltpu.SemaphoreType.DMA((21,)),
            pltpu.SemaphoreType.DMA((19,)),
        ],
        compiler_params=params(collective),
        name="gather_rows",
    )(x)
    return out.reshape(SHARDS * rows, columns)


def exchange_kernel(kinds, *refs):
    count = len(kinds)
    ins, outs = refs[:count], refs[count : 2 * count]
    local_sem, send_sem, recv_sem = refs[2 * count :]
    rep, shard = place()
    core = lax.rem(shard, 2)
    chip = shard // 2
    greet([(rep, lax.rem(shard + i, 16)) for i in range(1, 16)])
    sent, due = [], []

    def mine(device):
        return lax.rem(lax.rem(device, 2) + lax.rem(device // 2, 2), 2)

    for n, kind in enumerate(kinds):
        x, o = ins[n], outs[n]
        if kind == "all":
            local = pltpu.make_async_copy(x.at[shard], o.at[shard], local_sem.at[n])
            local.start()
            due.append(local)
            for i in range(1, 16):
                to = lax.rem(shard + i, 16)
                sent.append(
                    send(x.at[to], o.at[shard], send_sem.at[n, i], recv_sem.at[n, i], (rep, to))
                )
        elif kind == "heads":
            local = pltpu.make_async_copy(x.at[chip], o.at[shard], local_sem.at[n])
            local.start()
            due.append(local)
            for i in range(1, 16):
                to = lax.rem(shard + i, 16)
                sent.append(
                    send(
                        x.at[to // 2], o.at[shard], send_sem.at[n, i], recv_sem.at[n, i], (rep, to)
                    )
                )
        elif kind == "home":
            for i in range(8):
                c = lax.rem(chip + i, 8)
                to = 2 * c + lax.rem(c + core, 2)
                if i == 0:
                    same = to == shard

                    @pl.when(same)
                    def _(x=x, o=o, c=c, n=n):
                        local = pltpu.make_async_copy(x.at[c], o.at[chip], local_sem.at[n])
                        local.start()
                        local.wait()

                    @pl.when(jnp.logical_not(same))
                    def _(x=x, o=o, c=c, n=n, to=to):
                        copy = send(
                            x.at[c], o.at[chip], send_sem.at[n, 0], recv_sem.at[n, 0], (rep, to)
                        )
                        copy.wait_send()

                else:
                    sent.append(
                        send(
                            x.at[c], o.at[chip], send_sem.at[n, i], recv_sem.at[n, i], (rep, to)
                        )
                    )
        elif kind == "away":
            for i in range(8):
                c = lax.rem(chip + i, 8)
                to = 2 * c + mine(shard)
                if i == 0:
                    same = to == shard

                    @pl.when(same)
                    def _(x=x, o=o, c=c, n=n):
                        local = pltpu.make_async_copy(x.at[c], o.at[chip], local_sem.at[n])
                        local.start()
                        local.wait()

                    @pl.when(jnp.logical_not(same))
                    def _(x=x, o=o, c=c, n=n, to=to):
                        copy = send(
                            x.at[c], o.at[chip], send_sem.at[n, 0], recv_sem.at[n, 0], (rep, to)
                        )
                        copy.wait_send()

                else:
                    sent.append(
                        send(
                            x.at[c], o.at[chip], send_sem.at[n, i], recv_sem.at[n, i], (rep, to)
                        )
                    )

    def arrived(ref, n, i):
        pltpu.make_async_remote_copy(
            src_ref=ref,
            dst_ref=ref,
            send_sem=send_sem.at[n, 0],
            recv_sem=recv_sem.at[n, i],
            device_id=(rep, lax.rem(shard + 1, 16)),
            device_id_type=MESH,
        ).wait_recv()

    for n, kind in enumerate(kinds):
        o = outs[n]
        if kind in ("all", "heads"):
            for i in range(1, 16):
                arrived(o.at[lax.rem(shard + 16 - i, 16)], n, i)
        else:
            away = kind == "away"
            first = (
                2 * chip + lax.rem(chip + core, 2) if away else 2 * chip + mine(shard)
            )

            @pl.when(first != shard)
            def _(o=o, n=n):
                arrived(o.at[chip], n, 0)

            for i in range(1, 8):
                arrived(o.at[lax.rem(chip + 8 - i, 8)], n, i)
    for copy in sent:
        copy.wait_send()
    for copy in due:
        copy.wait()


def exchange(arrays, kinds, collective, name):
    shapes = []
    for x, kind in zip(arrays, kinds):
        lead = 16 if kind in ("all", "heads") else 8
        shapes.append(jax.ShapeDtypeStruct((lead,) + x.shape[1:], x.dtype))
    n = len(arrays)
    return pl.pallas_call(
        functools.partial(exchange_kernel, kinds),
        out_shape=tuple(shapes),
        in_specs=[ANY] * n,
        out_specs=(ANY,) * n,
        scratch_shapes=[
            pltpu.SemaphoreType.DMA((n,)),
            pltpu.SemaphoreType.DMA((n, 16)),
            pltpu.SemaphoreType.DMA((n, 16)),
        ],
        compiler_params=params(collective),
        name=name,
    )(*arrays)


def reduce_kernel(count, *refs):
    ins, outs = refs[:count], refs[count : 2 * count]
    held, near, landed, load_sem, s_near, r_near, s_far, r_far = refs[2 * count :]
    rep, shard = place()
    core = lax.rem(shard, 2)
    chip = shard // 2
    sib = shard + 1 - 2 * core
    peers = [2 * lax.rem(chip + i, 8) + core for i in range(1, 8)]
    greet([(rep, sib)] + [(rep, p) for p in peers])
    nears, loads, fars = [], [], []
    order = [1, 7, 2, 6, 3, 5, 4, 0]
    for n in range(count):
        for i in order:
            c = lax.rem(chip + i, 8)
            nears.append(
                send(
                    ins[n].at[2 * c + 1 - core],
                    near.at[n, i],
                    s_near.at[n, i],
                    r_near.at[n, i],
                    (rep, sib),
                )
            )
            load = pltpu.make_async_copy(
                ins[n].at[2 * c + core], held.at[n, i], load_sem.at[n, i]
            )
            load.start()
            loads.append(load)
    for n in range(count):
        for j, i in enumerate(order):
            nears[8 * n + j].wait_recv()
            loads[8 * n + j].wait()
            held[n, i] = (held[n, i].astype(f32) + near[n, i].astype(f32)).astype(bf16)
            if i:
                c = lax.rem(chip + i, 8)
                fars.append(
                    send(
                        held.at[n, i],
                        landed.at[n, i - 1],
                        s_far.at[n, i],
                        r_far.at[n, i],
                        (rep, 2 * c + core),
                    )
                )
    for n in range(count):
        for j in range(7):
            fars[7 * n + j].wait_recv()
        rows = outs[n].shape[0]
        step = 32

        def add(t, _, n=n):
            at = pl.ds(pl.multiple_of(t * step, step), step)
            total = held[n, 0, at].astype(f32)
            for i in range(7):
                total = total + landed[n, i, at].astype(f32)
            outs[n][at] = total
            return 0

        lax.fori_loop(0, rows // step, add, 0)
    for copy in nears + fars:
        copy.wait_send()


def reduce_blocks(arrays, collective):
    n = len(arrays)
    rows, columns = arrays[0].shape[1:]
    slot = (n, 8, rows, columns)
    return pl.pallas_call(
        functools.partial(reduce_kernel, n),
        out_shape=tuple(jax.ShapeDtypeStruct((rows, columns), f32) for _ in arrays),
        in_specs=[ANY] * n,
        out_specs=(VMEM,) * n,
        scratch_shapes=[
            pltpu.VMEM(slot, bf16),
            pltpu.VMEM(slot, bf16),
            pltpu.VMEM((n, 7, rows, columns), bf16),
            pltpu.SemaphoreType.DMA((n, 8)),
            pltpu.SemaphoreType.DMA((n, 8)),
            pltpu.SemaphoreType.DMA((n, 8)),
            pltpu.SemaphoreType.DMA((n, 8)),
            pltpu.SemaphoreType.DMA((n, 8)),
        ],
        compiler_params=params(collective, 60 * 2**20),
        name="reduce_rows",
    )(*arrays)


def total_kernel(count, *refs):
    ins, outs = refs[:count], refs[count : 2 * count]
    landed = refs[2 * count : 3 * count]
    local_sem, s_one, r_one, s_two, r_two = refs[3 * count :]
    rep, shard = place()
    greet([(lax.rem(rep + i, 8), shard) for i in range(1, 8)])
    ones, twos, locals_ = [], [], []
    for n in range(count):
        local = pltpu.make_async_copy(ins[n].at[rep], landed[n].at[0], local_sem.at[n])
        local.start()
        locals_.append(local)
        for i in range(1, 8):
            to = lax.rem(rep + i, 8)
            ones.append(
                send(ins[n].at[to], landed[n].at[i], s_one.at[n, i], r_one.at[n, i], (to, shard))
            )
    for n in range(count):
        locals_[n].wait()
        for i in range(7):
            ones[7 * n + i].wait_recv()
        rows = landed[n].shape[1]
        step = 16

        def add(t, _, n=n):
            at = pl.ds(pl.multiple_of(t * step, step), step)
            total = landed[n][0, at].astype(f32)
            for i in range(1, 8):
                total = total + landed[n][i, at].astype(f32)
            landed[n][0, at] = total.astype(bf16)
            return 0

        lax.fori_loop(0, rows // step, add, 0)
        local = pltpu.make_async_copy(landed[n].at[0], outs[n].at[rep], local_sem.at[n])
        local.start()
        locals_.append(local)
        for i in range(1, 8):
            to = lax.rem(rep + i, 8)
            twos.append(
                send(
                    landed[n].at[0], outs[n].at[rep], s_two.at[n, i], r_two.at[n, i], (to, shard)
                )
            )
    for n in range(count):
        locals_[count + n].wait()
        for i in range(1, 8):
            ref = outs[n].at[lax.rem(rep + 8 - i, 8)]
            pltpu.make_async_remote_copy(
                src_ref=ref,
                dst_ref=ref,
                send_sem=s_two.at[n, 0],
                recv_sem=r_two.at[n, i],
                device_id=(lax.rem(rep + 1, 8), shard),
                device_id_type=MESH,
            ).wait_recv()
    for copy in ones + twos:
        copy.wait_send()


def total_over_reps(arrays, collective):
    n = len(arrays)
    return pl.pallas_call(
        functools.partial(total_kernel, n),
        out_shape=tuple(jax.ShapeDtypeStruct(x.shape, x.dtype) for x in arrays),
        in_specs=[ANY] * n,
        out_specs=(ANY,) * n,
        scratch_shapes=[pltpu.VMEM(x.shape, bf16) for x in arrays]
        + [pltpu.SemaphoreType.DMA((n,))]
        + [pltpu.SemaphoreType.DMA((n, 8)) for _ in range(4)],
        compiler_params=params(collective, 60 * 2**20),
        name="total_over_reps",
    )(*arrays)


def swap_halves(values):
    lanes = values.shape[1]
    lane = lax.broadcasted_iota(jnp.int32, values.shape, 1)
    ahead = pltpu.roll(values, lanes - HEAD // 2, 1)
    behind = pltpu.roll(values, HEAD // 2, 1)
    return jnp.where(lax.rem(lane, HEAD) < HEAD // 2, ahead, behind)


def project_kernel(x_ref, w_ref, g_ref, cos_ref, sin_ref, q_ref, k_ref, v_ref, u_ref):
    i = pl.program_id(0)
    stream = x_ref[...].astype(f32)
    u_ref[...] = (stream * inverse_root(stream) * g_ref[...]).astype(bf16)
    core = lax.rem(lax.axis_index("shard"), 2)
    first = pl.multiple_of(lax.rem(i + core, 2) * OWN, OWN)
    own = pl.ds(first, OWN)
    queries = jnp.dot(u_ref[own, :], w_ref[:, :256], preferred_element_type=f32)
    cos, sin = cos_ref[own, :], sin_ref[own, :]
    cos, sin = jnp.concatenate([cos, cos], 1), jnp.concatenate([sin, sin], 1)
    turned = (queries * cos + swap_halves(queries) * sin).astype(bf16)
    turned = turned * jnp.bfloat16(HEAD**-0.5)
    for r in range(GROUP):
        q_ref[0, r * OWN : (r + 1) * OWN, :] = turned[:, r * HEAD : (r + 1) * HEAD]
    pairs = jnp.dot(u_ref[...], w_ref[:, 256:], preferred_element_type=f32)
    keys = pairs * cos_ref[...] + swap_halves(pairs) * sin_ref[...]
    k_ref[...] = keys[:, :HEAD].astype(bf16)
    lane = lax.broadcasted_iota(jnp.int32, pairs.shape, 1)
    v_ref[...] = jnp.where(lane < HEAD, pltpu.roll(pairs, HEAD, 1), 1.0).astype(bf16)


def project(x_all, weight, gain, cos, sin):
    return pl.pallas_call(
        project_kernel,
        grid=(BLOCKS,),
        in_specs=[
            pl.BlockSpec((KEYS, D), lambda i: (i, 0)),
            pl.BlockSpec((D, 384), lambda i: (0, 0)),
            pl.BlockSpec((1, D), lambda i: (0, 0)),
            pl.BlockSpec((KEYS, 128), lambda i: (i, 0)),
            pl.BlockSpec((KEYS, 128), lambda i: (i, 0)),
        ],
        out_specs=(
            pl.BlockSpec((1, ROWS, HEAD), lambda i: (i, 0, 0)),
            pl.BlockSpec((KEYS, HEAD), lambda i: (i, 0)),
            pl.BlockSpec((KEYS, 128), lambda i: (i, 0)),
            pl.BlockSpec((KEYS, D), lambda i: (i, 0)),
        ),
        out_shape=(
            jax.ShapeDtypeStruct((BLOCKS, ROWS, HEAD), bf16),
            jax.ShapeDtypeStruct((SEQ, HEAD), bf16),
            jax.ShapeDtypeStruct((SEQ, 128), bf16),
            jax.ShapeDtypeStruct((SEQ, D), bf16),
        ),
        compiler_params=pltpu.CompilerParams(vmem_limit_bytes=48 * 2**20),
        name="project_heads",
    )(x_all, weight, gain, cos, sin)


def contract(a, b, dims):
    return lax.dot_general(a, b, ((dims[0], dims[1]), ((), ())), preferred_element_type=f32)


def attend_kernel(q_ref, k_ref, v_ref, o_ref, l_ref):
    i = pl.program_id(0)
    core = lax.rem(lax.axis_index("shard"), 2)
    shift = lax.rem(i + core, 2) * OWN
    q = q_ref[0]

    def step(c, carry, last=False):
        top, total = carry
        at = pl.ds(pl.multiple_of(c * KEYS, KEYS), KEYS)
        scores = contract(q, k_ref[at, :], ((1,), (1,)))
        if last:
            row = lax.broadcasted_iota(jnp.int32, (OWN, KEYS), 0)
            column = lax.broadcasted_iota(jnp.int32, (OWN, KEYS), 1)
            bias = jnp.where(column <= row + shift, 0.0, -1e30)
            scores = scores + jnp.concatenate([bias] * GROUP, 0)
        high = jnp.maximum(top, jnp.max(scores, 1, keepdims=True))
        prob = jnp.exp(scores - high).astype(bf16)
        total = total * jnp.exp(top - high) + jnp.dot(
            prob, v_ref[at, :], preferred_element_type=f32
        )
        return high, total

    carry = (jnp.full((ROWS, 1), -1e30, f32), jnp.zeros((ROWS, 128), f32))
    carry = lax.fori_loop(0, i, step, carry)
    top, total = step(i, carry, True)
    weight = total[:, HEAD : HEAD + 1]
    result = (total[:, :HEAD] / weight).astype(bf16)
    o_ref[0] = jnp.concatenate([result[r * OWN : (r + 1) * OWN] for r in range(GROUP)], 1)
    l_ref[0] = jnp.broadcast_to(top + jnp.log(weight), (ROWS, 8))


def attend(q, k, v):
    return pl.pallas_call(
        attend_kernel,
        grid=(BLOCKS,),
        in_specs=[
            pl.BlockSpec((1, ROWS, HEAD), lambda i: (i, 0, 0)),
            pl.BlockSpec((SEQ, HEAD), lambda i: (0, 0)),
            pl.BlockSpec((SEQ, 128), lambda i: (0, 0)),
        ],
        out_specs=(
            pl.BlockSpec((1, OWN, GROUP * HEAD), lambda i: (i, 0, 0)),
            pl.BlockSpec((1, ROWS, 8), lambda i: (i, 0, 0)),
        ),
        out_shape=(
            jax.ShapeDtypeStruct((BLOCKS, OWN, GROUP * HEAD), bf16),
            jax.ShapeDtypeStruct((BLOCKS, ROWS, 8), f32),
        ),
        compiler_params=pltpu.CompilerParams(vmem_limit_bytes=48 * 2**20),
        name="attend",
    )(q, k, v)


def attend_back_kernel(
    q_ref, k_ref, v_ref, g_ref, l_ref, d_ref, cos_ref, sin_ref, qcos_ref, qsin_ref, dq_ref, dkv_ref,
    dk, dv, dq,
):
    i = pl.program_id(0)
    core = lax.rem(lax.axis_index("shard"), 2)
    shift = lax.rem(i + core, 2) * OWN

    @pl.when(i == 0)
    def _():
        dk[...] = jnp.zeros_like(dk)
        dv[...] = jnp.zeros_like(dv)

    q = q_ref[0]
    grad = jnp.concatenate([g_ref[0][:, r * HEAD : (r + 1) * HEAD] for r in range(GROUP)], 0)
    dq[...] = jnp.zeros_like(dq)

    def step(c, _, last=False):
        at = pl.ds(pl.multiple_of(c * KEYS, KEYS), KEYS)
        keys = k_ref[at, :]
        scores = contract(keys, q, ((1,), (1,)))
        if last:
            key = lax.broadcasted_iota(jnp.int32, (KEYS, OWN), 0)
            token = lax.broadcasted_iota(jnp.int32, (KEYS, OWN), 1)
            bias = jnp.where(key <= token + shift, 0.0, -1e30)
            scores = scores + jnp.concatenate([bias] * GROUP, 1)
        prob = jnp.exp(scores - l_ref[0])
        back = contract(v_ref[at, :HEAD], grad, ((1,), (1,)))
        slope = (prob * (back - d_ref[0])).astype(bf16)
        dv[at, :] += jnp.dot(prob.astype(bf16), grad, preferred_element_type=f32)
        dk[at, :] += jnp.dot(slope, q, preferred_element_type=f32)
        dq[...] += contract(slope, keys, ((0,), (0,)))
        return 0

    lax.fori_loop(0, i, step, 0)
    step(i, 0, True)
    wide = jnp.concatenate(
        [dq[r * OWN : (r + 1) * OWN, :] for r in range(GROUP)] + [jnp.zeros((OWN, HEAD), f32)], 1
    )
    wide = wide * (HEAD**-0.5)
    cos, sin = qcos_ref[...], qsin_ref[...]
    cos, sin = jnp.concatenate([cos, cos], 1), jnp.concatenate([sin, sin], 1)
    wide = wide * cos - swap_halves(wide) * sin
    dq_ref[0] = wide[:, : GROUP * HEAD].astype(bf16)

    @pl.when(i == BLOCKS - 1)
    def _():
        def turn(c, _):
            at = pl.ds(pl.multiple_of(c * OWN, OWN), OWN)
            both = jnp.concatenate([dk[at, :], dv[at, :]], 1)
            lane = lax.broadcasted_iota(jnp.int32, both.shape, 1)
            turned = both * cos_ref[at, :] - swap_halves(both) * sin_ref[at, :]
            dkv_ref[at, :] = jnp.where(lane < HEAD, turned, both).astype(bf16)
            return 0

        lax.fori_loop(0, SHARDS, turn, 0)


def attend_back(q, k, v, grad, lse, delta, cos, sin, core):
    def own(i):
        return (2 * i + lax.rem(i + lax.rem(lax.axis_index("shard"), 2), 2), 0)

    whole = lambda i: (0, 0)
    block = lambda i: (i, 0, 0)
    return pl.pallas_call(
        attend_back_kernel,
        grid=(BLOCKS,),
        in_specs=[
            pl.BlockSpec((1, ROWS, HEAD), block),
            pl.BlockSpec((SEQ, HEAD), whole),
            pl.BlockSpec((SEQ, 128), whole),
            pl.BlockSpec((1, OWN, GROUP * HEAD), block),
            pl.BlockSpec((1, 1, ROWS), block),
            pl.BlockSpec((1, 1, ROWS), block),
            pl.BlockSpec((SEQ, 128), whole),
            pl.BlockSpec((SEQ, 128), whole),
            pl.BlockSpec((OWN, 128), own),
            pl.BlockSpec((OWN, 128), own),
        ],
        out_specs=(
            pl.BlockSpec((1, OWN, GROUP * HEAD), block),
            pl.BlockSpec((SEQ, 128), whole),
        ),
        out_shape=(
            jax.ShapeDtypeStruct((BLOCKS, OWN, GROUP * HEAD), bf16),
            jax.ShapeDtypeStruct((SEQ, 128), bf16),
        ),
        scratch_shapes=[
            pltpu.VMEM((SEQ, HEAD), f32),
            pltpu.VMEM((SEQ, HEAD), f32),
            pltpu.VMEM((ROWS, HEAD), f32),
        ],
        compiler_params=pltpu.CompilerParams(vmem_limit_bytes=48 * 2**20),
        name="attend_back",
    )(q, k, v, grad, lse, delta, cos, sin, cos, sin)


def experts_kernel(u_ref, y_ref, c_ref, wl_ref, wd_ref, e_ref, out_ref, du_ref, act_ref, gl_ref):
    u = u_ref[...]
    lift = jnp.dot(u, wl_ref[...], preferred_element_type=f32)
    back = contract(y_ref[...], wd_ref[...], ((1,), (1,)))
    share = jnp.dot(c_ref[...], e_ref[...], preferred_element_type=f32)
    gate, raised = lift[:, :PAD], lift[:, PAD:]
    s = jax.nn.sigmoid(gate)
    swish = gate * s
    act = (share * swish * raised).astype(bf16)
    act_ref[...] = act
    back = back * share
    grad_gate = back * raised * s * (1.0 + gate * (1.0 - s))
    gl_ref[:, :PAD] = grad_gate.astype(bf16)
    gl_ref[:, PAD:] = (back * swish).astype(bf16)
    out_ref[...] = jnp.dot(act, wd_ref[...], preferred_element_type=f32).astype(bf16)
    du_ref[...] = contract(gl_ref[...], wl_ref[...], ((1,), (1,))).astype(bf16)


def experts(u_all, y_all, shares, wl, wd, spread):
    step = 384
    rows = lambda i: (i, 0)
    whole = lambda i: (0, 0)
    return pl.pallas_call(
        experts_kernel,
        grid=(SEQ // step,),
        in_specs=[
            pl.BlockSpec((step, D), rows),
            pl.BlockSpec((step, D), rows),
            pl.BlockSpec((step, 128), lambda i: (i, D // 128)),
            pl.BlockSpec((D, 2 * PAD), whole),
            pl.BlockSpec((PAD, D), whole),
            pl.BlockSpec((128, PAD), whole),
        ],
        out_specs=(
            pl.BlockSpec((step, D), rows),
            pl.BlockSpec((step, D), rows),
            pl.BlockSpec((step, PAD), rows),
            pl.BlockSpec((step, 2 * PAD), rows),
        ),
        out_shape=(
            jax.ShapeDtypeStruct((SEQ, D), bf16),
            jax.ShapeDtypeStruct((SEQ, D), bf16),
            jax.ShapeDtypeStruct((SEQ, PAD), bf16),
            jax.ShapeDtypeStruct((SEQ, 2 * PAD), bf16),
        ),
        compiler_params=pltpu.CompilerParams(vmem_limit_bytes=56 * 2**20),
        name="experts",
    )(u_all, y_all, shares, wl, wd, spread)


def tables():
    half = HEAD // 2
    frequency = np.float32(10000.0) ** (-(2.0 * np.arange(half, dtype=np.float32)) / HEAD)
    phases = np.arange(SEQ, dtype=np.float32)[:, None] * frequency[None, :].astype(np.float32)
    cos, sin = np.cos(phases).astype(np.float32), np.sin(phases).astype(np.float32)
    return (
        np.concatenate([cos, cos, cos, cos], 1),
        np.concatenate([-sin, sin, -sin, sin], 1),
    )


def spread_table():
    table = np.zeros((128, PAD), np.float32)
    for e in range(EXPERTS):
        table[e, 32 * e : 32 * e + 32] = 1.0
        table[16 + e, 32 * e : 32 * e + 32] = 1.0
    return table


def inverse_root(stream):
    return lax.rsqrt(jnp.mean(stream * stream, -1, keepdims=True) + norm_epsilon)


def norm_back(scaled, unit, inverse):
    return inverse * (scaled - unit * jnp.mean(scaled * unit, -1, keepdims=True))


def adam(weight, old_mean, square, gradient, step_rate, decay_rate):
    values = weight.astype(f32)
    moment = beta_one * old_mean.astype(f32) + (1.0 - beta_one) * gradient
    variance = beta_two * square.astype(f32) + (1.0 - beta_two) * gradient * gradient
    normed_step = (
        moment
        / (1.0 - beta_one**STEP)
        / (jnp.sqrt(variance / (1.0 - beta_two**STEP)) + adam_epsilon)
    )
    return (moment, variance, values - step_rate * (normed_step + decay_rate * values))


def per_device(
    layer_input,
    grad_output,
    routes,
    route_logits,
    norm_gains,
    inward,
    outward,
    lifting,
    lowering,
    mean_gains,
    mean_inward,
    mean_outward,
    mean_lifting,
    mean_lowering,
    square_gains,
    square_inward,
    square_outward,
    square_lifting,
    square_lowering,
):
    gains = norm_gains.astype(f32)
    cos, sin = (jnp.asarray(t) for t in tables())
    core = lax.rem(lax.axis_index("shard"), 2)

    by_head = jnp.concatenate(
        [
            inward[:, :1536].reshape(96, KV_HEADS, 192),
            jnp.broadcast_to(
                jnp.pad(norm_gains.T, ((0, 0), (0, HEAD - 2)))[:, None, :], (96, KV_HEADS, HEAD)
            ),
            inward[:, 1536:2048].reshape(96, KV_HEADS, HEAD),
            inward[:, 2048:].reshape(96, KV_HEADS, HEAD),
        ],
        2,
    ).transpose(1, 0, 2)
    by_unit = (
        lifting.reshape(96, EXPERTS, 2, SHARDS, 32)
        .transpose(3, 0, 2, 1, 4)
        .reshape(SHARDS, 96, 2, HID)
    )
    by_unit = jnp.pad(by_unit, ((0, 0), (0, 0), (0, 0), (0, PAD - HID)))
    by_unit = by_unit.reshape(SHARDS, 96, 2 * PAD)

    x_all = gather(layer_input, 2)

    head_weight, unit_weight = exchange((by_head, by_unit), ("heads", "all"), 1, "spread_weights")
    head_weight = head_weight.reshape(D, 384)
    unit_weight = unit_weight.reshape(D, 2 * PAD)
    down_weight = lowering.transpose(1, 0, 2).reshape(HID, D)
    down_weight = jnp.pad(down_weight, ((0, PAD - HID), (0, 0)))

    gain_rows = head_weight[:, 192:194].T.astype(f32)
    gain_one, gain_two = gain_rows[0:1], gain_rows[1:2]

    stream = layer_input.astype(f32)
    inverse_one = inverse_root(stream)
    unit_one = stream * inverse_one

    gates = jax.nn.softmax(route_logits, axis=-1)
    picked = routes[:, :, None] == jnp.arange(EXPERTS, dtype=jnp.int32)[None, None, :]
    combine = jnp.sum(jnp.where(picked, gates[:, :, None], 0.0), axis=1)
    high = lax.reduce_precision(combine, 8, 7)
    rest = combine - high
    shares = jnp.concatenate(
        [jnp.pad(high, ((0, 0), (0, 6))), jnp.pad(rest, ((0, 0), (0, 102)))], 1
    ).astype(bf16)
    y_all = lax.all_gather(
        jnp.concatenate([grad_output, shares], 1), "shard", axis=0, tiled=True
    )
    outward_all = lax.all_gather(outward, "shard", axis=0, tiled=True)

    q, k, v, u_one = project(x_all, head_weight, gain_one, cos, sin)
    attended, lse = attend(q, k, v)
    (own_attended,) = exchange((attended,), ("home",), 3, "attended_home")
    low_attended = own_attended.transpose(1, 0, 2).reshape(OWN, HEADS * HEAD)

    mixed = stream + jnp.dot(low_attended, outward_all, preferred_element_type=f32)
    inverse_two = inverse_root(mixed)
    unit_two = mixed * inverse_two
    low_two = (unit_two * gain_two).astype(bf16)
    u_two = gather(low_two, 4)

    out_part, du_part, act, grad_lift = experts(
        u_two, y_all, y_all, unit_weight, down_weight, jnp.asarray(spread_table(), bf16)
    )
    du, expert_out = reduce_blocks(
        (du_part.reshape(SHARDS, OWN, D), out_part.reshape(SHARDS, OWN, D)), 5
    )
    layer_output = mixed + expert_out
    lift_part = contract(u_two, grad_lift, ((0,), (0,))).astype(bf16)
    down_part = contract(act, y_all[:, :D], ((0,), (0,))).astype(bf16)

    grad_mixed = grad_output.astype(f32) + norm_back(du * gain_two, unit_two, inverse_two)
    low_mixed = grad_mixed.astype(bf16)
    grad_attended = contract(low_mixed, outward_all, ((1,), (1,))).astype(bf16)
    (head_grads,) = exchange(
        (grad_attended.reshape(OWN, KV_HEADS, 192).transpose(1, 0, 2),), ("away",), 6, "grads_away"
    )
    outward_part = contract(low_attended, low_mixed, ((0,), (0,))).astype(bf16)
    outward_own = lax.psum_scatter(outward_part, "shard", scatter_dimension=0, tiled=True)

    lse = lse[:, :, 0].reshape(BLOCKS, 1, ROWS)
    delta = jnp.sum(
        (attended.astype(f32) * head_grads.astype(f32)).reshape(BLOCKS, OWN, GROUP, HEAD), -1
    )
    delta = delta.transpose(0, 2, 1).reshape(BLOCKS, 1, ROWS)
    dq, dkv = attend_back(q, k, v, head_grads, lse, delta, cos, sin, core)
    inward_all = lax.all_gather(inward, "shard", axis=0, tiled=True)

    own_dq, own_dkv = exchange(
        (dq, dkv.reshape(SHARDS, OWN, 128)), ("home", "all"), 7, "pairs_home"
    )
    pairs = jnp.sum(own_dkv.reshape(CHIPS, 2, OWN, 128).astype(f32), 1)
    grad_joined = jnp.concatenate(
        [
            own_dq.transpose(1, 0, 2).reshape(OWN, 1536),
            pairs[:, :, :HEAD].transpose(1, 0, 2).reshape(OWN, 512).astype(bf16),
            pairs[:, :, HEAD:].transpose(1, 0, 2).reshape(OWN, 512).astype(bf16),
        ],
        1,
    )
    dh = contract(grad_joined, inward_all, ((1,), (1,)))
    input_grad = grad_mixed + norm_back(dh * gain_one, unit_one, inverse_one)

    u_pairs = u_one.reshape(BLOCKS, 2, OWN, D)
    even = u_pairs[:, 0]
    odd = u_pairs[:, 1]
    pick = (lax.rem(jnp.arange(BLOCKS), 2) == core)[:, None, None]
    u_own = jnp.where(pick, even, odd).reshape(BLOCKS * OWN, D)
    query_part = contract(u_own, dq.reshape(BLOCKS * OWN, 192), ((0,), (0,)))
    pair_part = contract(u_one, dkv, ((0,), (0,)))
    inward_part = jnp.concatenate([query_part, pair_part], 1).astype(bf16)
    inward_pad = jnp.pad(inward_part, ((0, 0), (0, 64)))
    lift_got, inward_got = exchange(
        (lift_part.reshape(SHARDS, 96, 2 * PAD), inward_pad.reshape(SHARDS, 96, 384)),
        ("all", "all"),
        8,
        "grads_to_owners",
    )
    inward_sum = jnp.sum(inward_got.reshape(CHIPS, 2, 96, 384).astype(f32), 1).astype(bf16)
    lift_sum, down_sum, inward_sum, outward_sum = total_over_reps(
        (
            lift_got.reshape(REPS, 192, 2 * PAD),
            down_part.reshape(REPS, 48, D),
            inward_sum,
            outward_own.reshape(REPS, 16, 1152),
        ),
        9,
    )
    lift_grad = (
        lift_sum.reshape(SHARDS, 96, 2, PAD)[..., :HID]
        .reshape(SHARDS, 96, 2, EXPERTS, 32)
        .transpose(1, 3, 2, 0, 4)
        .reshape(96, EXPERTS, 1024)
        .astype(f32)
    )
    down_grad = down_sum.reshape(PAD, D)[:HID].reshape(EXPERTS, 32, D).transpose(1, 0, 2).astype(f32)
    inward_sum = inward_sum.transpose(1, 0, 2)
    inward_grad = jnp.concatenate(
        [
            inward_sum[:, :, :192].reshape(96, 1536),
            inward_sum[:, :, 192:256].reshape(96, 512),
            inward_sum[:, :, 256:320].reshape(96, 512),
        ],
        1,
    ).astype(f32)
    outward_grad = outward_sum.reshape(96, D).astype(f32)
    gain_grad = jnp.stack(
        [
            jnp.sum(inward.astype(f32) * inward_grad, 1),
            jnp.sum(lifting.astype(f32) * lift_grad, (1, 2)),
        ]
    )
    gain_grad = gain_grad / gains

    new_gains = adam(norm_gains, mean_gains, square_gains, gain_grad, rate_gains, 0.0)
    new_inward = adam(inward, mean_inward, square_inward, inward_grad, rate_inward, weight_decay)
    new_outward = adam(
        outward, mean_outward, square_outward, outward_grad, rate_outward, weight_decay
    )
    new_lifting = adam(lifting, mean_lifting, square_lifting, lift_grad, rate_lifting, weight_decay)
    new_lowering = adam(
        lowering, mean_lowering, square_lowering, down_grad, rate_lowering, weight_decay
    )
    return (
        layer_output,
        input_grad,
        new_gains[0],
        new_inward[0],
        new_outward[0],
        new_lifting[0],
        new_lowering[0],
        new_gains[1],
        new_inward[1],
        new_outward[1],
        new_lifting[1],
        new_lowering[1],
        new_gains[2],
        new_inward[2],
        new_outward[2],
        new_lifting[2],
        new_lowering[2],
    )


def solution(mesh):
    tokens = P(("rep", "shard"), None)
    gains, flat, deep = P(None, "shard"), P("shard", None), P("shard", None, None)
    weights = (gains, flat, flat, deep, deep)
    return jax.shard_map(
        per_device,
        mesh=mesh,
        in_specs=(tokens,) * 4 + weights * 3,
        out_specs=(tokens,) * 2 + weights * 3,
        check_vma=False,
    )
```

```python
import functools

import jax
import jax.numpy as jnp
import numpy as np
from jax import lax
from jax.experimental import pallas as pl
from jax.experimental.pallas import tpu as pltpu
from jax.sharding import PartitionSpec as P

HEADS = 24
KV_HEADS = 8
HEAD = 64
GROUP = HEADS // KV_HEADS
FF_EXP = 512
EXPERTS = 10
STEP = 10

norm_epsilon = 1e-06
beta_one = 0.9
beta_two = 0.95
adam_epsilon = 1e-08
weight_decay = 0.1
rate_gains = 0.5
rate_inward = 0.05
rate_outward = 0.3
rate_lifting = 0.05
rate_lowering = 0.3

SHARDS = 16
CHIPS = 8
REPS = 8
OWN = 192
SEQ = OWN * SHARDS
D = 1536
HID = 320
BLOCKS = 8
ROWS = GROUP * OWN
KEYS = 2 * OWN

MESH = pl.DeviceIdType.MESH
bf16 = jnp.bfloat16
f32 = jnp.float32


def place():
    rep = lax.axis_index("rep")
    shard = lax.axis_index("shard")
    return rep, shard


def greet(devices):
    barrier = pltpu.get_barrier_semaphore()
    for device in devices:
        pl.semaphore_signal(barrier, inc=1, device_id=device, device_id_type=MESH)
    pl.semaphore_wait(barrier, len(devices))


def send(src, dst, send_sem, recv_sem, device):
    copy = pltpu.make_async_remote_copy(
        src_ref=src,
        dst_ref=dst,
        send_sem=send_sem,
        recv_sem=recv_sem,
        device_id=device,
        device_id_type=MESH,
    )
    copy.start()
    return copy


def params(collective, vmem=None):
    return pltpu.CompilerParams(
        collective_id=collective, has_side_effects=True, vmem_limit_bytes=vmem
    )


ANY = pl.BlockSpec(memory_space=pl.ANY)
VMEM = pl.BlockSpec(memory_space=pltpu.VMEM)


def gather_kernel(with_parts, *refs):
    if with_parts:
        x_ref, w_ref, o_ref, p_ref, local_sem, send_sem, recv_sem, s_part, r_part = refs
    else:
        x_ref, o_ref, local_sem, send_sem, recv_sem = refs
    rep, shard = place()
    half = x_ref.shape[0] // 2
    core = lax.rem(shard, 2)
    chip = shard // 2
    y = lax.rem(chip, 2)
    sib = shard + 1 - 2 * core
    pair = shard + 2 - 4 * y
    up = lax.rem(shard + 4, 16)
    down = lax.rem(shard + 12, 16)
    far = lax.rem(shard + 8, 16)
    peers = [2 * lax.rem(chip + i, 8) + core for i in range(1, 8)]

    def other(block):
        return block + 2 - 4 * y

    if with_parts:
        greet([(rep, sib)] + [(rep, p) for p in peers])
    else:
        greet([(rep, sib), (rep, pair), (rep, up), (rep, down)])
    own = pltpu.make_async_copy(x_ref, o_ref.at[shard], local_sem.at[0])
    own.start()
    sent = []

    def put(src, dst, slot, device):
        sent.append(send(src, dst, send_sem.at[len(sent)], recv_sem.at[slot], (rep, device)))

    def forward(block, slot, device, rows=None):
        ref = o_ref.at[block] if rows is None else o_ref.at[block, rows]
        put(ref, ref, slot, device)

    def landed(ref, sem):
        pltpu.make_async_remote_copy(
            src_ref=ref,
            dst_ref=ref,
            send_sem=send_sem.at[0],
            recv_sem=sem,
            device_id=(rep, sib),
            device_id_type=MESH,
        ).wait_recv()

    def arrived(block, slot, rows=None):
        landed(o_ref.at[block] if rows is None else o_ref.at[block, rows], recv_sem.at[slot])

    top, bottom = pl.ds(0, half), pl.ds(half, half)
    put(x_ref, o_ref.at[shard], 0, pair)
    put(x_ref, o_ref.at[shard], 1, up)
    put(x_ref, o_ref.at[shard], 5, down)
    put(x_ref, o_ref.at[shard], 9, sib)
    parts = []
    if with_parts:
        mine = pltpu.make_async_copy(w_ref.at[chip], p_ref.at[shard], local_sem.at[1])
        mine.start()
        parts.append(
            send(w_ref.at[chip], p_ref.at[shard], s_part.at[0], r_part.at[0], (rep, sib))
        )
        for i in range(1, 8):
            c = lax.rem(chip + i, 8)
            parts.append(
                send(
                    w_ref.at[c], p_ref.at[shard], s_part.at[i], r_part.at[i], (rep, 2 * c + core)
                )
            )
    arrived(pair, 0)
    forward(pair, 2, up)
    forward(pair, 6, down)
    forward(pair, 10, sib)
    arrived(down, 1)
    forward(down, 3, up, top)
    forward(down, 11, sib)
    arrived(up, 5)
    forward(up, 7, down, bottom)
    forward(up, 12, sib)
    arrived(other(down), 2)
    forward(other(down), 4, up, top)
    forward(other(down), 13, sib)
    arrived(other(up), 6)
    forward(other(up), 8, down, bottom)
    forward(other(up), 14, sib)
    if with_parts:
        for i in range(1, 8):
            block = 2 * lax.rem(chip + 8 - i, 8) + core
            landed(p_ref.at[block], r_part.at[i])
            parts.append(
                send(
                    p_ref.at[block], p_ref.at[block], s_part.at[7 + i], r_part.at[7 + i], (rep, sib)
                )
            )
    arrived(far, 3, top)
    forward(far, 15, sib, top)
    arrived(far, 7, bottom)
    forward(far, 16, sib, bottom)
    arrived(other(far), 4, top)
    forward(other(far), 17, sib, top)
    arrived(other(far), 8, bottom)
    forward(other(far), 18, sib, bottom)

    def twin(block):
        return block + 1 - 2 * core

    if with_parts:
        landed(p_ref.at[sib], r_part.at[0])
        for i in range(1, 8):
            landed(p_ref.at[twin(2 * lax.rem(chip + 8 - i, 8) + core)], r_part.at[7 + i])
        mine.wait()
    arrived(twin(shard), 9)
    arrived(twin(pair), 10)
    arrived(twin(down), 11)
    arrived(twin(up), 12)
    arrived(twin(other(down)), 13)
    arrived(twin(other(up)), 14)
    arrived(twin(far), 15, top)
    arrived(twin(far), 16, bottom)
    arrived(twin(other(far)), 17, top)
    arrived(twin(other(far)), 18, bottom)
    for copy in sent + parts:
        copy.wait_send()
    own.wait()


def gather(x, collective, parts=None):
    rows, columns = x.shape
    extra = () if parts is None else (parts,)
    shapes = (jax.ShapeDtypeStruct((SHARDS, rows, columns), x.dtype),)
    if extra:
        shapes += (jax.ShapeDtypeStruct((SHARDS,) + parts.shape[1:], parts.dtype),)
    out = pl.pallas_call(
        functools.partial(gather_kernel, bool(extra)),
        out_shape=shapes,
        in_specs=[ANY] * len(shapes),
        out_specs=(ANY,) * len(shapes),
        scratch_shapes=[
            pltpu.SemaphoreType.DMA((2,)),
            pltpu.SemaphoreType.DMA((21,)),
            pltpu.SemaphoreType.DMA((19,)),
        ]
        + [pltpu.SemaphoreType.DMA((15,))] * (2 * len(extra)),
        compiler_params=params(collective),
        name="gather_rows",
    )(x, *extra)
    return (out[0].reshape(SHARDS * rows, columns),) + tuple(out[1:])


def exchange_kernel(kinds, *refs):
    count = len(kinds)
    ins, outs = refs[:count], refs[count : 2 * count]
    local_sem, send_sem, recv_sem = refs[2 * count :]
    rep, shard = place()
    core = lax.rem(shard, 2)
    chip = shard // 2
    greet([(rep, lax.rem(shard + i, 16)) for i in range(1, 16)])
    sent, due = [], []

    def mine(device):
        return lax.rem(lax.rem(device, 2) + lax.rem(device // 2, 2), 2)

    for n, kind in enumerate(kinds):
        x, o = ins[n], outs[n]
        if kind == "all":
            local = pltpu.make_async_copy(x.at[shard], o.at[shard], local_sem.at[n])
            local.start()
            due.append(local)
            for i in range(1, 16):
                to = lax.rem(shard + i, 16)
                sent.append(
                    send(x.at[to], o.at[shard], send_sem.at[n, i], recv_sem.at[n, i], (rep, to))
                )
        elif kind == "heads":
            local = pltpu.make_async_copy(x.at[chip], o.at[shard], local_sem.at[n])
            local.start()
            due.append(local)
            for i in range(1, 16):
                to = lax.rem(shard + i, 16)
                sent.append(
                    send(
                        x.at[to // 2], o.at[shard], send_sem.at[n, i], recv_sem.at[n, i], (rep, to)
                    )
                )
        elif kind == "home":
            for i in range(8):
                c = lax.rem(chip + i, 8)
                to = 2 * c + lax.rem(c + core, 2)
                if i == 0:
                    same = to == shard

                    @pl.when(same)
                    def _(x=x, o=o, c=c, n=n):
                        local = pltpu.make_async_copy(x.at[c], o.at[chip], local_sem.at[n])
                        local.start()
                        local.wait()

                    @pl.when(jnp.logical_not(same))
                    def _(x=x, o=o, c=c, n=n, to=to):
                        copy = send(
                            x.at[c], o.at[chip], send_sem.at[n, 0], recv_sem.at[n, 0], (rep, to)
                        )
                        copy.wait_send()

                else:
                    sent.append(
                        send(
                            x.at[c], o.at[chip], send_sem.at[n, i], recv_sem.at[n, i], (rep, to)
                        )
                    )
        elif kind == "away":
            for i in range(8):
                c = lax.rem(chip + i, 8)
                to = 2 * c + mine(shard)
                if i == 0:
                    same = to == shard

                    @pl.when(same)
                    def _(x=x, o=o, c=c, n=n):
                        local = pltpu.make_async_copy(x.at[c], o.at[chip], local_sem.at[n])
                        local.start()
                        local.wait()

                    @pl.when(jnp.logical_not(same))
                    def _(x=x, o=o, c=c, n=n, to=to):
                        copy = send(
                            x.at[c], o.at[chip], send_sem.at[n, 0], recv_sem.at[n, 0], (rep, to)
                        )
                        copy.wait_send()

                else:
                    sent.append(
                        send(
                            x.at[c], o.at[chip], send_sem.at[n, i], recv_sem.at[n, i], (rep, to)
                        )
                    )

    def arrived(ref, n, i):
        pltpu.make_async_remote_copy(
            src_ref=ref,
            dst_ref=ref,
            send_sem=send_sem.at[n, 0],
            recv_sem=recv_sem.at[n, i],
            device_id=(rep, lax.rem(shard + 1, 16)),
            device_id_type=MESH,
        ).wait_recv()

    for n, kind in enumerate(kinds):
        o = outs[n]
        if kind in ("all", "heads"):
            for i in range(1, 16):
                arrived(o.at[lax.rem(shard + 16 - i, 16)], n, i)
        else:
            away = kind == "away"
            first = (
                2 * chip + lax.rem(chip + core, 2) if away else 2 * chip + mine(shard)
            )

            @pl.when(first != shard)
            def _(o=o, n=n):
                arrived(o.at[chip], n, 0)

            for i in range(1, 8):
                arrived(o.at[lax.rem(chip + 8 - i, 8)], n, i)
    for copy in sent:
        copy.wait_send()
    for copy in due:
        copy.wait()


def exchange(arrays, kinds, collective, name):
    shapes = []
    for x, kind in zip(arrays, kinds):
        lead = 16 if kind in ("all", "heads") else 8
        shapes.append(jax.ShapeDtypeStruct((lead,) + x.shape[1:], x.dtype))
    n = len(arrays)
    return pl.pallas_call(
        functools.partial(exchange_kernel, kinds),
        out_shape=tuple(shapes),
        in_specs=[ANY] * n,
        out_specs=(ANY,) * n,
        scratch_shapes=[
            pltpu.SemaphoreType.DMA((n,)),
            pltpu.SemaphoreType.DMA((n, 16)),
            pltpu.SemaphoreType.DMA((n, 16)),
        ],
        compiler_params=params(collective),
        name=name,
    )(*arrays)


SPLIT = 768


def reduce_kernel(*refs):
    du_ref, out_ref, lift_ref, down_ref = refs[:4]
    ins = (du_ref, out_ref)
    outs, lift_o, down_o = refs[4:6], refs[6], refs[7]
    (
        held, near, land_a, land_b, land_c, land_d,
        lift_own, lift_land, lift_half, down_own, down_land, down_half,
        load_sem, s_near, r_near, s_one, r_one, s_two, r_two,
        a_load, a_s1, a_r1, a_s2, a_r2, a_s3, a_r3, a_s4, a_r4, a_out,
    ) = refs[8:]
    rep, shard = place()
    core = lax.rem(shard, 2)
    chip = shard // 2
    y = lax.rem(chip, 2)
    z = chip // 2
    sib = shard + 1 - 2 * core
    pair = shard + 2 - 4 * y
    x, far_y = rep // 2, lax.rem(rep, 2)
    mate = rep + 1 - 2 * far_y
    first, last = pl.ds(0, SPLIT), pl.ds(SPLIT, D - SPLIT)

    def ahead(dz):
        return lax.rem(z + dz, 4)

    def device(zz, yy):
        return 4 * zz + 2 * yy + core

    def along(dx):
        return 2 * lax.rem(x + dx, 4) + far_y

    greet(
        [(rep, sib), (rep, pair)]
        + [(rep, device(ahead(dz), y)) for dz in (1, 2, 3)]
        + [(along(dx), shard) for dx in (1, 2, 3)]
        + [(mate, shard)]
    )

    def block(j):
        dz, dy = j // 2, j % 2
        return 2 * ahead(dz) + (y if dy == 0 else 1 - y)

    order = [1, 3, 5, 7, 2, 4, 6, 0]
    nears, loads = {}, {}
    for n in range(2):
        for j in order:
            c = block(j)
            nears[n, j] = send(
                ins[n].at[2 * c + 1 - core], near.at[n, j], s_near.at[n, j], r_near.at[n, j], (rep, sib)
            )
            loads[n, j] = pltpu.make_async_copy(
                ins[n].at[2 * c + core], held.at[n, j], load_sem.at[n, j]
            )
            loads[n, j].start()
    sums = ((lift_ref, lift_own, lift_land, lift_half, lift_o), (down_ref, down_own, down_land, down_half, down_o))
    steps_one, steps_load = [], []
    for m, (src, own, land, half, dst) in enumerate(sums):
        load = pltpu.make_async_copy(src.at[x], own, a_load.at[m])
        load.start()
        steps_load.append(load)
        for dx in (1, 2, 3):
            steps_one.append(
                send(
                    src.at[lax.rem(x + dx, 4)], land.at[dx - 1], a_s1.at[m, dx], a_r1.at[m, dx],
                    (along(dx), shard),
                )
            )
    ones = {}
    for n in range(2):
        for j in order:
            nears[n, j].wait_recv()
            loads[n, j].wait()

            def add(t, _, n=n, j=j):
                at = pl.ds(pl.multiple_of(t * 32, 32), 32)
                held[n, j, at] = (
                    held[n, j, at].astype(f32) + near[n, j, at].astype(f32)
                ).astype(bf16)
                return 0

            lax.fori_loop(0, OWN // 32, add, 0)
            dz, dy = j // 2, j % 2
            if dy:
                ones[n, 0, j] = send(
                    held.at[n, j, :, first], land_a.at[n, dz], s_one.at[n, 0, j], r_one.at[n, 0, j],
                    (rep, pair),
                )
            if dz:
                ones[n, 1, j] = send(
                    held.at[n, j, :, last], land_b.at[n, j - 2], s_one.at[n, 1, j], r_one.at[n, 1, j],
                    (rep, device(ahead(dz), y)),
                )

    step = 32

    def rows_of(t):
        return pl.ds(pl.multiple_of(t * step, step), step)

    twos = {}

    def first_sums(n):
        for dz in (1, 2, 3, 0):
            ones[n, 0, 2 * dz + 1].wait_recv()

            def add(t, _, dz=dz):
                at = rows_of(t)
                held[n, 2 * dz, at, first] = (
                    held[n, 2 * dz, at, first].astype(f32) + land_a[n, dz, at].astype(f32)
                ).astype(bf16)
                return 0

            lax.fori_loop(0, OWN // step, add, 0)
            if dz:
                twos[n, 0, dz] = send(
                    held.at[n, 2 * dz, :, first], land_c.at[n, dz - 1], s_two.at[n, dz], r_two.at[n, dz],
                    (rep, device(ahead(dz), y)),
                )
        for dy in (1, 0):
            for dz in (1, 2, 3):
                ones[n, 1, 2 * dz + dy].wait_recv()

            def add(t, _, dy=dy):
                at = rows_of(t)
                total = held[n, dy, at, last].astype(f32)
                for dz in (1, 2, 3):
                    total = total + land_b[n, 2 * dz + dy - 2, at].astype(f32)
                held[n, dy, at, last] = total.astype(bf16)
                return 0

            lax.fori_loop(0, OWN // step, add, 0)
            if dy:
                twos[n, 1, 0] = send(
                    held.at[n, 1, :, last], land_d.at[n], s_two.at[n, 0], r_two.at[n, 0], (rep, pair)
                )

    def last_sums(n):
        for dz in (1, 2, 3):
            twos[n, 0, dz].wait_recv()
        twos[n, 1, 0].wait_recv()

        def add(t, _):
            at = rows_of(t)
            total = held[n, 0, at, first].astype(f32)
            for dz in (1, 2, 3):
                total = total + land_c[n, dz - 1, at].astype(f32)
            outs[n][at, first] = total
            outs[n][at, last] = held[n, 0, at, last].astype(f32) + land_d[n, at].astype(f32)
            return 0

        lax.fori_loop(0, OWN // step, add, 0)

    first_sums(0)
    for load in steps_load:
        load.wait()
    steps_two = []
    for m, (src, own, land, half, dst) in enumerate(sums):
        for dx in (1, 2, 3):
            steps_one[3 * m + dx - 1].wait_recv()
        size = own.shape[1]
        for h in (0, 1):

            def add(t, _, own=own, land=land, h=h):
                at = pl.ds(pl.multiple_of(t * 16, 16), 16)
                total = own[h, at].astype(f32)
                for dx in range(3):
                    total = total + land[dx, h, at].astype(f32)
                own[h, at] = total.astype(bf16)
                return 0

            lax.fori_loop(0, size // 16, add, 0)
        steps_two.append(
            send(own.at[1 - far_y], half, a_s2.at[m], a_r2.at[m], (mate, shard))
        )
    first_sums(1)
    steps_three, steps_four = [], []
    for m, (src, own, land, half, dst) in enumerate(sums):
        steps_two[m].wait_recv()

        def add(t, _, own=own, half=half):
            at = pl.ds(pl.multiple_of(t * 16, 16), 16)
            half[at] = (own[far_y, at].astype(f32) + half[at].astype(f32)).astype(bf16)
            return 0

        lax.fori_loop(0, own.shape[1] // 16, add, 0)
        steps_three.append(
            send(half, dst.at[x, far_y], a_s3.at[m], a_r3.at[m], (mate, shard))
        )
        keep = pltpu.make_async_copy(half, dst.at[x, far_y], a_out.at[m])
        keep.start()
        steps_load.append(keep)
        for dx in (1, 2, 3):
            steps_four.append(
                send(
                    half, dst.at[x, far_y], a_s4.at[m, 0, dx], a_r4.at[m, 0, dx], (along(dx), shard)
                )
            )
    last_sums(0)

    def landed(ref, sem):
        pltpu.make_async_remote_copy(
            src_ref=ref,
            dst_ref=ref,
            send_sem=a_s3.at[0],
            recv_sem=sem,
            device_id=(mate, shard),
            device_id_type=MESH,
        ).wait_recv()

    for m, (src, own, land, half, dst) in enumerate(sums):
        landed(dst.at[x, 1 - far_y], a_r3.at[m])
        for dx in (1, 2, 3):
            ref = dst.at[x, 1 - far_y]
            steps_four.append(
                send(ref, ref, a_s4.at[m, 1, dx], a_r4.at[m, 1, dx], (along(dx), shard))
            )
    last_sums(1)
    for m, (src, own, land, half, dst) in enumerate(sums):
        for dx in (1, 2, 3):
            back = lax.rem(x + 4 - dx, 4)
            landed(dst.at[back, far_y], a_r4.at[m, 0, dx])
            landed(dst.at[back, 1 - far_y], a_r4.at[m, 1, dx])
    for keep in steps_load[2:]:
        keep.wait()
    for copies in (nears.values(), ones.values(), twos.values(), steps_one, steps_two, steps_three, steps_four):
        for copy in copies:
            copy.wait_send()


def reduce_blocks(du, out, lift, down, collective):
    lift = lift.reshape(4, 2, 192, 2 * HID)
    down = down.reshape(4, 80, 2, D // 2).transpose(0, 2, 1, 3)
    dma = pltpu.SemaphoreType.DMA
    result = pl.pallas_call(
        reduce_kernel,
        out_shape=(
            jax.ShapeDtypeStruct((OWN, D), f32),
            jax.ShapeDtypeStruct((OWN, D), f32),
            jax.ShapeDtypeStruct(lift.shape, bf16),
            jax.ShapeDtypeStruct(down.shape, bf16),
        ),
        in_specs=[ANY] * 4,
        out_specs=(VMEM, VMEM, ANY, ANY),
        scratch_shapes=[
            pltpu.VMEM((2, 8, OWN, D), bf16),
            pltpu.VMEM((2, 8, OWN, D), bf16),
            pltpu.VMEM((2, 4, OWN, SPLIT), bf16),
            pltpu.VMEM((2, 6, OWN, D - SPLIT), bf16),
            pltpu.VMEM((2, 3, OWN, SPLIT), bf16),
            pltpu.VMEM((2, OWN, D - SPLIT), bf16),
            pltpu.VMEM(lift.shape[1:], bf16),
            pltpu.VMEM((3,) + lift.shape[1:], bf16),
            pltpu.VMEM(lift.shape[2:], bf16),
            pltpu.VMEM(down.shape[1:], bf16),
            pltpu.VMEM((3,) + down.shape[1:], bf16),
            pltpu.VMEM(down.shape[2:], bf16),
            dma((2, 8)),
            dma((2, 8)),
            dma((2, 8)),
            dma((2, 2, 8)),
            dma((2, 2, 8)),
            dma((2, 4)),
            dma((2, 4)),
            dma((2,)),
            dma((2, 4)),
            dma((2, 4)),
            dma((2,)),
            dma((2,)),
            dma((2,)),
            dma((2,)),
            dma((2, 2, 4)),
            dma((2, 2, 4)),
            dma((2,)),
        ],
        compiler_params=params(collective, 60 * 2**20),
        name="reduce_rows",
    )(du, out, lift, down)
    du, out, lift, down = result
    down = down.transpose(0, 2, 1, 3).reshape(HID, D)
    return du, out, lift.reshape(D, 2 * HID), down


def total_kernel(count, *refs):
    ins, outs = refs[:count], refs[count : 2 * count]
    landed = refs[2 * count : 3 * count]
    local_sem, s_one, r_one, s_two, r_two = refs[3 * count :]
    rep, shard = place()
    greet([(lax.rem(rep + i, 8), shard) for i in range(1, 8)])
    ones, twos, locals_ = [], [], []
    for n in range(count):
        local = pltpu.make_async_copy(ins[n].at[rep], landed[n].at[0], local_sem.at[n])
        local.start()
        locals_.append(local)
        for i in range(1, 8):
            to = lax.rem(rep + i, 8)
            ones.append(
                send(ins[n].at[to], landed[n].at[i], s_one.at[n, i], r_one.at[n, i], (to, shard))
            )
    for n in range(count):
        locals_[n].wait()
        for i in range(7):
            ones[7 * n + i].wait_recv()
        rows = landed[n].shape[1]
        step = 16

        def add(t, _, n=n):
            at = pl.ds(pl.multiple_of(t * step, step), step)
            total = landed[n][0, at].astype(f32)
            for i in range(1, 8):
                total = total + landed[n][i, at].astype(f32)
            landed[n][0, at] = total.astype(bf16)
            return 0

        lax.fori_loop(0, rows // step, add, 0)
        local = pltpu.make_async_copy(landed[n].at[0], outs[n].at[rep], local_sem.at[n])
        local.start()
        locals_.append(local)
        for i in range(1, 8):
            to = lax.rem(rep + i, 8)
            twos.append(
                send(
                    landed[n].at[0], outs[n].at[rep], s_two.at[n, i], r_two.at[n, i], (to, shard)
                )
            )
    for n in range(count):
        locals_[count + n].wait()
        for i in range(1, 8):
            ref = outs[n].at[lax.rem(rep + 8 - i, 8)]
            pltpu.make_async_remote_copy(
                src_ref=ref,
                dst_ref=ref,
                send_sem=s_two.at[n, 0],
                recv_sem=r_two.at[n, i],
                device_id=(lax.rem(rep + 1, 8), shard),
                device_id_type=MESH,
            ).wait_recv()
    for copy in ones + twos:
        copy.wait_send()


def total_over_reps(arrays, collective):
    n = len(arrays)
    return pl.pallas_call(
        functools.partial(total_kernel, n),
        out_shape=tuple(jax.ShapeDtypeStruct(x.shape, x.dtype) for x in arrays),
        in_specs=[ANY] * n,
        out_specs=(ANY,) * n,
        scratch_shapes=[pltpu.VMEM(x.shape, bf16) for x in arrays]
        + [pltpu.SemaphoreType.DMA((n,))]
        + [pltpu.SemaphoreType.DMA((n, 8)) for _ in range(4)],
        compiler_params=params(collective, 60 * 2**20),
        name="total_over_reps",
    )(*arrays)


def swap_halves(values):
    lanes = values.shape[1]
    lane = lax.broadcasted_iota(jnp.int32, values.shape, 1)
    ahead = pltpu.roll(values, lanes - HEAD // 2, 1)
    behind = pltpu.roll(values, HEAD // 2, 1)
    return jnp.where(lax.rem(lane, HEAD) < HEAD // 2, ahead, behind)


def project_kernel(x_ref, w_ref, g_ref, cos_ref, sin_ref, q_ref, k_ref, v_ref, u_ref):
    i = pl.program_id(0)
    stream = x_ref[...].astype(f32)
    u_ref[...] = (stream * inverse_root(stream) * g_ref[...]).astype(bf16)
    core = lax.rem(lax.axis_index("shard"), 2)
    first = pl.multiple_of(lax.rem(i + core, 2) * OWN, OWN)
    own = pl.ds(first, OWN)
    queries = jnp.dot(u_ref[own, :], w_ref[:, :256], preferred_element_type=f32)
    cos, sin = cos_ref[own, :], sin_ref[own, :]
    cos, sin = jnp.concatenate([cos, cos], 1), jnp.concatenate([sin, sin], 1)
    turned = (queries * cos + swap_halves(queries) * sin).astype(bf16)
    turned = turned * jnp.bfloat16(HEAD**-0.5)
    for r in range(GROUP):
        q_ref[0, r * OWN : (r + 1) * OWN, :] = turned[:, r * HEAD : (r + 1) * HEAD]
    pairs = jnp.dot(u_ref[...], w_ref[:, 256:], preferred_element_type=f32)
    keys = pairs * cos_ref[...] + swap_halves(pairs) * sin_ref[...]
    k_ref[...] = keys[:, :HEAD].astype(bf16)
    lane = lax.broadcasted_iota(jnp.int32, pairs.shape, 1)
    v_ref[...] = jnp.where(lane < HEAD, pltpu.roll(pairs, HEAD, 1), 1.0).astype(bf16)


def project(x_all, weight, gain, cos, sin):
    return pl.pallas_call(
        project_kernel,
        grid=(BLOCKS,),
        in_specs=[
            pl.BlockSpec((KEYS, D), lambda i: (i, 0)),
            pl.BlockSpec((D, 384), lambda i: (0, 0)),
            pl.BlockSpec((1, D), lambda i: (0, 0)),
            pl.BlockSpec((KEYS, 128), lambda i: (i, 0)),
            pl.BlockSpec((KEYS, 128), lambda i: (i, 0)),
        ],
        out_specs=(
            pl.BlockSpec((1, ROWS, HEAD), lambda i: (i, 0, 0)),
            pl.BlockSpec((KEYS, HEAD), lambda i: (i, 0)),
            pl.BlockSpec((KEYS, 128), lambda i: (i, 0)),
            pl.BlockSpec((KEYS, D), lambda i: (i, 0)),
        ),
        out_shape=(
            jax.ShapeDtypeStruct((BLOCKS, ROWS, HEAD), bf16),
            jax.ShapeDtypeStruct((SEQ, HEAD), bf16),
            jax.ShapeDtypeStruct((SEQ, 128), bf16),
            jax.ShapeDtypeStruct((SEQ, D), bf16),
        ),
        compiler_params=pltpu.CompilerParams(vmem_limit_bytes=48 * 2**20),
        name="project_heads",
    )(x_all, weight, gain, cos, sin)


def contract(a, b, dims, precision=None):
    return lax.dot_general(
        a, b, ((dims[0], dims[1]), ((), ())), preferred_element_type=f32, precision=precision
    )


def behind(x, o, local_sem, s_sem, r_sem):
    rep, shard = place()
    local = pltpu.make_async_copy(x.at[shard], o.at[shard], local_sem)

    def copy(i, slot):
        to = lax.rem(shard + i, 16)
        return pltpu.make_async_remote_copy(
            src_ref=x.at[to],
            dst_ref=o.at[slot],
            send_sem=s_sem.at[i],
            recv_sem=r_sem.at[i],
            device_id=(rep, to),
            device_id_type=MESH,
        )

    def start():
        local.start()
        for i in range(1, 16):
            copy(i, shard).start()

    def wait():
        local.wait()
        for i in range(1, 16):
            copy(i, lax.rem(shard + 16 - i, 16)).wait_recv()
        for i in range(1, 16):
            copy(i, shard).wait_send()

    return start, wait


def attend_kernel(q_ref, k_ref, v_ref, b_ref, o_ref, l_ref, bo_ref, local_sem, s_sem, r_sem):
    i = pl.program_id(0)
    start, wait = behind(b_ref, bo_ref, local_sem.at[0], s_sem, r_sem)

    @pl.when(i == 0)
    def _():
        rep, shard = place()
        greet([(rep, lax.rem(shard + n, 16)) for n in range(1, 16)])
        start()

    core = lax.rem(lax.axis_index("shard"), 2)
    shift = lax.rem(i + core, 2) * OWN
    q = q_ref[0]

    def step(c, carry, last=False):
        top, total = carry
        at = pl.ds(pl.multiple_of(c * KEYS, KEYS), KEYS)
        scores = contract(q, k_ref[at, :], ((1,), (1,)))
        if last:
            row = lax.broadcasted_iota(jnp.int32, (OWN, KEYS), 0)
            column = lax.broadcasted_iota(jnp.int32, (OWN, KEYS), 1)
            bias = jnp.where(column <= row + shift, 0.0, -1e30)
            scores = scores + jnp.concatenate([bias] * GROUP, 0)
        high = jnp.maximum(top, jnp.max(scores, 1, keepdims=True))
        prob = jnp.exp(scores - high).astype(bf16)
        total = total * jnp.exp(top - high) + jnp.dot(
            prob, v_ref[at, :], preferred_element_type=f32
        )
        return high, total

    carry = (jnp.full((ROWS, 1), -1e30, f32), jnp.zeros((ROWS, 128), f32))
    carry = lax.fori_loop(0, i, step, carry)
    top, total = step(i, carry, True)
    weight = total[:, HEAD : HEAD + 1]
    result = (total[:, :HEAD] / weight).astype(bf16)
    o_ref[0] = jnp.concatenate([result[r * OWN : (r + 1) * OWN] for r in range(GROUP)], 1)
    column = lax.broadcasted_iota(jnp.int32, (8, 8), 1)
    l_ref[0] = contract(
        jnp.where(column == 0, 1.0, 0.0).astype(f32),
        jnp.broadcast_to(top + jnp.log(weight), (ROWS, 8)),
        ((1,), (1,)),
        lax.Precision.HIGHEST,
    )

    @pl.when(i == BLOCKS - 1)
    def _():
        wait()


def attend(q, k, v, units, collective):
    return pl.pallas_call(
        attend_kernel,
        grid=(BLOCKS,),
        in_specs=[
            pl.BlockSpec((1, ROWS, HEAD), lambda i: (i, 0, 0)),
            pl.BlockSpec((SEQ, HEAD), lambda i: (0, 0)),
            pl.BlockSpec((SEQ, 128), lambda i: (0, 0)),
            ANY,
        ],
        out_specs=(
            pl.BlockSpec((1, OWN, GROUP * HEAD), lambda i: (i, 0, 0)),
            pl.BlockSpec((1, 8, ROWS), lambda i: (i, 0, 0)),
            ANY,
        ),
        out_shape=(
            jax.ShapeDtypeStruct((BLOCKS, OWN, GROUP * HEAD), bf16),
            jax.ShapeDtypeStruct((BLOCKS, 8, ROWS), f32),
            jax.ShapeDtypeStruct(units.shape, bf16),
        ),
        scratch_shapes=[
            pltpu.SemaphoreType.DMA((1,)),
            pltpu.SemaphoreType.DMA((16,)),
            pltpu.SemaphoreType.DMA((16,)),
        ],
        compiler_params=params(collective, 48 * 2**20),
        name="attend",
    )(q, k, v, units)


def attend_back_kernel(
    q_ref, k_ref, v_ref, g_ref, a_ref, l_ref, cos_ref, sin_ref, qcos_ref, qsin_ref, lift_ref, part_ref,
    dq_ref, dkv_ref, lift_out, part_out,
    dk, dv, dq, held, near, landed, local_sem, s_sem, r_sem, h_sem, s_near, r_near, s_far, r_far,
):
    i = pl.program_id(0)
    rep, shard = place()
    core = lax.rem(shard, 2)
    chip = shard // 2
    sib = shard + 1 - 2 * core
    shift = lax.rem(i + core, 2) * OWN
    start, wait = behind(lift_ref, lift_out, local_sem.at[0], s_sem, r_sem)

    def copy_near(j):
        return pltpu.make_async_remote_copy(
            src_ref=part_ref.at[2 * lax.rem(chip + j, 8) + 1 - core],
            dst_ref=near.at[j],
            send_sem=s_near.at[j],
            recv_sem=r_near.at[j],
            device_id=(rep, sib),
            device_id_type=MESH,
        )

    def copy_own(j):
        return pltpu.make_async_copy(
            part_ref.at[2 * lax.rem(chip + j, 8) + core], held.at[j], h_sem.at[j]
        )

    def copy_far(j):
        return pltpu.make_async_remote_copy(
            src_ref=held.at[j],
            dst_ref=landed.at[j - 1],
            send_sem=s_far.at[j],
            recv_sem=r_far.at[j],
            device_id=(rep, 2 * lax.rem(chip + j, 8) + core),
            device_id_type=MESH,
        )

    @pl.when(i == 0)
    def _():
        greet([(rep, lax.rem(shard + n, 16)) for n in range(1, 16)])
        for j in range(8):
            copy_near(j).start()
            copy_own(j).start()
        start()
        dk[...] = jnp.zeros_like(dk)
        dv[...] = jnp.zeros_like(dv)

    @pl.when(i == 3)
    def _():
        for j in range(8):
            copy_near(j).wait_recv()
            copy_own(j).wait()

            def add(t, _, j=j):
                at = pl.ds(pl.multiple_of(t * 32, 32), 32)
                held[j, at] = (held[j, at].astype(f32) + near[j, at].astype(f32)).astype(bf16)
                return 0

            lax.fori_loop(0, 3, add, 0)
            if j:
                copy_far(j).start()

    q = q_ref[0]
    grad = jnp.concatenate([g_ref[0][:, r * HEAD : (r + 1) * HEAD] for r in range(GROUP)], 0)
    dq[...] = jnp.zeros_like(dq)
    lse = l_ref[0][:1]
    lane = lax.broadcasted_iota(jnp.int32, (8, GROUP * HEAD), 1)
    row = lax.broadcasted_iota(jnp.int32, (8, GROUP * HEAD), 0)
    sums = contract(
        jnp.where(lane // HEAD == row, 1.0, 0.0).astype(f32),
        g_ref[0].astype(f32) * a_ref[0].astype(f32),
        ((1,), (1,)),
        lax.Precision.HIGHEST,
    )
    delta = jnp.concatenate([sums[r : r + 1] for r in range(GROUP)], 1)

    def step(c, _, last=False):
        at = pl.ds(pl.multiple_of(c * KEYS, KEYS), KEYS)
        keys = k_ref[at, :]
        scores = contract(keys, q, ((1,), (1,)))
        if last:
            key = lax.broadcasted_iota(jnp.int32, (KEYS, OWN), 0)
            token = lax.broadcasted_iota(jnp.int32, (KEYS, OWN), 1)
            bias = jnp.where(key <= token + shift, 0.0, -1e30)
            scores = scores + jnp.concatenate([bias] * GROUP, 1)
        prob = jnp.exp(scores - lse)
        back = contract(v_ref[at, :HEAD], grad, ((1,), (1,)))
        slope = (prob * (back - delta)).astype(bf16)
        dv[at, :] += jnp.dot(prob.astype(bf16), grad, preferred_element_type=f32)
        dk[at, :] += jnp.dot(slope, q, preferred_element_type=f32)
        dq[...] += contract(slope, keys, ((0,), (0,)))
        return 0

    lax.fori_loop(0, i, step, 0)
    step(i, 0, True)
    wide = jnp.concatenate(
        [dq[r * OWN : (r + 1) * OWN, :] for r in range(GROUP)] + [jnp.zeros((OWN, HEAD), f32)], 1
    )
    wide = wide * (HEAD**-0.5)
    cos, sin = qcos_ref[...], qsin_ref[...]
    cos, sin = jnp.concatenate([cos, cos], 1), jnp.concatenate([sin, sin], 1)
    wide = wide * cos - swap_halves(wide) * sin
    dq_ref[0] = wide[:, : GROUP * HEAD].astype(bf16)

    @pl.when(i == BLOCKS - 1)
    def _():
        def turn(c, _):
            at = pl.ds(pl.multiple_of(c * OWN, OWN), OWN)
            both = jnp.concatenate([dk[at, :], dv[at, :]], 1)
            lane = lax.broadcasted_iota(jnp.int32, both.shape, 1)
            turned = both * cos_ref[at, :] - swap_halves(both) * sin_ref[at, :]
            dkv_ref[at, :] = jnp.where(lane < HEAD, turned, both).astype(bf16)
            return 0

        lax.fori_loop(0, SHARDS, turn, 0)
        for j in range(1, 8):
            copy_far(j).wait_recv()

        def add(t, _):
            at = pl.ds(pl.multiple_of(t * 32, 32), 32)
            total = held[0, at].astype(f32)
            for j in range(7):
                total = total + landed[j, at].astype(f32)
            part_out[at] = total.astype(bf16)
            return 0

        lax.fori_loop(0, 3, add, 0)
        wait()
        for j in range(8):
            copy_near(j).wait_send()
            if j:
                copy_far(j).wait_send()


def attend_back(q, k, v, grad, attended, lse, cos, sin, lift, part, collective):
    def own(i):
        return (2 * i + lax.rem(i + lax.rem(lax.axis_index("shard"), 2), 2), 0)

    whole = lambda i: (0, 0)
    block = lambda i: (i, 0, 0)
    return pl.pallas_call(
        attend_back_kernel,
        grid=(BLOCKS,),
        in_specs=[
            pl.BlockSpec((1, ROWS, HEAD), block),
            pl.BlockSpec((SEQ, HEAD), whole),
            pl.BlockSpec((SEQ, 128), whole),
            pl.BlockSpec((1, OWN, GROUP * HEAD), block),
            pl.BlockSpec((1, OWN, GROUP * HEAD), block),
            pl.BlockSpec((1, 8, ROWS), block),
            pl.BlockSpec((SEQ, 128), whole),
            pl.BlockSpec((SEQ, 128), whole),
            pl.BlockSpec((OWN, 128), own),
            pl.BlockSpec((OWN, 128), own),
            ANY,
            ANY,
        ],
        out_specs=(
            pl.BlockSpec((1, OWN, GROUP * HEAD), block),
            pl.BlockSpec((SEQ, 128), whole),
            ANY,
            pl.BlockSpec(part.shape[1:], whole),
        ),
        out_shape=(
            jax.ShapeDtypeStruct((BLOCKS, OWN, GROUP * HEAD), bf16),
            jax.ShapeDtypeStruct((SEQ, 128), bf16),
            jax.ShapeDtypeStruct(lift.shape, bf16),
            jax.ShapeDtypeStruct(part.shape[1:], bf16),
        ),
        scratch_shapes=[
            pltpu.VMEM((SEQ, HEAD), f32),
            pltpu.VMEM((SEQ, HEAD), f32),
            pltpu.VMEM((ROWS, HEAD), f32),
            pltpu.VMEM((8,) + part.shape[1:], bf16),
            pltpu.VMEM((8,) + part.shape[1:], bf16),
            pltpu.VMEM((7,) + part.shape[1:], bf16),
            pltpu.SemaphoreType.DMA((1,)),
            pltpu.SemaphoreType.DMA((16,)),
            pltpu.SemaphoreType.DMA((16,)),
        ]
        + [pltpu.SemaphoreType.DMA((8,))] * 5,
        compiler_params=params(collective, 48 * 2**20),
        name="attend_back",
    )(q, k, v, grad, attended, lse, cos, sin, cos, sin, lift, part)


def experts_kernel(
    u_ref, y_ref, c_ref, wl_ref, wd_ref, e_ref, out_ref, du_ref, lift_ref, down_ref, lift, down
):
    i = pl.program_id(0)
    u, y = u_ref[...], y_ref[...]
    lifted = jnp.dot(u, wl_ref[...], preferred_element_type=f32)
    back = contract(y, wd_ref[...], ((1,), (1,)))
    share = jnp.dot(c_ref[...], e_ref[...], preferred_element_type=f32)
    gate, raised = lifted[:, :HID], lifted[:, HID:]
    s = jax.nn.sigmoid(gate)
    swish = gate * s
    act = (share * swish * raised).astype(bf16)
    back = back * share
    grad_gate = back * raised * s * (1.0 + gate * (1.0 - s))
    grad_lift = jnp.concatenate([grad_gate, back * swish], 1).astype(bf16)
    out_ref[...] = jnp.dot(act, wd_ref[...], preferred_element_type=f32).astype(bf16)
    du_ref[...] = contract(grad_lift, wl_ref[...], ((1,), (1,))).astype(bf16)

    @pl.when(i == 0)
    def _():
        lift[...] = jnp.zeros_like(lift)
        down[...] = jnp.zeros_like(down)

    lift[...] += contract(u, grad_lift, ((0,), (0,)))
    down[...] += contract(act, y, ((0,), (0,)))

    @pl.when(i == pl.num_programs(0) - 1)
    def _():
        lift_ref[...] = lift[...].astype(bf16)
        down_ref[...] = down[...].astype(bf16)


def experts(u_all, y_all, wl, wd, spread):
    step = 384
    rows = lambda i: (i, 0)
    whole = lambda i: (0, 0)
    return pl.pallas_call(
        experts_kernel,
        grid=(SEQ // step,),
        in_specs=[
            pl.BlockSpec((step, D), rows),
            pl.BlockSpec((step, D), rows),
            pl.BlockSpec((step, 128), lambda i: (i, D // 128)),
            pl.BlockSpec((D, 2 * HID), whole),
            pl.BlockSpec((HID, D), whole),
            pl.BlockSpec((128, HID), whole),
        ],
        out_specs=(
            pl.BlockSpec((step, D), rows),
            pl.BlockSpec((step, D), rows),
            pl.BlockSpec((D, 2 * HID), whole),
            pl.BlockSpec((HID, D), whole),
        ),
        out_shape=(
            jax.ShapeDtypeStruct((SEQ, D), bf16),
            jax.ShapeDtypeStruct((SEQ, D), bf16),
            jax.ShapeDtypeStruct((D, 2 * HID), bf16),
            jax.ShapeDtypeStruct((HID, D), bf16),
        ),
        scratch_shapes=[pltpu.VMEM((D, 2 * HID), f32), pltpu.VMEM((HID, D), f32)],
        compiler_params=pltpu.CompilerParams(vmem_limit_bytes=58 * 2**20),
        name="experts",
    )(u_all, y_all, y_all, wl, wd, spread)


def one_step(kernel, arrays, shapes, name):
    return pl.pallas_call(
        kernel,
        in_specs=[VMEM] * len(arrays),
        out_specs=(VMEM,) * len(shapes),
        out_shape=tuple(jax.ShapeDtypeStruct(shape, dtype) for shape, dtype in shapes),
        compiler_params=pltpu.CompilerParams(vmem_limit_bytes=56 * 2**20),
        name=name,
    )(*arrays)


def side_by_side(ref):
    return jnp.concatenate([ref[c] for c in range(CHIPS)], 1)


def mix_kernel(a_ref, w_ref, x_ref, g_ref, mixed_ref, low_ref):
    mixed = x_ref[...].astype(f32) + jnp.dot(
        side_by_side(a_ref), w_ref[...], preferred_element_type=f32
    )
    mixed_ref[...] = mixed
    low_ref[...] = (mixed * inverse_root(mixed) * g_ref[...]).astype(bf16)


def unmix_kernel(du_ref, e_ref, mixed_ref, y_ref, g_ref, w_ref, a_ref, out_ref, dz_ref, ga_ref, part_ref):
    mixed = mixed_ref[...]
    out_ref[...] = mixed + e_ref[...]
    inverse = inverse_root(mixed)
    dz = y_ref[...].astype(f32) + norm_back(du_ref[...] * g_ref[...], mixed * inverse, inverse)
    dz_ref[...] = dz
    low = dz.astype(bf16)
    back = contract(low, w_ref[...], ((1,), (1,))).astype(bf16)
    for c in range(CHIPS):
        ga_ref[c] = back[:, c * 192 : (c + 1) * 192]
    part = contract(side_by_side(a_ref), low, ((0,), (0,))).astype(bf16)
    for s in range(SHARDS):
        part_ref[s] = part[s * 96 : (s + 1) * 96]


def finish_kernel(dq_ref, dkv_ref, w_ref, dz_ref, x_ref, g_ref, out_ref):
    pairs = [dkv_ref[2 * c].astype(f32) + dkv_ref[2 * c + 1].astype(f32) for c in range(CHIPS)]
    joined = jnp.concatenate(
        [side_by_side(dq_ref)]
        + [p[:, :HEAD].astype(bf16) for p in pairs]
        + [p[:, HEAD:].astype(bf16) for p in pairs],
        1,
    )
    dh = contract(joined, w_ref[...], ((1,), (1,)))
    stream = x_ref[...].astype(f32)
    inverse = inverse_root(stream)
    out_ref[...] = dz_ref[...] + norm_back(dh * g_ref[...], stream * inverse, inverse)


def inward_part_kernel(u_ref, dq_ref, dkv_ref, out_ref, total):
    i = pl.program_id(0)
    core = lax.rem(lax.axis_index("shard"), 2)
    first = pl.multiple_of(lax.rem(i + core, 2) * OWN, OWN)

    @pl.when(i == 0)
    def _():
        total[...] = jnp.zeros_like(total)

    total[:, :192] += contract(u_ref[pl.ds(first, OWN), :], dq_ref[0], ((0,), (0,)))
    total[:, 256:] += contract(u_ref[...], dkv_ref[...], ((0,), (0,)))

    @pl.when(i == BLOCKS - 1)
    def _():
        both = jnp.concatenate([total[:, :192], total[:, 256:]], 1).astype(bf16)
        for s in range(SHARDS):
            out_ref[s] = both[s * 96 : (s + 1) * 96]


def inward_parts(u_all, dq, dkv):
    return pl.pallas_call(
        inward_part_kernel,
        grid=(BLOCKS,),
        in_specs=[
            pl.BlockSpec((KEYS, D), lambda i: (i, 0)),
            pl.BlockSpec((1, OWN, GROUP * HEAD), lambda i: (i, 0, 0)),
            pl.BlockSpec((KEYS, 128), lambda i: (i, 0)),
        ],
        out_specs=pl.BlockSpec((SHARDS, 96, 320), lambda i: (0, 0, 0)),
        out_shape=jax.ShapeDtypeStruct((SHARDS, 96, 320), bf16),
        scratch_shapes=[pltpu.VMEM((D, 384), f32)],
        compiler_params=pltpu.CompilerParams(vmem_limit_bytes=48 * 2**20),
        name="inward_parts",
    )(u_all, dq, dkv)


def adam(weight, old_mean, square, gradient, step_rate, decay_rate):
    values = weight.astype(f32)
    moment = beta_one * old_mean.astype(f32) + (1.0 - beta_one) * gradient
    variance = beta_two * square.astype(f32) + (1.0 - beta_two) * gradient * gradient
    normed_step = (
        moment
        / (1.0 - beta_one**STEP)
        / (jnp.sqrt(variance / (1.0 - beta_two**STEP)) + adam_epsilon)
    )
    return (moment, variance, values - step_rate * (normed_step + decay_rate * values))


def adam_lifting_kernel(w_ref, m_ref, s_ref, g_ref, mo_ref, so_ref, wo_ref, dot_ref, grad):
    e = pl.program_id(0)
    for k in range(EXPERTS):

        @pl.when(e == k)
        def _(k=k):
            for part in range(2):
                low = HID * part + 32 * k
                grad[:, FF_EXP * part : FF_EXP * (part + 1)] = jnp.concatenate(
                    [g_ref[s][:, low : low + 32].astype(f32) for s in range(SHARDS)], 1
                )

    @pl.when(e == 0)
    def _():
        dot_ref[...] = jnp.zeros_like(dot_ref)

    dot = jnp.sum(w_ref[0].astype(f32) * grad[...], 1, keepdims=True)
    dot_ref[...] += jnp.broadcast_to(dot, dot_ref.shape)
    mo_ref[0], so_ref[0], wo_ref[0] = adam(
        w_ref[0], m_ref[0], s_ref[0], grad[...], rate_lifting, weight_decay
    )


def adam_lifting(weight, mean, square, grad):
    block = pl.BlockSpec((1, 96, 2 * FF_EXP), lambda e: (e, 0, 0))
    shape = jax.ShapeDtypeStruct(weight.shape, f32)
    return pl.pallas_call(
        adam_lifting_kernel,
        grid=(EXPERTS,),
        in_specs=[block, block, block, pl.BlockSpec(grad.shape, lambda e: (0, 0, 0))],
        out_specs=(block, block, block, pl.BlockSpec((96, 128), lambda e: (0, 0))),
        out_shape=(shape, shape, shape, jax.ShapeDtypeStruct((96, 128), f32)),
        scratch_shapes=[pltpu.VMEM((96, 2 * FF_EXP), f32)],
        compiler_params=pltpu.CompilerParams(vmem_limit_bytes=48 * 2**20),
        name="adam_lifting",
    )(weight, mean, square, grad)


def adam_inward_kernel(w_ref, m_ref, s_ref, g_ref, mo_ref, so_ref, wo_ref, dot_ref):
    parts = [g_ref[c].astype(f32) for c in range(CHIPS)]
    grad = jnp.concatenate(
        [p[:, :192] for p in parts] + [p[:, 192:256] for p in parts] + [p[:, 256:] for p in parts], 1
    )
    dot = jnp.sum(w_ref[...].astype(f32) * grad, 1, keepdims=True)
    dot_ref[...] = jnp.broadcast_to(dot, dot_ref.shape)
    mo_ref[...], so_ref[...], wo_ref[...] = adam(
        w_ref[...], m_ref[...], s_ref[...], grad, rate_inward, weight_decay
    )


def adam_inward(weight, mean, square, grad):
    shape = jax.ShapeDtypeStruct(weight.shape, f32)
    return pl.pallas_call(
        adam_inward_kernel,
        in_specs=[VMEM] * 4,
        out_specs=(VMEM,) * 4,
        out_shape=(shape, shape, shape, jax.ShapeDtypeStruct((96, 128), f32)),
        compiler_params=pltpu.CompilerParams(vmem_limit_bytes=48 * 2**20),
        name="adam_inward",
    )(weight, mean, square, grad)


def tables():
    half = HEAD // 2
    frequency = np.float32(10000.0) ** (-(2.0 * np.arange(half, dtype=np.float32)) / HEAD)
    phases = np.arange(SEQ, dtype=np.float32)[:, None] * frequency[None, :].astype(np.float32)
    cos, sin = np.cos(phases).astype(np.float32), np.sin(phases).astype(np.float32)
    return (
        np.concatenate([cos, cos, cos, cos], 1),
        np.concatenate([-sin, sin, -sin, sin], 1),
    )


def spread_table():
    table = np.zeros((128, HID), np.float32)
    for e in range(EXPERTS):
        table[e, 32 * e : 32 * e + 32] = 1.0
        table[16 + e, 32 * e : 32 * e + 32] = 1.0
    return table


def inverse_root(stream):
    return lax.rsqrt(jnp.mean(stream * stream, -1, keepdims=True) + norm_epsilon)


def norm_back(scaled, unit, inverse):
    return inverse * (scaled - unit * jnp.mean(scaled * unit, -1, keepdims=True))


def per_device(
    layer_input,
    grad_output,
    routes,
    route_logits,
    norm_gains,
    inward,
    outward,
    lifting,
    lowering,
    mean_gains,
    mean_inward,
    mean_outward,
    mean_lifting,
    mean_lowering,
    square_gains,
    square_inward,
    square_outward,
    square_lifting,
    square_lowering,
):
    gains = norm_gains.astype(f32)
    cos, sin = (jnp.asarray(t) for t in tables())

    by_head = jnp.concatenate(
        [
            inward[:, :1536].reshape(96, KV_HEADS, 192),
            jnp.broadcast_to(
                jnp.pad(norm_gains.T, ((0, 0), (0, HEAD - 2)))[:, None, :], (96, KV_HEADS, HEAD)
            ),
            inward[:, 1536:2048].reshape(96, KV_HEADS, HEAD),
            inward[:, 2048:].reshape(96, KV_HEADS, HEAD),
        ],
        2,
    ).transpose(1, 0, 2)
    lifting_rows = lifting.transpose(1, 0, 2)
    by_unit = (
        lifting.reshape(96, EXPERTS, 2, SHARDS, 32)
        .transpose(3, 0, 2, 1, 4)
        .reshape(SHARDS, 96, 2 * HID)
    )
    down_weight = lowering.transpose(1, 0, 2).reshape(HID, D)

    x_all, head_weight = gather(layer_input, 2, by_head)
    head_weight = head_weight.reshape(D, 384)
    gain_rows = head_weight[:, 192:194].T.astype(f32)
    gain_one, gain_two = gain_rows[0:1], gain_rows[1:2]

    gates = jax.nn.softmax(route_logits, axis=-1)
    picked = routes[:, :, None] == jnp.arange(EXPERTS, dtype=jnp.int32)[None, None, :]
    combine = jnp.sum(jnp.where(picked, gates[:, :, None], 0.0), axis=1)
    high = lax.reduce_precision(combine, 8, 7)
    rest = combine - high
    shares = jnp.concatenate(
        [jnp.pad(high, ((0, 0), (0, 6))), jnp.pad(rest, ((0, 0), (0, 102)))], 1
    ).astype(bf16)
    late_outward, late_y, x_all = lax.optimization_barrier(
        (outward, jnp.concatenate([grad_output, shares], 1), x_all)
    )
    outward_all = lax.all_gather(late_outward, "shard", axis=0, tiled=True)
    y_all = lax.all_gather(late_y, "shard", axis=0, tiled=True)

    q, k, v, u_one = project(x_all, head_weight, gain_one, cos, sin)
    attended, lse, unit_weight = attend(q, k, v, by_unit, 1)
    unit_weight = unit_weight.reshape(D, 2 * HID)
    (own_attended,) = exchange((attended,), ("home",), 3, "attended_home")
    mixed, low_two = one_step(
        mix_kernel,
        (own_attended, outward_all, layer_input, gain_two),
        (((OWN, D), f32), ((OWN, D), bf16)),
        "mix",
    )
    (u_two,) = gather(low_two, 4)
    late_inward, u_two = lax.optimization_barrier((inward, u_two))
    inward_all = lax.all_gather(late_inward, "shard", axis=0, tiled=True)

    out_part, du_part, lift_part, down_part = experts(
        u_two, y_all, unit_weight, down_weight, jnp.asarray(spread_table(), bf16)
    )
    du, expert_out, lift_sum, down_sum = reduce_blocks(
        du_part.reshape(SHARDS, OWN, D), out_part.reshape(SHARDS, OWN, D), lift_part, down_part, 5
    )
    layer_output, grad_mixed, away, outward_part = one_step(
        unmix_kernel,
        (du, expert_out, mixed, grad_output, gain_two, outward_all, own_attended),
        (((OWN, D), f32), ((OWN, D), f32), ((CHIPS, OWN, 192), bf16), ((SHARDS, 96, D), bf16)),
        "unmix",
    )
    (head_grads,) = exchange((away,), ("away",), 6, "grads_away")
    dq, dkv, lift_got, outward_own = attend_back(
        q, k, v, head_grads, attended, lse, cos, sin,
        lift_sum.reshape(SHARDS, 96, 2 * HID), outward_part, 8,
    )
    inward_part = inward_parts(u_one, dq, dkv)
    own_dq, own_dkv, inward_got = exchange(
        (dq, dkv.reshape(SHARDS, OWN, 128), inward_part),
        ("home", "all", "all"),
        7,
        "pairs_home",
    )
    (input_grad,) = one_step(
        finish_kernel,
        (own_dq, own_dkv, inward_all, grad_mixed, layer_input, gain_one),
        (((OWN, D), f32),),
        "finish",
    )
    inward_sum = jnp.sum(inward_got.reshape(CHIPS, 2, 96, 320).astype(f32), 1).astype(bf16)
    inward_sum, outward_sum = total_over_reps(
        (inward_sum, outward_own.reshape(REPS, 16, 1152)), 9
    )
    outward_grad = outward_sum.reshape(96, D).astype(f32)
    down_grad = down_sum.reshape(EXPERTS, 32, D).transpose(1, 0, 2).astype(f32)

    new_lifting = adam_lifting(
        lifting_rows, mean_lifting.transpose(1, 0, 2), square_lifting.transpose(1, 0, 2), lift_got
    )
    lifting_dot = new_lifting[3]
    new_lifting = tuple(t.transpose(1, 0, 2) for t in new_lifting[:3])
    new_inward = adam_inward(inward, mean_inward, square_inward, inward_sum)
    gain_grad = jnp.stack([new_inward[3][:, 0], lifting_dot[:, 0]]) / gains
    new_gains = adam(norm_gains, mean_gains, square_gains, gain_grad, rate_gains, 0.0)
    new_outward = adam(
        outward, mean_outward, square_outward, outward_grad, rate_outward, weight_decay
    )
    new_lowering = adam(
        lowering, mean_lowering, square_lowering, down_grad, rate_lowering, weight_decay
    )
    return (
        layer_output,
        input_grad,
        new_gains[0],
        new_inward[0],
        new_outward[0],
        new_lifting[0],
        new_lowering[0],
        new_gains[1],
        new_inward[1],
        new_outward[1],
        new_lifting[1],
        new_lowering[1],
        new_gains[2],
        new_inward[2],
        new_outward[2],
        new_lifting[2],
        new_lowering[2],
    )


def solution(mesh):
    tokens = P(("rep", "shard"), None)
    gains, flat, deep = P(None, "shard"), P("shard", None), P("shard", None, None)
    weights = (gains, flat, flat, deep, deep)
    return jax.shard_map(
        per_device,
        mesh=mesh,
        in_specs=(tokens,) * 4 + weights * 3,
        out_specs=(tokens,) * 2 + weights * 3,
        check_vma=False,
    )
```

```python
import functools

import jax
import jax.numpy as jnp
import numpy as np
from jax import lax
from jax.experimental import pallas as pl
from jax.experimental.pallas import tpu as pltpu
from jax.sharding import PartitionSpec as P

HEADS = 24
KV_HEADS = 8
HEAD = 64
GROUP = HEADS // KV_HEADS
FF_EXP = 512
EXPERTS = 10
STEP = 10

norm_epsilon = 1e-06
beta_one = 0.9
beta_two = 0.95
adam_epsilon = 1e-08
weight_decay = 0.1
rate_gains = 0.5
rate_inward = 0.05
rate_outward = 0.3
rate_lifting = 0.05
rate_lowering = 0.3

SHARDS = 16
CHIPS = 8
REPS = 8
OWN = 192
SEQ = OWN * SHARDS
D = 1536
PEERS = 8
FLAT = 40
FLAT_PAD = 48
HID = SHARDS * FLAT
EXP = 2 * HID
BLOCKS = 8
ROWS = GROUP * OWN
KEYS = 2 * OWN

MESH = pl.DeviceIdType.MESH
bf16 = jnp.bfloat16
f32 = jnp.float32


def place():
    rep = lax.axis_index("rep")
    shard = lax.axis_index("shard")
    return rep, shard


def greet(devices):
    barrier = pltpu.get_barrier_semaphore()
    for device in devices:
        pl.semaphore_signal(barrier, inc=1, device_id=device, device_id_type=MESH)
    pl.semaphore_wait(barrier, len(devices))


def send(src, dst, send_sem, recv_sem, device):
    copy = pltpu.make_async_remote_copy(
        src_ref=src,
        dst_ref=dst,
        send_sem=send_sem,
        recv_sem=recv_sem,
        device_id=device,
        device_id_type=MESH,
    )
    copy.start()
    return copy


def params(collective, vmem=None):
    return pltpu.CompilerParams(
        collective_id=collective, has_side_effects=True, vmem_limit_bytes=vmem
    )


ANY = pl.BlockSpec(memory_space=pl.ANY)
VMEM = pl.BlockSpec(memory_space=pltpu.VMEM)


def along_x(rep, dx):
    return 2 * lax.rem(rep // 2 + dx, 4) + lax.rem(rep, 2)


def landed_on(ref, recv_sem, any_send_sem, device):
    pltpu.make_async_remote_copy(
        src_ref=ref,
        dst_ref=ref,
        send_sem=any_send_sem,
        recv_sem=recv_sem,
        device_id=device,
        device_id_type=MESH,
    ).wait_recv()


def x_gather(x_ref, o_ref, local_sem, send_sem, recv_sem):
    rep, shard = place()
    core = lax.rem(shard, 2)
    sib = shard + 1 - 2 * core
    half = x_ref.shape[0] // 2
    top, bottom = pl.ds(0, half), pl.ds(half, half)
    up, down, far = (along_x(rep, d) for d in (1, 3, 2))

    def block(r, other=False):
        return 2 * (r // 2) + (1 - core if other else core)

    mine = block(rep)
    own = pltpu.make_async_copy(x_ref, o_ref.at[mine], local_sem)
    sent = []

    def put(ref, dst, slot, device):
        sent.append(send(ref, dst, send_sem.at[len(sent)], recv_sem.at[slot], device))

    def arrived(ref, slot):
        landed_on(ref, recv_sem.at[slot], send_sem.at[0], (rep, sib))

    def start():
        own.start()
        put(x_ref, o_ref.at[mine], 0, (up, shard))
        put(x_ref, o_ref.at[mine], 1, (down, shard))
        put(x_ref, o_ref.at[mine], 4, (rep, sib))

    def relay():
        ref = o_ref.at[block(down)]
        arrived(ref, 0)
        put(o_ref.at[block(down), top], o_ref.at[block(down), top], 2, (up, shard))
        put(ref, ref, 5, (rep, sib))
        ref = o_ref.at[block(up)]
        arrived(ref, 1)
        put(o_ref.at[block(up), bottom], o_ref.at[block(up), bottom], 3, (down, shard))
        put(ref, ref, 6, (rep, sib))

    def relay_far():
        for slot, part in ((2, top), (3, bottom)):
            ref = o_ref.at[block(far), part]
            arrived(ref, slot)
            put(ref, ref, slot + 5, (rep, sib))

    def finish():
        arrived(o_ref.at[block(rep, True)], 4)
        arrived(o_ref.at[block(down, True)], 5)
        arrived(o_ref.at[block(up, True)], 6)
        arrived(o_ref.at[block(far, True), top], 7)
        arrived(o_ref.at[block(far, True), bottom], 8)
        for copy in sent:
            copy.wait_send()
        own.wait()

    return start, relay, relay_far, finish


def spread(x_ref, o_ref, local_sem, send_sem, recv_sem):
    rep, shard = place()
    core = lax.rem(shard, 2)
    chip = shard // 2
    sib = shard + 1 - 2 * core
    own = pltpu.make_async_copy(x_ref.at[core], o_ref.at[shard], local_sem)

    def copy(src, slot, kind, i):
        return pltpu.make_async_remote_copy(
            src_ref=src,
            dst_ref=o_ref.at[slot],
            send_sem=send_sem.at[kind, i],
            recv_sem=recv_sem.at[kind, i],
            device_id=(rep, 2 * lax.rem(chip + i, 8) + core if i else sib),
            device_id_type=MESH,
        )

    def start():
        own.start()
        copy(x_ref.at[1 - core], shard, 1, 0).start()
        for i in range(1, 8):
            copy(x_ref.at[core], shard, 0, i).start()

    def relay():
        copy(x_ref.at[core], sib, 1, 0).wait_recv()
        for i in range(1, 8):
            copy(o_ref.at[sib], sib, 1, i).start()

    def finish():
        own.wait()
        copy(x_ref.at[1 - core], shard, 1, 0).wait_send()
        for i in range(1, 8):
            back = 2 * lax.rem(chip + 8 - i, 8)
            copy(x_ref.at[core], back + core, 0, i).wait_recv()
            copy(x_ref.at[core], back + 1 - core, 1, i).wait_recv()
        for i in range(1, 8):
            copy(x_ref.at[core], shard, 0, i).wait_send()
            copy(o_ref.at[sib], sib, 1, i).wait_send()

    return start, relay, finish


def start_kernel(
    x_ref, w_ref, t_ref, o_ref, p_ref, g_ref,
    local_sem, send_sem, recv_sem, s_part, r_part, s_x, r_x,
):
    with_parts = True
    rep, shard = place()
    half = x_ref.shape[0] // 2
    core = lax.rem(shard, 2)
    chip = shard // 2
    y = lax.rem(chip, 2)
    sib = shard + 1 - 2 * core
    pair = shard + 2 - 4 * y
    up = lax.rem(shard + 4, 16)
    down = lax.rem(shard + 12, 16)
    far = lax.rem(shard + 8, 16)
    peers = [2 * lax.rem(chip + i, 8) + core for i in range(1, 8)]

    def other(block):
        return block + 2 - 4 * y

    greet(
        [(rep, sib)]
        + [(rep, p) for p in peers]
        + [(along_x(rep, 1), shard), (along_x(rep, 3), shard)]
    )
    x_steps = x_gather(t_ref, g_ref, local_sem.at[2], s_x, r_x)
    own = pltpu.make_async_copy(x_ref, o_ref.at[shard], local_sem.at[0])
    own.start()
    sent = []

    def put(src, dst, slot, device):
        sent.append(send(src, dst, send_sem.at[len(sent)], recv_sem.at[slot], (rep, device)))

    def forward(block, slot, device, rows=None):
        ref = o_ref.at[block] if rows is None else o_ref.at[block, rows]
        put(ref, ref, slot, device)

    def landed(ref, sem):
        pltpu.make_async_remote_copy(
            src_ref=ref,
            dst_ref=ref,
            send_sem=send_sem.at[0],
            recv_sem=sem,
            device_id=(rep, sib),
            device_id_type=MESH,
        ).wait_recv()

    def arrived(block, slot, rows=None):
        landed(o_ref.at[block] if rows is None else o_ref.at[block, rows], recv_sem.at[slot])

    top, bottom = pl.ds(0, half), pl.ds(half, half)
    put(x_ref, o_ref.at[shard], 0, pair)
    put(x_ref, o_ref.at[shard], 1, up)
    put(x_ref, o_ref.at[shard], 5, down)
    put(x_ref, o_ref.at[shard], 9, sib)
    x_steps[0]()
    parts = []
    if with_parts:
        mine = pltpu.make_async_copy(w_ref.at[chip], p_ref.at[shard], local_sem.at[1])
        mine.start()
        parts.append(
            send(w_ref.at[chip], p_ref.at[shard], s_part.at[0], r_part.at[0], (rep, sib))
        )
        for i in range(1, 8):
            c = lax.rem(chip + i, 8)
            parts.append(
                send(
                    w_ref.at[c], p_ref.at[shard], s_part.at[i], r_part.at[i], (rep, 2 * c + core)
                )
            )
    arrived(pair, 0)
    forward(pair, 2, up)
    forward(pair, 6, down)
    forward(pair, 10, sib)
    arrived(down, 1)
    forward(down, 3, up, top)
    forward(down, 11, sib)
    arrived(up, 5)
    forward(up, 7, down, bottom)
    forward(up, 12, sib)
    x_steps[1]()
    arrived(other(down), 2)
    forward(other(down), 4, up, top)
    forward(other(down), 13, sib)
    arrived(other(up), 6)
    forward(other(up), 8, down, bottom)
    forward(other(up), 14, sib)
    x_steps[2]()
    if with_parts:
        for i in range(1, 8):
            block = 2 * lax.rem(chip + 8 - i, 8) + core
            landed(p_ref.at[block], r_part.at[i])
            parts.append(
                send(
                    p_ref.at[block], p_ref.at[block], s_part.at[7 + i], r_part.at[7 + i], (rep, sib)
                )
            )
    arrived(far, 3, top)
    forward(far, 15, sib, top)
    arrived(far, 7, bottom)
    forward(far, 16, sib, bottom)
    arrived(other(far), 4, top)
    forward(other(far), 17, sib, top)
    arrived(other(far), 8, bottom)
    forward(other(far), 18, sib, bottom)

    def twin(block):
        return block + 1 - 2 * core

    if with_parts:
        landed(p_ref.at[sib], r_part.at[0])
        for i in range(1, 8):
            landed(p_ref.at[twin(2 * lax.rem(chip + 8 - i, 8) + core)], r_part.at[7 + i])
        mine.wait()
    arrived(twin(shard), 9)
    arrived(twin(pair), 10)
    arrived(twin(down), 11)
    arrived(twin(up), 12)
    arrived(twin(other(down)), 13)
    arrived(twin(other(up)), 14)
    arrived(twin(far), 15, top)
    arrived(twin(far), 16, bottom)
    arrived(twin(other(far)), 17, top)
    arrived(twin(other(far)), 18, bottom)
    x_steps[3]()
    for copy in sent + parts:
        copy.wait_send()
    own.wait()


def start(x, parts, tokens, collective):
    rows, columns = x.shape
    dma = pltpu.SemaphoreType.DMA
    gathered, parts, tokens = pl.pallas_call(
        start_kernel,
        out_shape=(
            jax.ShapeDtypeStruct((SHARDS, rows, columns), x.dtype),
            jax.ShapeDtypeStruct((SHARDS,) + parts.shape[1:], parts.dtype),
            jax.ShapeDtypeStruct((PEERS,) + tokens.shape, tokens.dtype),
        ),
        in_specs=[ANY] * 3,
        out_specs=(ANY,) * 3,
        scratch_shapes=[dma((3,)), dma((21,)), dma((19,)), dma((15,)), dma((15,)), dma((9,)), dma((9,))],
        compiler_params=params(collective),
        name="start",
    )(x, parts, tokens)
    return gathered.reshape(SHARDS * rows, columns), parts, tokens.reshape(PEERS * rows, -1)


def second_kernel(x_ref, w_ref, o_ref, wo_ref, local_sem, s_x, r_x, s_w, r_w):
    rep, shard = place()
    core = lax.rem(shard, 2)
    chip = shard // 2
    greet(
        [(rep, shard + 1 - 2 * core)]
        + [(rep, 2 * lax.rem(chip + i, 8) + core) for i in range(1, 8)]
        + [(along_x(rep, 1), shard), (along_x(rep, 3), shard)]
    )
    steps = x_gather(x_ref, o_ref, local_sem.at[0], s_x, r_x)
    begin, relay, finish = spread(w_ref, wo_ref, local_sem.at[1], s_w, r_w)
    steps[0]()
    begin()
    relay()
    for step in steps[1:]:
        step()
    finish()


def second(x, weights, collective):
    dma = pltpu.SemaphoreType.DMA
    gathered, weights = pl.pallas_call(
        second_kernel,
        out_shape=(
            jax.ShapeDtypeStruct((PEERS,) + x.shape, x.dtype),
            jax.ShapeDtypeStruct((SHARDS,) + weights.shape[1:], weights.dtype),
        ),
        in_specs=[ANY] * 2,
        out_specs=(ANY,) * 2,
        scratch_shapes=[dma((2,)), dma((9,)), dma((9,)), dma((2, 8)), dma((2, 8))],
        compiler_params=params(collective),
        name="second_gather",
    )(x, weights)
    return gathered.reshape(PEERS * OWN, D), weights


def exchange_kernel(kinds, *refs):
    count = len(kinds)
    ins, outs = refs[:count], refs[count : 2 * count]
    local_sem, send_sem, recv_sem = refs[2 * count :]
    rep, shard = place()
    core = lax.rem(shard, 2)
    chip = shard // 2
    greet([(rep, lax.rem(shard + i, 16)) for i in range(1, 16)])
    sent, due = [], []

    def mine(device):
        return lax.rem(lax.rem(device, 2) + lax.rem(device // 2, 2), 2)

    for n, kind in enumerate(kinds):
        x, o = ins[n], outs[n]
        if kind == "all":
            local = pltpu.make_async_copy(x.at[shard], o.at[shard], local_sem.at[n])
            local.start()
            due.append(local)
            for i in range(1, 16):
                to = lax.rem(shard + i, 16)
                sent.append(
                    send(x.at[to], o.at[shard], send_sem.at[n, i], recv_sem.at[n, i], (rep, to))
                )
        elif kind == "heads":
            local = pltpu.make_async_copy(x.at[chip], o.at[shard], local_sem.at[n])
            local.start()
            due.append(local)
            for i in range(1, 16):
                to = lax.rem(shard + i, 16)
                sent.append(
                    send(
                        x.at[to // 2], o.at[shard], send_sem.at[n, i], recv_sem.at[n, i], (rep, to)
                    )
                )
        elif kind == "home":
            for i in range(8):
                c = lax.rem(chip + i, 8)
                to = 2 * c + lax.rem(c + core, 2)
                if i == 0:
                    same = to == shard

                    @pl.when(same)
                    def _(x=x, o=o, c=c, n=n):
                        local = pltpu.make_async_copy(x.at[c], o.at[chip], local_sem.at[n])
                        local.start()
                        local.wait()

                    @pl.when(jnp.logical_not(same))
                    def _(x=x, o=o, c=c, n=n, to=to):
                        copy = send(
                            x.at[c], o.at[chip], send_sem.at[n, 0], recv_sem.at[n, 0], (rep, to)
                        )
                        copy.wait_send()

                else:
                    sent.append(
                        send(
                            x.at[c], o.at[chip], send_sem.at[n, i], recv_sem.at[n, i], (rep, to)
                        )
                    )
        elif kind == "away":
            for i in range(8):
                c = lax.rem(chip + i, 8)
                to = 2 * c + mine(shard)
                if i == 0:
                    same = to == shard

                    @pl.when(same)
                    def _(x=x, o=o, c=c, n=n):
                        local = pltpu.make_async_copy(x.at[c], o.at[chip], local_sem.at[n])
                        local.start()
                        local.wait()

                    @pl.when(jnp.logical_not(same))
                    def _(x=x, o=o, c=c, n=n, to=to):
                        copy = send(
                            x.at[c], o.at[chip], send_sem.at[n, 0], recv_sem.at[n, 0], (rep, to)
                        )
                        copy.wait_send()

                else:
                    sent.append(
                        send(
                            x.at[c], o.at[chip], send_sem.at[n, i], recv_sem.at[n, i], (rep, to)
                        )
                    )

    def arrived(ref, n, i):
        pltpu.make_async_remote_copy(
            src_ref=ref,
            dst_ref=ref,
            send_sem=send_sem.at[n, 0],
            recv_sem=recv_sem.at[n, i],
            device_id=(rep, lax.rem(shard + 1, 16)),
            device_id_type=MESH,
        ).wait_recv()

    for n, kind in enumerate(kinds):
        o = outs[n]
        if kind in ("all", "heads"):
            for i in range(1, 16):
                arrived(o.at[lax.rem(shard + 16 - i, 16)], n, i)
        else:
            away = kind == "away"
            first = (
                2 * chip + lax.rem(chip + core, 2) if away else 2 * chip + mine(shard)
            )

            @pl.when(first != shard)
            def _(o=o, n=n):
                arrived(o.at[chip], n, 0)

            for i in range(1, 8):
                arrived(o.at[lax.rem(chip + 8 - i, 8)], n, i)
    for copy in sent:
        copy.wait_send()
    for copy in due:
        copy.wait()


def exchange(arrays, kinds, collective, name):
    shapes = []
    for x, kind in zip(arrays, kinds):
        lead = 16 if kind in ("all", "heads") else 8
        shapes.append(jax.ShapeDtypeStruct((lead,) + x.shape[1:], x.dtype))
    n = len(arrays)
    return pl.pallas_call(
        functools.partial(exchange_kernel, kinds),
        out_shape=tuple(shapes),
        in_specs=[ANY] * n,
        out_specs=(ANY,) * n,
        scratch_shapes=[
            pltpu.SemaphoreType.DMA((n,)),
            pltpu.SemaphoreType.DMA((n, 16)),
            pltpu.SemaphoreType.DMA((n, 16)),
        ],
        compiler_params=params(collective),
        name=name,
    )(*arrays)


def reduce_kernel(*refs):
    ins, grads = refs[:2], refs[2:4]
    outs, grad_outs = refs[4:6], refs[6:8]
    token_held, token_near, token_land = refs[8:11]
    scratch = (refs[11:16], refs[16:21])
    t_load, t_sn, t_rn, t_s, t_r, g_load, s_one, r_one, s_two, r_two = refs[21:]
    rep, shard = place()
    core = lax.rem(shard, 2)
    chip = shard // 2
    y = lax.rem(chip, 2)
    z = chip // 2
    x = rep // 2
    sib = shard + 1 - 2 * core
    pair = shard + 2 - 4 * y

    def ahead(dz):
        return lax.rem(z + dz, 4)

    def device(dz):
        return (rep, 4 * ahead(dz) + 2 * y + core)

    greet(
        [(rep, sib), (rep, pair)]
        + [device(dz) for dz in (1, 2, 3)]
        + [(along_x(rep, dx), shard) for dx in (1, 2, 3)]
    )
    near_copies, loads, token_sends = {}, {}, {}
    for n in range(2):
        for dx in (2, 1, 3, 0):
            to = lax.rem(x + dx, 4)
            near_copies[n, dx] = send(
                ins[n].at[2 * to + 1 - core], token_near.at[n, dx], t_sn.at[n, dx], t_rn.at[n, dx],
                (rep, sib),
            )
            loads[n, dx] = pltpu.make_async_copy(
                ins[n].at[2 * to + core], token_held.at[n, dx], t_load.at[n, dx]
            )
            loads[n, dx].start()

    ones, twos, grad_loads = {}, {}, {}
    for m in range(2):
        held, land_a, land_b, land_c, land_d = scratch[m]
        columns = grads[m].shape[2]
        first, last = pl.ds(0, columns // 2), pl.ds(columns // 2, columns // 2)
        for j in (3, 5, 7, 1, 4, 2, 6, 0):
            dz, dy = j // 2, j % 2
            block = grads[m].at[2 * ahead(dz) + (1 - y if dy else y)]
            if dy:
                ones[m, 0, j] = send(
                    block.at[:, first], land_a.at[dz], s_one.at[m, 0, j], r_one.at[m, 0, j], (rep, pair)
                )
            if dz:
                ones[m, 1, j] = send(
                    block.at[:, last], land_b.at[j - 2], s_one.at[m, 1, j], r_one.at[m, 1, j], device(dz)
                )
            if dy == 0 or dz == 0:
                slot = dz if dy == 0 else 4
                grad_loads[m, slot] = pltpu.make_async_copy(block, held.at[slot], g_load.at[m, slot])
                grad_loads[m, slot].start()

    def rows_of(t, step):
        return pl.ds(pl.multiple_of(t * step, step), step)

    def token_sums(n):
        for dx in (2, 1, 3, 0):
            near_copies[n, dx].wait_recv()
            loads[n, dx].wait()

            def add(t, _, dx=dx):
                at = rows_of(t, 32)
                token_held[n, dx, at] = (
                    token_held[n, dx, at].astype(f32) + token_near[n, dx, at].astype(f32)
                ).astype(bf16)
                return 0

            lax.fori_loop(0, OWN // 32, add, 0)
            if dx:
                token_sends[n, dx] = send(
                    token_held.at[n, dx], token_land.at[n, dx - 1], t_s.at[n, dx], t_r.at[n, dx],
                    (along_x(rep, dx), shard),
                )

    def token_result(n):
        for dx in (1, 2, 3):
            token_sends[n, dx].wait_recv()

        def add(t, _):
            at = rows_of(t, 32)
            total = token_held[n, 0, at].astype(f32)
            for dx in (1, 2, 3):
                total = total + token_land[n, dx - 1, at].astype(f32)
            outs[n][at] = total
            return 0

        lax.fori_loop(0, OWN // 32, add, 0)

    def first_sums(m):
        held, land_a, land_b, land_c, land_d = scratch[m]
        rows, columns = held.shape[1:]
        first, last = pl.ds(0, columns // 2), pl.ds(columns // 2, columns // 2)
        for slot in range(5):
            grad_loads[m, slot].wait()
        for dz in (2, 1, 3, 0):
            ones[m, 0, 2 * dz + 1].wait_recv()

            def add(t, _, dz=dz):
                at = rows_of(t, 16)
                held[dz, at, first] = (
                    held[dz, at, first].astype(f32) + land_a[dz, at].astype(f32)
                ).astype(bf16)
                return 0

            lax.fori_loop(0, rows // 16, add, 0)
            if dz:
                twos[m, dz] = send(
                    held.at[dz, :, first], land_c.at[dz - 1], s_two.at[m, dz], r_two.at[m, dz], device(dz)
                )
        for dy in (1, 0):
            for dz in (1, 2, 3):
                ones[m, 1, 2 * dz + dy].wait_recv()
            slot = 4 if dy else 0

            def add(t, _, dy=dy, slot=slot):
                at = rows_of(t, 16)
                total = held[slot, at, last].astype(f32)
                for dz in (1, 2, 3):
                    total = total + land_b[2 * dz + dy - 2, at].astype(f32)
                held[slot, at, last] = total.astype(bf16)
                return 0

            lax.fori_loop(0, rows // 16, add, 0)
            if dy:
                twos[m, 0] = send(
                    held.at[4, :, last], land_d, s_two.at[m, 0], r_two.at[m, 0], (rep, pair)
                )

    def last_sums(m):
        held, land_a, land_b, land_c, land_d = scratch[m]
        rows, columns = held.shape[1:]
        first, last = pl.ds(0, columns // 2), pl.ds(columns // 2, columns // 2)
        for dz in range(4):
            twos[m, dz].wait_recv()

        def add(t, _):
            at = rows_of(t, 16)
            total = held[0, at, first].astype(f32)
            for dz in (1, 2, 3):
                total = total + land_c[dz - 1, at].astype(f32)
            grad_outs[m][at, first] = total.astype(bf16)
            grad_outs[m][at, last] = (
                held[0, at, last].astype(f32) + land_d[at].astype(f32)
            ).astype(bf16)
            return 0

        lax.fori_loop(0, rows // 16, add, 0)

    token_sums(0)
    token_sums(1)
    first_sums(0)
    token_result(0)
    first_sums(1)
    token_result(1)
    last_sums(0)
    last_sums(1)
    for copies in (near_copies, token_sends, ones, twos):
        for copy in copies.values():
            copy.wait_send()


def reduce_blocks(du, out, lift, down, collective):
    dma = pltpu.SemaphoreType.DMA

    def slots(rows, columns):
        half = columns // 2
        return [
            pltpu.VMEM((5, rows, columns), bf16),
            pltpu.VMEM((4, rows, half), bf16),
            pltpu.VMEM((6, rows, half), bf16),
            pltpu.VMEM((3, rows, half), bf16),
            pltpu.VMEM((rows, half), bf16),
        ]

    return pl.pallas_call(
        reduce_kernel,
        out_shape=(
            jax.ShapeDtypeStruct((OWN, D), f32),
            jax.ShapeDtypeStruct((OWN, D), f32),
            jax.ShapeDtypeStruct(lift.shape[1:], bf16),
            jax.ShapeDtypeStruct(down.shape[1:], bf16),
        ),
        in_specs=[ANY] * 4,
        out_specs=(VMEM,) * 4,
        scratch_shapes=[
            pltpu.VMEM((2, 4, OWN, D), bf16),
            pltpu.VMEM((2, 4, OWN, D), bf16),
            pltpu.VMEM((2, 3, OWN, D), bf16),
        ]
        + slots(*lift.shape[1:])
        + slots(*down.shape[1:])
        + [dma((2, 4))] * 5
        + [dma((2, 5)), dma((2, 2, 8)), dma((2, 2, 8)), dma((2, 4)), dma((2, 4))],
        compiler_params=params(collective, 60 * 2**20),
        name="reduce_rows",
    )(du, out, lift, down)


def away_kernel(
    x_ref, lift_ref, down_ref, o_ref, lift_o, down_o,
    lift_own, lift_land, down_own, down_land,
    local_sem, s_x, r_x, s_mate, r_mate, s_sib, r_sib,
):
    rep, shard = place()
    core = lax.rem(shard, 2)
    chip = shard // 2
    sib = shard + 1 - 2 * core
    mate = rep + 1 - 2 * lax.rem(rep, 2)
    greet([(rep, lax.rem(shard + i, 16)) for i in range(1, 16)] + [(mate, shard)])
    sent = []
    for i in range(1, 8):
        c = lax.rem(chip + i, 8)
        sent.append(
            send(
                x_ref.at[c], o_ref.at[chip], s_x.at[i], r_x.at[i],
                (rep, 2 * c + lax.rem(core + chip, 2)),
            )
        )
    mates, loads = [], []
    for n, (src, own, land) in enumerate(
        ((lift_ref, lift_own, lift_land), (down_ref, down_own, down_land))
    ):
        mates.append(send(src, land, s_mate.at[n], r_mate.at[n], (mate, shard)))
        load = pltpu.make_async_copy(src, own, local_sem.at[n])
        load.start()
        loads.append(load)
    same = lax.rem(chip, 2) == 0

    @pl.when(same)
    def _():
        copy = pltpu.make_async_copy(x_ref.at[chip], o_ref.at[chip], local_sem.at[2])
        copy.start()
        copy.wait()

    @pl.when(jnp.logical_not(same))
    def _():
        send(x_ref.at[chip], o_ref.at[chip], s_x.at[0], r_x.at[0], (rep, sib)).wait_send()
        landed_on(o_ref.at[chip], r_x.at[0], s_x.at[0], (rep, sib))

    keeps, halves = [], []
    for n, (own, land, out) in enumerate(
        ((lift_own, lift_land, lift_o), (down_own, down_land, down_o))
    ):
        loads[n].wait()
        mates[n].wait_recv()
        for k in range(2):

            def add(t, _, own=own, land=land, k=k):
                at = pl.ds(pl.multiple_of(t * 16, 16), 16)
                own[k, at] = (own[k, at].astype(f32) + land[k, at].astype(f32)).astype(bf16)
                return 0

            lax.fori_loop(0, own.shape[1] // 16, add, 0)
        halves.append(
            send(own.at[1 - core], out.at[core], s_sib.at[n], r_sib.at[n], (rep, sib))
        )
        keep = pltpu.make_async_copy(own.at[core], out.at[core], local_sem.at[3 + n])
        keep.start()
        keeps.append(keep)
    for i in range(1, 8):
        landed_on(o_ref.at[lax.rem(chip + 8 - i, 8)], r_x.at[i], s_x.at[0], (rep, sib))
    for n, out in enumerate((lift_o, down_o)):
        landed_on(out.at[1 - core], r_sib.at[n], s_x.at[0], (rep, sib))
        keeps[n].wait()
    for copy in sent + mates + halves:
        copy.wait_send()


def grads_away(x, lift, down, collective):
    dma = pltpu.SemaphoreType.DMA
    return pl.pallas_call(
        away_kernel,
        out_shape=tuple(jax.ShapeDtypeStruct(a.shape, a.dtype) for a in (x, lift, down)),
        in_specs=[ANY] * 3,
        out_specs=(ANY,) * 3,
        scratch_shapes=[
            pltpu.VMEM(lift.shape, bf16),
            pltpu.VMEM(lift.shape, bf16),
            pltpu.VMEM(down.shape, bf16),
            pltpu.VMEM(down.shape, bf16),
            dma((5,)),
            dma((8,)),
            dma((8,)),
        ]
        + [dma((2,))] * 4,
        compiler_params=params(collective, 32 * 2**20),
        name="grads_away",
    )(x, lift, down)


PART = (48, 384)


def part_of(r):
    rows = pl.ds(pl.multiple_of((r // 4) * PART[0], PART[0]), PART[0])
    return rows, pl.ds(pl.multiple_of(lax.rem(r, 4) * PART[1], PART[1]), PART[1])


def tail_kernel(
    dq_ref, dkv_ref, in_ref, out_ref, w_ref,
    dh_ref, in_sum, out_sum,
    held_k, near_k, held_i, near_i, got_q, got_k, got_i, land_i, land_o, own_o, sum_i, sum_o,
    l_sem, s_q, r_q, s_nk, r_nk, s_ni, r_ni, s_k, r_k, s_i, r_i, s_ri, r_ri, s_ro, r_ro, s_gi, r_gi, s_go, r_go,
):
    rep, shard = place()
    core = lax.rem(shard, 2)
    chip = shard // 2
    sib = shard + 1 - 2 * core
    greet(
        [(rep, lax.rem(shard + i, 16)) for i in range(1, 16)]
        + [(lax.rem(rep + i, 8), shard) for i in range(1, 8)]
    )
    sent = []

    def put(src, dst, s_sem, r_sem, device):
        copy = send(src, dst, s_sem, r_sem, device)
        sent.append(copy)
        return copy

    def landed(ref, sem):
        pltpu.make_async_remote_copy(
            src_ref=ref, dst_ref=ref, send_sem=s_q.at[0], recv_sem=sem,
            device_id=(rep, sib), device_id_type=MESH,
        ).wait_recv()

    order = [1, 7, 2, 6, 3, 5, 4, 0]
    nears, loads = {}, {}
    for name, src, held, near, s_n, r_n, base in (
        ("i", in_ref, held_i, near_i, s_ni, r_ni, 0),
        ("k", dkv_ref, held_k, near_k, s_nk, r_nk, 8),
    ):
        for j in order:
            c = lax.rem(chip + j, 8)
            nears[name, j] = put(
                src.at[2 * c + 1 - core], near.at[j], s_n.at[j], r_n.at[j], (rep, sib)
            )
            loads[name, j] = pltpu.make_async_copy(
                src.at[2 * c + core], held.at[j], l_sem.at[base + j]
            )
            loads[name, j].start()
    own = pltpu.make_async_copy(out_ref.at[part_of(rep)], own_o, l_sem.at[16])
    own.start()
    for i in range(1, 8):
        c = lax.rem(chip + i, 8)
        put(
            dq_ref.at[c], got_q.at[chip], s_q.at[i], r_q.at[i],
            (rep, 2 * c + lax.rem(c + core, 2)),
        )
    mine = lax.rem(chip, 2) == 0

    @pl.when(mine)
    def _():
        copy = pltpu.make_async_copy(dq_ref.at[chip], got_q.at[chip], l_sem.at[17])
        copy.start()
        copy.wait()

    @pl.when(jnp.logical_not(mine))
    def _():
        send(dq_ref.at[chip], got_q.at[chip], s_q.at[0], r_q.at[0], (rep, sib)).wait_send()

    def add_near(name, held, near, j, rows, step):
        nears[name, j].wait_recv()
        loads[name, j].wait()

        def add(t, _):
            at = pl.ds(pl.multiple_of(t * step, step), step)
            held[j, at] = (held[j, at].astype(f32) + near[j, at].astype(f32)).astype(bf16)
            return 0

        lax.fori_loop(0, rows // step, add, 0)

    for name, held, near, got, s_x, r_x, rows in (
        ("i", held_i, near_i, got_i, s_i, r_i, 96),
        ("k", held_k, near_k, got_k, s_k, r_k, OWN),
    ):
        for j in order:
            add_near(name, held, near, j, rows, 32)
            if j:
                c = lax.rem(chip + j, 8)
                put(held.at[j], got.at[chip], s_x.at[j], r_x.at[j], (rep, 2 * c + core))
            else:

                def keep(t, _, held=held, got=got):
                    at = pl.ds(pl.multiple_of(t * 32, 32), 32)
                    got[chip, at] = held[0, at]
                    return 0

                lax.fori_loop(0, rows // 32, keep, 0)
    for i in range(1, 8):
        to = lax.rem(rep + i, 8)
        put(out_ref.at[part_of(to)], land_o.at[i - 1], s_ro.at[i], r_ro.at[i], (to, shard))
    for i in range(1, 8):
        landed(got_i.at[lax.rem(chip + 8 - i, 8)], r_i.at[i])
    for i in range(1, 8):
        to = lax.rem(rep + i, 8)
        put(got_i.at[to], land_i.at[i - 1], s_ri.at[i], r_ri.at[i], (to, shard))

    @pl.when(jnp.logical_not(mine))
    def _():
        landed(got_q.at[chip], r_q.at[0])

    for i in range(1, 8):
        landed(got_q.at[lax.rem(chip + 8 - i, 8)], r_q.at[i])
        landed(got_k.at[lax.rem(chip + 8 - i, 8)], r_k.at[i])
    joined = jnp.concatenate(
        [got_q[c] for c in range(CHIPS)]
        + [got_k[c][:, :HEAD] for c in range(CHIPS)]
        + [got_k[c][:, HEAD:] for c in range(CHIPS)],
        1,
    )
    dh_ref[...] = contract(joined, w_ref[...], ((1,), (1,)))

    own.wait()
    for land, total, part, r_x in ((land_o, sum_o, None, r_ro), (land_i, sum_i, got_i, r_ri)):
        for i in range(1, 8):
            landed(land.at[i - 1], r_x.at[i])

        def add(t, _, land=land, total=total, part=part):
            at = pl.ds(pl.multiple_of(t * 16, 16), 16)
            value = own_o[at] if part is None else part[rep, at]
            value = value.astype(f32)
            for i in range(7):
                value = value + land[i, at].astype(f32)
            total[at] = value.astype(bf16)
            return 0

        lax.fori_loop(0, total.shape[0] // 16, add, 0)
    keeps = [
        pltpu.make_async_copy(sum_o, out_sum.at[part_of(rep)], l_sem.at[18]),
        pltpu.make_async_copy(sum_i, in_sum.at[rep], l_sem.at[19]),
    ]
    for keep in keeps:
        keep.start()
    for i in range(1, 8):
        to = lax.rem(rep + i, 8)
        put(sum_o, out_sum.at[part_of(rep)], s_go.at[i], r_go.at[i], (to, shard))
        put(sum_i, in_sum.at[rep], s_gi.at[i], r_gi.at[i], (to, shard))
    for i in range(1, 8):
        back = lax.rem(rep + 8 - i, 8)
        landed(out_sum.at[part_of(back)], r_go.at[i])
        landed(in_sum.at[back], r_gi.at[i])
    for keep in keeps:
        keep.wait()
    for copy in sent:
        copy.wait_send()


def tail(dq, dkv, inward_part, outward_own, inward_all, collective):
    dma = pltpu.SemaphoreType.DMA
    return pl.pallas_call(
        tail_kernel,
        out_shape=(
            jax.ShapeDtypeStruct((OWN, D), f32),
            jax.ShapeDtypeStruct((CHIPS, 96, 320), bf16),
            jax.ShapeDtypeStruct((96, D), bf16),
        ),
        in_specs=[ANY, ANY, ANY, ANY, VMEM],
        out_specs=(VMEM, ANY, ANY),
        scratch_shapes=[
            pltpu.VMEM((8, OWN, 128), bf16),
            pltpu.VMEM((8, OWN, 128), bf16),
            pltpu.VMEM((8, 96, 320), bf16),
            pltpu.VMEM((8, 96, 320), bf16),
            pltpu.VMEM((8, OWN, 192), bf16),
            pltpu.VMEM((8, OWN, 128), bf16),
            pltpu.VMEM((8, 96, 320), bf16),
            pltpu.VMEM((7, 96, 320), bf16),
            pltpu.VMEM((7,) + PART, bf16),
            pltpu.VMEM(PART, bf16),
            pltpu.VMEM((96, 320), bf16),
            pltpu.VMEM(PART, bf16),
            dma((20,)),
        ]
        + [dma((8,))] * 18,
        compiler_params=params(collective, 56 * 2**20),
        name="tail",
    )(dq, dkv, inward_part, outward_own, inward_all)


def swap_halves(values):
    lanes = values.shape[1]
    lane = lax.broadcasted_iota(jnp.int32, values.shape, 1)
    ahead = pltpu.roll(values, lanes - HEAD // 2, 1)
    behind = pltpu.roll(values, HEAD // 2, 1)
    return jnp.where(lax.rem(lane, HEAD) < HEAD // 2, ahead, behind)


def project_kernel(x_ref, w_ref, g_ref, cos_ref, sin_ref, q_ref, k_ref, v_ref, u_ref):
    i = pl.program_id(0)
    stream = x_ref[...].astype(f32)
    u_ref[...] = (stream * inverse_root(stream) * g_ref[...]).astype(bf16)
    core = lax.rem(lax.axis_index("shard"), 2)
    first = pl.multiple_of(lax.rem(i + core, 2) * OWN, OWN)
    own = pl.ds(first, OWN)
    queries = jnp.dot(u_ref[own, :], w_ref[:, :256], preferred_element_type=f32)
    cos, sin = cos_ref[own, :], sin_ref[own, :]
    cos, sin = jnp.concatenate([cos, cos], 1), jnp.concatenate([sin, sin], 1)
    turned = (queries * cos + swap_halves(queries) * sin).astype(bf16)
    turned = turned * jnp.bfloat16(HEAD**-0.5)
    for r in range(GROUP):
        q_ref[0, r * OWN : (r + 1) * OWN, :] = turned[:, r * HEAD : (r + 1) * HEAD]
    pairs = jnp.dot(u_ref[...], w_ref[:, 256:], preferred_element_type=f32)
    keys = pairs * cos_ref[...] + swap_halves(pairs) * sin_ref[...]
    k_ref[...] = keys[:, :HEAD].astype(bf16)
    lane = lax.broadcasted_iota(jnp.int32, pairs.shape, 1)
    v_ref[...] = jnp.where(lane < HEAD, pltpu.roll(pairs, HEAD, 1), 1.0).astype(bf16)


def project(x_all, weight, gain, cos, sin):
    return pl.pallas_call(
        project_kernel,
        grid=(BLOCKS,),
        in_specs=[
            pl.BlockSpec((KEYS, D), lambda i: (i, 0)),
            pl.BlockSpec((D, 384), lambda i: (0, 0)),
            pl.BlockSpec((1, D), lambda i: (0, 0)),
            pl.BlockSpec((KEYS, 128), lambda i: (i, 0)),
            pl.BlockSpec((KEYS, 128), lambda i: (i, 0)),
        ],
        out_specs=(
            pl.BlockSpec((1, ROWS, HEAD), lambda i: (i, 0, 0)),
            pl.BlockSpec((KEYS, HEAD), lambda i: (i, 0)),
            pl.BlockSpec((KEYS, 128), lambda i: (i, 0)),
            pl.BlockSpec((KEYS, D), lambda i: (i, 0)),
        ),
        out_shape=(
            jax.ShapeDtypeStruct((BLOCKS, ROWS, HEAD), bf16),
            jax.ShapeDtypeStruct((SEQ, HEAD), bf16),
            jax.ShapeDtypeStruct((SEQ, 128), bf16),
            jax.ShapeDtypeStruct((SEQ, D), bf16),
        ),
        compiler_params=pltpu.CompilerParams(vmem_limit_bytes=48 * 2**20),
        name="project_heads",
    )(x_all, weight, gain, cos, sin)


def contract(a, b, dims, precision=None):
    return lax.dot_general(
        a, b, ((dims[0], dims[1]), ((), ())), preferred_element_type=f32, precision=precision
    )


def attend_kernel(q_ref, k_ref, v_ref, b_ref, o_ref, l_ref, bo_ref, local_sem, s_sem, r_sem):
    i = pl.program_id(0)
    core = lax.rem(lax.axis_index("shard"), 2)
    begin, relay, finish = spread(b_ref, bo_ref, local_sem.at[0], s_sem, r_sem)

    @pl.when(i == 0)
    def _():
        rep, shard = place()
        chip = shard // 2
        greet(
            [(rep, shard + 1 - 2 * core)]
            + [(rep, 2 * lax.rem(chip + n, 8) + core) for n in range(1, 8)]
        )
        begin()

    @pl.when(i == 1)
    def _():
        relay()

    shift = lax.rem(i + core, 2) * OWN
    q = q_ref[0]

    def step(c, carry, last=False):
        top, total = carry
        at = pl.ds(pl.multiple_of(c * KEYS, KEYS), KEYS)
        scores = contract(q, k_ref[at, :], ((1,), (1,)))
        if last:
            row = lax.broadcasted_iota(jnp.int32, (OWN, KEYS), 0)
            column = lax.broadcasted_iota(jnp.int32, (OWN, KEYS), 1)
            bias = jnp.where(column <= row + shift, 0.0, -1e30)
            scores = scores + jnp.concatenate([bias] * GROUP, 0)
        high = jnp.maximum(top, jnp.max(scores, 1, keepdims=True))
        prob = jnp.exp(scores - high).astype(bf16)
        total = total * jnp.exp(top - high) + jnp.dot(
            prob, v_ref[at, :], preferred_element_type=f32
        )
        return high, total

    carry = (jnp.full((ROWS, 1), -1e30, f32), jnp.zeros((ROWS, 128), f32))
    carry = lax.fori_loop(0, i, step, carry)
    top, total = step(i, carry, True)
    weight = total[:, HEAD : HEAD + 1]
    result = (total[:, :HEAD] / weight).astype(bf16)
    o_ref[0] = jnp.concatenate([result[r * OWN : (r + 1) * OWN] for r in range(GROUP)], 1)
    column = lax.broadcasted_iota(jnp.int32, (8, 8), 1)
    l_ref[0] = contract(
        jnp.where(column == 0, 1.0, 0.0).astype(f32),
        jnp.broadcast_to(top + jnp.log(weight), (ROWS, 8)),
        ((1,), (1,)),
        lax.Precision.HIGHEST,
    )

    @pl.when(i == BLOCKS - 1)
    def _():
        finish()


def attend(q, k, v, units, collective):
    return pl.pallas_call(
        attend_kernel,
        grid=(BLOCKS,),
        in_specs=[
            pl.BlockSpec((1, ROWS, HEAD), lambda i: (i, 0, 0)),
            pl.BlockSpec((SEQ, HEAD), lambda i: (0, 0)),
            pl.BlockSpec((SEQ, 128), lambda i: (0, 0)),
            ANY,
        ],
        out_specs=(
            pl.BlockSpec((1, OWN, GROUP * HEAD), lambda i: (i, 0, 0)),
            pl.BlockSpec((1, 8, ROWS), lambda i: (i, 0, 0)),
            ANY,
        ),
        out_shape=(
            jax.ShapeDtypeStruct((BLOCKS, OWN, GROUP * HEAD), bf16),
            jax.ShapeDtypeStruct((BLOCKS, 8, ROWS), f32),
            jax.ShapeDtypeStruct((SHARDS,) + units.shape[1:], bf16),
        ),
        scratch_shapes=[
            pltpu.SemaphoreType.DMA((1,)),
            pltpu.SemaphoreType.DMA((2, 8)),
            pltpu.SemaphoreType.DMA((2, 8)),
        ],
        compiler_params=params(collective, 48 * 2**20),
        name="attend",
    )(q, k, v, units)


def attend_back_kernel(
    q_ref, k_ref, v_ref, g_ref, a_ref, l_ref, cos_ref, sin_ref, qcos_ref, qsin_ref, part_ref,
    lift_ref, down_ref, dq_ref, dkv_ref, part_out, lift_out, down_out,
    dk, dv, dq, held, near, landed, local_sem, s_sem, r_sem, h_sem, s_near, r_near, s_far, r_far,
):
    i = pl.program_id(0)
    rep, shard = place()
    core = lax.rem(shard, 2)
    chip = shard // 2
    sib = shard + 1 - 2 * core
    shift = lax.rem(i + core, 2) * OWN
    x = rep // 2
    kept = [
        (n, src, dst)
        for n, (src, dst) in enumerate(((lift_ref, lift_out), (down_ref, down_out)))
    ]

    def copy_same(n, src, dst):
        return pltpu.make_async_copy(src, dst.at[pl.ds(2 * x, 2)], local_sem.at[n])

    def copy_x(n, src, dst, dx, at):
        return pltpu.make_async_remote_copy(
            src_ref=src,
            dst_ref=dst.at[pl.ds(2 * at, 2)],
            send_sem=s_sem.at[n, dx],
            recv_sem=r_sem.at[n, dx],
            device_id=(along_x(rep, dx), shard),
            device_id_type=MESH,
        )

    def copy_near(j):
        return pltpu.make_async_remote_copy(
            src_ref=part_ref.at[2 * lax.rem(chip + j, 8) + 1 - core],
            dst_ref=near.at[j],
            send_sem=s_near.at[j],
            recv_sem=r_near.at[j],
            device_id=(rep, sib),
            device_id_type=MESH,
        )

    def copy_own(j):
        return pltpu.make_async_copy(
            part_ref.at[2 * lax.rem(chip + j, 8) + core], held.at[j], h_sem.at[j]
        )

    def copy_far(j):
        return pltpu.make_async_remote_copy(
            src_ref=held.at[j],
            dst_ref=landed.at[j - 1],
            send_sem=s_far.at[j],
            recv_sem=r_far.at[j],
            device_id=(rep, 2 * lax.rem(chip + j, 8) + core),
            device_id_type=MESH,
        )

    @pl.when(i == 0)
    def _():
        greet(
            [(rep, sib)]
            + [(rep, 2 * lax.rem(chip + n, 8) + core) for n in range(1, 8)]
            + [(along_x(rep, dx), shard) for dx in (1, 2, 3)]
        )
        for j in range(8):
            copy_near(j).start()
            copy_own(j).start()
        for n, src, dst in kept:
            copy_same(n, src, dst).start()
            for dx in (1, 2, 3):
                copy_x(n, src, dst, dx, x).start()
        dk[...] = jnp.zeros_like(dk)
        dv[...] = jnp.zeros_like(dv)

    @pl.when(i == 3)
    def _():
        for j in range(8):
            copy_near(j).wait_recv()
            copy_own(j).wait()

            def add(t, _, j=j):
                at = pl.ds(pl.multiple_of(t * 32, 32), 32)
                held[j, at] = (held[j, at].astype(f32) + near[j, at].astype(f32)).astype(bf16)
                return 0

            lax.fori_loop(0, 3, add, 0)
            if j:
                copy_far(j).start()

    q = q_ref[0]
    grad = jnp.concatenate([g_ref[0][:, r * HEAD : (r + 1) * HEAD] for r in range(GROUP)], 0)
    dq[...] = jnp.zeros_like(dq)
    lse = l_ref[0][:1]
    lane = lax.broadcasted_iota(jnp.int32, (8, GROUP * HEAD), 1)
    row = lax.broadcasted_iota(jnp.int32, (8, GROUP * HEAD), 0)
    sums = contract(
        jnp.where(lane // HEAD == row, 1.0, 0.0).astype(f32),
        g_ref[0].astype(f32) * a_ref[0].astype(f32),
        ((1,), (1,)),
        lax.Precision.HIGHEST,
    )
    delta = jnp.concatenate([sums[r : r + 1] for r in range(GROUP)], 1)

    def step(c, _, last=False):
        at = pl.ds(pl.multiple_of(c * KEYS, KEYS), KEYS)
        keys = k_ref[at, :]
        scores = contract(keys, q, ((1,), (1,)))
        if last:
            key = lax.broadcasted_iota(jnp.int32, (KEYS, OWN), 0)
            token = lax.broadcasted_iota(jnp.int32, (KEYS, OWN), 1)
            bias = jnp.where(key <= token + shift, 0.0, -1e30)
            scores = scores + jnp.concatenate([bias] * GROUP, 1)
        prob = jnp.exp(scores - lse)
        back = contract(v_ref[at, :HEAD], grad, ((1,), (1,)))
        slope = (prob * (back - delta)).astype(bf16)
        dv[at, :] += jnp.dot(prob.astype(bf16), grad, preferred_element_type=f32)
        dk[at, :] += jnp.dot(slope, q, preferred_element_type=f32)
        dq[...] += contract(slope, keys, ((0,), (0,)))
        return 0

    lax.fori_loop(0, i, step, 0)
    step(i, 0, True)
    wide = jnp.concatenate(
        [dq[r * OWN : (r + 1) * OWN, :] for r in range(GROUP)] + [jnp.zeros((OWN, HEAD), f32)], 1
    )
    wide = wide * (HEAD**-0.5)
    cos, sin = qcos_ref[...], qsin_ref[...]
    cos, sin = jnp.concatenate([cos, cos], 1), jnp.concatenate([sin, sin], 1)
    wide = wide * cos - swap_halves(wide) * sin
    dq_ref[0] = wide[:, : GROUP * HEAD].astype(bf16)

    @pl.when(i == BLOCKS - 1)
    def _():
        def turn(c, _):
            at = pl.ds(pl.multiple_of(c * OWN, OWN), OWN)
            both = jnp.concatenate([dk[at, :], dv[at, :]], 1)
            lane = lax.broadcasted_iota(jnp.int32, both.shape, 1)
            turned = both * cos_ref[at, :] - swap_halves(both) * sin_ref[at, :]
            dkv_ref[at, :] = jnp.where(lane < HEAD, turned, both).astype(bf16)
            return 0

        lax.fori_loop(0, SHARDS, turn, 0)
        for j in range(1, 8):
            copy_far(j).wait_recv()

        def add(t, _):
            at = pl.ds(pl.multiple_of(t * 32, 32), 32)
            total = held[0, at].astype(f32)
            for j in range(7):
                total = total + landed[j, at].astype(f32)
            part_out[at] = total.astype(bf16)
            return 0

        lax.fori_loop(0, 3, add, 0)
        for n, src, dst in kept:
            copy_same(n, src, dst).wait()
            for dx in (1, 2, 3):
                copy_x(n, src, dst, dx, lax.rem(x + 4 - dx, 4)).wait_recv()
            for dx in (1, 2, 3):
                copy_x(n, src, dst, dx, x).wait_send()
        for j in range(8):
            copy_near(j).wait_send()
            if j:
                copy_far(j).wait_send()


def attend_back(q, k, v, grad, attended, lse, cos, sin, part, lift, down, collective):
    def own(i):
        return (2 * i + lax.rem(i + lax.rem(lax.axis_index("shard"), 2), 2), 0)

    whole = lambda i: (0, 0)
    block = lambda i: (i, 0, 0)
    return pl.pallas_call(
        attend_back_kernel,
        grid=(BLOCKS,),
        in_specs=[
            pl.BlockSpec((1, ROWS, HEAD), block),
            pl.BlockSpec((SEQ, HEAD), whole),
            pl.BlockSpec((SEQ, 128), whole),
            pl.BlockSpec((1, OWN, GROUP * HEAD), block),
            pl.BlockSpec((1, OWN, GROUP * HEAD), block),
            pl.BlockSpec((1, 8, ROWS), block),
            pl.BlockSpec((SEQ, 128), whole),
            pl.BlockSpec((SEQ, 128), whole),
            pl.BlockSpec((OWN, 128), own),
            pl.BlockSpec((OWN, 128), own),
            ANY,
            ANY,
            ANY,
        ],
        out_specs=(
            pl.BlockSpec((1, OWN, GROUP * HEAD), block),
            pl.BlockSpec((SEQ, 128), whole),
            pl.BlockSpec(part.shape[1:], whole),
            ANY,
            ANY,
        ),
        out_shape=(
            jax.ShapeDtypeStruct((BLOCKS, OWN, GROUP * HEAD), bf16),
            jax.ShapeDtypeStruct((SEQ, 128), bf16),
            jax.ShapeDtypeStruct(part.shape[1:], bf16),
            jax.ShapeDtypeStruct((PEERS,) + lift.shape[1:], bf16),
            jax.ShapeDtypeStruct((PEERS,) + down.shape[1:], bf16),
        ),
        scratch_shapes=[
            pltpu.VMEM((SEQ, HEAD), f32),
            pltpu.VMEM((SEQ, HEAD), f32),
            pltpu.VMEM((ROWS, HEAD), f32),
            pltpu.VMEM((8,) + part.shape[1:], bf16),
            pltpu.VMEM((8,) + part.shape[1:], bf16),
            pltpu.VMEM((7,) + part.shape[1:], bf16),
            pltpu.SemaphoreType.DMA((2,)),
            pltpu.SemaphoreType.DMA((2, 4)),
            pltpu.SemaphoreType.DMA((2, 4)),
        ]
        + [pltpu.SemaphoreType.DMA((8,))] * 5,
        compiler_params=params(collective, 48 * 2**20),
        name="attend_back",
    )(q, k, v, grad, attended, lse, cos, sin, cos, sin, part, lift, down)


def experts_kernel(
    u_ref, y_ref, c_ref, wl_ref, wd_ref, e_ref, out_ref, du_ref, lift_ref, down_ref, lift, down
):
    i = pl.program_id(0)
    u, y = u_ref[...], y_ref[...]
    lifted = jnp.dot(u, wl_ref[...], preferred_element_type=f32)
    back = contract(y, wd_ref[...], ((1,), (1,)))
    share = jnp.dot(c_ref[...], e_ref[...], preferred_element_type=f32)
    gate, raised = lifted[:, :HID], lifted[:, HID:]
    s = jax.nn.sigmoid(gate)
    swish = gate * s
    act = (share * swish * raised).astype(bf16)
    back = back * share
    grad_gate = back * raised * s * (1.0 + gate * (1.0 - s))
    grad_lift = jnp.concatenate([grad_gate, back * swish], 1).astype(bf16)
    out_ref[...] = jnp.dot(act, wd_ref[...], preferred_element_type=f32).astype(bf16)
    du_ref[...] = contract(grad_lift, wl_ref[...], ((1,), (1,))).astype(bf16)

    @pl.when(i == 0)
    def _():
        lift[...] = jnp.zeros_like(lift)
        down[...] = jnp.zeros_like(down)

    lift[...] += contract(u, grad_lift, ((0,), (0,)))
    down[...] += contract(act, y, ((0,), (0,)))

    @pl.when(i == pl.num_programs(0) - 1)
    def _():
        lift_ref[...] = lift[...].astype(bf16)
        down_ref[...] = down[...].astype(bf16)


def experts(u_all, y_all, wl, wd, spread):
    step = 384
    rows = lambda i: (i, 0)
    whole = lambda i: (0, 0)
    once = pl.Buffered(1)
    return pl.pallas_call(
        experts_kernel,
        grid=(PEERS * OWN // step,),
        in_specs=[
            pl.BlockSpec((step, D), rows),
            pl.BlockSpec((step, D), rows),
            pl.BlockSpec((step, 128), lambda i: (i, D // 128)),
            pl.BlockSpec((D, EXP), whole, pipeline_mode=once),
            pl.BlockSpec((HID, D), whole, pipeline_mode=once),
            pl.BlockSpec((128, HID), whole, pipeline_mode=once),
        ],
        out_specs=(
            pl.BlockSpec((step, D), rows),
            pl.BlockSpec((step, D), rows),
            pl.BlockSpec((D, EXP), whole),
            pl.BlockSpec((HID, D), whole),
        ),
        out_shape=(
            jax.ShapeDtypeStruct((PEERS * OWN, D), bf16),
            jax.ShapeDtypeStruct((PEERS * OWN, D), bf16),
            jax.ShapeDtypeStruct((D, EXP), bf16),
            jax.ShapeDtypeStruct((HID, D), bf16),
        ),
        scratch_shapes=[pltpu.VMEM((D, EXP), f32), pltpu.VMEM((HID, D), f32)],
        compiler_params=pltpu.CompilerParams(vmem_limit_bytes=60 * 2**20),
        name="experts",
    )(u_all, y_all, y_all, wl, wd, spread)


def units_kernel(w_ref, code_ref, out_ref):
    x = lax.axis_index("rep") // 2
    row = lax.broadcasted_iota(jnp.int32, (FF_EXP, HID), 0)
    there = (row // 32) * 1024 + lax.rem(row, 32)
    here = jnp.broadcast_to(code_ref[...], (FF_EXP, HID))
    base = (5 * x) // 2
    for k in range(2):
        for part in range(2):
            total = jnp.zeros((96, HID), f32)
            for i in range(3):
                chosen = there + 32 * (base + i) == here + FLAT * (2 * x + k)
                total = total + jnp.dot(
                    w_ref[base + i][:, FF_EXP * part : FF_EXP * (part + 1)],
                    jnp.where(chosen, 1.0, 0.0).astype(bf16),
                    preferred_element_type=f32,
                )
            out_ref[k, :, HID * part : HID * (part + 1)] = total.astype(bf16)


def one_step(kernel, arrays, shapes, name):
    return pl.pallas_call(
        kernel,
        in_specs=[VMEM] * len(arrays),
        out_specs=(VMEM,) * len(shapes),
        out_shape=tuple(jax.ShapeDtypeStruct(shape, dtype) for shape, dtype in shapes),
        compiler_params=pltpu.CompilerParams(vmem_limit_bytes=56 * 2**20),
        name=name,
    )(*arrays)


def side_by_side(ref):
    return jnp.concatenate([ref[c] for c in range(CHIPS)], 1)


def mix_kernel(a_ref, w_ref, x_ref, g_ref, mixed_ref, low_ref):
    mixed = x_ref[...].astype(f32) + jnp.dot(
        side_by_side(a_ref), w_ref[...], preferred_element_type=f32
    )
    mixed_ref[...] = mixed
    low_ref[...] = (mixed * inverse_root(mixed) * g_ref[...]).astype(bf16)


def unmix_kernel(du_ref, e_ref, mixed_ref, y_ref, g_ref, w_ref, a_ref, out_ref, dz_ref, ga_ref, part_ref):
    mixed = mixed_ref[...]
    out_ref[...] = mixed + e_ref[...]
    inverse = inverse_root(mixed)
    dz = y_ref[...].astype(f32) + norm_back(du_ref[...] * g_ref[...], mixed * inverse, inverse)
    dz_ref[...] = dz
    low = dz.astype(bf16)
    back = contract(low, w_ref[...], ((1,), (1,))).astype(bf16)
    for c in range(CHIPS):
        ga_ref[c] = back[:, c * 192 : (c + 1) * 192]
    part = contract(side_by_side(a_ref), low, ((0,), (0,))).astype(bf16)
    for s in range(SHARDS):
        part_ref[s] = part[s * 96 : (s + 1) * 96]


def finish_kernel(dh_ref, dz_ref, x_ref, g_ref, out_ref):
    stream = x_ref[...].astype(f32)
    inverse = inverse_root(stream)
    out_ref[...] = dz_ref[...] + norm_back(dh_ref[...] * g_ref[...], stream * inverse, inverse)


def inward_part_kernel(u_ref, dq_ref, dkv_ref, out_ref, total):
    i = pl.program_id(0)
    core = lax.rem(lax.axis_index("shard"), 2)
    first = pl.multiple_of(lax.rem(i + core, 2) * OWN, OWN)

    @pl.when(i == 0)
    def _():
        total[...] = jnp.zeros_like(total)

    total[:, :192] += contract(u_ref[pl.ds(first, OWN), :], dq_ref[0], ((0,), (0,)))
    total[:, 256:] += contract(u_ref[...], dkv_ref[...], ((0,), (0,)))

    @pl.when(i == BLOCKS - 1)
    def _():
        both = jnp.concatenate([total[:, :192], total[:, 256:]], 1).astype(bf16)
        for s in range(SHARDS):
            out_ref[s] = both[s * 96 : (s + 1) * 96]


def inward_parts(u_all, dq, dkv):
    return pl.pallas_call(
        inward_part_kernel,
        grid=(BLOCKS,),
        in_specs=[
            pl.BlockSpec((KEYS, D), lambda i: (i, 0)),
            pl.BlockSpec((1, OWN, GROUP * HEAD), lambda i: (i, 0, 0)),
            pl.BlockSpec((KEYS, 128), lambda i: (i, 0)),
        ],
        out_specs=pl.BlockSpec((SHARDS, 96, 320), lambda i: (0, 0, 0)),
        out_shape=jax.ShapeDtypeStruct((SHARDS, 96, 320), bf16),
        scratch_shapes=[pltpu.VMEM((D, 384), f32)],
        compiler_params=pltpu.CompilerParams(vmem_limit_bytes=48 * 2**20),
        name="inward_parts",
    )(u_all, dq, dkv)


def adam(weight, old_mean, square, gradient, step_rate, decay_rate):
    values = weight.astype(f32)
    moment = beta_one * old_mean.astype(f32) + (1.0 - beta_one) * gradient
    variance = beta_two * square.astype(f32) + (1.0 - beta_two) * gradient * gradient
    normed_step = (
        moment
        / (1.0 - beta_one**STEP)
        / (jnp.sqrt(variance / (1.0 - beta_two**STEP)) + adam_epsilon)
    )
    return (moment, variance, values - step_rate * (normed_step + decay_rate * values))


def adam_lifting_kernel(w_ref, m_ref, s_ref, g_ref, code_ref, mo_ref, so_ref, wo_ref, dot_ref, grad):
    e = pl.program_id(0)
    first, last = (4 * e) // 5, (4 * e + 3) // 5
    column = lax.broadcasted_iota(jnp.int32, (HID, FF_EXP), 1)
    there = (column // 32) * 1024 + lax.rem(column, 32) + 32 * e
    here = jnp.broadcast_to(code_ref[...], (HID, FF_EXP))
    chosen_first = jnp.where(there == here + FLAT * first, 1.0, 0.0).astype(bf16)
    skip = jnp.where(first == last, 1 << 20, 0)
    chosen_last = jnp.where(there == here + (FLAT * last + skip), 1.0, 0.0).astype(bf16)
    for part in range(2):
        columns = slice(HID * part, HID * (part + 1))
        grad[:, FF_EXP * part : FF_EXP * (part + 1)] = jnp.dot(
            g_ref[first][:, columns], chosen_first, preferred_element_type=f32
        ) + jnp.dot(g_ref[last][:, columns], chosen_last, preferred_element_type=f32)

    @pl.when(e == 0)
    def _():
        dot_ref[...] = jnp.zeros_like(dot_ref)

    dot = jnp.sum(w_ref[0].astype(f32) * grad[...], 1, keepdims=True)
    dot_ref[...] += jnp.broadcast_to(dot, dot_ref.shape)
    mo_ref[0], so_ref[0], wo_ref[0] = adam(
        w_ref[0], m_ref[0], s_ref[0], grad[...], rate_lifting, weight_decay
    )


def adam_lifting(weight, mean, square, grad, code):
    block = pl.BlockSpec((1, 96, 2 * FF_EXP), lambda e: (e, 0, 0))
    shape = jax.ShapeDtypeStruct(weight.shape, f32)
    return pl.pallas_call(
        adam_lifting_kernel,
        grid=(EXPERTS,),
        in_specs=[
            block,
            block,
            block,
            pl.BlockSpec(grad.shape, lambda e: (0, 0, 0)),
            pl.BlockSpec(code.shape, lambda e: (0, 0)),
        ],
        out_specs=(block, block, block, pl.BlockSpec((96, 128), lambda e: (0, 0))),
        out_shape=(shape, shape, shape, jax.ShapeDtypeStruct((96, 128), f32)),
        scratch_shapes=[pltpu.VMEM((96, 2 * FF_EXP), f32)],
        compiler_params=pltpu.CompilerParams(vmem_limit_bytes=48 * 2**20),
        name="adam_lifting",
    )(weight, mean, square, grad, code)


def adam_inward_kernel(w_ref, m_ref, s_ref, g_ref, mo_ref, so_ref, wo_ref, dot_ref):
    parts = [g_ref[c].astype(f32) for c in range(CHIPS)]
    grad = jnp.concatenate(
        [p[:, :192] for p in parts] + [p[:, 192:256] for p in parts] + [p[:, 256:] for p in parts], 1
    )
    dot = jnp.sum(w_ref[...].astype(f32) * grad, 1, keepdims=True)
    dot_ref[...] = jnp.broadcast_to(dot, dot_ref.shape)
    mo_ref[...], so_ref[...], wo_ref[...] = adam(
        w_ref[...], m_ref[...], s_ref[...], grad, rate_inward, weight_decay
    )


def adam_inward(weight, mean, square, grad):
    shape = jax.ShapeDtypeStruct(weight.shape, f32)
    return pl.pallas_call(
        adam_inward_kernel,
        in_specs=[VMEM] * 4,
        out_specs=(VMEM,) * 4,
        out_shape=(shape, shape, shape, jax.ShapeDtypeStruct((96, 128), f32)),
        compiler_params=pltpu.CompilerParams(vmem_limit_bytes=48 * 2**20),
        name="adam_inward",
    )(weight, mean, square, grad)


def tables():
    half = HEAD // 2
    frequency = np.float32(10000.0) ** (-(2.0 * np.arange(half, dtype=np.float32)) / HEAD)
    phases = np.arange(SEQ, dtype=np.float32)[:, None] * frequency[None, :].astype(np.float32)
    cos, sin = np.cos(phases).astype(np.float32), np.sin(phases).astype(np.float32)
    return (
        np.concatenate([cos, cos, cos, cos], 1),
        np.concatenate([-sin, sin, -sin, sin], 1),
    )


def unit_codes():
    unit = np.arange(HID, dtype=np.int32)
    return (unit // FLAT) * 1024 + unit % FLAT


def inverse_root(stream):
    return lax.rsqrt(jnp.mean(stream * stream, -1, keepdims=True) + norm_epsilon)


def norm_back(scaled, unit, inverse):
    return inverse * (scaled - unit * jnp.mean(scaled * unit, -1, keepdims=True))


def per_device(
    layer_input,
    grad_output,
    routes,
    route_logits,
    norm_gains,
    inward,
    outward,
    lifting,
    lowering,
    mean_gains,
    mean_inward,
    mean_outward,
    mean_lifting,
    mean_lowering,
    square_gains,
    square_inward,
    square_outward,
    square_lifting,
    square_lowering,
):
    gains = norm_gains.astype(f32)
    cos, sin = (jnp.asarray(t) for t in tables())

    by_head = jnp.concatenate(
        [
            inward[:, :1536].reshape(96, KV_HEADS, 192),
            jnp.broadcast_to(
                jnp.pad(norm_gains.T, ((0, 0), (0, HEAD - 2)))[:, None, :], (96, KV_HEADS, HEAD)
            ),
            inward[:, 1536:2048].reshape(96, KV_HEADS, HEAD),
            inward[:, 2048:].reshape(96, KV_HEADS, HEAD),
        ],
        2,
    ).transpose(1, 0, 2)
    lifting_rows = lifting.transpose(1, 0, 2)
    codes = jnp.asarray(unit_codes())
    x = lax.axis_index("rep") // 2
    position = 2 * x + lax.rem(lax.axis_index("shard"), 2)
    (by_unit,) = one_step(
        units_kernel, (lifting_rows, codes[None, :]), (((2, 96, EXP), bf16),), "choose_units"
    )
    low_rows = lowering.transpose(1, 0, 2).reshape(EXPERTS * 32, D)
    low_rows = lax.dynamic_slice(low_rows, (2 * FLAT * x, 0), (2 * FLAT, D)).reshape(2, FLAT, D)
    low_rows = jnp.pad(low_rows, ((0, 0), (0, FLAT_PAD - FLAT), (0, 0)))
    expert = (FLAT * position + lax.rem(jnp.arange(HID), FLAT)) // 32
    row = jnp.arange(128)[:, None]
    share_table = ((row == expert) | (row == expert + 16)).astype(bf16)

    gates = jax.nn.softmax(route_logits, axis=-1)
    picked = routes[:, :, None] == jnp.arange(EXPERTS, dtype=jnp.int32)[None, None, :]
    combine = jnp.sum(jnp.where(picked, gates[:, :, None], 0.0), axis=1)
    high = lax.reduce_precision(combine, 8, 7)
    rest = combine - high
    shares = jnp.concatenate(
        [jnp.pad(high, ((0, 0), (0, 6))), jnp.pad(rest, ((0, 0), (0, 102)))], 1
    ).astype(bf16)
    x_all, head_weight, y_all = start(
        layer_input, by_head, jnp.concatenate([grad_output, shares], 1), 2
    )
    head_weight = head_weight.reshape(D, 384)
    gain_rows = head_weight[:, 192:194].T.astype(f32)
    gain_one, gain_two = gain_rows[0:1], gain_rows[1:2]
    late_outward, x_all = lax.optimization_barrier((outward, x_all))
    outward_all = lax.all_gather(late_outward, "shard", axis=0, tiled=True)

    q, k, v, u_one = project(x_all, head_weight, gain_one, cos, sin)
    attended, lse, unit_weight = attend(q, k, v, by_unit, 1)
    unit_weight = unit_weight.reshape(D, EXP)
    (own_attended,) = exchange((attended,), ("home",), 3, "attended_home")
    mixed, low_two = one_step(
        mix_kernel,
        (own_attended, outward_all, layer_input, gain_two),
        (((OWN, D), f32), ((OWN, D), bf16)),
        "mix",
    )
    u_two, down_weight = second(low_two, low_rows, 4)
    down_weight = down_weight[:, :FLAT].reshape(HID, D)
    late_inward, u_two = lax.optimization_barrier((inward, u_two))
    inward_all = lax.all_gather(late_inward, "shard", axis=0, tiled=True)

    out_part, du_part, lift_part, down_part = experts(
        u_two, y_all, unit_weight, down_weight, share_table
    )
    du, expert_out, lift_sum, down_sum = reduce_blocks(
        du_part.reshape(PEERS, OWN, D),
        out_part.reshape(PEERS, OWN, D),
        lift_part.reshape(CHIPS, 192, EXP),
        down_part.reshape(CHIPS, 2 * FLAT, D),
        5,
    )
    layer_output, grad_mixed, away, outward_part = one_step(
        unmix_kernel,
        (du, expert_out, mixed, grad_output, gain_two, outward_all, own_attended),
        (((OWN, D), f32), ((OWN, D), f32), ((CHIPS, OWN, 192), bf16), ((SHARDS, 96, D), bf16)),
        "unmix",
    )
    down_sum = jnp.pad(down_sum.reshape(2, FLAT, D), ((0, 0), (0, FLAT_PAD - FLAT), (0, 0)))
    head_grads, lift_pair, down_pair = grads_away(
        away, lift_sum.reshape(2, 96, EXP), down_sum, 6
    )
    dq, dkv, outward_own, lift_got, down_got = attend_back(
        q, k, v, head_grads, attended, lse, cos, sin, outward_part, lift_pair, down_pair, 8
    )
    inward_part = inward_parts(u_one, dq, dkv)
    dh, inward_sum, outward_sum = tail(
        dq, dkv.reshape(SHARDS, OWN, 128), inward_part, outward_own, inward_all, 7
    )
    (input_grad,) = one_step(
        finish_kernel, (dh, grad_mixed, layer_input, gain_one), (((OWN, D), f32),), "finish"
    )
    outward_grad = outward_sum.astype(f32)
    down_grad = (
        down_got[:, :FLAT].reshape(EXPERTS, 32, D).transpose(1, 0, 2).astype(f32)
    )

    new_lifting = adam_lifting(
        lifting_rows,
        mean_lifting.transpose(1, 0, 2),
        square_lifting.transpose(1, 0, 2),
        lift_got,
        codes[:, None],
    )
    lifting_dot = new_lifting[3]
    new_lifting = tuple(t.transpose(1, 0, 2) for t in new_lifting[:3])
    new_inward = adam_inward(inward, mean_inward, square_inward, inward_sum)
    gain_grad = jnp.stack([new_inward[3][:, 0], lifting_dot[:, 0]]) / gains
    new_gains = adam(norm_gains, mean_gains, square_gains, gain_grad, rate_gains, 0.0)
    new_outward = adam(
        outward, mean_outward, square_outward, outward_grad, rate_outward, weight_decay
    )
    new_lowering = adam(
        lowering, mean_lowering, square_lowering, down_grad, rate_lowering, weight_decay
    )
    return (
        layer_output,
        input_grad,
        new_gains[0],
        new_inward[0],
        new_outward[0],
        new_lifting[0],
        new_lowering[0],
        new_gains[1],
        new_inward[1],
        new_outward[1],
        new_lifting[1],
        new_lowering[1],
        new_gains[2],
        new_inward[2],
        new_outward[2],
        new_lifting[2],
        new_lowering[2],
    )


def solution(mesh):
    tokens = P(("rep", "shard"), None)
    gains, flat, deep = P(None, "shard"), P("shard", None), P("shard", None, None)
    weights = (gains, flat, flat, deep, deep)
    return jax.shard_map(
        per_device,
        mesh=mesh,
        in_specs=(tokens,) * 4 + weights * 3,
        out_specs=(tokens,) * 2 + weights * 3,
        check_vma=False,
    )
```

```python
import functools

import jax
import jax.numpy as jnp
import numpy as np
from jax import lax
from jax.experimental import pallas as pl
from jax.experimental.pallas import tpu as pltpu
from jax.sharding import PartitionSpec as P

HEADS = 24
KV_HEADS = 8
HEAD = 64
GROUP = HEADS // KV_HEADS
FF_EXP = 512
EXPERTS = 10
STEP = 10

norm_epsilon = 1e-06
beta_one = 0.9
beta_two = 0.95
adam_epsilon = 1e-08
weight_decay = 0.1
rate_gains = 0.5
rate_inward = 0.05
rate_outward = 0.3
rate_lifting = 0.05
rate_lowering = 0.3

SHARDS = 16
CHIPS = 8
REPS = 8
OWN = 192
SEQ = OWN * SHARDS
D = 1536
PEERS = 8
FLAT = 40
FLAT_PAD = 48
HID = SHARDS * FLAT
EXP = 2 * HID
BLOCKS = 8
ROWS = GROUP * OWN
KEYS = 2 * OWN

MESH = pl.DeviceIdType.MESH
bf16 = jnp.bfloat16
f32 = jnp.float32


def place():
    rep = lax.axis_index("rep")
    shard = lax.axis_index("shard")
    return rep, shard


def greet(devices):
    barrier = pltpu.get_barrier_semaphore()
    for device in devices:
        pl.semaphore_signal(barrier, inc=1, device_id=device, device_id_type=MESH)
    pl.semaphore_wait(barrier, len(devices))


def send(src, dst, send_sem, recv_sem, device):
    copy = pltpu.make_async_remote_copy(
        src_ref=src,
        dst_ref=dst,
        send_sem=send_sem,
        recv_sem=recv_sem,
        device_id=device,
        device_id_type=MESH,
    )
    copy.start()
    return copy


def params(collective, vmem=None):
    return pltpu.CompilerParams(
        collective_id=collective, has_side_effects=True, vmem_limit_bytes=vmem
    )


ANY = pl.BlockSpec(memory_space=pl.ANY)
VMEM = pl.BlockSpec(memory_space=pltpu.VMEM)
HBM = pl.BlockSpec(memory_space=pltpu.HBM)


def along_x(rep, dx):
    return 2 * lax.rem(rep // 2 + dx, 4) + lax.rem(rep, 2)


def landed_on(ref, recv_sem, any_send_sem, device):
    pltpu.make_async_remote_copy(
        src_ref=ref,
        dst_ref=ref,
        send_sem=any_send_sem,
        recv_sem=recv_sem,
        device_id=device,
        device_id_type=MESH,
    ).wait_recv()


def x_gather(x_ref, o_ref, local_sem, send_sem, recv_sem):
    rep, shard = place()
    core = lax.rem(shard, 2)
    sib = shard + 1 - 2 * core
    half = x_ref.shape[0] // 2
    top, bottom = pl.ds(0, half), pl.ds(half, half)
    up, down, far = (along_x(rep, d) for d in (1, 3, 2))

    def block(r, other=False):
        return 2 * (r // 2) + (1 - core if other else core)

    mine = block(rep)
    own = pltpu.make_async_copy(x_ref, o_ref.at[mine], local_sem)
    sent = []

    def put(ref, dst, slot, device):
        sent.append(send(ref, dst, send_sem.at[len(sent)], recv_sem.at[slot], device))

    def arrived(ref, slot):
        landed_on(ref, recv_sem.at[slot], send_sem.at[0], (rep, sib))

    def start():
        own.start()
        put(x_ref, o_ref.at[mine], 0, (up, shard))
        put(x_ref, o_ref.at[mine], 1, (down, shard))
        put(x_ref, o_ref.at[mine], 4, (rep, sib))

    def relay():
        ref = o_ref.at[block(down)]
        arrived(ref, 0)
        put(o_ref.at[block(down), top], o_ref.at[block(down), top], 2, (up, shard))
        put(ref, ref, 5, (rep, sib))
        ref = o_ref.at[block(up)]
        arrived(ref, 1)
        put(o_ref.at[block(up), bottom], o_ref.at[block(up), bottom], 3, (down, shard))
        put(ref, ref, 6, (rep, sib))

    def relay_far():
        for slot, part in ((2, top), (3, bottom)):
            ref = o_ref.at[block(far), part]
            arrived(ref, slot)
            put(ref, ref, slot + 5, (rep, sib))

    def finish():
        arrived(o_ref.at[block(rep, True)], 4)
        arrived(o_ref.at[block(down, True)], 5)
        arrived(o_ref.at[block(up, True)], 6)
        arrived(o_ref.at[block(far, True), top], 7)
        arrived(o_ref.at[block(far, True), bottom], 8)
        for copy in sent:
            copy.wait_send()
        own.wait()

    return start, relay, relay_far, finish


def ring_spread(x_ref, o_ref, split, local_sem, send_sem, recv_sem):
    rep, shard = place()
    core = lax.rem(shard, 2)
    chip = shard // 2
    y = lax.rem(chip, 2)
    sib = shard + 1 - 2 * core
    pair = chip + 1 - 2 * y
    up, down, far = (lax.rem(chip + d, 8) for d in (2, 6, 4))
    own = pltpu.make_async_copy(x_ref.at[core], o_ref.at[shard], local_sem)
    first, last = pl.ds(0, split), pl.ds(split, x_ref.shape[2] - split)

    def copy(src, dst, slot, chip_to=None):
        return pltpu.make_async_remote_copy(
            src_ref=src,
            dst_ref=dst,
            send_sem=send_sem.at[slot],
            recv_sem=recv_sem.at[slot],
            device_id=(rep, sib if chip_to is None else 2 * chip_to + core),
            device_id_type=MESH,
        )

    def other(c):
        return c + 1 - 2 * y

    def block(c, columns, part=None):
        if part is None:
            return o_ref.at[pl.ds(2 * c, 2), :, columns]
        return o_ref.at[2 * c + part, :, columns]

    def push(ref, slot, to):
        copy(ref, ref, slot, to).start()

    def arrived(ref, slot):
        copy(ref, ref, slot, pair).wait_recv()

    def start():
        own.start()
        copy(x_ref.at[1 - core], o_ref.at[shard], 0).start()

    def one():
        copy(o_ref.at[sib], o_ref.at[sib], 0).wait_recv()
        own.wait()
        push(block(chip, first), 1, pair)
        push(block(chip, last), 10, up)
        push(block(chip, last), 12, down)
        push(block(chip, first), 2, up)
        push(block(chip, first), 6, down)
        push(block(chip, last), 14, pair)

    def two():
        arrived(block(pair, first), 1)
        push(block(pair, first), 3, up)
        push(block(pair, first), 7, down)
        arrived(block(down, last), 10)
        push(block(down, last), 15, pair)
        push(block(down, last, 0), 11, up)
        arrived(block(up, last), 12)
        push(block(up, last), 16, pair)
        push(block(up, last, 1), 13, down)

    def three():
        arrived(block(down, first), 2)
        push(block(down, first, 0), 4, up)
        arrived(block(up, first), 6)
        push(block(up, first, 1), 8, down)
        arrived(block(far, last, 0), 11)
        push(block(far, last, 0), 17, pair)
        arrived(block(far, last, 1), 13)
        push(block(far, last, 1), 18, pair)
        arrived(block(other(down), first), 3)
        push(block(other(down), first, 0), 5, up)
        arrived(block(other(up), first), 7)
        push(block(other(up), first, 1), 9, down)

    def finish():
        arrived(block(far, first, 0), 4)
        arrived(block(far, first, 1), 8)
        arrived(block(other(far), first, 0), 5)
        arrived(block(other(far), first, 1), 9)
        arrived(block(pair, last), 14)
        arrived(block(other(down), last), 15)
        arrived(block(other(up), last), 16)
        arrived(block(other(far), last, 0), 17)
        arrived(block(other(far), last, 1), 18)
        copy(x_ref.at[1 - core], o_ref.at[shard], 0).wait_send()
        for slot in (1, 2, 3, 6, 7):
            copy(block(chip, first), block(chip, first), slot, pair).wait_send()
        for slot in (4, 5, 8, 9):
            copy(block(chip, first, 0), block(chip, first, 0), slot, pair).wait_send()
        for slot in (10, 12, 14, 15, 16):
            copy(block(chip, last), block(chip, last), slot, pair).wait_send()
        for slot in (11, 13, 17, 18):
            copy(block(chip, last, 0), block(chip, last, 0), slot, pair).wait_send()

    return start, one, two, three, finish


START_SPLIT = 896


def start_kernel(
    x_ref, t_ref, in_hbm, gain_hbm, routes_hbm, logits_hbm, lift_hbm, code_hbm,
    o_ref, p_ref, g_ref, share_o, unit_ref,
    in_ref, gain_ref, routes_ref, logits_ref, lift_ref, code_ref, fetch_sem,
    w_ref, share_ref, local_sem, send_sem, recv_sem, s_part, r_part, s_x, r_x, s_y, r_y,
):
    with_parts = True
    rep, shard = place()
    half = x_ref.shape[0] // 2
    core = lax.rem(shard, 2)
    chip = shard // 2
    y = lax.rem(chip, 2)
    sib = shard + 1 - 2 * core
    pair = shard + 2 - 4 * y
    up = lax.rem(shard + 4, 16)
    down = lax.rem(shard + 12, 16)
    far = lax.rem(shard + 8, 16)
    first, last = pl.ds(0, START_SPLIT), pl.ds(START_SPLIT, D - START_SPLIT)
    rows, top, bottom = pl.ds(0, 2 * half), pl.ds(0, half), pl.ds(half, half)
    peers = [2 * lax.rem(chip + i, 8) + core for i in range(1, 8)]

    def other(block):
        return block + 2 - 4 * y

    greet(
        [(rep, sib)]
        + [(rep, p) for p in peers]
        + [(along_x(rep, 1), shard), (along_x(rep, 3), shard)]
    )
    fetches = [
        pltpu.make_async_copy(src, dst, fetch_sem.at[n])
        for n, (src, dst) in enumerate(
            (
                (in_hbm, in_ref),
                (gain_hbm, gain_ref),
                (routes_hbm, routes_ref),
                (logits_hbm, logits_ref),
                (lift_hbm.at[pl.ds((5 * (rep // 2)) // 2, 3)], lift_ref),
                (code_hbm, code_ref),
            )
        )
    ]
    for fetch in fetches:
        fetch.start()
    x_steps = x_gather(t_ref, g_ref, local_sem.at[2], s_x, r_x)
    y_steps = x_gather(share_ref, share_o, local_sem.at[3], s_y, r_y)
    own = pltpu.make_async_copy(x_ref, o_ref.at[shard], local_sem.at[0])
    own.start()
    sent = []

    def put(src, dst, slot, device):
        sent.append(send(src, dst, send_sem.at[len(sent)], recv_sem.at[slot], (rep, device)))

    def landed(ref, sem):
        landed_on(ref, sem, send_sem.at[0], (rep, sib))

    arrivals = {
        0: (pair, first, rows, ((2, up, rows), (6, down, rows))),
        9: (down, last, rows, ((14, pair, rows), (10, up, top))),
        1: (down, first, rows, ((3, up, top),)),
        11: (up, last, rows, ((15, pair, rows), (12, down, bottom))),
        5: (up, first, rows, ((7, down, bottom),)),
        13: (pair, last, rows, ()),
        2: (other(down), first, rows, ((4, up, top),)),
        6: (other(up), first, rows, ((8, down, bottom),)),
        10: (far, last, top, ((16, pair, top),)),
        12: (far, last, bottom, ((17, pair, bottom),)),
        3: (far, first, top, ()),
        7: (far, first, bottom, ()),
        14: (other(down), last, rows, ()),
        15: (other(up), last, rows, ()),
        4: (other(far), first, top, ()),
        8: (other(far), first, bottom, ()),
        16: (other(far), last, top, ()),
        17: (other(far), last, bottom, ()),
    }

    def arrive(slots):
        for slot in slots:
            block, columns, part, onward = arrivals[slot]
            ref = o_ref.at[block, part, columns]
            landed(ref, recv_sem.at[slot])
            for to_slot, device, rows_on in onward:
                ref_on = o_ref.at[block, rows_on, columns]
                put(ref_on, ref_on, to_slot, device)
            put(ref, ref, 19 + slot, sib)

    for columns, slots in ((first, (0, 1, 5)), (last, (13, 9, 11))):
        for slot, device in zip(slots, (pair, up, down)):
            put(x_ref.at[:, columns], o_ref.at[shard, :, columns], slot, device)
    put(x_ref, o_ref.at[shard], 18, sib)
    x_steps[0]()

    for fetch in fetches:
        fetch.wait()
    row, column = (lax.broadcasted_iota(jnp.int32, (96, 96), d) for d in (0, 1))
    gains = contract(jnp.where(row == column, 1.0, 0.0).astype(bf16), gain_ref[...], ((1,), (1,)))
    gains = jnp.concatenate([gains.astype(bf16), jnp.zeros((96, HEAD - 2), bf16)], 1)
    for c in range(CHIPS):
        w_ref[c] = jnp.concatenate(
            [
                in_ref[:, 192 * c : 192 * (c + 1)],
                gains,
                in_ref[:, 1536 + HEAD * c : 1536 + HEAD * (c + 1)],
                in_ref[:, 2048 + HEAD * c : 2048 + HEAD * (c + 1)],
            ],
            1,
        )
    parts = []
    if with_parts:
        mine = pltpu.make_async_copy(w_ref.at[chip], p_ref.at[shard], local_sem.at[1])
        mine.start()
        parts.append(
            send(w_ref.at[chip], p_ref.at[shard], s_part.at[0], r_part.at[0], (rep, sib))
        )
        for i in range(1, 8):
            c = lax.rem(chip + i, 8)
            parts.append(
                send(
                    w_ref.at[c], p_ref.at[shard], s_part.at[i], r_part.at[i], (rep, 2 * c + core)
                )
            )
    logits = logits_ref[...]
    gates = jnp.exp(logits - jnp.max(logits, 1, keepdims=True))
    gates = gates / jnp.sum(gates, 1, keepdims=True)
    lane = lax.broadcasted_iota(jnp.int32, (OWN, 128), 1)
    shares = jnp.zeros((OWN, 128), f32)
    for e in range(EXPERTS):
        one = jnp.sum(jnp.where(routes_ref[...] == e, gates, 0.0), 1, keepdims=True)
        shares = jnp.where(lane == e, one, shares)
    high = shares.astype(bf16)
    rest = pltpu.roll(shares - high.astype(f32), 16, 1)
    share_ref[...] = jnp.where(lane < 16, high, rest.astype(bf16))
    y_steps[0]()
    choose_units(lift_ref, code_ref, unit_ref)
    arrive((0, 9, 1, 11, 5, 13))
    x_steps[1]()
    y_steps[1]()
    arrive((2, 6, 10, 12))
    x_steps[2]()
    y_steps[2]()
    if with_parts:
        for i in range(1, 8):
            block = 2 * lax.rem(chip + 8 - i, 8) + core
            landed(p_ref.at[block], r_part.at[i])
            parts.append(
                send(
                    p_ref.at[block], p_ref.at[block], s_part.at[7 + i], r_part.at[7 + i], (rep, sib)
                )
            )
    arrive((3, 7, 14, 15, 4, 8, 16, 17))

    def twin(block):
        return block + 1 - 2 * core

    if with_parts:
        landed(p_ref.at[sib], r_part.at[0])
        for i in range(1, 8):
            landed(p_ref.at[twin(2 * lax.rem(chip + 8 - i, 8) + core)], r_part.at[7 + i])
        mine.wait()
    landed(o_ref.at[sib], recv_sem.at[18])
    for slot, (block, columns, part, _) in arrivals.items():
        landed(o_ref.at[twin(block), part, columns], recv_sem.at[19 + slot])
    x_steps[3]()
    y_steps[3]()
    for copy in sent + parts:
        copy.wait_send()
    own.wait()


def start(x, tokens, inward, gains, routes, logits, lifting, codes, collective):
    rows, columns = x.shape
    dma = pltpu.SemaphoreType.DMA
    gathered, parts, tokens, shares, units = pl.pallas_call(
        start_kernel,
        out_shape=(
            jax.ShapeDtypeStruct((SHARDS, rows, columns), bf16),
            jax.ShapeDtypeStruct((SHARDS, 96, 384), bf16),
            jax.ShapeDtypeStruct((PEERS, rows, columns), bf16),
            jax.ShapeDtypeStruct((PEERS, rows, 128), bf16),
            jax.ShapeDtypeStruct((2, 96, EXP), bf16),
        ),
        in_specs=[HBM] * 8,
        out_specs=(ANY,) * 4 + (VMEM,),
        scratch_shapes=[
            pltpu.VMEM(inward.shape, bf16),
            pltpu.VMEM(gains.shape, bf16),
            pltpu.VMEM(routes.shape, jnp.int32),
            pltpu.VMEM(logits.shape, f32),
            pltpu.VMEM((3,) + lifting.shape[1:], bf16),
            pltpu.VMEM(codes.shape, jnp.int32),
            dma((6,)),
            pltpu.VMEM((CHIPS, 96, 384), bf16),
            pltpu.VMEM((rows, 128), bf16),
            dma((4,)),
            dma((37,)),
            dma((37,)),
            dma((15,)),
            dma((15,)),
        ]
        + [dma((9,))] * 4,
        compiler_params=params(collective, 62 * 2**20),
        name="start",
    )(x, tokens, inward, gains, routes, logits, lifting, codes)
    return (
        gathered.reshape(SHARDS * rows, columns),
        parts,
        tokens.reshape(PEERS * rows, columns),
        shares.reshape(PEERS * rows, 128),
        units,
    )


def second_kernel(x_ref, o_ref, local_sem, s_x, r_x):
    rep, shard = place()
    core = lax.rem(shard, 2)
    greet(
        [(rep, shard + 1 - 2 * core), (along_x(rep, 1), shard), (along_x(rep, 3), shard)]
    )
    for step in x_gather(x_ref, o_ref, local_sem.at[0], s_x, r_x):
        step()


def second(x, collective):
    dma = pltpu.SemaphoreType.DMA
    gathered = pl.pallas_call(
        second_kernel,
        out_shape=jax.ShapeDtypeStruct((PEERS,) + x.shape, x.dtype),
        in_specs=[ANY],
        out_specs=ANY,
        scratch_shapes=[dma((1,)), dma((9,)), dma((9,))],
        compiler_params=params(collective, 62 * 2**20),
        name="second_gather",
    )(x)
    return gathered.reshape(PEERS * OWN, D)


def exchange_kernel(kinds, *refs):
    count = len(kinds)
    ins, outs = refs[:count], refs[count : 2 * count]
    local_sem, send_sem, recv_sem = refs[2 * count :]
    rep, shard = place()
    core = lax.rem(shard, 2)
    chip = shard // 2
    greet([(rep, lax.rem(shard + i, 16)) for i in range(1, 16)])
    sent, due = [], []

    def mine(device):
        return lax.rem(lax.rem(device, 2) + lax.rem(device // 2, 2), 2)

    for n, kind in enumerate(kinds):
        x, o = ins[n], outs[n]
        if kind == "all":
            local = pltpu.make_async_copy(x.at[shard], o.at[shard], local_sem.at[n])
            local.start()
            due.append(local)
            for i in range(1, 16):
                to = lax.rem(shard + i, 16)
                sent.append(
                    send(x.at[to], o.at[shard], send_sem.at[n, i], recv_sem.at[n, i], (rep, to))
                )
        elif kind == "heads":
            local = pltpu.make_async_copy(x.at[chip], o.at[shard], local_sem.at[n])
            local.start()
            due.append(local)
            for i in range(1, 16):
                to = lax.rem(shard + i, 16)
                sent.append(
                    send(
                        x.at[to // 2], o.at[shard], send_sem.at[n, i], recv_sem.at[n, i], (rep, to)
                    )
                )
        elif kind == "home":
            for i in range(8):
                c = lax.rem(chip + i, 8)
                to = 2 * c + lax.rem(c + core, 2)
                if i == 0:
                    same = to == shard

                    @pl.when(same)
                    def _(x=x, o=o, c=c, n=n):
                        local = pltpu.make_async_copy(x.at[c], o.at[chip], local_sem.at[n])
                        local.start()
                        local.wait()

                    @pl.when(jnp.logical_not(same))
                    def _(x=x, o=o, c=c, n=n, to=to):
                        copy = send(
                            x.at[c], o.at[chip], send_sem.at[n, 0], recv_sem.at[n, 0], (rep, to)
                        )
                        copy.wait_send()

                else:
                    sent.append(
                        send(
                            x.at[c], o.at[chip], send_sem.at[n, i], recv_sem.at[n, i], (rep, to)
                        )
                    )
        elif kind == "away":
            for i in range(8):
                c = lax.rem(chip + i, 8)
                to = 2 * c + mine(shard)
                if i == 0:
                    same = to == shard

                    @pl.when(same)
                    def _(x=x, o=o, c=c, n=n):
                        local = pltpu.make_async_copy(x.at[c], o.at[chip], local_sem.at[n])
                        local.start()
                        local.wait()

                    @pl.when(jnp.logical_not(same))
                    def _(x=x, o=o, c=c, n=n, to=to):
                        copy = send(
                            x.at[c], o.at[chip], send_sem.at[n, 0], recv_sem.at[n, 0], (rep, to)
                        )
                        copy.wait_send()

                else:
                    sent.append(
                        send(
                            x.at[c], o.at[chip], send_sem.at[n, i], recv_sem.at[n, i], (rep, to)
                        )
                    )

    def arrived(ref, n, i):
        pltpu.make_async_remote_copy(
            src_ref=ref,
            dst_ref=ref,
            send_sem=send_sem.at[n, 0],
            recv_sem=recv_sem.at[n, i],
            device_id=(rep, lax.rem(shard + 1, 16)),
            device_id_type=MESH,
        ).wait_recv()

    for n, kind in enumerate(kinds):
        o = outs[n]
        if kind in ("all", "heads"):
            for i in range(1, 16):
                arrived(o.at[lax.rem(shard + 16 - i, 16)], n, i)
        else:
            away = kind == "away"
            first = (
                2 * chip + lax.rem(chip + core, 2) if away else 2 * chip + mine(shard)
            )

            @pl.when(first != shard)
            def _(o=o, n=n):
                arrived(o.at[chip], n, 0)

            for i in range(1, 8):
                arrived(o.at[lax.rem(chip + 8 - i, 8)], n, i)
    for copy in sent:
        copy.wait_send()
    for copy in due:
        copy.wait()


def exchange(arrays, kinds, collective, name):
    shapes = []
    for x, kind in zip(arrays, kinds):
        lead = 16 if kind in ("all", "heads") else 8
        shapes.append(jax.ShapeDtypeStruct((lead,) + x.shape[1:], x.dtype))
    n = len(arrays)
    return pl.pallas_call(
        functools.partial(exchange_kernel, kinds),
        out_shape=tuple(shapes),
        in_specs=[ANY] * n,
        out_specs=(ANY,) * n,
        scratch_shapes=[
            pltpu.SemaphoreType.DMA((n,)),
            pltpu.SemaphoreType.DMA((n, 16)),
            pltpu.SemaphoreType.DMA((n, 16)),
        ],
        compiler_params=params(collective, 62 * 2**20),
        name=name,
    )(*arrays)


def reduce_kernel(*refs):
    ins, grads = refs[:2], refs[2:4]
    outs, grad_outs = refs[4:6], refs[6:8]
    token_held, token_near, token_land = refs[8:11]
    scratch = (refs[11:16], refs[16:21])
    t_load, t_sn, t_rn, t_s, t_r, g_load, s_one, r_one, s_two, r_two = refs[21:]
    rep, shard = place()
    core = lax.rem(shard, 2)
    chip = shard // 2
    y = lax.rem(chip, 2)
    z = chip // 2
    x = rep // 2
    sib = shard + 1 - 2 * core
    pair = shard + 2 - 4 * y

    def ahead(dz):
        return lax.rem(z + dz, 4)

    def device(dz):
        return (rep, 4 * ahead(dz) + 2 * y + core)

    greet(
        [(rep, sib), (rep, pair)]
        + [device(dz) for dz in (1, 2, 3)]
        + [(along_x(rep, dx), shard) for dx in (1, 2, 3)]
    )
    near_copies, loads, token_sends = {}, {}, {}
    for n in range(2):
        for dx in (2, 1, 3, 0):
            to = lax.rem(x + dx, 4)
            near_copies[n, dx] = send(
                ins[n].at[2 * to + 1 - core], token_near.at[n, dx], t_sn.at[n, dx], t_rn.at[n, dx],
                (rep, sib),
            )
            loads[n, dx] = pltpu.make_async_copy(
                ins[n].at[2 * to + core], token_held.at[n, dx], t_load.at[n, dx]
            )
            loads[n, dx].start()

    ones, twos, grad_loads = {}, {}, {}
    for m in range(2):
        held, land_a, land_b, land_c, land_d = scratch[m]
        columns = grads[m].shape[2]
        first, last = pl.ds(0, columns // 2), pl.ds(columns // 2, columns // 2)
        for j in (3, 5, 7, 1, 4, 2, 6, 0):
            dz, dy = j // 2, j % 2
            block = grads[m].at[2 * ahead(dz) + (1 - y if dy else y)]
            if dy:
                ones[m, 0, j] = send(
                    block.at[:, first], land_a.at[dz], s_one.at[m, 0, j], r_one.at[m, 0, j], (rep, pair)
                )
            if dz:
                ones[m, 1, j] = send(
                    block.at[:, last], land_b.at[j - 2], s_one.at[m, 1, j], r_one.at[m, 1, j], device(dz)
                )
            if dy == 0 or dz == 0:
                slot = dz if dy == 0 else 4
                grad_loads[m, slot] = pltpu.make_async_copy(block, held.at[slot], g_load.at[m, slot])
                grad_loads[m, slot].start()

    def rows_of(t, step):
        return pl.ds(pl.multiple_of(t * step, step), step)

    def token_sums(n):
        for dx in (2, 1, 3, 0):
            near_copies[n, dx].wait_recv()
            loads[n, dx].wait()

            def add(t, _, dx=dx):
                at = rows_of(t, 32)
                token_held[n, dx, at] = (
                    token_held[n, dx, at].astype(f32) + token_near[n, dx, at].astype(f32)
                ).astype(bf16)
                return 0

            lax.fori_loop(0, OWN // 32, add, 0)
            if dx:
                token_sends[n, dx] = send(
                    token_held.at[n, dx], token_land.at[n, dx - 1], t_s.at[n, dx], t_r.at[n, dx],
                    (along_x(rep, dx), shard),
                )

    def token_result(n):
        for dx in (1, 2, 3):
            token_sends[n, dx].wait_recv()

        def add(t, _):
            at = rows_of(t, 32)
            total = token_held[n, 0, at].astype(f32)
            for dx in (1, 2, 3):
                total = total + token_land[n, dx - 1, at].astype(f32)
            outs[n][at] = total
            return 0

        lax.fori_loop(0, OWN // 32, add, 0)

    def first_sums(m):
        held, land_a, land_b, land_c, land_d = scratch[m]
        rows, columns = held.shape[1:]
        first, last = pl.ds(0, columns // 2), pl.ds(columns // 2, columns // 2)
        for slot in range(5):
            grad_loads[m, slot].wait()
        for dz in (2, 1, 3, 0):
            ones[m, 0, 2 * dz + 1].wait_recv()

            def add(t, _, dz=dz):
                at = rows_of(t, 16)
                held[dz, at, first] = (
                    held[dz, at, first].astype(f32) + land_a[dz, at].astype(f32)
                ).astype(bf16)
                return 0

            lax.fori_loop(0, rows // 16, add, 0)
            if dz:
                twos[m, dz] = send(
                    held.at[dz, :, first], land_c.at[dz - 1], s_two.at[m, dz], r_two.at[m, dz], device(dz)
                )
        for dy in (1, 0):
            for dz in (1, 2, 3):
                ones[m, 1, 2 * dz + dy].wait_recv()
            slot = 4 if dy else 0

            def add(t, _, dy=dy, slot=slot):
                at = rows_of(t, 16)
                total = held[slot, at, last].astype(f32)
                for dz in (1, 2, 3):
                    total = total + land_b[2 * dz + dy - 2, at].astype(f32)
                held[slot, at, last] = total.astype(bf16)
                return 0

            lax.fori_loop(0, rows // 16, add, 0)
            if dy:
                twos[m, 0] = send(
                    held.at[4, :, last], land_d, s_two.at[m, 0], r_two.at[m, 0], (rep, pair)
                )

    def last_sums(m):
        held, land_a, land_b, land_c, land_d = scratch[m]
        rows, columns = held.shape[1:]
        first, last = pl.ds(0, columns // 2), pl.ds(columns // 2, columns // 2)
        for dz in range(4):
            twos[m, dz].wait_recv()

        def add(t, _):
            at = rows_of(t, 16)
            total = held[0, at, first].astype(f32)
            for dz in (1, 2, 3):
                total = total + land_c[dz - 1, at].astype(f32)
            grad_outs[m][at, first] = total.astype(bf16)
            grad_outs[m][at, last] = (
                held[0, at, last].astype(f32) + land_d[at].astype(f32)
            ).astype(bf16)
            return 0

        lax.fori_loop(0, rows // 16, add, 0)

    token_sums(0)
    token_sums(1)
    first_sums(0)
    token_result(0)
    first_sums(1)
    token_result(1)
    last_sums(0)
    last_sums(1)
    for copies in (near_copies, token_sends, ones, twos):
        for copy in copies.values():
            copy.wait_send()


def reduce_blocks(du, out, lift, down, collective):
    dma = pltpu.SemaphoreType.DMA

    def slots(rows, columns):
        half = columns // 2
        return [
            pltpu.VMEM((5, rows, columns), bf16),
            pltpu.VMEM((4, rows, half), bf16),
            pltpu.VMEM((6, rows, half), bf16),
            pltpu.VMEM((3, rows, half), bf16),
            pltpu.VMEM((rows, half), bf16),
        ]

    return pl.pallas_call(
        reduce_kernel,
        out_shape=(
            jax.ShapeDtypeStruct((OWN, D), f32),
            jax.ShapeDtypeStruct((OWN, D), f32),
            jax.ShapeDtypeStruct(lift.shape[1:], bf16),
            jax.ShapeDtypeStruct(down.shape[1:], bf16),
        ),
        in_specs=[ANY] * 4,
        out_specs=(VMEM,) * 4,
        scratch_shapes=[
            pltpu.VMEM((2, 4, OWN, D), bf16),
            pltpu.VMEM((2, 4, OWN, D), bf16),
            pltpu.VMEM((2, 3, OWN, D), bf16),
        ]
        + slots(*lift.shape[1:])
        + slots(*down.shape[1:])
        + [dma((2, 4))] * 5
        + [dma((2, 5)), dma((2, 2, 8)), dma((2, 2, 8)), dma((2, 4)), dma((2, 4))],
        compiler_params=params(collective, 62 * 2**20),
        name="reduce_rows",
    )(du, out, lift, down)


def away_kernel(
    du_ref, mixed_ref, y_ref, gain_ref, w_ref, a_ref, lift_ref, down_ref,
    dz_ref, part_ref, o_ref, lift_o, down_o,
    x_ref, lift_own, lift_land, down_own, down_land,
    local_sem, s_x, r_x, s_mate, r_mate, s_sib, r_sib,
):
    rep, shard = place()
    core = lax.rem(shard, 2)
    chip = shard // 2
    sib = shard + 1 - 2 * core
    mate = rep + 1 - 2 * lax.rem(rep, 2)
    greet([(rep, lax.rem(shard + i, 16)) for i in range(1, 16)] + [(mate, shard)])
    sent = []
    mates, loads = [], []
    for n, (src, own, land) in enumerate(
        ((lift_ref, lift_own, lift_land), (down_ref, down_own, down_land))
    ):
        mates.append(send(src, land, s_mate.at[n], r_mate.at[n], (mate, shard)))
        load = pltpu.make_async_copy(src, own, local_sem.at[n])
        load.start()
        loads.append(load)

    mixed = mixed_ref[...]
    inverse = inverse_root(mixed)
    dz = y_ref[...].astype(f32) + norm_back(du_ref[...] * gain_ref[...], mixed * inverse, inverse)
    dz_ref[...] = dz
    low = dz.astype(bf16)
    back = contract(low, w_ref[...], ((1,), (1,))).astype(bf16)
    for c in range(CHIPS):
        x_ref[c] = back[:, c * 192 : (c + 1) * 192]
    for i in range(1, 8):
        c = lax.rem(chip + i, 8)
        sent.append(
            send(
                x_ref.at[c], o_ref.at[chip], s_x.at[i], r_x.at[i],
                (rep, 2 * c + lax.rem(core + chip, 2)),
            )
        )
    part = contract(side_by_side(a_ref), low, ((0,), (0,))).astype(bf16)
    for s in range(SHARDS):
        part_ref[s] = part[s * 96 : (s + 1) * 96]
    same = lax.rem(chip, 2) == 0

    @pl.when(same)
    def _():
        copy = pltpu.make_async_copy(x_ref.at[chip], o_ref.at[chip], local_sem.at[2])
        copy.start()
        copy.wait()

    @pl.when(jnp.logical_not(same))
    def _():
        send(x_ref.at[chip], o_ref.at[chip], s_x.at[0], r_x.at[0], (rep, sib)).wait_send()
        landed_on(o_ref.at[chip], r_x.at[0], s_x.at[0], (rep, sib))

    keeps, halves = [], []
    for n, (own, land, out) in enumerate(
        ((lift_own, lift_land, lift_o), (down_own, down_land, down_o))
    ):
        loads[n].wait()
        mates[n].wait_recv()
        for k in range(2):

            def add(t, _, own=own, land=land, k=k):
                at = pl.ds(pl.multiple_of(t * 16, 16), 16)
                own[k, at] = (own[k, at].astype(f32) + land[k, at].astype(f32)).astype(bf16)
                return 0

            lax.fori_loop(0, own.shape[1] // 16, add, 0)
        halves.append(
            send(own.at[1 - core], out.at[core], s_sib.at[n], r_sib.at[n], (rep, sib))
        )
        keep = pltpu.make_async_copy(own.at[core], out.at[core], local_sem.at[3 + n])
        keep.start()
        keeps.append(keep)
    for i in range(1, 8):
        landed_on(o_ref.at[lax.rem(chip + 8 - i, 8)], r_x.at[i], s_x.at[0], (rep, sib))
    for n, out in enumerate((lift_o, down_o)):
        landed_on(out.at[1 - core], r_sib.at[n], s_x.at[0], (rep, sib))
        keeps[n].wait()
    for copy in sent + mates + halves:
        copy.wait_send()


def grads_away(du, mixed, y, gain, outward_all, attended, lift, down, collective):
    dma = pltpu.SemaphoreType.DMA
    heads = (CHIPS, OWN, 192)
    return pl.pallas_call(
        away_kernel,
        out_shape=(
            jax.ShapeDtypeStruct((OWN, D), f32),
            jax.ShapeDtypeStruct((SHARDS, 96, D), bf16),
            jax.ShapeDtypeStruct(heads, bf16),
            jax.ShapeDtypeStruct(lift.shape, bf16),
            jax.ShapeDtypeStruct(down.shape, bf16),
        ),
        in_specs=[VMEM] * 6 + [ANY] * 2,
        out_specs=(VMEM, VMEM, ANY, ANY, ANY),
        scratch_shapes=[
            pltpu.VMEM(heads, bf16),
            pltpu.VMEM(lift.shape, bf16),
            pltpu.VMEM(lift.shape, bf16),
            pltpu.VMEM(down.shape, bf16),
            pltpu.VMEM(down.shape, bf16),
            dma((5,)),
            dma((8,)),
            dma((8,)),
        ]
        + [dma((2,))] * 4,
        compiler_params=params(collective, 62 * 2**20),
        name="grads_away",
    )(du, mixed, y, gain, outward_all, attended, lift, down)


PART = (48, 384)


def part_of(r):
    rows = pl.ds(pl.multiple_of((r // 4) * PART[0], PART[0]), PART[0])
    return rows, pl.ds(pl.multiple_of(lax.rem(r, 4) * PART[1], PART[1]), PART[1])


def tail_kernel(
    dq_ref, dkv_ref, in_ref, out_ref, w_hbm,
    dh_ref, in_sum, out_sum,
    w_ref, held_k, near_k, held_i, near_i, got_q, got_k, land_i, land_o, own_o, sum_i, sum_o,
    l_sem, s_q, r_q, s_nk, r_nk, s_ni, r_ni, s_k, r_k, s_ri, r_ri, s_ro, r_ro, s_gi, r_gi, s_go, r_go,
):
    rep, shard = place()
    core = lax.rem(shard, 2)
    chip = shard // 2
    sib = shard + 1 - 2 * core
    fetch = pltpu.make_async_copy(w_hbm, w_ref, l_sem.at[20])
    fetch.start()
    own = pltpu.make_async_copy(out_ref.at[part_of(rep)], own_o, l_sem.at[16])
    own.start()
    loads = {}
    for c in range(8):
        for name, src, held, base in (("i", in_ref, held_i, 0), ("k", dkv_ref, held_k, 8)):
            loads[name, c] = pltpu.make_async_copy(
                src.at[2 * c + core], held.at[c], l_sem.at[base + c]
            )
            loads[name, c].start()
    alone = rep == chip
    barrier = pltpu.get_barrier_semaphore()
    for device in [(rep, lax.rem(shard + i, 16)) for i in range(1, 16)] + [
        (lax.rem(rep + i, 8), shard) for i in range(1, 8)
    ]:
        pl.semaphore_signal(barrier, inc=1, device_id=device, device_id_type=MESH)
    for i in range(8):
        device = (chip, 2 * lax.rem(chip + i, 8) + core)
        if i:
            pl.semaphore_signal(barrier, inc=1, device_id=device, device_id_type=MESH)
        else:

            @pl.when(jnp.logical_not(alone))
            def _(device=device):
                pl.semaphore_signal(barrier, inc=1, device_id=device, device_id_type=MESH)

    pl.semaphore_wait(barrier, jnp.where(alone, 29, 30))

    sent = []

    def put(src, dst, s_sem, r_sem, device):
        copy = send(src, dst, s_sem, r_sem, device)
        sent.append(copy)
        return copy

    def landed(ref, sem):
        landed_on(ref, sem, s_q.at[0], (rep, sib))

    nears = {}
    for name, src, near, s_n, r_n in (
        ("i", in_ref, near_i, s_ni, r_ni),
        ("k", dkv_ref, near_k, s_nk, r_nk),
    ):
        for c in range(8):
            nears[name, c] = put(
                src.at[2 * c + 1 - core], near.at[c], s_n.at[c], r_n.at[c], (rep, sib)
            )
    for i in range(1, 8):
        to = lax.rem(rep + i, 8)
        put(out_ref.at[part_of(to)], land_o.at[i - 1], s_ro.at[i], r_ro.at[i], (to, shard))

    def add_near(name, held, near, rows):
        for c in range(8):
            nears[name, c].wait_recv()
            loads[name, c].wait()

        def add(t, _):
            at = pl.ds(pl.multiple_of(t * 32, 32), 32)
            for c in range(8):
                held[c, at] = (held[c, at].astype(f32) + near[c, at].astype(f32)).astype(bf16)
            return 0

        lax.fori_loop(0, rows // 32, add, 0)

    add_near("i", held_i, near_i, 96)
    for i in range(1, 8):
        to = lax.rem(rep + i, 8)
        put(held_i.at[to], land_i.at[i - 1], s_ri.at[i], r_ri.at[i], (to, shard))
    add_near("k", held_k, near_k, OWN)
    for i in range(1, 8):
        c = lax.rem(chip + i, 8)
        put(held_k.at[c], got_k.at[chip], s_k.at[i], r_k.at[i], (rep, 2 * c + core))
        put(
            dq_ref.at[c], got_q.at[chip], s_q.at[i], r_q.at[i],
            (rep, 2 * c + lax.rem(c + core, 2)),
        )
    got_k[chip] = held_k[chip]
    mine = lax.rem(chip, 2) == 0

    @pl.when(mine)
    def _():
        copy = pltpu.make_async_copy(dq_ref.at[chip], got_q.at[chip], l_sem.at[17])
        copy.start()
        copy.wait()

    @pl.when(jnp.logical_not(mine))
    def _():
        send(dq_ref.at[chip], got_q.at[chip], s_q.at[0], r_q.at[0], (rep, sib)).wait_send()

    own.wait()
    for land, total, r_x in ((land_o, sum_o, r_ro), (land_i, sum_i, r_ri)):
        for i in range(1, 8):
            landed(land.at[i - 1], r_x.at[i])

        def add(t, _, land=land, total=total):
            at = pl.ds(pl.multiple_of(t * 16, 16), 16)
            value = own_o[at] if land is land_o else held_i[rep, at]
            value = value.astype(f32)
            for i in range(7):
                value = value + land[i, at].astype(f32)
            total[at] = value.astype(bf16)
            return 0

        lax.fori_loop(0, total.shape[0] // 16, add, 0)
        if land is land_o:
            keep = pltpu.make_async_copy(sum_o, out_sum.at[part_of(rep)], l_sem.at[18])
            keep.start()
            for i in range(1, 8):
                to = lax.rem(rep + i, 8)
                put(sum_o, out_sum.at[part_of(rep)], s_go.at[i], r_go.at[i], (to, shard))
    owner = 2 * rep + core
    for i in range(1, 8):
        put(sum_i, in_sum.at[chip], s_gi.at[i], r_gi.at[chip], (lax.rem(rep + i, 8), owner))

    @pl.when(alone)
    def _():
        copy = pltpu.make_async_copy(sum_i, in_sum.at[chip], l_sem.at[19])
        copy.start()
        copy.wait()

    @pl.when(jnp.logical_not(alone))
    def _():
        send(sum_i, in_sum.at[chip], s_gi.at[0], r_gi.at[chip], (rep, owner)).wait_send()

    @pl.when(jnp.logical_not(mine))
    def _():
        landed(got_q.at[chip], r_q.at[0])

    for i in range(1, 8):
        landed(got_q.at[lax.rem(chip + 8 - i, 8)], r_q.at[i])
        landed(got_k.at[lax.rem(chip + 8 - i, 8)], r_k.at[i])
    joined = jnp.concatenate(
        [got_q[c] for c in range(CHIPS)]
        + [got_k[c][:, :HEAD] for c in range(CHIPS)]
        + [got_k[c][:, HEAD:] for c in range(CHIPS)],
        1,
    )
    fetch.wait()
    dh_ref[...] = contract(joined, w_ref[...], ((1,), (1,)))

    for i in range(1, 8):
        landed(out_sum.at[part_of(lax.rem(rep + 8 - i, 8))], r_go.at[i])
    for j in range(8):

        @pl.when(jnp.logical_not(jnp.logical_and(alone, chip == j)))
        def _(j=j):
            landed(in_sum.at[j], r_gi.at[j])

    keep.wait()
    for copy in sent:
        copy.wait_send()


def tail(dq, dkv, inward_part, outward_own, inward_all, collective):
    dma = pltpu.SemaphoreType.DMA
    return pl.pallas_call(
        tail_kernel,
        out_shape=(
            jax.ShapeDtypeStruct((OWN, D), f32),
            jax.ShapeDtypeStruct((CHIPS, 96, 320), bf16),
            jax.ShapeDtypeStruct((96, D), bf16),
        ),
        in_specs=[ANY, ANY, ANY, ANY, HBM],
        out_specs=(VMEM, ANY, ANY),
        scratch_shapes=[
            pltpu.VMEM(inward_all.shape, bf16),
            pltpu.VMEM((8, OWN, 128), bf16),
            pltpu.VMEM((8, OWN, 128), bf16),
            pltpu.VMEM((8, 96, 320), bf16),
            pltpu.VMEM((8, 96, 320), bf16),
            pltpu.VMEM((8, OWN, 192), bf16),
            pltpu.VMEM((8, OWN, 128), bf16),
            pltpu.VMEM((7, 96, 320), bf16),
            pltpu.VMEM((7,) + PART, bf16),
            pltpu.VMEM(PART, bf16),
            pltpu.VMEM((96, 320), bf16),
            pltpu.VMEM(PART, bf16),
            dma((21,)),
        ]
        + [dma((8,))] * 16,
        compiler_params=params(collective, 62 * 2**20),
        name="tail",
    )(dq, dkv, inward_part, outward_own, inward_all)


def swap_halves(values):
    lanes = values.shape[1]
    lane = lax.broadcasted_iota(jnp.int32, values.shape, 1)
    ahead = pltpu.roll(values, lanes - HEAD // 2, 1)
    behind = pltpu.roll(values, HEAD // 2, 1)
    return jnp.where(lax.rem(lane, HEAD) < HEAD // 2, ahead, behind)


def project_step(i, core, x_ref, w_ref, g_ref, cos_ref, sin_ref, q_ref, k_ref, v_ref, u_ref):
    stream = x_ref[...].astype(f32)
    u_ref[...] = (stream * inverse_root(stream) * g_ref[...]).astype(bf16)
    first = pl.multiple_of(lax.rem(i + core, 2) * OWN, OWN)
    own = pl.ds(first, OWN)
    queries = jnp.dot(u_ref[own, :], w_ref[:, :256], preferred_element_type=f32)
    cos, sin = cos_ref[own, :], sin_ref[own, :]
    cos, sin = jnp.concatenate([cos, cos], 1), jnp.concatenate([sin, sin], 1)
    turned = (queries * cos + swap_halves(queries) * sin).astype(bf16)
    turned = turned * jnp.bfloat16(HEAD**-0.5)
    for r in range(GROUP):
        q_ref[i, r * OWN : (r + 1) * OWN, :] = turned[:, r * HEAD : (r + 1) * HEAD]
    pairs = jnp.dot(u_ref[...], w_ref[:, 256:], preferred_element_type=f32)
    keys = pairs * cos_ref[...] + swap_halves(pairs) * sin_ref[...]
    rows = pl.ds(pl.multiple_of(i * KEYS, KEYS), KEYS)
    k_ref[rows, :] = keys[:, :HEAD].astype(bf16)
    lane = lax.broadcasted_iota(jnp.int32, pairs.shape, 1)
    v_ref[rows, :] = jnp.where(lane < HEAD, pltpu.roll(pairs, HEAD, 1), 1.0).astype(bf16)


def contract(a, b, dims, precision=None):
    return lax.dot_general(
        a, b, ((dims[0], dims[1]), ((), ())), preferred_element_type=f32, precision=precision
    )


def attend_kernel(
    x_ref, w_ref, g_ref, cos_ref, sin_ref, b_ref, d_ref,
    q_ref, k_ref, v_ref, u_ref, o_ref, l_ref, bo_ref, do_ref,
    local_sem, s_sem, r_sem, s_low, r_low,
):
    i = pl.program_id(0)
    core = lax.rem(lax.axis_index("shard"), 2)
    steps = ring_spread(b_ref, bo_ref, 768, local_sem.at[0], s_sem, r_sem)
    low_steps = ring_spread(d_ref, do_ref, 896, local_sem.at[1], s_low, r_low)

    @pl.when(i == 0)
    def _():
        rep, shard = place()
        y = lax.rem(shard // 2, 2)
        greet(
            [(rep, shard + 1 - 2 * core), (rep, shard + 2 - 4 * y)]
            + [(rep, lax.rem(shard + 4, 16)), (rep, lax.rem(shard + 12, 16))]
        )
        steps[0]()
        low_steps[0]()

    @pl.when(i == 1)
    def _():
        steps[1]()

    @pl.when(i == 6)
    def _():
        low_steps[1]()

    @pl.when(i == 11)
    def _():
        steps[2]()

    @pl.when(i == 13)
    def _():
        low_steps[2]()

    @pl.when(i == 15)
    def _():
        steps[3]()

    @pl.when(i < BLOCKS)
    def _():
        project_step(i, core, x_ref, w_ref, g_ref, cos_ref, sin_ref, q_ref, k_ref, v_ref, u_ref)

    @pl.when(i >= BLOCKS)
    def _():
        attend_step(i - BLOCKS, core, q_ref, k_ref, v_ref, o_ref, l_ref)

    @pl.when(i == 2 * BLOCKS - 1)
    def _():
        low_steps[3]()
        steps[4]()
        low_steps[4]()


def attend_step(i, core, q_ref, k_ref, v_ref, o_ref, l_ref):
    shift = lax.rem(i + core, 2) * OWN
    q = q_ref[i]

    def step(c, carry, last=False):
        top, total = carry
        at = pl.ds(pl.multiple_of(c * KEYS, KEYS), KEYS)
        scores = contract(q, k_ref[at, :], ((1,), (1,)))
        if last:
            row = lax.broadcasted_iota(jnp.int32, (OWN, KEYS), 0)
            column = lax.broadcasted_iota(jnp.int32, (OWN, KEYS), 1)
            bias = jnp.where(column <= row + shift, 0.0, -1e30)
            scores = scores + jnp.concatenate([bias] * GROUP, 0)
        high = jnp.maximum(top, jnp.max(scores, 1, keepdims=True))
        prob = jnp.exp(scores - high).astype(bf16)
        total = total * jnp.exp(top - high) + jnp.dot(
            prob, v_ref[at, :], preferred_element_type=f32
        )
        return high, total

    carry = (jnp.full((ROWS, 1), -1e30, f32), jnp.zeros((ROWS, 128), f32))
    carry = lax.fori_loop(0, i, step, carry)
    top, total = step(i, carry, True)
    weight = total[:, HEAD : HEAD + 1]
    result = (total[:, :HEAD] / weight).astype(bf16)
    o_ref[0] = jnp.concatenate([result[r * OWN : (r + 1) * OWN] for r in range(GROUP)], 1)
    column = lax.broadcasted_iota(jnp.int32, (8, 8), 1)
    l_ref[0] = contract(
        jnp.where(column == 0, 1.0, 0.0).astype(f32),
        jnp.broadcast_to(top + jnp.log(weight), (ROWS, 8)),
        ((1,), (1,)),
        lax.Precision.HIGHEST,
    )


def attend(x_all, weight, gain, cos, sin, units, low, collective):
    dma = pltpu.SemaphoreType.DMA
    whole = lambda i: (0, 0)
    early = lambda i: (jnp.minimum(i, BLOCKS - 1), 0)
    late = lambda i: (jnp.maximum(i - BLOCKS, 0), 0, 0)
    return pl.pallas_call(
        attend_kernel,
        grid=(2 * BLOCKS,),
        in_specs=[
            pl.BlockSpec((KEYS, D), early),
            pl.BlockSpec((D, 384), whole),
            pl.BlockSpec((1, D), whole),
            pl.BlockSpec((KEYS, 128), early),
            pl.BlockSpec((KEYS, 128), early),
            ANY,
            ANY,
        ],
        out_specs=(
            pl.BlockSpec((BLOCKS, ROWS, HEAD), lambda i: (0, 0, 0)),
            pl.BlockSpec((SEQ, HEAD), whole),
            pl.BlockSpec((SEQ, 128), whole),
            pl.BlockSpec((KEYS, D), early),
            pl.BlockSpec((1, OWN, GROUP * HEAD), late),
            pl.BlockSpec((1, 8, ROWS), late),
            ANY,
            ANY,
        ),
        out_shape=(
            jax.ShapeDtypeStruct((BLOCKS, ROWS, HEAD), bf16),
            jax.ShapeDtypeStruct((SEQ, HEAD), bf16),
            jax.ShapeDtypeStruct((SEQ, 128), bf16),
            jax.ShapeDtypeStruct((SEQ, D), bf16),
            jax.ShapeDtypeStruct((BLOCKS, OWN, GROUP * HEAD), bf16),
            jax.ShapeDtypeStruct((BLOCKS, 8, ROWS), f32),
            jax.ShapeDtypeStruct((SHARDS,) + units.shape[1:], bf16),
            jax.ShapeDtypeStruct((SHARDS,) + low.shape[1:], bf16),
        ),
        scratch_shapes=[dma((2,))] + [dma((19,))] * 4,
        compiler_params=params(collective, 62 * 2**20),
        name="attend",
    )(x_all, weight, gain, cos, sin, units, low)


def attend_back_kernel(
    q_ref, k_ref, v_ref, g_ref, a_ref, l_ref, cos_ref, sin_ref, qcos_ref, qsin_ref, u_hbm, part_ref,
    lift_ref, down_ref, dq_ref, dkv_ref, in_ref, part_out, lift_out, down_out,
    u_ref, u_sem, dk, dv, dq, total_q, held, near, landed, local_sem, s_sem, r_sem, h_sem, s_near, r_near, s_far, r_far,
):
    i = pl.program_id(0)
    rep, shard = place()
    core = lax.rem(shard, 2)
    chip = shard // 2
    sib = shard + 1 - 2 * core
    shift = lax.rem(i + core, 2) * OWN
    x = rep // 2
    kept = [
        (n, src, dst)
        for n, (src, dst) in enumerate(((lift_ref, lift_out), (down_ref, down_out)))
    ]

    def copy_same(n, src, dst):
        return pltpu.make_async_copy(src, dst.at[pl.ds(2 * x, 2)], local_sem.at[n])

    def copy_x(n, src, dst, dx, at):
        return pltpu.make_async_remote_copy(
            src_ref=src,
            dst_ref=dst.at[pl.ds(2 * at, 2)],
            send_sem=s_sem.at[n, dx],
            recv_sem=r_sem.at[n, dx],
            device_id=(along_x(rep, dx), shard),
            device_id_type=MESH,
        )

    def copy_near(j):
        return pltpu.make_async_remote_copy(
            src_ref=part_ref.at[2 * lax.rem(chip + j, 8) + 1 - core],
            dst_ref=near.at[j],
            send_sem=s_near.at[j],
            recv_sem=r_near.at[j],
            device_id=(rep, sib),
            device_id_type=MESH,
        )

    def copy_own(j):
        return pltpu.make_async_copy(
            part_ref.at[2 * lax.rem(chip + j, 8) + core], held.at[j], h_sem.at[j]
        )

    def copy_far(j):
        return pltpu.make_async_remote_copy(
            src_ref=held.at[j],
            dst_ref=landed.at[j - 1],
            send_sem=s_far.at[j],
            recv_sem=r_far.at[j],
            device_id=(rep, 2 * lax.rem(chip + j, 8) + core),
            device_id_type=MESH,
        )

    @pl.when(i == 0)
    def _():
        greet(
            [(rep, sib)]
            + [(rep, 2 * lax.rem(chip + n, 8) + core) for n in range(1, 8)]
            + [(along_x(rep, dx), shard) for dx in (1, 2, 3)]
        )
        for j in range(8):
            copy_near(j).start()
            copy_own(j).start()
        for n, src, dst in kept:
            copy_same(n, src, dst).start()
            for dx in (1, 2, 3):
                copy_x(n, src, dst, dx, x).start()
        pltpu.make_async_copy(u_hbm, u_ref, u_sem).start()
        total_q[...] = jnp.zeros_like(total_q)
        dk[...] = jnp.zeros_like(dk)
        dv[...] = jnp.zeros_like(dv)

    @pl.when(i == 3)
    def _():
        for j in range(8):
            copy_near(j).wait_recv()
            copy_own(j).wait()

            def add(t, _, j=j):
                at = pl.ds(pl.multiple_of(t * 32, 32), 32)
                held[j, at] = (held[j, at].astype(f32) + near[j, at].astype(f32)).astype(bf16)
                return 0

            lax.fori_loop(0, 3, add, 0)
            if j:
                copy_far(j).start()

    q = q_ref[0]
    grad = jnp.concatenate([g_ref[0][:, r * HEAD : (r + 1) * HEAD] for r in range(GROUP)], 0)
    dq[...] = jnp.zeros_like(dq)
    lse = l_ref[0][:1]
    lane = lax.broadcasted_iota(jnp.int32, (8, GROUP * HEAD), 1)
    row = lax.broadcasted_iota(jnp.int32, (8, GROUP * HEAD), 0)
    sums = contract(
        jnp.where(lane // HEAD == row, 1.0, 0.0).astype(f32),
        g_ref[0].astype(f32) * a_ref[0].astype(f32),
        ((1,), (1,)),
        lax.Precision.HIGHEST,
    )
    delta = jnp.concatenate([sums[r : r + 1] for r in range(GROUP)], 1)

    def step(c, _, last=False):
        at = pl.ds(pl.multiple_of(c * KEYS, KEYS), KEYS)
        keys = k_ref[at, :]
        scores = contract(keys, q, ((1,), (1,)))
        if last:
            key = lax.broadcasted_iota(jnp.int32, (KEYS, OWN), 0)
            token = lax.broadcasted_iota(jnp.int32, (KEYS, OWN), 1)
            bias = jnp.where(key <= token + shift, 0.0, -1e30)
            scores = scores + jnp.concatenate([bias] * GROUP, 1)
        prob = jnp.exp(scores - lse)
        back = contract(v_ref[at, :HEAD], grad, ((1,), (1,)))
        slope = (prob * (back - delta)).astype(bf16)
        dv[at, :] += jnp.dot(prob.astype(bf16), grad, preferred_element_type=f32)
        dk[at, :] += jnp.dot(slope, q, preferred_element_type=f32)
        dq[...] += contract(slope, keys, ((0,), (0,)))
        return 0

    lax.fori_loop(0, i, step, 0)
    step(i, 0, True)
    wide = jnp.concatenate(
        [dq[r * OWN : (r + 1) * OWN, :] for r in range(GROUP)] + [jnp.zeros((OWN, HEAD), f32)], 1
    )
    wide = wide * (HEAD**-0.5)
    cos, sin = qcos_ref[...], qsin_ref[...]
    cos, sin = jnp.concatenate([cos, cos], 1), jnp.concatenate([sin, sin], 1)
    wide = wide * cos - swap_halves(wide) * sin
    wide = wide[:, : GROUP * HEAD].astype(bf16)
    dq_ref[0] = wide

    @pl.when(i == 0)
    def _():
        pltpu.make_async_copy(u_hbm, u_ref, u_sem).wait()

    mine = pl.ds(pl.multiple_of(i * KEYS + shift, OWN), OWN)
    total_q[...] += contract(wide, u_ref[mine, :], ((0,), (0,)))

    @pl.when(i == BLOCKS - 1)
    def _():
        def turn(c, _):
            at = pl.ds(pl.multiple_of(c * OWN, OWN), OWN)
            both = jnp.concatenate([dk[at, :], dv[at, :]], 1)
            lane = lax.broadcasted_iota(jnp.int32, both.shape, 1)
            turned = both * cos_ref[at, :] - swap_halves(both) * sin_ref[at, :]
            dkv_ref[at, :] = jnp.where(lane < HEAD, turned, both).astype(bf16)
            return 0

        lax.fori_loop(0, SHARDS, turn, 0)
        def add_pairs(c, both):
            at = pl.ds(pl.multiple_of(c * 768, 768), 768)
            return both + contract(dkv_ref[at, :], u_ref[at, :], ((0,), (0,)))

        both = lax.fori_loop(0, SEQ // 768, add_pairs, jnp.zeros((128, D), f32))
        both = jnp.concatenate([total_q[...], both], 0).T.astype(bf16)
        for s in range(SHARDS):
            in_ref[s] = both[s * 96 : (s + 1) * 96]

        for j in range(1, 8):
            copy_far(j).wait_recv()

        def add(t, _):
            at = pl.ds(pl.multiple_of(t * 32, 32), 32)
            total = held[0, at].astype(f32)
            for j in range(7):
                total = total + landed[j, at].astype(f32)
            part_out[at] = total.astype(bf16)
            return 0

        lax.fori_loop(0, 3, add, 0)
        for n, src, dst in kept:
            copy_same(n, src, dst).wait()
            for dx in (1, 2, 3):
                copy_x(n, src, dst, dx, lax.rem(x + 4 - dx, 4)).wait_recv()
            for dx in (1, 2, 3):
                copy_x(n, src, dst, dx, x).wait_send()
        for j in range(8):
            copy_near(j).wait_send()
            if j:
                copy_far(j).wait_send()


def attend_back(q, k, v, grad, attended, lse, cos, sin, u_all, part, lift, down, collective):
    def own(i):
        return (2 * i + lax.rem(i + lax.rem(lax.axis_index("shard"), 2), 2), 0)

    whole = lambda i: (0, 0)
    block = lambda i: (i, 0, 0)
    return pl.pallas_call(
        attend_back_kernel,
        grid=(BLOCKS,),
        in_specs=[
            pl.BlockSpec((1, ROWS, HEAD), block),
            pl.BlockSpec((SEQ, HEAD), whole),
            pl.BlockSpec((SEQ, 128), whole),
            pl.BlockSpec((1, OWN, GROUP * HEAD), block),
            pl.BlockSpec((1, OWN, GROUP * HEAD), block),
            pl.BlockSpec((1, 8, ROWS), block),
            pl.BlockSpec((SEQ, 128), whole),
            pl.BlockSpec((SEQ, 128), whole),
            pl.BlockSpec((OWN, 128), own),
            pl.BlockSpec((OWN, 128), own),
            HBM,
            ANY,
            ANY,
            ANY,
        ],
        out_specs=(
            pl.BlockSpec((1, OWN, GROUP * HEAD), block),
            pl.BlockSpec((SEQ, 128), whole),
            pl.BlockSpec((SHARDS, 96, 320), lambda i: (0, 0, 0)),
            pl.BlockSpec(part.shape[1:], whole),
            ANY,
            ANY,
        ),
        out_shape=(
            jax.ShapeDtypeStruct((BLOCKS, OWN, GROUP * HEAD), bf16),
            jax.ShapeDtypeStruct((SEQ, 128), bf16),
            jax.ShapeDtypeStruct((SHARDS, 96, 320), bf16),
            jax.ShapeDtypeStruct(part.shape[1:], bf16),
            jax.ShapeDtypeStruct((PEERS,) + lift.shape[1:], bf16),
            jax.ShapeDtypeStruct((PEERS,) + down.shape[1:], bf16),
        ),
        scratch_shapes=[
            pltpu.VMEM((SEQ, D), bf16),
            pltpu.SemaphoreType.DMA,
            pltpu.VMEM((SEQ, HEAD), f32),
            pltpu.VMEM((SEQ, HEAD), f32),
            pltpu.VMEM((ROWS, HEAD), f32),
            pltpu.VMEM((GROUP * HEAD, D), f32),
            pltpu.VMEM((8,) + part.shape[1:], bf16),
            pltpu.VMEM((8,) + part.shape[1:], bf16),
            pltpu.VMEM((7,) + part.shape[1:], bf16),
            pltpu.SemaphoreType.DMA((2,)),
            pltpu.SemaphoreType.DMA((2, 4)),
            pltpu.SemaphoreType.DMA((2, 4)),
        ]
        + [pltpu.SemaphoreType.DMA((8,))] * 5,
        compiler_params=params(collective, 62 * 2**20),
        name="attend_back",
    )(q, k, v, grad, attended, lse, cos, sin, cos, sin, u_all, part, lift, down)


def experts_kernel(
    u_ref, y_ref, c_ref, wl_ref, wd_ref, e_ref, out_ref, du_ref, lift_ref, down_ref, lift, down
):
    i = pl.program_id(0)
    u, y = u_ref[...], y_ref[...]
    lifted = jnp.dot(u, wl_ref[...], preferred_element_type=f32)
    back = contract(y, wd_ref[...], ((1,), (1,)))
    share = jnp.dot(c_ref[...], e_ref[...], preferred_element_type=f32)
    gate, raised = lifted[:, :HID], lifted[:, HID:]
    s = jax.nn.sigmoid(gate)
    swish = gate * s
    act = (share * swish * raised).astype(bf16)
    back = back * share
    grad_gate = back * raised * s * (1.0 + gate * (1.0 - s))
    grad_lift = jnp.concatenate([grad_gate, back * swish], 1).astype(bf16)
    out_ref[...] = jnp.dot(act, wd_ref[...], preferred_element_type=f32).astype(bf16)
    du_ref[...] = contract(grad_lift, wl_ref[...], ((1,), (1,))).astype(bf16)

    @pl.when(i == 0)
    def _():
        lift[...] = jnp.zeros_like(lift)
        down[...] = jnp.zeros_like(down)

    lift[...] += contract(u, grad_lift, ((0,), (0,)))
    down[...] += contract(act, y, ((0,), (0,)))

    @pl.when(i == pl.num_programs(0) - 1)
    def _():
        lift_ref[...] = lift[...].astype(bf16)
        down_ref[...] = down[...].astype(bf16)


def experts(u_all, y_all, shares, wl, wd, spread):
    step = 384
    rows = lambda i: (i, 0)
    whole = lambda i: (0, 0)
    once = pl.Buffered(1)
    return pl.pallas_call(
        experts_kernel,
        grid=(PEERS * OWN // step,),
        in_specs=[
            pl.BlockSpec((step, D), rows),
            pl.BlockSpec((step, D), rows),
            pl.BlockSpec((step, 128), rows),
            pl.BlockSpec((D, EXP), whole, pipeline_mode=once),
            pl.BlockSpec((HID, D), whole, pipeline_mode=once),
            pl.BlockSpec((128, HID), whole, pipeline_mode=once),
        ],
        out_specs=(
            pl.BlockSpec((step, D), rows),
            pl.BlockSpec((step, D), rows),
            pl.BlockSpec((D, EXP), whole),
            pl.BlockSpec((HID, D), whole),
        ),
        out_shape=(
            jax.ShapeDtypeStruct((PEERS * OWN, D), bf16),
            jax.ShapeDtypeStruct((PEERS * OWN, D), bf16),
            jax.ShapeDtypeStruct((D, EXP), bf16),
            jax.ShapeDtypeStruct((HID, D), bf16),
        ),
        scratch_shapes=[pltpu.VMEM((D, EXP), f32), pltpu.VMEM((HID, D), f32)],
        compiler_params=pltpu.CompilerParams(vmem_limit_bytes=62 * 2**20),
        name="experts",
    )(u_all, y_all, shares, wl, wd, spread)


def choose_units(w_ref, code_ref, out_ref):
    x = lax.axis_index("rep") // 2
    row = lax.broadcasted_iota(jnp.int32, (FF_EXP, HID), 0)
    there = (row // 32) * 1024 + lax.rem(row, 32)
    here = jnp.broadcast_to(code_ref[...], (FF_EXP, HID))
    base = (5 * x) // 2
    for k in range(2):
        for part in range(2):
            total = jnp.zeros((96, HID), f32)
            for i in range(3):
                chosen = there + 32 * (base + i) == here + FLAT * (2 * x + k)
                total = total + jnp.dot(
                    w_ref[i][:, FF_EXP * part : FF_EXP * (part + 1)],
                    jnp.where(chosen, 1.0, 0.0).astype(bf16),
                    preferred_element_type=f32,
                )
            out_ref[k, :, HID * part : HID * (part + 1)] = total.astype(bf16)


def one_step(kernel, arrays, shapes, name):
    return pl.pallas_call(
        kernel,
        in_specs=[VMEM] * len(arrays),
        out_specs=(VMEM,) * len(shapes),
        out_shape=tuple(jax.ShapeDtypeStruct(shape, dtype) for shape, dtype in shapes),
        compiler_params=pltpu.CompilerParams(vmem_limit_bytes=62 * 2**20),
        name=name,
    )(*arrays)


def side_by_side(ref):
    return jnp.concatenate([ref[c] for c in range(CHIPS)], 1)


def mix_kernel(a_ref, w_ref, x_ref, g_ref, mixed_ref, low_ref):
    mixed = x_ref[...].astype(f32) + jnp.dot(
        side_by_side(a_ref), w_ref[...], preferred_element_type=f32
    )
    mixed_ref[...] = mixed
    low_ref[...] = (mixed * inverse_root(mixed) * g_ref[...]).astype(bf16)


def finish_kernel(dh_ref, dz_ref, x_ref, g_ref, out_ref):
    stream = x_ref[...].astype(f32)
    inverse = inverse_root(stream)
    out_ref[...] = dz_ref[...] + norm_back(dh_ref[...] * g_ref[...], stream * inverse, inverse)


def adam(weight, old_mean, square, gradient, step_rate, decay_rate):
    values = weight.astype(f32)
    moment = beta_one * old_mean.astype(f32) + (1.0 - beta_one) * gradient
    variance = beta_two * square.astype(f32) + (1.0 - beta_two) * gradient * gradient
    normed_step = (
        moment
        / (1.0 - beta_one**STEP)
        / (jnp.sqrt(variance / (1.0 - beta_two**STEP)) + adam_epsilon)
    )
    return (moment, variance, values - step_rate * (normed_step + decay_rate * values))


def adam_lifting_kernel(w_ref, m_ref, s_ref, g_ref, code_ref, mo_ref, so_ref, wo_ref, dot_ref, grad):
    e = pl.program_id(0)
    first, last = (4 * e) // 5, (4 * e + 3) // 5
    column = lax.broadcasted_iota(jnp.int32, (HID, FF_EXP), 1)
    there = (column // 32) * 1024 + lax.rem(column, 32) + 32 * e
    here = jnp.broadcast_to(code_ref[...], (HID, FF_EXP))
    chosen_first = jnp.where(there == here + FLAT * first, 1.0, 0.0).astype(bf16)
    skip = jnp.where(first == last, 1 << 20, 0)
    chosen_last = jnp.where(there == here + (FLAT * last + skip), 1.0, 0.0).astype(bf16)

    def both(p):
        return jnp.concatenate([g_ref[p][:, :HID], g_ref[p][:, HID:]], 0)

    ordered = jnp.dot(both(first), chosen_first, preferred_element_type=f32) + jnp.dot(
        both(last), chosen_last, preferred_element_type=f32
    )
    grad[:, :FF_EXP] = ordered[:96]
    grad[:, FF_EXP:] = ordered[96:]

    @pl.when(e == 0)
    def _():
        dot_ref[...] = jnp.zeros_like(dot_ref)

    dot = jnp.sum(w_ref[0].astype(f32) * grad[...], 1, keepdims=True)
    dot_ref[...] += jnp.broadcast_to(dot, dot_ref.shape)
    mo_ref[0], so_ref[0], wo_ref[0] = adam(
        w_ref[0], m_ref[0], s_ref[0], grad[...], rate_lifting, weight_decay
    )


def adam_lifting(weight, mean, square, grad, code):
    block = pl.BlockSpec((1, 96, 2 * FF_EXP), lambda e: (e, 0, 0))
    shape = jax.ShapeDtypeStruct(weight.shape, f32)
    return pl.pallas_call(
        adam_lifting_kernel,
        grid=(EXPERTS,),
        in_specs=[
            block,
            block,
            block,
            pl.BlockSpec(grad.shape, lambda e: (0, 0, 0)),
            pl.BlockSpec(code.shape, lambda e: (0, 0)),
        ],
        out_specs=(block, block, block, pl.BlockSpec((96, 128), lambda e: (0, 0))),
        out_shape=(shape, shape, shape, jax.ShapeDtypeStruct((96, 128), f32)),
        scratch_shapes=[pltpu.VMEM((96, 2 * FF_EXP), f32)],
        compiler_params=pltpu.CompilerParams(vmem_limit_bytes=62 * 2**20),
        name="adam_lifting",
    )(weight, mean, square, grad, code)


def adam_inward_kernel(w_ref, m_ref, s_ref, g_ref, mo_ref, so_ref, wo_ref, dot_ref):
    parts = [g_ref[c].astype(f32) for c in range(CHIPS)]
    grad = jnp.concatenate(
        [p[:, :192] for p in parts] + [p[:, 192:256] for p in parts] + [p[:, 256:] for p in parts], 1
    )
    dot = jnp.sum(w_ref[...].astype(f32) * grad, 1, keepdims=True)
    dot_ref[...] = jnp.broadcast_to(dot, dot_ref.shape)
    mo_ref[...], so_ref[...], wo_ref[...] = adam(
        w_ref[...], m_ref[...], s_ref[...], grad, rate_inward, weight_decay
    )


def adam_inward(weight, mean, square, grad):
    shape = jax.ShapeDtypeStruct(weight.shape, f32)
    return pl.pallas_call(
        adam_inward_kernel,
        in_specs=[VMEM] * 4,
        out_specs=(VMEM,) * 4,
        out_shape=(shape, shape, shape, jax.ShapeDtypeStruct((96, 128), f32)),
        compiler_params=pltpu.CompilerParams(vmem_limit_bytes=62 * 2**20),
        name="adam_inward",
    )(weight, mean, square, grad)


def tables():
    half = HEAD // 2
    frequency = np.float32(10000.0) ** (-(2.0 * np.arange(half, dtype=np.float32)) / HEAD)
    phases = np.arange(SEQ, dtype=np.float32)[:, None] * frequency[None, :].astype(np.float32)
    cos, sin = np.cos(phases).astype(np.float32), np.sin(phases).astype(np.float32)
    return (
        np.concatenate([cos, cos, cos, cos], 1),
        np.concatenate([-sin, sin, -sin, sin], 1),
    )


def unit_codes():
    unit = np.arange(HID, dtype=np.int32)
    return (unit // FLAT) * 1024 + unit % FLAT


def inverse_root(stream):
    return lax.rsqrt(jnp.mean(stream * stream, -1, keepdims=True) + norm_epsilon)


def norm_back(scaled, unit, inverse):
    return inverse * (scaled - unit * jnp.mean(scaled * unit, -1, keepdims=True))


def per_device(
    layer_input,
    grad_output,
    routes,
    route_logits,
    norm_gains,
    inward,
    outward,
    lifting,
    lowering,
    mean_gains,
    mean_inward,
    mean_outward,
    mean_lifting,
    mean_lowering,
    square_gains,
    square_inward,
    square_outward,
    square_lifting,
    square_lowering,
):
    gains = norm_gains.astype(f32)
    cos, sin = (jnp.asarray(t) for t in tables())

    lifting_rows = lifting.transpose(1, 0, 2)
    codes = jnp.asarray(unit_codes())
    x = lax.axis_index("rep") // 2
    position = 2 * x + lax.rem(lax.axis_index("shard"), 2)
    low_rows = lowering.transpose(1, 0, 2).reshape(EXPERTS * 32, D)
    low_rows = lax.dynamic_slice(low_rows, (2 * FLAT * x, 0), (2 * FLAT, D)).reshape(2, FLAT, D)
    low_rows = jnp.pad(low_rows, ((0, 0), (0, FLAT_PAD - FLAT), (0, 0)))
    expert = (FLAT * position + lax.rem(jnp.arange(HID), FLAT)) // 32
    row = jnp.arange(128)[:, None]
    share_table = ((row == expert) | (row == expert + 16)).astype(bf16)

    x_all, head_weight, y_all, shares, by_unit = start(
        layer_input, grad_output, inward, norm_gains, routes, route_logits, lifting_rows, codes[None, :], 2
    )
    head_weight = head_weight.reshape(D, 384)
    gain_rows = head_weight[:, 192:194].T.astype(f32)
    gain_one, gain_two = gain_rows[0:1], gain_rows[1:2]
    late_outward, x_all = lax.optimization_barrier((outward, x_all))
    outward_all = lax.all_gather(late_outward, "shard", axis=0, tiled=True)

    q, k, v, u_one, attended, lse, unit_weight, down_weight = attend(
        x_all, head_weight, gain_one, cos, sin, by_unit, low_rows, 1
    )
    unit_weight = unit_weight.reshape(D, EXP)
    (own_attended,) = exchange((attended,), ("home",), 3, "attended_home")
    mixed, low_two = one_step(
        mix_kernel,
        (own_attended, outward_all, layer_input, gain_two),
        (((OWN, D), f32), ((OWN, D), bf16)),
        "mix",
    )
    u_two = second(low_two, 4)
    down_weight = down_weight[:, :FLAT].reshape(HID, D)
    late_inward, u_two = lax.optimization_barrier((inward, u_two))
    inward_all = lax.all_gather(late_inward, "shard", axis=0, tiled=True)

    out_part, du_part, lift_part, down_part = experts(
        u_two, y_all, shares, unit_weight, down_weight, share_table
    )
    du, expert_out, lift_sum, down_sum = reduce_blocks(
        du_part.reshape(PEERS, OWN, D),
        out_part.reshape(PEERS, OWN, D),
        lift_part.reshape(CHIPS, 192, EXP),
        down_part.reshape(CHIPS, 2 * FLAT, D),
        5,
    )
    layer_output = mixed + expert_out
    down_sum = jnp.pad(down_sum.reshape(2, FLAT, D), ((0, 0), (0, FLAT_PAD - FLAT), (0, 0)))
    grad_mixed, outward_part, head_grads, lift_pair, down_pair = grads_away(
        du, mixed, grad_output, gain_two, outward_all, own_attended,
        lift_sum.reshape(2, 96, EXP), down_sum, 6,
    )
    dq, dkv, inward_part, outward_own, lift_got, down_got = attend_back(
        q, k, v, head_grads, attended, lse, cos, sin, u_one, outward_part, lift_pair, down_pair, 8
    )
    dh, inward_sum, outward_sum = tail(
        dq, dkv.reshape(SHARDS, OWN, 128), inward_part, outward_own, inward_all, 7
    )
    (input_grad,) = one_step(
        finish_kernel, (dh, grad_mixed, layer_input, gain_one), (((OWN, D), f32),), "finish"
    )
    outward_grad = outward_sum.astype(f32)
    down_grad = (
        down_got[:, :FLAT].reshape(EXPERTS, 32, D).transpose(1, 0, 2).astype(f32)
    )

    new_lifting = adam_lifting(
        lifting_rows,
        mean_lifting.transpose(1, 0, 2),
        square_lifting.transpose(1, 0, 2),
        lift_got,
        codes[:, None],
    )
    lifting_dot = new_lifting[3]
    new_lifting = tuple(t.transpose(1, 0, 2) for t in new_lifting[:3])
    new_inward = adam_inward(inward, mean_inward, square_inward, inward_sum)
    gain_grad = jnp.stack([new_inward[3][:, 0], lifting_dot[:, 0]]) / gains
    new_gains = adam(norm_gains, mean_gains, square_gains, gain_grad, rate_gains, 0.0)
    new_outward = adam(
        outward, mean_outward, square_outward, outward_grad, rate_outward, weight_decay
    )
    new_lowering = adam(
        lowering, mean_lowering, square_lowering, down_grad, rate_lowering, weight_decay
    )
    return (
        layer_output,
        input_grad,
        new_gains[0],
        new_inward[0],
        new_outward[0],
        new_lifting[0],
        new_lowering[0],
        new_gains[1],
        new_inward[1],
        new_outward[1],
        new_lifting[1],
        new_lowering[1],
        new_gains[2],
        new_inward[2],
        new_outward[2],
        new_lifting[2],
        new_lowering[2],
    )


def solution(mesh):
    tokens = P(("rep", "shard"), None)
    gains, flat, deep = P(None, "shard"), P("shard", None), P("shard", None, None)
    weights = (gains, flat, flat, deep, deep)
    return jax.shard_map(
        per_device,
        mesh=mesh,
        in_specs=(tokens,) * 4 + weights * 3,
        out_specs=(tokens,) * 2 + weights * 3,
        check_vma=False,
    )
```

```python
import functools

import jax
import jax.numpy as jnp
import numpy as np
from jax import lax
from jax.experimental import pallas as pl
from jax.experimental.pallas import tpu as pltpu
from jax.sharding import PartitionSpec as P

HEADS = 24
KV_HEADS = 8
HEAD = 64
GROUP = HEADS // KV_HEADS
FF_EXP = 512
EXPERTS = 10
STEP = 10

norm_epsilon = 1e-06
beta_one = 0.9
beta_two = 0.95
adam_epsilon = 1e-08
weight_decay = 0.1
rate_gains = 0.5
rate_inward = 0.05
rate_outward = 0.3
rate_lifting = 0.05
rate_lowering = 0.3

SHARDS = 16
CHIPS = 8
REPS = 8
OWN = 192
SEQ = OWN * SHARDS
D = 1536
PEERS = 8
FLAT = 40
FLAT_PAD = 48
HID = SHARDS * FLAT
EXP = 2 * HID
BLOCKS = 8
ROWS = GROUP * OWN
KEYS = 2 * OWN

MESH = pl.DeviceIdType.MESH
bf16 = jnp.bfloat16
f32 = jnp.float32


def place():
    rep = lax.axis_index("rep")
    shard = lax.axis_index("shard")
    return rep, shard


def greet(devices):
    barrier = pltpu.get_barrier_semaphore()
    for device in devices:
        pl.semaphore_signal(barrier, inc=1, device_id=device, device_id_type=MESH)
    pl.semaphore_wait(barrier, len(devices))


def send(src, dst, send_sem, recv_sem, device):
    copy = pltpu.make_async_remote_copy(
        src_ref=src,
        dst_ref=dst,
        send_sem=send_sem,
        recv_sem=recv_sem,
        device_id=device,
        device_id_type=MESH,
    )
    copy.start()
    return copy


def params(collective, vmem=None):
    return pltpu.CompilerParams(
        collective_id=collective, has_side_effects=True, vmem_limit_bytes=vmem
    )


ANY = pl.BlockSpec(memory_space=pl.ANY)
VMEM = pl.BlockSpec(memory_space=pltpu.VMEM)
HBM = pl.BlockSpec(memory_space=pltpu.HBM)


def along_x(rep, dx):
    return 2 * lax.rem(rep // 2 + dx, 4) + lax.rem(rep, 2)


def landed_on(ref, recv_sem, any_send_sem, device):
    pltpu.make_async_remote_copy(
        src_ref=ref,
        dst_ref=ref,
        send_sem=any_send_sem,
        recv_sem=recv_sem,
        device_id=device,
        device_id_type=MESH,
    ).wait_recv()


def x_gather(x_ref, o_ref, local_sem, send_sem, recv_sem):
    rep, shard = place()
    core = lax.rem(shard, 2)
    sib = shard + 1 - 2 * core
    half = x_ref.shape[0] // 2
    top, bottom = pl.ds(0, half), pl.ds(half, half)
    up, down, far = (along_x(rep, d) for d in (1, 3, 2))

    def block(r, other=False):
        return 2 * (r // 2) + (1 - core if other else core)

    mine = block(rep)
    own = pltpu.make_async_copy(x_ref, o_ref.at[mine], local_sem)
    sent = []

    def put(ref, dst, slot, device):
        sent.append(send(ref, dst, send_sem.at[len(sent)], recv_sem.at[slot], device))

    def arrived(ref, slot):
        landed_on(ref, recv_sem.at[slot], send_sem.at[0], (rep, sib))

    def start():
        own.start()
        put(x_ref, o_ref.at[mine], 0, (up, shard))
        put(x_ref, o_ref.at[mine], 1, (down, shard))
        put(x_ref, o_ref.at[mine], 4, (rep, sib))

    def relay():
        ref = o_ref.at[block(down)]
        arrived(ref, 0)
        put(o_ref.at[block(down), top], o_ref.at[block(down), top], 2, (up, shard))
        put(ref, ref, 5, (rep, sib))
        ref = o_ref.at[block(up)]
        arrived(ref, 1)
        put(o_ref.at[block(up), bottom], o_ref.at[block(up), bottom], 3, (down, shard))
        put(ref, ref, 6, (rep, sib))

    def relay_far():
        for slot, part in ((2, top), (3, bottom)):
            ref = o_ref.at[block(far), part]
            arrived(ref, slot)
            put(ref, ref, slot + 5, (rep, sib))

    def finish():
        arrived(o_ref.at[block(rep, True)], 4)
        arrived(o_ref.at[block(down, True)], 5)
        arrived(o_ref.at[block(up, True)], 6)
        arrived(o_ref.at[block(far, True), top], 7)
        arrived(o_ref.at[block(far, True), bottom], 8)
        for copy in sent:
            copy.wait_send()
        own.wait()

    return start, relay, relay_far, finish


def ring_spread(x_ref, o_ref, split, local_sem, send_sem, recv_sem):
    rep, shard = place()
    core = lax.rem(shard, 2)
    chip = shard // 2
    y = lax.rem(chip, 2)
    sib = shard + 1 - 2 * core
    pair = chip + 1 - 2 * y
    up, down, far = (lax.rem(chip + d, 8) for d in (2, 6, 4))
    own = pltpu.make_async_copy(x_ref.at[core], o_ref.at[shard], local_sem)
    first, last = pl.ds(0, split), pl.ds(split, x_ref.shape[2] - split)

    mate = rep + 1 - 2 * lax.rem(rep, 2)

    def copy(src, dst, slot, chip_to=None):
        across = slot in (18, 19, 20, 21, 22)
        return pltpu.make_async_remote_copy(
            src_ref=src,
            dst_ref=dst,
            send_sem=send_sem.at[slot],
            recv_sem=recv_sem.at[slot],
            device_id=(mate if across else rep, sib if chip_to is None else 2 * chip_to + core),
            device_id_type=MESH,
        )

    def push_pair(c, columns, slot, across):
        push(block(c, columns, 0), slot, pair)
        push(block(c, columns, 1), across, pair)

    def other(c):
        return c + 1 - 2 * y

    def block(c, columns, part=None):
        if part is None:
            return o_ref.at[pl.ds(2 * c, 2), :, columns]
        return o_ref.at[2 * c + part, :, columns]

    def push(ref, slot, to):
        copy(ref, ref, slot, to).start()

    def arrived(ref, slot):
        copy(ref, ref, slot, pair).wait_recv()

    def start():
        own.start()
        copy(x_ref.at[1 - core], o_ref.at[shard], 0).start()

    def one():
        copy(o_ref.at[sib], o_ref.at[sib], 0).wait_recv()
        own.wait()
        push_pair(chip, first, 1, 19)
        push(block(chip, last), 10, up)
        push(block(chip, last), 12, down)
        push(block(chip, first), 2, up)
        push(block(chip, first), 6, down)
        push_pair(chip, last, 14, 20)

    def two():
        arrived(block(pair, first, 0), 1)
        arrived(block(pair, first, 1), 19)
        push(block(pair, first), 3, up)
        push(block(pair, first), 7, down)
        arrived(block(down, last), 10)
        push_pair(down, last, 15, 21)
        push(block(down, last, 0), 11, up)
        arrived(block(up, last), 12)
        push_pair(up, last, 16, 22)
        push(block(up, last, 1), 13, down)

    def three():
        arrived(block(down, first), 2)
        push(block(down, first, 0), 4, up)
        arrived(block(up, first), 6)
        push(block(up, first, 1), 8, down)
        arrived(block(far, last, 0), 11)
        push(block(far, last, 0), 17, pair)
        arrived(block(far, last, 1), 13)
        push(block(far, last, 1), 18, pair)
        arrived(block(other(down), first), 3)
        push(block(other(down), first, 0), 5, up)
        arrived(block(other(up), first), 7)
        push(block(other(up), first, 1), 9, down)

    def finish():
        arrived(block(far, first, 0), 4)
        arrived(block(far, first, 1), 8)
        arrived(block(other(far), first, 0), 5)
        arrived(block(other(far), first, 1), 9)
        for c, slot, across in ((pair, 14, 20), (other(down), 15, 21), (other(up), 16, 22)):
            arrived(block(c, last, 0), slot)
            arrived(block(c, last, 1), across)
        arrived(block(other(far), last, 0), 17)
        arrived(block(other(far), last, 1), 18)
        copy(x_ref.at[1 - core], o_ref.at[shard], 0).wait_send()
        for slot in (2, 3, 6, 7):
            copy(block(chip, first), block(chip, first), slot, pair).wait_send()
        for slot in (1, 4, 5, 8, 9, 19):
            copy(block(chip, first, 0), block(chip, first, 0), slot, pair).wait_send()
        for slot in (10, 12):
            copy(block(chip, last), block(chip, last), slot, pair).wait_send()
        for slot in (11, 13, 14, 15, 16, 17, 18, 20, 21, 22):
            copy(block(chip, last, 0), block(chip, last, 0), slot, pair).wait_send()

    return start, one, two, three, finish


START_SPLIT = 896


def start_kernel(
    x_ref, t_ref, in_hbm, gain_hbm, routes_hbm, logits_hbm, lift_hbm, code_hbm,
    o_ref, p_ref, g_ref, share_o, unit_ref,
    in_ref, gain_ref, routes_ref, logits_ref, lift_ref, code_ref, fetch_sem,
    w_ref, share_ref, local_sem, send_sem, recv_sem, s_part, r_part, s_x, r_x, s_y, r_y,
):
    with_parts = True
    rep, shard = place()
    half = x_ref.shape[0] // 2
    core = lax.rem(shard, 2)
    chip = shard // 2
    y = lax.rem(chip, 2)
    sib = shard + 1 - 2 * core
    pair = shard + 2 - 4 * y
    up = lax.rem(shard + 4, 16)
    down = lax.rem(shard + 12, 16)
    far = lax.rem(shard + 8, 16)
    first, last = pl.ds(0, START_SPLIT), pl.ds(START_SPLIT, D - START_SPLIT)
    rows, top, bottom = pl.ds(0, 2 * half), pl.ds(0, half), pl.ds(half, half)
    peers = [2 * lax.rem(chip + i, 8) + core for i in range(1, 8)]

    def other(block):
        return block + 2 - 4 * y

    greet(
        [(rep, sib)]
        + [(rep, p) for p in peers]
        + [(along_x(rep, 1), shard), (along_x(rep, 3), shard)]
    )
    fetches = [
        pltpu.make_async_copy(src, dst, fetch_sem.at[n])
        for n, (src, dst) in enumerate(
            (
                (in_hbm, in_ref),
                (gain_hbm, gain_ref),
                (routes_hbm, routes_ref),
                (logits_hbm, logits_ref),
                (lift_hbm.at[pl.ds((5 * (rep // 2)) // 2, 3)], lift_ref),
                (code_hbm, code_ref),
            )
        )
    ]
    for fetch in fetches:
        fetch.start()
    x_steps = x_gather(t_ref, g_ref, local_sem.at[2], s_x, r_x)
    y_steps = x_gather(share_ref, share_o, local_sem.at[3], s_y, r_y)
    own = pltpu.make_async_copy(x_ref, o_ref.at[shard], local_sem.at[0])
    own.start()
    sent = []

    def put(src, dst, slot, device):
        sent.append(send(src, dst, send_sem.at[len(sent)], recv_sem.at[slot], (rep, device)))

    def landed(ref, sem):
        landed_on(ref, sem, send_sem.at[0], (rep, sib))

    arrivals = {
        0: (pair, first, rows, ((2, up, rows), (6, down, rows))),
        9: (down, last, rows, ((14, pair, rows), (10, up, top))),
        1: (down, first, rows, ((3, up, top),)),
        11: (up, last, rows, ((15, pair, rows), (12, down, bottom))),
        5: (up, first, rows, ((7, down, bottom),)),
        13: (pair, last, rows, ()),
        2: (other(down), first, rows, ((4, up, top),)),
        6: (other(up), first, rows, ((8, down, bottom),)),
        10: (far, last, top, ((16, pair, top),)),
        12: (far, last, bottom, ((17, pair, bottom),)),
        3: (far, first, top, ()),
        7: (far, first, bottom, ()),
        14: (other(down), last, rows, ()),
        15: (other(up), last, rows, ()),
        4: (other(far), first, top, ()),
        8: (other(far), first, bottom, ()),
        16: (other(far), last, top, ()),
        17: (other(far), last, bottom, ()),
    }

    def arrive(slots):
        for slot in slots:
            block, columns, part, onward = arrivals[slot]
            ref = o_ref.at[block, part, columns]
            landed(ref, recv_sem.at[slot])
            for to_slot, device, rows_on in onward:
                ref_on = o_ref.at[block, rows_on, columns]
                put(ref_on, ref_on, to_slot, device)
            put(ref, ref, 19 + slot, sib)

    for columns, slots in ((first, (0, 1, 5)), (last, (13, 9, 11))):
        for slot, device in zip(slots, (pair, up, down)):
            put(x_ref.at[:, columns], o_ref.at[shard, :, columns], slot, device)
    put(x_ref, o_ref.at[shard], 18, sib)
    x_steps[0]()

    for fetch in fetches:
        fetch.wait()
    row, column = (lax.broadcasted_iota(jnp.int32, (96, 96), d) for d in (0, 1))
    gains = contract(jnp.where(row == column, 1.0, 0.0).astype(bf16), gain_ref[...], ((1,), (1,)))
    gains = jnp.concatenate([gains.astype(bf16), jnp.zeros((96, HEAD - 2), bf16)], 1)
    for c in range(CHIPS):
        w_ref[c] = jnp.concatenate(
            [
                in_ref[:, 192 * c : 192 * (c + 1)],
                gains,
                in_ref[:, 1536 + HEAD * c : 1536 + HEAD * (c + 1)],
                in_ref[:, 2048 + HEAD * c : 2048 + HEAD * (c + 1)],
            ],
            1,
        )
    parts = []
    if with_parts:
        mine = pltpu.make_async_copy(w_ref.at[chip], p_ref.at[shard], local_sem.at[1])
        mine.start()
        parts.append(
            send(w_ref.at[chip], p_ref.at[shard], s_part.at[0], r_part.at[0], (rep, sib))
        )
        for i in range(1, 8):
            c = lax.rem(chip + i, 8)
            parts.append(
                send(
                    w_ref.at[c], p_ref.at[shard], s_part.at[i], r_part.at[i], (rep, 2 * c + core)
                )
            )
    logits = logits_ref[...]
    gates = jnp.exp(logits - jnp.max(logits, 1, keepdims=True))
    gates = gates / jnp.sum(gates, 1, keepdims=True)
    lane = lax.broadcasted_iota(jnp.int32, (OWN, 128), 1)
    shares = jnp.zeros((OWN, 128), f32)
    for e in range(EXPERTS):
        one = jnp.sum(jnp.where(routes_ref[...] == e, gates, 0.0), 1, keepdims=True)
        shares = jnp.where(lane == e, one, shares)
    high = shares.astype(bf16)
    rest = pltpu.roll(shares - high.astype(f32), 16, 1)
    share_ref[...] = jnp.where(lane < 16, high, rest.astype(bf16))
    y_steps[0]()
    choose_units(lift_ref, code_ref, unit_ref)
    arrive((0, 9, 1, 11, 5, 13))
    x_steps[1]()
    y_steps[1]()
    arrive((2, 6, 10, 12))
    x_steps[2]()
    y_steps[2]()
    if with_parts:
        for i in range(1, 8):
            block = 2 * lax.rem(chip + 8 - i, 8) + core
            landed(p_ref.at[block], r_part.at[i])
            parts.append(
                send(
                    p_ref.at[block], p_ref.at[block], s_part.at[7 + i], r_part.at[7 + i], (rep, sib)
                )
            )
    arrive((3, 7, 14, 15, 4, 8, 16, 17))

    def twin(block):
        return block + 1 - 2 * core

    if with_parts:
        landed(p_ref.at[sib], r_part.at[0])
        for i in range(1, 8):
            landed(p_ref.at[twin(2 * lax.rem(chip + 8 - i, 8) + core)], r_part.at[7 + i])
        mine.wait()
    landed(o_ref.at[sib], recv_sem.at[18])
    for slot, (block, columns, part, _) in arrivals.items():
        landed(o_ref.at[twin(block), part, columns], recv_sem.at[19 + slot])
    x_steps[3]()
    y_steps[3]()
    for copy in sent + parts:
        copy.wait_send()
    own.wait()


def start(x, tokens, inward, gains, routes, logits, lifting, codes, collective):
    rows, columns = x.shape
    dma = pltpu.SemaphoreType.DMA
    gathered, parts, tokens, shares, units = pl.pallas_call(
        start_kernel,
        out_shape=(
            jax.ShapeDtypeStruct((SHARDS, rows, columns), bf16),
            jax.ShapeDtypeStruct((SHARDS, 96, 384), bf16),
            jax.ShapeDtypeStruct((PEERS, rows, columns), bf16),
            jax.ShapeDtypeStruct((PEERS, rows, 128), bf16),
            jax.ShapeDtypeStruct((2, 96, EXP), bf16),
        ),
        in_specs=[HBM] * 8,
        out_specs=(ANY,) * 4 + (VMEM,),
        scratch_shapes=[
            pltpu.VMEM(inward.shape, bf16),
            pltpu.VMEM(gains.shape, bf16),
            pltpu.VMEM(routes.shape, jnp.int32),
            pltpu.VMEM(logits.shape, f32),
            pltpu.VMEM((3,) + lifting.shape[1:], bf16),
            pltpu.VMEM(codes.shape, jnp.int32),
            dma((6,)),
            pltpu.VMEM((CHIPS, 96, 384), bf16),
            pltpu.VMEM((rows, 128), bf16),
            dma((4,)),
            dma((37,)),
            dma((37,)),
            dma((15,)),
            dma((15,)),
        ]
        + [dma((9,))] * 4,
        compiler_params=params(collective, 62 * 2**20),
        name="start",
    )(x, tokens, inward, gains, routes, logits, lifting, codes)
    return (
        gathered.reshape(SHARDS * rows, columns),
        parts,
        tokens.reshape(PEERS * rows, columns),
        shares.reshape(PEERS * rows, 128),
        units,
    )


def home_kernel(
    x_ref, half_ref, in_ref, gain_ref,
    mixed_ref, low_ref, o_ref, w_ref,
    got, halves, local_sem, s_x, r_x, s_w, r_w,
):
    rep, shard = place()
    core = lax.rem(shard, 2)
    chip = shard // 2
    sib = shard + 1 - 2 * core
    own_half = pltpu.make_async_copy(half_ref, halves.at[core], local_sem.at[0])
    own_half.start()
    holder = lax.rem(core + chip, 2)
    greet([(rep, 2 * lax.rem(chip + i, 8) + holder) for i in range(1, 8)] + [(rep, sib)])
    sent = [send(half_ref, halves.at[core], s_w, r_w, (rep, sib))]
    for i in range(1, 8):
        c = lax.rem(chip + i, 8)
        sent.append(
            send(
                x_ref.at[c], got.at[chip], s_x.at[i], r_x.at[i], (rep, 2 * c + lax.rem(c + core, 2))
            )
        )
    same = lax.rem(chip, 2) == 0

    @pl.when(same)
    def _():
        copy = pltpu.make_async_copy(x_ref.at[chip], got.at[chip], local_sem.at[1])
        copy.start()
        copy.wait()

    @pl.when(jnp.logical_not(same))
    def _():
        send(x_ref.at[chip], got.at[chip], s_x.at[0], r_x.at[0], (rep, sib)).wait_send()
        landed_on(got.at[chip], r_x.at[0], s_x.at[0], (rep, sib))

    own_half.wait()
    landed_on(halves.at[1 - core], r_w, s_w, (rep, sib))
    keeps = [pltpu.make_async_copy(halves, w_ref, local_sem.at[2])]
    keeps[0].start()
    for i in range(1, 8):
        landed_on(got.at[lax.rem(chip + 8 - i, 8)], r_x.at[i], s_x.at[0], (rep, sib))
    keeps.append(pltpu.make_async_copy(got, o_ref, local_sem.at[3]))
    keeps[1].start()
    rows = side_by_side(got)
    mixed = in_ref[...].astype(f32) + jnp.concatenate(
        [jnp.dot(rows, halves[k], preferred_element_type=f32) for k in range(2)], 1
    )
    mixed_ref[...] = mixed
    low_ref[...] = (mixed * inverse_root(mixed) * gain_ref[...]).astype(bf16)
    for copy in sent:
        copy.wait_send()
    for keep in keeps:
        keep.wait()


def home(attended, half, x, gain, collective):
    dma = pltpu.SemaphoreType.DMA
    halves = (2, D, D // 2)
    return pl.pallas_call(
        home_kernel,
        out_shape=(
            jax.ShapeDtypeStruct((OWN, D), f32),
            jax.ShapeDtypeStruct((OWN, D), bf16),
            jax.ShapeDtypeStruct(attended.shape, bf16),
            jax.ShapeDtypeStruct(halves, bf16),
        ),
        in_specs=[HBM, HBM, VMEM, VMEM],
        out_specs=(VMEM, VMEM, ANY, ANY),
        scratch_shapes=[
            pltpu.VMEM(attended.shape, bf16),
            pltpu.VMEM(halves, bf16),
            dma((4,)),
            dma((8,)),
            dma((8,)),
            dma,
            dma,
        ],
        compiler_params=params(collective, 62 * 2**20),
        name="attended_home",
    )(attended, half, x, gain)


def away_kernel(
    du_ref, mixed_ref, y_ref, gain_ref, w_ref, a_ref, lift_ref, down_ref,
    dz_ref, part_ref, o_ref, lift_o, down_o,
    x_ref, lift_own, lift_land, down_own, down_land,
    local_sem, s_x, r_x, s_mate, r_mate, s_sib, r_sib,
):
    rep, shard = place()
    core = lax.rem(shard, 2)
    chip = shard // 2
    sib = shard + 1 - 2 * core
    mate = rep + 1 - 2 * lax.rem(rep, 2)
    greet(
        [(rep, 2 * c + lax.rem(c + core, 2)) for c in (lax.rem(chip + i, 8) for i in range(1, 8))]
        + [(rep, sib), (mate, shard)]
    )
    sent = []
    mates, loads = [], []
    for n, (src, own, land) in enumerate(
        ((lift_ref, lift_own, lift_land), (down_ref, down_own, down_land))
    ):
        mates.append(send(src, land, s_mate.at[n], r_mate.at[n], (mate, shard)))
        load = pltpu.make_async_copy(src, own, local_sem.at[n])
        load.start()
        loads.append(load)

    mixed = mixed_ref[...]
    inverse = inverse_root(mixed)
    dz = y_ref[...].astype(f32) + norm_back(du_ref[...] * gain_ref[...], mixed * inverse, inverse)
    dz_ref[...] = dz
    low = dz.astype(bf16)
    back = contract(low[:, : D // 2], w_ref[0], ((1,), (1,)))
    back = (back + contract(low[:, D // 2 :], w_ref[1], ((1,), (1,)))).astype(bf16)
    for c in range(CHIPS):
        x_ref[c] = back[:, c * 192 : (c + 1) * 192]
    for i in range(1, 8):
        c = lax.rem(chip + i, 8)
        sent.append(
            send(
                x_ref.at[c], o_ref.at[chip], s_x.at[i], r_x.at[i],
                (rep, 2 * c + lax.rem(core + chip, 2)),
            )
        )
    part = contract(side_by_side(a_ref), low, ((0,), (0,))).astype(bf16)
    for s in range(SHARDS):
        part_ref[s] = part[s * 96 : (s + 1) * 96]
    same = lax.rem(chip, 2) == 0

    @pl.when(same)
    def _():
        copy = pltpu.make_async_copy(x_ref.at[chip], o_ref.at[chip], local_sem.at[2])
        copy.start()
        copy.wait()

    @pl.when(jnp.logical_not(same))
    def _():
        send(x_ref.at[chip], o_ref.at[chip], s_x.at[0], r_x.at[0], (rep, sib)).wait_send()
        landed_on(o_ref.at[chip], r_x.at[0], s_x.at[0], (rep, sib))

    keeps, halves = [], []
    for n, (own, land, out) in enumerate(
        ((lift_own, lift_land, lift_o), (down_own, down_land, down_o))
    ):
        loads[n].wait()
        mates[n].wait_recv()
        for k in range(2):

            def add(t, _, own=own, land=land, k=k):
                at = pl.ds(pl.multiple_of(t * 16, 16), 16)
                own[k, at] = (own[k, at].astype(f32) + land[k, at].astype(f32)).astype(bf16)
                return 0

            lax.fori_loop(0, own.shape[1] // 16, add, 0)
        halves.append(
            send(own.at[1 - core], out.at[core], s_sib.at[n], r_sib.at[n], (rep, sib))
        )
        keep = pltpu.make_async_copy(own.at[core], out.at[core], local_sem.at[3 + n])
        keep.start()
        keeps.append(keep)
    for i in range(1, 8):
        landed_on(o_ref.at[lax.rem(chip + 8 - i, 8)], r_x.at[i], s_x.at[0], (rep, sib))
    for n, out in enumerate((lift_o, down_o)):
        landed_on(out.at[1 - core], r_sib.at[n], s_x.at[0], (rep, sib))
        keeps[n].wait()
    for copy in sent + mates + halves:
        copy.wait_send()


def grads_away(du, mixed, y, gain, outward_all, attended, lift, down, collective):
    dma = pltpu.SemaphoreType.DMA
    heads = (CHIPS, OWN, 192)
    return pl.pallas_call(
        away_kernel,
        out_shape=(
            jax.ShapeDtypeStruct((OWN, D), f32),
            jax.ShapeDtypeStruct((SHARDS, 96, D), bf16),
            jax.ShapeDtypeStruct(heads, bf16),
            jax.ShapeDtypeStruct(lift.shape, bf16),
            jax.ShapeDtypeStruct(down.shape, bf16),
        ),
        in_specs=[VMEM] * 6 + [ANY] * 2,
        out_specs=(VMEM, VMEM, ANY, ANY, ANY),
        scratch_shapes=[
            pltpu.VMEM(heads, bf16),
            pltpu.VMEM(lift.shape, bf16),
            pltpu.VMEM(lift.shape, bf16),
            pltpu.VMEM(down.shape, bf16),
            pltpu.VMEM(down.shape, bf16),
            dma((5,)),
            dma((8,)),
            dma((8,)),
        ]
        + [dma((2,))] * 4,
        compiler_params=params(collective, 62 * 2**20),
        name="grads_away",
    )(du, mixed, y, gain, outward_all, attended, lift, down)


PART = (48, 384)


def part_of(r):
    rows = pl.ds(pl.multiple_of((r // 4) * PART[0], PART[0]), PART[0])
    return rows, pl.ds(pl.multiple_of(lax.rem(r, 4) * PART[1], PART[1]), PART[1])


def tail_kernel(
    dq_ref, dkv_ref, in_ref, out_ref, w_hbm,
    dh_ref, in_sum, out_sum,
    w_ref, held_k, near_k, held_i, near_i, got_q, got_k, land_i, land_o, own_o, sum_i, sum_o,
    l_sem, s_q, r_q, s_nk, r_nk, s_ni, r_ni, s_k, r_k, s_ri, r_ri, s_ro, r_ro, s_gi, r_gi, s_go, r_go,
):
    rep, shard = place()
    core = lax.rem(shard, 2)
    chip = shard // 2
    sib = shard + 1 - 2 * core
    fetch = pltpu.make_async_copy(w_hbm, w_ref, l_sem.at[20])
    fetch.start()
    own = pltpu.make_async_copy(out_ref.at[part_of(rep)], own_o, l_sem.at[16])
    own.start()
    loads = {}
    for c in range(8):
        for name, src, held, base in (("i", in_ref, held_i, 0), ("k", dkv_ref, held_k, 8)):
            loads[name, c] = pltpu.make_async_copy(
                src.at[2 * c + core], held.at[c], l_sem.at[base + c]
            )
            loads[name, c].start()
    alone = rep == chip
    barrier = pltpu.get_barrier_semaphore()
    for device in [(rep, lax.rem(shard + i, 16)) for i in range(1, 16)] + [
        (lax.rem(rep + i, 8), shard) for i in range(1, 8)
    ]:
        pl.semaphore_signal(barrier, inc=1, device_id=device, device_id_type=MESH)
    for i in range(8):
        device = (chip, 2 * lax.rem(chip + i, 8) + core)
        if i:
            pl.semaphore_signal(barrier, inc=1, device_id=device, device_id_type=MESH)
        else:

            @pl.when(jnp.logical_not(alone))
            def _(device=device):
                pl.semaphore_signal(barrier, inc=1, device_id=device, device_id_type=MESH)

    pl.semaphore_wait(barrier, jnp.where(alone, 29, 30))

    sent = []

    def put(src, dst, s_sem, r_sem, device):
        copy = send(src, dst, s_sem, r_sem, device)
        sent.append(copy)
        return copy

    def landed(ref, sem):
        landed_on(ref, sem, s_q.at[0], (rep, sib))

    nears = {}
    for name, src, near, s_n, r_n in (
        ("i", in_ref, near_i, s_ni, r_ni),
        ("k", dkv_ref, near_k, s_nk, r_nk),
    ):
        for c in range(8):
            nears[name, c] = put(
                src.at[2 * c + 1 - core], near.at[c], s_n.at[c], r_n.at[c], (rep, sib)
            )
    for i in range(1, 8):
        to = lax.rem(rep + i, 8)
        put(out_ref.at[part_of(to)], land_o.at[i - 1], s_ro.at[i], r_ro.at[i], (to, shard))

    def add_near(name, held, near, rows):
        for c in range(8):
            nears[name, c].wait_recv()
            loads[name, c].wait()

        def add(t, _):
            at = pl.ds(pl.multiple_of(t * 32, 32), 32)
            for c in range(8):
                held[c, at] = (held[c, at].astype(f32) + near[c, at].astype(f32)).astype(bf16)
            return 0

        lax.fori_loop(0, rows // 32, add, 0)

    add_near("i", held_i, near_i, 96)
    for i in range(1, 8):
        to = lax.rem(rep + i, 8)
        put(held_i.at[to], land_i.at[i - 1], s_ri.at[i], r_ri.at[i], (to, shard))
    add_near("k", held_k, near_k, OWN)
    for i in range(1, 8):
        c = lax.rem(chip + i, 8)
        put(held_k.at[c], got_k.at[chip], s_k.at[i], r_k.at[i], (rep, 2 * c + core))
        put(
            dq_ref.at[c], got_q.at[chip], s_q.at[i], r_q.at[i],
            (rep, 2 * c + lax.rem(c + core, 2)),
        )
    got_k[chip] = held_k[chip]
    mine = lax.rem(chip, 2) == 0

    @pl.when(mine)
    def _():
        copy = pltpu.make_async_copy(dq_ref.at[chip], got_q.at[chip], l_sem.at[17])
        copy.start()
        copy.wait()

    @pl.when(jnp.logical_not(mine))
    def _():
        send(dq_ref.at[chip], got_q.at[chip], s_q.at[0], r_q.at[0], (rep, sib)).wait_send()

    own.wait()
    for land, total, r_x in ((land_o, sum_o, r_ro), (land_i, sum_i, r_ri)):
        for i in range(1, 8):
            landed(land.at[i - 1], r_x.at[i])

        def add(t, _, land=land, total=total):
            at = pl.ds(pl.multiple_of(t * 16, 16), 16)
            value = own_o[at] if land is land_o else held_i[rep, at]
            value = value.astype(f32)
            for i in range(7):
                value = value + land[i, at].astype(f32)
            total[at] = value.astype(bf16)
            return 0

        lax.fori_loop(0, total.shape[0] // 16, add, 0)
        if land is land_o:
            keep = pltpu.make_async_copy(sum_o, out_sum.at[part_of(rep)], l_sem.at[18])
            keep.start()
            for i in range(1, 8):
                to = lax.rem(rep + i, 8)
                put(sum_o, out_sum.at[part_of(rep)], s_go.at[i], r_go.at[i], (to, shard))
    owner = 2 * rep + core
    for i in range(1, 8):
        put(sum_i, in_sum.at[chip], s_gi.at[i], r_gi.at[chip], (lax.rem(rep + i, 8), owner))

    @pl.when(alone)
    def _():
        copy = pltpu.make_async_copy(sum_i, in_sum.at[chip], l_sem.at[19])
        copy.start()
        copy.wait()

    @pl.when(jnp.logical_not(alone))
    def _():
        send(sum_i, in_sum.at[chip], s_gi.at[0], r_gi.at[chip], (rep, owner)).wait_send()

    @pl.when(jnp.logical_not(mine))
    def _():
        landed(got_q.at[chip], r_q.at[0])

    for i in range(1, 8):
        landed(got_q.at[lax.rem(chip + 8 - i, 8)], r_q.at[i])
        landed(got_k.at[lax.rem(chip + 8 - i, 8)], r_k.at[i])
    joined = jnp.concatenate(
        [got_q[c] for c in range(CHIPS)]
        + [got_k[c][:, :HEAD] for c in range(CHIPS)]
        + [got_k[c][:, HEAD:] for c in range(CHIPS)],
        1,
    )
    fetch.wait()
    dh_ref[...] = contract(joined, w_ref[...], ((1,), (1,)))

    for i in range(1, 8):
        landed(out_sum.at[part_of(lax.rem(rep + 8 - i, 8))], r_go.at[i])
    for j in range(8):

        @pl.when(jnp.logical_not(jnp.logical_and(alone, chip == j)))
        def _(j=j):
            landed(in_sum.at[j], r_gi.at[j])

    keep.wait()
    for copy in sent:
        copy.wait_send()


def tail(dq, dkv, inward_part, outward_own, inward_all, collective):
    dma = pltpu.SemaphoreType.DMA
    return pl.pallas_call(
        tail_kernel,
        out_shape=(
            jax.ShapeDtypeStruct((OWN, D), f32),
            jax.ShapeDtypeStruct((CHIPS, 96, 320), bf16),
            jax.ShapeDtypeStruct((96, D), bf16),
        ),
        in_specs=[ANY, ANY, ANY, ANY, HBM],
        out_specs=(VMEM, ANY, ANY),
        scratch_shapes=[
            pltpu.VMEM(inward_all.shape, bf16),
            pltpu.VMEM((8, OWN, 128), bf16),
            pltpu.VMEM((8, OWN, 128), bf16),
            pltpu.VMEM((8, 96, 320), bf16),
            pltpu.VMEM((8, 96, 320), bf16),
            pltpu.VMEM((8, OWN, 192), bf16),
            pltpu.VMEM((8, OWN, 128), bf16),
            pltpu.VMEM((7, 96, 320), bf16),
            pltpu.VMEM((7,) + PART, bf16),
            pltpu.VMEM(PART, bf16),
            pltpu.VMEM((96, 320), bf16),
            pltpu.VMEM(PART, bf16),
            dma((21,)),
        ]
        + [dma((8,))] * 16,
        compiler_params=params(collective, 62 * 2**20),
        name="tail",
    )(dq, dkv, inward_part, outward_own, inward_all)


def swap_halves(values):
    lanes = values.shape[1]
    lane = lax.broadcasted_iota(jnp.int32, values.shape, 1)
    ahead = pltpu.roll(values, lanes - HEAD // 2, 1)
    behind = pltpu.roll(values, HEAD // 2, 1)
    return jnp.where(lax.rem(lane, HEAD) < HEAD // 2, ahead, behind)


def project_step(i, core, x_ref, w_ref, g_ref, cos_ref, sin_ref, q_ref, k_ref, v_ref, u_ref):
    stream = x_ref[...].astype(f32)
    u_ref[...] = (stream * inverse_root(stream) * g_ref[...]).astype(bf16)
    first = pl.multiple_of(lax.rem(i + core, 2) * OWN, OWN)
    own = pl.ds(first, OWN)
    queries = jnp.dot(u_ref[own, :], w_ref[:, :256], preferred_element_type=f32)
    cos, sin = cos_ref[own, :], sin_ref[own, :]
    cos, sin = jnp.concatenate([cos, cos], 1), jnp.concatenate([sin, sin], 1)
    turned = (queries * cos + swap_halves(queries) * sin).astype(bf16)
    turned = turned * jnp.bfloat16(HEAD**-0.5)
    for r in range(GROUP):
        q_ref[i, r * OWN : (r + 1) * OWN, :] = turned[:, r * HEAD : (r + 1) * HEAD]
    pairs = jnp.dot(u_ref[...], w_ref[:, 256:], preferred_element_type=f32)
    keys = pairs * cos_ref[...] + swap_halves(pairs) * sin_ref[...]
    rows = pl.ds(pl.multiple_of(i * KEYS, KEYS), KEYS)
    k_ref[rows, :] = keys[:, :HEAD].astype(bf16)
    lane = lax.broadcasted_iota(jnp.int32, pairs.shape, 1)
    v_ref[rows, :] = jnp.where(lane < HEAD, pltpu.roll(pairs, HEAD, 1), 1.0).astype(bf16)


def contract(a, b, dims, precision=None):
    return lax.dot_general(
        a, b, ((dims[0], dims[1]), ((), ())), preferred_element_type=f32, precision=precision
    )


def attend_kernel(
    x_ref, w_ref, g_ref, cos_ref, sin_ref, b_ref, d_ref, f_ref,
    q_ref, k_ref, v_ref, u_ref, o_ref, l_ref, bo_ref, do_ref, fo_ref,
    local_sem, s_sem, r_sem, s_low, r_low, s_out, r_out,
):
    i = pl.program_id(0)
    core = lax.rem(lax.axis_index("shard"), 2)
    steps = ring_spread(b_ref, bo_ref, 256, local_sem.at[0], s_sem, r_sem)
    low_steps = ring_spread(d_ref, do_ref, 256, local_sem.at[1], s_low, r_low)
    out_steps = ring_spread(f_ref, fo_ref, 128, local_sem.at[2], s_out, r_out)

    @pl.when(i == 0)
    def _():
        rep, shard = place()
        y = lax.rem(shard // 2, 2)
        greet(
            [(rep, shard + 1 - 2 * core), (rep, shard + 2 - 4 * y)]
            + [(rep + 1 - 2 * lax.rem(rep, 2), shard + 2 - 4 * y)]
            + [(rep, lax.rem(shard + 4, 16)), (rep, lax.rem(shard + 12, 16))]
        )
        out_steps[0]()
        steps[0]()
        low_steps[0]()

    @pl.when(i == 1)
    def _():
        out_steps[1]()
        steps[1]()

    @pl.when(i == 4)
    def _():
        low_steps[1]()

    @pl.when(i == 9)
    def _():
        out_steps[2]()

    @pl.when(i == 11)
    def _():
        steps[2]()

    @pl.when(i == 13)
    def _():
        out_steps[3]()
        low_steps[2]()

    @pl.when(i == 14)
    def _():
        steps[3]()

    @pl.when(i == 15)
    def _():
        low_steps[3]()

    @pl.when(i < BLOCKS)
    def _():
        project_step(i, core, x_ref, w_ref, g_ref, cos_ref, sin_ref, q_ref, k_ref, v_ref, u_ref)

    @pl.when(i >= BLOCKS)
    def _():
        attend_step(i - BLOCKS, core, q_ref, k_ref, v_ref, o_ref, l_ref)

    @pl.when(i == 2 * BLOCKS - 1)
    def _():
        out_steps[4]()
        steps[4]()
        low_steps[4]()


def attend_step(i, core, q_ref, k_ref, v_ref, o_ref, l_ref):
    shift = lax.rem(i + core, 2) * OWN
    q = q_ref[i]

    def step(c, carry, last=False):
        top, total = carry
        at = pl.ds(pl.multiple_of(c * KEYS, KEYS), KEYS)
        scores = contract(q, k_ref[at, :], ((1,), (1,)))
        if last:
            row = lax.broadcasted_iota(jnp.int32, (OWN, KEYS), 0)
            column = lax.broadcasted_iota(jnp.int32, (OWN, KEYS), 1)
            bias = jnp.where(column <= row + shift, 0.0, -1e30)
            scores = scores + jnp.concatenate([bias] * GROUP, 0)
        high = jnp.maximum(top, jnp.max(scores, 1, keepdims=True))
        prob = jnp.exp(scores - high).astype(bf16)
        total = total * jnp.exp(top - high) + jnp.dot(
            prob, v_ref[at, :], preferred_element_type=f32
        )
        return high, total

    carry = (jnp.full((ROWS, 1), -1e30, f32), jnp.zeros((ROWS, 128), f32))
    carry = lax.fori_loop(0, i, step, carry)
    top, total = step(i, carry, True)
    weight = total[:, HEAD : HEAD + 1]
    result = (total[:, :HEAD] / weight).astype(bf16)
    o_ref[0] = jnp.concatenate([result[r * OWN : (r + 1) * OWN] for r in range(GROUP)], 1)
    column = lax.broadcasted_iota(jnp.int32, (8, 8), 1)
    l_ref[0] = contract(
        jnp.where(column == 0, 1.0, 0.0).astype(f32),
        jnp.broadcast_to(top + jnp.log(weight), (ROWS, 8)),
        ((1,), (1,)),
        lax.Precision.HIGHEST,
    )


def attend(x_all, weight, gain, cos, sin, units, low, half, collective):
    dma = pltpu.SemaphoreType.DMA
    whole = lambda i: (0, 0)
    early = lambda i: (jnp.minimum(i, BLOCKS - 1), 0)
    late = lambda i: (jnp.maximum(i - BLOCKS, 0), 0, 0)
    return pl.pallas_call(
        attend_kernel,
        grid=(2 * BLOCKS,),
        in_specs=[
            pl.BlockSpec((KEYS, D), early),
            pl.BlockSpec((D, 384), whole),
            pl.BlockSpec((1, D), whole),
            pl.BlockSpec((KEYS, 128), early),
            pl.BlockSpec((KEYS, 128), early),
            ANY,
            ANY,
            ANY,
        ],
        out_specs=(
            pl.BlockSpec((BLOCKS, ROWS, HEAD), lambda i: (0, 0, 0)),
            pl.BlockSpec((SEQ, HEAD), whole),
            pl.BlockSpec((SEQ, 128), whole),
            pl.BlockSpec((KEYS, D), early),
            pl.BlockSpec((1, OWN, GROUP * HEAD), late),
            pl.BlockSpec((1, 8, ROWS), late),
            ANY,
            ANY,
            ANY,
        ),
        out_shape=(
            jax.ShapeDtypeStruct((BLOCKS, ROWS, HEAD), bf16),
            jax.ShapeDtypeStruct((SEQ, HEAD), bf16),
            jax.ShapeDtypeStruct((SEQ, 128), bf16),
            jax.ShapeDtypeStruct((SEQ, D), bf16),
            jax.ShapeDtypeStruct((BLOCKS, OWN, GROUP * HEAD), bf16),
            jax.ShapeDtypeStruct((BLOCKS, 8, ROWS), f32),
            jax.ShapeDtypeStruct((SHARDS,) + units.shape[1:], bf16),
            jax.ShapeDtypeStruct((SHARDS,) + low.shape[1:], bf16),
            jax.ShapeDtypeStruct((SHARDS,) + half.shape[1:], bf16),
        ),
        scratch_shapes=[dma((3,))] + [dma((23,))] * 6,
        compiler_params=params(collective, 62 * 2**20),
        name="attend",
    )(x_all, weight, gain, cos, sin, units, low, half)


def attend_back_kernel(
    q_ref, k_ref, v_ref, g_ref, a_ref, l_ref, cos_ref, sin_ref, qcos_ref, qsin_ref, u_hbm, part_ref,
    lift_ref, down_ref, dq_ref, dkv_ref, in_ref, part_out, lift_out, down_out,
    u_ref, u_sem, dk, dv, dq, total_q, held, near, landed, local_sem, s_sem, r_sem, h_sem, s_near, r_near, s_far, r_far,
):
    i = pl.program_id(0)
    rep, shard = place()
    core = lax.rem(shard, 2)
    chip = shard // 2
    sib = shard + 1 - 2 * core
    shift = lax.rem(i + core, 2) * OWN
    x = rep // 2
    kept = [
        (n, src, dst)
        for n, (src, dst) in enumerate(((lift_ref, lift_out), (down_ref, down_out)))
    ]

    def copy_same(n, src, dst):
        return pltpu.make_async_copy(src, dst.at[pl.ds(2 * x, 2)], local_sem.at[n])

    x_up, x_down, x_far = (lax.rem(x + d, 4) for d in (1, 3, 2))

    def copy_x(n, src, dst, way):
        return pltpu.make_async_remote_copy(
            src_ref=src,
            dst_ref=dst,
            send_sem=s_sem.at[n, way],
            recv_sem=r_sem.at[n, way],
            device_id=(along_x(rep, 3 if way % 2 else 1), shard),
            device_id_type=MESH,
        )

    def two_of(dst, at):
        return dst.at[pl.ds(2 * at, 2)]

    def copy_near(j):
        return pltpu.make_async_remote_copy(
            src_ref=part_ref.at[2 * lax.rem(chip + j, 8) + 1 - core],
            dst_ref=near.at[j],
            send_sem=s_near.at[j],
            recv_sem=r_near.at[j],
            device_id=(rep, sib),
            device_id_type=MESH,
        )

    def copy_own(j):
        return pltpu.make_async_copy(
            part_ref.at[2 * lax.rem(chip + j, 8) + core], held.at[j], h_sem.at[j]
        )

    def copy_far(j):
        return pltpu.make_async_remote_copy(
            src_ref=held.at[j],
            dst_ref=landed.at[j - 1],
            send_sem=s_far.at[j],
            recv_sem=r_far.at[j],
            device_id=(rep, 2 * lax.rem(chip + j, 8) + core),
            device_id_type=MESH,
        )

    @pl.when(i == 0)
    def _():
        greet(
            [(rep, sib)]
            + [(rep, 2 * lax.rem(chip + n, 8) + core) for n in range(1, 8)]
            + [(along_x(rep, dx), shard) for dx in (1, 3)]
        )
        for j in range(8):
            copy_near(j).start()
            copy_own(j).start()
        for n, src, dst in kept:
            copy_same(n, src, dst).start()
            copy_x(n, src, two_of(dst, x), 0).start()
            copy_x(n, src, two_of(dst, x), 1).start()
        pltpu.make_async_copy(u_hbm, u_ref, u_sem).start()
        total_q[...] = jnp.zeros_like(total_q)
        dk[...] = jnp.zeros_like(dk)
        dv[...] = jnp.zeros_like(dv)

    @pl.when(i == 6)
    def _():
        for n, src, dst in kept:
            ref = two_of(dst, x_down)
            copy_x(n, ref, ref, 0).wait_recv()
            ref = dst.at[2 * x_down]
            copy_x(n, ref, ref, 2).start()
            ref = two_of(dst, x_up)
            copy_x(n, ref, ref, 1).wait_recv()
            ref = dst.at[2 * x_up + 1]
            copy_x(n, ref, ref, 3).start()

    @pl.when(i == 3)
    def _():
        for j in range(8):
            copy_near(j).wait_recv()
            copy_own(j).wait()

            def add(t, _, j=j):
                at = pl.ds(pl.multiple_of(t * 32, 32), 32)
                held[j, at] = (held[j, at].astype(f32) + near[j, at].astype(f32)).astype(bf16)
                return 0

            lax.fori_loop(0, 3, add, 0)
            if j:
                copy_far(j).start()

    q = q_ref[0]
    grad = jnp.concatenate([g_ref[0][:, r * HEAD : (r + 1) * HEAD] for r in range(GROUP)], 0)
    dq[...] = jnp.zeros_like(dq)
    lse = l_ref[0][:1]
    lane = lax.broadcasted_iota(jnp.int32, (8, GROUP * HEAD), 1)
    row = lax.broadcasted_iota(jnp.int32, (8, GROUP * HEAD), 0)
    sums = contract(
        jnp.where(lane // HEAD == row, 1.0, 0.0).astype(f32),
        g_ref[0].astype(f32) * a_ref[0].astype(f32),
        ((1,), (1,)),
        lax.Precision.HIGHEST,
    )
    delta = jnp.concatenate([sums[r : r + 1] for r in range(GROUP)], 1)

    def step(c, _, last=False):
        at = pl.ds(pl.multiple_of(c * KEYS, KEYS), KEYS)
        keys = k_ref[at, :]
        scores = contract(keys, q, ((1,), (1,)))
        if last:
            key = lax.broadcasted_iota(jnp.int32, (KEYS, OWN), 0)
            token = lax.broadcasted_iota(jnp.int32, (KEYS, OWN), 1)
            bias = jnp.where(key <= token + shift, 0.0, -1e30)
            scores = scores + jnp.concatenate([bias] * GROUP, 1)
        prob = jnp.exp(scores - lse)
        back = contract(v_ref[at, :HEAD], grad, ((1,), (1,)))
        slope = (prob * (back - delta)).astype(bf16)
        dv[at, :] += jnp.dot(prob.astype(bf16), grad, preferred_element_type=f32)
        dk[at, :] += jnp.dot(slope, q, preferred_element_type=f32)
        dq[...] += contract(keys, slope, ((0,), (0,)))
        return 0

    def two_steps(c, _):
        step(2 * c, 0)
        return step(2 * c + 1, 0)

    lax.fori_loop(0, i // 2, two_steps, 0)

    @pl.when(lax.rem(i, 2) == 1)
    def _():
        step(i - 1, 0)

    step(i, 0, True)
    turned = dq[...].T
    wide = jnp.concatenate(
        [turned[r * OWN : (r + 1) * OWN, :] for r in range(GROUP)] + [jnp.zeros((OWN, HEAD), f32)], 1
    )
    wide = wide * (HEAD**-0.5)
    cos, sin = qcos_ref[...], qsin_ref[...]
    cos, sin = jnp.concatenate([cos, cos], 1), jnp.concatenate([sin, sin], 1)
    wide = wide * cos - swap_halves(wide) * sin
    wide = wide[:, : GROUP * HEAD].astype(bf16)
    dq_ref[0] = wide

    @pl.when(i == 0)
    def _():
        pltpu.make_async_copy(u_hbm, u_ref, u_sem).wait()

    mine = pl.ds(pl.multiple_of(i * KEYS + shift, OWN), OWN)
    total_q[...] += contract(wide, u_ref[mine, :], ((0,), (0,)))

    @pl.when(i == BLOCKS - 1)
    def _():
        def turn(c, _):
            at = pl.ds(pl.multiple_of(c * OWN, OWN), OWN)
            both = jnp.concatenate([dk[at, :], dv[at, :]], 1)
            lane = lax.broadcasted_iota(jnp.int32, both.shape, 1)
            turned = both * cos_ref[at, :] - swap_halves(both) * sin_ref[at, :]
            dkv_ref[at, :] = jnp.where(lane < HEAD, turned, both).astype(bf16)
            return 0

        lax.fori_loop(0, SHARDS, turn, 0)
        def add_pairs(c, both):
            at = pl.ds(pl.multiple_of(c * 768, 768), 768)
            return both + contract(dkv_ref[at, :], u_ref[at, :], ((0,), (0,)))

        both = lax.fori_loop(0, SEQ // 768, add_pairs, jnp.zeros((128, D), f32))
        both = jnp.concatenate([total_q[...], both], 0).T.astype(bf16)
        for s in range(SHARDS):
            in_ref[s] = both[s * 96 : (s + 1) * 96]

        for j in range(1, 8):
            copy_far(j).wait_recv()

        def add(t, _):
            at = pl.ds(pl.multiple_of(t * 32, 32), 32)
            total = held[0, at].astype(f32)
            for j in range(7):
                total = total + landed[j, at].astype(f32)
            part_out[at] = total.astype(bf16)
            return 0

        lax.fori_loop(0, 3, add, 0)
        for n, src, dst in kept:
            copy_same(n, src, dst).wait()
            for k in range(2):
                ref = dst.at[2 * x_far + k]
                copy_x(n, ref, ref, 2 + k).wait_recv()
            for way in range(4):
                ref = two_of(dst, x) if way < 2 else dst.at[2 * x]
                copy_x(n, ref, ref, way).wait_send()
        for j in range(8):
            copy_near(j).wait_send()
            if j:
                copy_far(j).wait_send()


def attend_back(q, k, v, grad, attended, lse, cos, sin, u_all, part, lift, down, collective):
    def own(i):
        return (2 * i + lax.rem(i + lax.rem(lax.axis_index("shard"), 2), 2), 0)

    whole = lambda i: (0, 0)
    block = lambda i: (i, 0, 0)
    return pl.pallas_call(
        attend_back_kernel,
        grid=(BLOCKS,),
        in_specs=[
            pl.BlockSpec((1, ROWS, HEAD), block),
            pl.BlockSpec((SEQ, HEAD), whole),
            pl.BlockSpec((SEQ, 128), whole),
            pl.BlockSpec((1, OWN, GROUP * HEAD), block),
            pl.BlockSpec((1, OWN, GROUP * HEAD), block),
            pl.BlockSpec((1, 8, ROWS), block),
            pl.BlockSpec((SEQ, 128), whole),
            pl.BlockSpec((SEQ, 128), whole),
            pl.BlockSpec((OWN, 128), own),
            pl.BlockSpec((OWN, 128), own),
            HBM,
            ANY,
            ANY,
            ANY,
        ],
        out_specs=(
            pl.BlockSpec((1, OWN, GROUP * HEAD), block),
            pl.BlockSpec((SEQ, 128), whole),
            pl.BlockSpec((SHARDS, 96, 320), lambda i: (0, 0, 0)),
            pl.BlockSpec(part.shape[1:], whole),
            ANY,
            ANY,
        ),
        out_shape=(
            jax.ShapeDtypeStruct((BLOCKS, OWN, GROUP * HEAD), bf16),
            jax.ShapeDtypeStruct((SEQ, 128), bf16),
            jax.ShapeDtypeStruct((SHARDS, 96, 320), bf16),
            jax.ShapeDtypeStruct(part.shape[1:], bf16),
            jax.ShapeDtypeStruct((PEERS,) + lift.shape[1:], bf16),
            jax.ShapeDtypeStruct((PEERS,) + down.shape[1:], bf16),
        ),
        scratch_shapes=[
            pltpu.VMEM((SEQ, D), bf16),
            pltpu.SemaphoreType.DMA,
            pltpu.VMEM((SEQ, HEAD), f32),
            pltpu.VMEM((SEQ, HEAD), f32),
            pltpu.VMEM((HEAD, ROWS), f32),
            pltpu.VMEM((GROUP * HEAD, D), f32),
            pltpu.VMEM((8,) + part.shape[1:], bf16),
            pltpu.VMEM((8,) + part.shape[1:], bf16),
            pltpu.VMEM((7,) + part.shape[1:], bf16),
            pltpu.SemaphoreType.DMA((2,)),
            pltpu.SemaphoreType.DMA((2, 4)),
            pltpu.SemaphoreType.DMA((2, 4)),
        ]
        + [pltpu.SemaphoreType.DMA((8,))] * 5,
        compiler_params=params(collective, 62 * 2**20),
        name="attend_back",
    )(q, k, v, grad, attended, lse, cos, sin, cos, sin, u_all, part, lift, down)


def distance(i):
    return jnp.where(i == 0, 0, jnp.where(i == 1, 1, jnp.where(i == 2, 3, 2)))


def experts_kernel(
    x_hbm, y_ref, c_ref, wl_hbm, wd_hbm, e_ref,
    du_o, out_o, lift_o, down_o,
    u, wl, wd, gl, acc, down, part, near, land, total,
    la, lb, lc, ld, da, db, dc, dd,
    l_sem, s_g, r_g, s_near, r_near, s_land, r_land, s_one, r_one, s_two, r_two,
):
    i = pl.program_id(0)
    rep, shard = place()
    core = lax.rem(shard, 2)
    chip = shard // 2
    y = lax.rem(chip, 2)
    z = chip // 2
    x = rep // 2
    sib = shard + 1 - 2 * core
    pair = shard + 2 - 4 * y

    def remote(src, dst, s_sem, r_sem, device):
        return pltpu.make_async_remote_copy(
            src_ref=src, dst_ref=dst, send_sem=s_sem, recv_sem=r_sem,
            device_id=device, device_id_type=MESH,
        )

    def tokens(dx, k, low=0, size=OWN):
        return u.at[lax.rem(x + dx, 4), pl.ds(pl.multiple_of(OWN * k + low, 96), size)]

    half = OWN // 2
    ups, downs, sibs = (along_x(rep, 1), shard), (along_x(rep, 3), shard), (rep, sib)
    slots = {
        0: (tokens(3, core), None, ups),
        1: (tokens(1, core), None, downs),
        2: (tokens(2, core, 0, half), tokens(3, core, 0, half), ups),
        3: (tokens(2, core, half, half), tokens(1, core, half, half), downs),
        4: (tokens(0, 1 - core), None, sibs),
        5: (tokens(3, 1 - core), tokens(3, core), sibs),
        6: (tokens(1, 1 - core), tokens(1, core), sibs),
        7: (tokens(2, 1 - core, 0, half), tokens(2, core, 0, half), sibs),
        8: (tokens(2, 1 - core, half, half), tokens(2, core, half, half), sibs),
    }

    def gather_send(n):
        _, out, device = slots[n]
        src, dst = (x_hbm, tokens(0, core)) if out is None else (out, out)
        return remote(src, dst, s_g.at[n], r_g.at[n], device)

    def gather_arrival(n):
        ref = slots[n][0]
        remote(ref, ref, s_g.at[n], r_g.at[n], sibs).wait_recv()

    own_tokens = pltpu.make_async_copy(x_hbm, tokens(0, core), l_sem.at[0])
    fetch_wl = pltpu.make_async_copy(wl_hbm, wl, l_sem.at[1])
    fetch_wd = pltpu.make_async_copy(wd_hbm, wd, l_sem.at[2])

    def rows(k):
        return pl.ds(pl.multiple_of(OWN * k, OWN), OWN)

    def near_copy(n, t):
        return remote(
            part.at[t, n, rows(1 - core)], near.at[t, n], s_near.at[t, n], r_near.at[t, n], sibs
        )

    def land_copy(n, t):
        return remote(
            part.at[t, n, rows(core)], land.at[t - 1, n], s_land.at[t, n], r_land.at[t, n],
            (along_x(rep, distance(t)), shard),
        )

    def pass_on(t):
        for n in range(2):
            near_copy(n, t).wait_recv()

            def add(r, _, n=n):
                at = pl.ds(pl.multiple_of(r * 32, 32), 32)
                mine = pl.ds(pl.multiple_of(OWN * core + r * 32, 32), 32)
                part[t, n, mine] = (
                    part[t, n, mine].astype(f32) + near[t, n, at].astype(f32)
                ).astype(bf16)
                return 0

            lax.fori_loop(0, OWN // 32, add, 0)

            @pl.when(t > 0)
            def _(n=n):
                land_copy(n, t).start()

    grads = ((wl, la, lb, lc, ld, lift_o, 192), (wd, da, db, dc, dd, down_o, 2 * FLAT))

    def piece(m, dz, dy, columns):
        buffer, size = grads[m][0], grads[m][6]
        c = 2 * lax.rem(z + dz, 4) + (1 - y if dy else y)
        return buffer.at[pl.ds(pl.multiple_of(size * c, size), size), columns]

    def columns_of(m):
        width = grads[m][0].shape[1] // 2
        return pl.ds(0, width), pl.ds(width, width)

    def to_z(dz):
        return (rep, 4 * lax.rem(z + dz, 4) + 2 * y + core)

    def one_a(m, dz):
        return remote(
            piece(m, dz, 1, columns_of(m)[0]), grads[m][1].at[dz], s_one.at[m, 0, dz], r_one.at[m, 0, dz],
            (rep, pair),
        )

    def one_b(m, dz, dy):
        j = 2 * dz + dy
        return remote(
            piece(m, dz, dy, columns_of(m)[1]), grads[m][2].at[j - 2], s_one.at[m, 1, j], r_one.at[m, 1, j],
            to_z(dz),
        )

    def two_a(m, dz):
        return remote(
            piece(m, dz, 0, columns_of(m)[0]), grads[m][3].at[dz - 1], s_two.at[m, dz], r_two.at[m, dz],
            to_z(dz),
        )

    def two_b(m):
        return remote(
            piece(m, 0, 1, columns_of(m)[1]), grads[m][4], s_two.at[m, 0], r_two.at[m, 0], (rep, pair)
        )

    def first_sums(m):
        land_a, land_b, size = grads[m][1], grads[m][2], grads[m][6]
        first, last = columns_of(m)
        for dz in (2, 1, 3, 0):
            one_a(m, dz).wait_recv()
            mine = piece(m, dz, 0, first)

            def add(t, _, mine=mine, dz=dz):
                at = pl.ds(pl.multiple_of(t * 16, 16), 16)
                mine[at] = (mine[at].astype(f32) + land_a[dz, at].astype(f32)).astype(bf16)
                return 0

            lax.fori_loop(0, size // 16, add, 0)
            if dz:
                two_a(m, dz).start()
        for dy in (1, 0):
            for dz in (1, 2, 3):
                one_b(m, dz, dy).wait_recv()
            mine = piece(m, 0, dy, last)

            def add(t, _, mine=mine, dy=dy):
                at = pl.ds(pl.multiple_of(t * 16, 16), 16)
                value = mine[at].astype(f32)
                for dz in (1, 2, 3):
                    value = value + land_b[2 * dz + dy - 2, at].astype(f32)
                mine[at] = value.astype(bf16)
                return 0

            lax.fori_loop(0, size // 16, add, 0)
            if dy:
                two_b(m).start()

    def last_sums(m):
        land_c, land_d, out, size = grads[m][3], grads[m][4], grads[m][5], grads[m][6]
        first, last = columns_of(m)
        for dz in (1, 2, 3):
            two_a(m, dz).wait_recv()
        two_b(m).wait_recv()
        mine_a, mine_b = piece(m, 0, 0, first), piece(m, 0, 0, last)

        def add(t, _):
            at = pl.ds(pl.multiple_of(t * 16, 16), 16)
            value = mine_a[at].astype(f32)
            for dz in (1, 2, 3):
                value = value + land_c[dz - 1, at].astype(f32)
            out[at, first] = value.astype(bf16)
            out[at, last] = (mine_b[at].astype(f32) + land_d[at].astype(f32)).astype(bf16)
            return 0

        lax.fori_loop(0, size // 16, add, 0)

    @pl.when(i == 0)
    def _():
        fetch_wl.start()
        fetch_wd.start()
        own_tokens.start()
        greet(
            [(rep, sib), (rep, pair)]
            + [to_z(dz) for dz in (1, 2, 3)]
            + [(along_x(rep, dx), shard) for dx in (1, 2, 3)]
        )
        for n in (4, 0, 1):
            gather_send(n).start()
        down[...] = jnp.zeros_like(down)
        fetch_wl.wait()
        fetch_wd.wait()
        own_tokens.wait()
        gather_arrival(4)

    @pl.when(i == 1)
    def _():
        gather_arrival(1)
        gather_send(6).start()
        gather_send(3).start()
        gather_arrival(0)
        gather_send(5).start()
        gather_send(2).start()
        gather_arrival(6)

    @pl.when(i == 2)
    def _():
        gather_arrival(2)
        gather_send(7).start()
        gather_arrival(3)
        gather_send(8).start()
        gather_arrival(5)

    @pl.when(i == 3)
    def _():
        gather_arrival(7)
        gather_arrival(8)

    @pl.when(i > 0)
    def _():
        pass_on(i - 1)

    @pl.when(i < 4)
    def _():
        h, dy = u[lax.rem(x + distance(i), 4)], y_ref[...]
        lifted = jnp.dot(h, wl[...], preferred_element_type=f32)
        back = contract(dy, wd[...], ((1,), (1,)))
        share = jnp.dot(c_ref[...], e_ref[...], preferred_element_type=f32)
        gate, raised = lifted[:, :HID], lifted[:, HID:]
        s = jax.nn.sigmoid(gate)
        swish = gate * s
        act = (share * swish * raised).astype(bf16)
        back = back * share
        grad_gate = back * raised * s * (1.0 + gate * (1.0 - s))
        gl[i] = jnp.concatenate([grad_gate, back * swish], 1).astype(bf16)
        part[i, 0] = contract(gl[i], wl[...], ((1,), (1,))).astype(bf16)
        near_copy(0, i).start()
        part[i, 1] = jnp.dot(act, wd[...], preferred_element_type=f32).astype(bf16)
        near_copy(1, i).start()
        down[...] += contract(act, dy, ((0,), (0,)))

    @pl.when(i == 4)
    def _():
        wd[...] = down[...].astype(bf16)
        for dz in (2, 1, 3, 0):
            one_a(1, dz).start()
            if dz:
                one_b(1, dz, 1).start()
                one_b(1, dz, 0).start()
        for part_of_lift in range(2):
            columns = slice(HID * part_of_lift, HID * (part_of_lift + 1))
            for t in range(4):
                dx = (0, 1, 3, 2)[t]
                term = contract(u[lax.rem(x + dx, 4)], gl[t][:, columns], ((0,), (0,)))
                if t == 0:
                    acc[...] = term
                elif t < 3:
                    acc[...] += term
                else:
                    wl[:, columns] = (acc[...] + term).astype(bf16)
            if part_of_lift == 0:
                for dz in (2, 1, 3, 0):
                    one_a(0, dz).start()
            else:
                for dz in (2, 1, 3):
                    one_b(0, dz, 1).start()
                    one_b(0, dz, 0).start()
        first_sums(1)
        for n, out in ((0, du_o), (1, out_o)):
            for t in (1, 2, 3):
                land_copy(n, t).wait_recv()

            def add(r, _, n=n):
                at = pl.ds(pl.multiple_of(r * 32, 32), 32)
                mine = pl.ds(pl.multiple_of(OWN * core + r * 32, 32), 32)
                value = part[0, n, mine].astype(f32)
                for t in range(3):
                    value = value + land[t, n, at].astype(f32)
                total[n, at] = value
                return 0

            lax.fori_loop(0, OWN // 32, add, 0)
            pltpu.make_async_copy(total.at[n], out, l_sem.at[3 + n]).start()
        first_sums(0)
        last_sums(1)
        last_sums(0)
        for n, out in ((0, du_o), (1, out_o)):
            pltpu.make_async_copy(total.at[n], out, l_sem.at[3 + n]).wait()
        for n in range(9):
            gather_send(n).wait_send()
        for n in range(2):
            for t in range(4):
                near_copy(n, t).wait_send()
                if t:
                    land_copy(n, t).wait_send()
        for m in range(2):
            for dz in range(4):
                one_a(m, dz).wait_send()
                if dz:
                    one_b(m, dz, 0).wait_send()
                    one_b(m, dz, 1).wait_send()
                    two_a(m, dz).wait_send()
            two_b(m).wait_send()


def experts(h, y_all, shares, wl, wd, table, collective):
    dma = pltpu.SemaphoreType.DMA

    def chip_at(i):
        return (lax.rem(lax.axis_index("rep") // 2 + distance(jnp.minimum(i, 3)), 4), 0)

    whole = lambda i: (0, 0)
    once = pl.Buffered(1)

    def slots(size, width):
        return [
            pltpu.VMEM((4, size, width // 2), bf16),
            pltpu.VMEM((6, size, width // 2), bf16),
            pltpu.VMEM((3, size, width // 2), bf16),
            pltpu.VMEM((size, width // 2), bf16),
        ]

    return pl.pallas_call(
        experts_kernel,
        grid=(5,),
        in_specs=[
            HBM,
            pl.BlockSpec((2 * OWN, D), chip_at),
            pl.BlockSpec((2 * OWN, 128), chip_at),
            HBM,
            HBM,
            pl.BlockSpec((128, HID), whole, pipeline_mode=once),
        ],
        out_specs=(
            ANY,
            ANY,
            pl.BlockSpec((192, EXP), whole),
            pl.BlockSpec((2 * FLAT, D), whole),
        ),
        out_shape=(
            jax.ShapeDtypeStruct((OWN, D), f32),
            jax.ShapeDtypeStruct((OWN, D), f32),
            jax.ShapeDtypeStruct((192, EXP), bf16),
            jax.ShapeDtypeStruct((2 * FLAT, D), bf16),
        ),
        scratch_shapes=[
            pltpu.VMEM((4, 2 * OWN, D), bf16),
            pltpu.VMEM((D, EXP), bf16),
            pltpu.VMEM((HID, D), bf16),
            pltpu.VMEM((4, 2 * OWN, EXP), bf16),
            pltpu.VMEM((D, HID), f32),
            pltpu.VMEM((HID, D), f32),
            pltpu.VMEM((4, 2, 2 * OWN, D), bf16),
            pltpu.VMEM((4, 2, OWN, D), bf16),
            pltpu.VMEM((3, 2, OWN, D), bf16),
            pltpu.VMEM((2, OWN, D), f32),
        ]
        + slots(192, EXP)
        + slots(2 * FLAT, D)
        + [
            dma((5,)),
            dma((9,)),
            dma((9,)),
            dma((4, 2)),
            dma((4, 2)),
            dma((4, 2)),
            dma((4, 2)),
            dma((2, 2, 8)),
            dma((2, 2, 8)),
            dma((2, 4)),
            dma((2, 4)),
        ],
        compiler_params=params(collective, 63 * 2**20),
        name="experts",
    )(h, y_all, shares, wl, wd, table)


def choose_units(w_ref, code_ref, out_ref):
    x = lax.axis_index("rep") // 2
    row = lax.broadcasted_iota(jnp.int32, (FF_EXP, HID), 0)
    there = (row // 32) * 1024 + lax.rem(row, 32)
    here = jnp.broadcast_to(code_ref[...], (FF_EXP, HID))
    base = (5 * x) // 2
    for k in range(2):
        for part in range(2):
            total = jnp.zeros((96, HID), f32)
            for i in range(3):
                chosen = there + 32 * (base + i) == here + FLAT * (2 * x + k)
                total = total + jnp.dot(
                    w_ref[i][:, FF_EXP * part : FF_EXP * (part + 1)],
                    jnp.where(chosen, 1.0, 0.0).astype(bf16),
                    preferred_element_type=f32,
                )
            out_ref[k, :, HID * part : HID * (part + 1)] = total.astype(bf16)


def one_step(kernel, arrays, shapes, name):
    return pl.pallas_call(
        kernel,
        in_specs=[VMEM] * len(arrays),
        out_specs=(VMEM,) * len(shapes),
        out_shape=tuple(jax.ShapeDtypeStruct(shape, dtype) for shape, dtype in shapes),
        compiler_params=pltpu.CompilerParams(vmem_limit_bytes=62 * 2**20),
        name=name,
    )(*arrays)


def side_by_side(ref):
    return jnp.concatenate([ref[c] for c in range(CHIPS)], 1)


def finish_kernel(dh_ref, dz_ref, x_ref, g_ref, out_ref):
    stream = x_ref[...].astype(f32)
    inverse = inverse_root(stream)
    out_ref[...] = dz_ref[...] + norm_back(dh_ref[...] * g_ref[...], stream * inverse, inverse)


def adam(weight, old_mean, square, gradient, step_rate, decay_rate):
    values = weight.astype(f32)
    moment = beta_one * old_mean.astype(f32) + (1.0 - beta_one) * gradient
    variance = beta_two * square.astype(f32) + (1.0 - beta_two) * gradient * gradient
    normed_step = (
        moment
        / (1.0 - beta_one**STEP)
        / (jnp.sqrt(variance / (1.0 - beta_two**STEP)) + adam_epsilon)
    )
    return (moment, variance, values - step_rate * (normed_step + decay_rate * values))


def adam_lifting_kernel(w_ref, m_ref, s_ref, g_ref, code_ref, mo_ref, so_ref, wo_ref, dot_ref, grad):
    e = pl.program_id(0)
    first, last = (4 * e) // 5, (4 * e + 3) // 5
    column = lax.broadcasted_iota(jnp.int32, (HID, FF_EXP), 1)
    there = (column // 32) * 1024 + lax.rem(column, 32) + 32 * e
    here = jnp.broadcast_to(code_ref[...], (HID, FF_EXP))
    chosen_first = jnp.where(there == here + FLAT * first, 1.0, 0.0).astype(bf16)
    skip = jnp.where(first == last, 1 << 20, 0)
    chosen_last = jnp.where(there == here + (FLAT * last + skip), 1.0, 0.0).astype(bf16)

    def both(p):
        return jnp.concatenate([g_ref[p][:, :HID], g_ref[p][:, HID:]], 0)

    ordered = jnp.dot(both(first), chosen_first, preferred_element_type=f32) + jnp.dot(
        both(last), chosen_last, preferred_element_type=f32
    )
    grad[:, :FF_EXP] = ordered[:96]
    grad[:, FF_EXP:] = ordered[96:]

    @pl.when(e == 0)
    def _():
        dot_ref[...] = jnp.zeros_like(dot_ref)

    dot = jnp.sum(w_ref[0].astype(f32) * grad[...], 1, keepdims=True)
    dot_ref[...] += jnp.broadcast_to(dot, dot_ref.shape)
    mo_ref[0], so_ref[0], wo_ref[0] = adam(
        w_ref[0], m_ref[0], s_ref[0], grad[...], rate_lifting, weight_decay
    )


def adam_lifting(weight, mean, square, grad, code):
    block = pl.BlockSpec((1, 96, 2 * FF_EXP), lambda e: (e, 0, 0))
    shape = jax.ShapeDtypeStruct(weight.shape, f32)
    return pl.pallas_call(
        adam_lifting_kernel,
        grid=(EXPERTS,),
        in_specs=[
            block,
            block,
            block,
            pl.BlockSpec(grad.shape, lambda e: (0, 0, 0)),
            pl.BlockSpec(code.shape, lambda e: (0, 0)),
        ],
        out_specs=(block, block, block, pl.BlockSpec((96, 128), lambda e: (0, 0))),
        out_shape=(shape, shape, shape, jax.ShapeDtypeStruct((96, 128), f32)),
        scratch_shapes=[pltpu.VMEM((96, 2 * FF_EXP), f32)],
        compiler_params=pltpu.CompilerParams(vmem_limit_bytes=62 * 2**20),
        name="adam_lifting",
    )(weight, mean, square, grad, code)


def adam_inward_kernel(w_ref, m_ref, s_ref, g_ref, mo_ref, so_ref, wo_ref, dot_ref):
    parts = [g_ref[c].astype(f32) for c in range(CHIPS)]
    grad = jnp.concatenate(
        [p[:, :192] for p in parts] + [p[:, 192:256] for p in parts] + [p[:, 256:] for p in parts], 1
    )
    dot = jnp.sum(w_ref[...].astype(f32) * grad, 1, keepdims=True)
    dot_ref[...] = jnp.broadcast_to(dot, dot_ref.shape)
    mo_ref[...], so_ref[...], wo_ref[...] = adam(
        w_ref[...], m_ref[...], s_ref[...], grad, rate_inward, weight_decay
    )


def adam_inward(weight, mean, square, grad):
    shape = jax.ShapeDtypeStruct(weight.shape, f32)
    return pl.pallas_call(
        adam_inward_kernel,
        in_specs=[VMEM] * 4,
        out_specs=(VMEM,) * 4,
        out_shape=(shape, shape, shape, jax.ShapeDtypeStruct((96, 128), f32)),
        compiler_params=pltpu.CompilerParams(vmem_limit_bytes=62 * 2**20),
        name="adam_inward",
    )(weight, mean, square, grad)


def tables():
    half = HEAD // 2
    frequency = np.float32(10000.0) ** (-(2.0 * np.arange(half, dtype=np.float32)) / HEAD)
    phases = np.arange(SEQ, dtype=np.float32)[:, None] * frequency[None, :].astype(np.float32)
    cos, sin = np.cos(phases).astype(np.float32), np.sin(phases).astype(np.float32)
    return (
        np.concatenate([cos, cos, cos, cos], 1),
        np.concatenate([-sin, sin, -sin, sin], 1),
    )


def unit_codes():
    unit = np.arange(HID, dtype=np.int32)
    return (unit // FLAT) * 1024 + unit % FLAT


def inverse_root(stream):
    return lax.rsqrt(jnp.mean(stream * stream, -1, keepdims=True) + norm_epsilon)


def norm_back(scaled, unit, inverse):
    return inverse * (scaled - unit * jnp.mean(scaled * unit, -1, keepdims=True))


def per_device(
    layer_input,
    grad_output,
    routes,
    route_logits,
    norm_gains,
    inward,
    outward,
    lifting,
    lowering,
    mean_gains,
    mean_inward,
    mean_outward,
    mean_lifting,
    mean_lowering,
    square_gains,
    square_inward,
    square_outward,
    square_lifting,
    square_lowering,
):
    gains = norm_gains.astype(f32)
    cos, sin = (jnp.asarray(t) for t in tables())

    lifting_rows = lifting.transpose(1, 0, 2)
    codes = jnp.asarray(unit_codes())
    x = lax.axis_index("rep") // 2
    position = 2 * x + lax.rem(lax.axis_index("shard"), 2)
    low_rows = lowering.transpose(1, 0, 2).reshape(EXPERTS * 32, D)
    low_rows = lax.dynamic_slice(low_rows, (2 * FLAT * x, 0), (2 * FLAT, D)).reshape(2, FLAT, D)
    low_rows = jnp.pad(low_rows, ((0, 0), (0, FLAT_PAD - FLAT), (0, 0)))
    expert = (FLAT * position + lax.rem(jnp.arange(HID), FLAT)) // 32
    row = jnp.arange(128)[:, None]
    share_table = ((row == expert) | (row == expert + 16)).astype(bf16)

    x_all, head_weight, y_all, shares, by_unit = start(
        layer_input, grad_output, inward, norm_gains, routes, route_logits, lifting_rows, codes[None, :], 2
    )
    head_weight = head_weight.reshape(D, 384)
    gain_rows = head_weight[:, 192:194].T.astype(f32)
    gain_one, gain_two = gain_rows[0:1], gain_rows[1:2]
    by_half = outward.reshape(96, 2, D // 2).transpose(1, 0, 2)

    q, k, v, u_one, attended, lse, unit_weight, down_weight, half = attend(
        x_all, head_weight, gain_one, cos, sin, by_unit, low_rows, by_half, 1
    )
    unit_weight = unit_weight.reshape(D, EXP)
    mixed, low_two, own_attended, outward_all = home(
        attended, half.reshape(D, D // 2), layer_input, gain_two, 3
    )
    late_inward, low_two = lax.optimization_barrier((inward, low_two))
    inward_all = lax.all_gather(late_inward, "shard", axis=0, tiled=True)
    down_weight = down_weight[:, :FLAT].reshape(HID, D)
    du, expert_out, lift_sum, down_sum = experts(
        low_two, y_all, shares, unit_weight, down_weight, share_table, 5
    )
    layer_output = mixed + expert_out
    down_sum = jnp.pad(down_sum.reshape(2, FLAT, D), ((0, 0), (0, FLAT_PAD - FLAT), (0, 0)))
    grad_mixed, outward_part, head_grads, lift_pair, down_pair = grads_away(
        du, mixed, grad_output, gain_two, outward_all, own_attended,
        lift_sum.reshape(2, 96, EXP), down_sum, 6,
    )
    dq, dkv, inward_part, outward_own, lift_got, down_got = attend_back(
        q, k, v, head_grads, attended, lse, cos, sin, u_one, outward_part, lift_pair, down_pair, 8
    )
    dh, inward_sum, outward_sum = tail(
        dq, dkv.reshape(SHARDS, OWN, 128), inward_part, outward_own, inward_all, 7
    )
    (input_grad,) = one_step(
        finish_kernel, (dh, grad_mixed, layer_input, gain_one), (((OWN, D), f32),), "finish"
    )
    outward_grad = outward_sum.astype(f32)
    down_grad = (
        down_got[:, :FLAT].reshape(EXPERTS, 32, D).transpose(1, 0, 2).astype(f32)
    )

    new_lifting = adam_lifting(
        lifting_rows,
        mean_lifting.transpose(1, 0, 2),
        square_lifting.transpose(1, 0, 2),
        lift_got,
        codes[:, None],
    )
    lifting_dot = new_lifting[3]
    new_lifting = tuple(t.transpose(1, 0, 2) for t in new_lifting[:3])
    new_inward = adam_inward(inward, mean_inward, square_inward, inward_sum)
    gain_grad = jnp.stack([new_inward[3][:, 0], lifting_dot[:, 0]]) / gains
    new_gains = adam(norm_gains, mean_gains, square_gains, gain_grad, rate_gains, 0.0)
    new_outward = adam(
        outward, mean_outward, square_outward, outward_grad, rate_outward, weight_decay
    )
    new_lowering = adam(
        lowering, mean_lowering, square_lowering, down_grad, rate_lowering, weight_decay
    )
    return (
        layer_output,
        input_grad,
        new_gains[0],
        new_inward[0],
        new_outward[0],
        new_lifting[0],
        new_lowering[0],
        new_gains[1],
        new_inward[1],
        new_outward[1],
        new_lifting[1],
        new_lowering[1],
        new_gains[2],
        new_inward[2],
        new_outward[2],
        new_lifting[2],
        new_lowering[2],
    )


def solution(mesh):
    tokens = P(("rep", "shard"), None)
    gains, flat, deep = P(None, "shard"), P("shard", None), P("shard", None, None)
    weights = (gains, flat, flat, deep, deep)
    return jax.shard_map(
        per_device,
        mesh=mesh,
        in_specs=(tokens,) * 4 + weights * 3,
        out_specs=(tokens,) * 2 + weights * 3,
        check_vma=False,
    )
```

```python
import functools

import jax
import jax.numpy as jnp
import numpy as np
from jax import lax
from jax.experimental import pallas as pl
from jax.experimental.pallas import tpu as pltpu
from jax.sharding import PartitionSpec as P

HEADS = 24
KV_HEADS = 8
HEAD = 64
GROUP = HEADS // KV_HEADS
FF_EXP = 512
EXPERTS = 10
STEP = 10

norm_epsilon = 1e-06
beta_one = 0.9
beta_two = 0.95
adam_epsilon = 1e-08
weight_decay = 0.1
rate_gains = 0.5
rate_inward = 0.05
rate_outward = 0.3
rate_lifting = 0.05
rate_lowering = 0.3

SHARDS = 16
CHIPS = 8
REPS = 8
OWN = 192
SEQ = OWN * SHARDS
D = 1536
PEERS = 8
FLAT = 40
FLAT_PAD = 48
HID = SHARDS * FLAT
EXP = 2 * HID
BLOCKS = 8
ROWS = GROUP * OWN
KEYS = 2 * OWN

MESH = pl.DeviceIdType.MESH
bf16 = jnp.bfloat16
f32 = jnp.float32


def place():
    rep = lax.axis_index("rep")
    shard = lax.axis_index("shard")
    return rep, shard


def greet(devices):
    barrier = pltpu.get_barrier_semaphore()
    for device in devices:
        pl.semaphore_signal(barrier, inc=1, device_id=device, device_id_type=MESH)
    pl.semaphore_wait(barrier, len(devices))


def send(src, dst, send_sem, recv_sem, device):
    copy = pltpu.make_async_remote_copy(
        src_ref=src,
        dst_ref=dst,
        send_sem=send_sem,
        recv_sem=recv_sem,
        device_id=device,
        device_id_type=MESH,
    )
    copy.start()
    return copy


def params(collective, vmem=None):
    return pltpu.CompilerParams(
        collective_id=collective, has_side_effects=True, vmem_limit_bytes=vmem
    )


ANY = pl.BlockSpec(memory_space=pl.ANY)
VMEM = pl.BlockSpec(memory_space=pltpu.VMEM)
HBM = pl.BlockSpec(memory_space=pltpu.HBM)


def along_x(rep, dx):
    return 2 * lax.rem(rep // 2 + dx, 4) + lax.rem(rep, 2)


def landed_on(ref, recv_sem, any_send_sem, device):
    pltpu.make_async_remote_copy(
        src_ref=ref,
        dst_ref=ref,
        send_sem=any_send_sem,
        recv_sem=recv_sem,
        device_id=device,
        device_id_type=MESH,
    ).wait_recv()


def x_gather(x_ref, o_ref, local_sem, send_sem, recv_sem):
    rep, shard = place()
    core = lax.rem(shard, 2)
    sib = shard + 1 - 2 * core
    half = x_ref.shape[0] // 2
    top, bottom = pl.ds(0, half), pl.ds(half, half)
    up, down, far = (along_x(rep, d) for d in (1, 3, 2))

    def block(r, other=False):
        return 2 * (r // 2) + (1 - core if other else core)

    mine = block(rep)
    own = pltpu.make_async_copy(x_ref, o_ref.at[mine], local_sem)
    sent = []

    def put(ref, dst, slot, device):
        sent.append(send(ref, dst, send_sem.at[len(sent)], recv_sem.at[slot], device))

    def arrived(ref, slot):
        landed_on(ref, recv_sem.at[slot], send_sem.at[0], (rep, sib))

    def start():
        own.start()
        put(x_ref, o_ref.at[mine], 0, (up, shard))
        put(x_ref, o_ref.at[mine], 1, (down, shard))
        put(x_ref, o_ref.at[mine], 4, (rep, sib))

    def relay():
        ref = o_ref.at[block(down)]
        arrived(ref, 0)
        put(o_ref.at[block(down), top], o_ref.at[block(down), top], 2, (up, shard))
        put(ref, ref, 5, (rep, sib))
        ref = o_ref.at[block(up)]
        arrived(ref, 1)
        put(o_ref.at[block(up), bottom], o_ref.at[block(up), bottom], 3, (down, shard))
        put(ref, ref, 6, (rep, sib))

    def relay_far():
        for slot, part in ((2, top), (3, bottom)):
            ref = o_ref.at[block(far), part]
            arrived(ref, slot)
            put(ref, ref, slot + 5, (rep, sib))

    def finish():
        arrived(o_ref.at[block(rep, True)], 4)
        arrived(o_ref.at[block(down, True)], 5)
        arrived(o_ref.at[block(up, True)], 6)
        arrived(o_ref.at[block(far, True), top], 7)
        arrived(o_ref.at[block(far, True), bottom], 8)
        for copy in sent:
            copy.wait_send()
        own.wait()

    return start, relay, relay_far, finish


def ring_spread(x_ref, o_ref, split, local_sem, send_sem, recv_sem):
    rep, shard = place()
    core = lax.rem(shard, 2)
    chip = shard // 2
    y = lax.rem(chip, 2)
    sib = shard + 1 - 2 * core
    pair = chip + 1 - 2 * y
    up, down, far = (lax.rem(chip + d, 8) for d in (2, 6, 4))
    own = pltpu.make_async_copy(x_ref.at[core], o_ref.at[shard], local_sem)
    first, last = pl.ds(0, split), pl.ds(split, x_ref.shape[1] - split)

    mate = rep + 1 - 2 * lax.rem(rep, 2)

    def copy(src, dst, slot, chip_to=None):
        across = slot in (18, 19, 20, 21, 22)
        return pltpu.make_async_remote_copy(
            src_ref=src,
            dst_ref=dst,
            send_sem=send_sem.at[slot],
            recv_sem=recv_sem.at[slot],
            device_id=(mate if across else rep, sib if chip_to is None else 2 * chip_to + core),
            device_id_type=MESH,
        )

    def push_pair(c, rows, slot, across):
        push(block(c, rows, 0), slot, pair)
        push(block(c, rows, 1), across, pair)

    def other(c):
        return c + 1 - 2 * y

    def block(c, rows, part=None):
        if part is None:
            return o_ref.at[pl.ds(2 * c, 2), rows]
        return o_ref.at[2 * c + part, rows]

    def push(ref, slot, to):
        copy(ref, ref, slot, to).start()

    def arrived(ref, slot):
        copy(ref, ref, slot, pair).wait_recv()

    def start():
        own.start()
        copy(x_ref.at[1 - core], o_ref.at[shard], 0).start()

    def one():
        copy(o_ref.at[sib], o_ref.at[sib], 0).wait_recv()
        own.wait()
        push_pair(chip, first, 1, 19)
        push(block(chip, last), 10, up)
        push(block(chip, last), 12, down)
        push(block(chip, first), 2, up)
        push(block(chip, first), 6, down)
        push_pair(chip, last, 14, 20)

    def two():
        arrived(block(pair, first, 0), 1)
        arrived(block(pair, first, 1), 19)
        push(block(pair, first), 3, up)
        push(block(pair, first), 7, down)
        arrived(block(down, last), 10)
        push_pair(down, last, 15, 21)
        push(block(down, last, 0), 11, up)
        arrived(block(up, last), 12)
        push_pair(up, last, 16, 22)
        push(block(up, last, 1), 13, down)

    def three():
        arrived(block(down, first), 2)
        push(block(down, first, 0), 4, up)
        arrived(block(up, first), 6)
        push(block(up, first, 1), 8, down)
        arrived(block(far, last, 0), 11)
        push(block(far, last, 0), 17, pair)
        arrived(block(far, last, 1), 13)
        push(block(far, last, 1), 18, pair)
        arrived(block(other(down), first), 3)
        push(block(other(down), first, 0), 5, up)
        arrived(block(other(up), first), 7)
        push(block(other(up), first, 1), 9, down)

    def finish():
        arrived(block(far, first, 0), 4)
        arrived(block(far, first, 1), 8)
        arrived(block(other(far), first, 0), 5)
        arrived(block(other(far), first, 1), 9)
        for c, slot, across in ((pair, 14, 20), (other(down), 15, 21), (other(up), 16, 22)):
            arrived(block(c, last, 0), slot)
            arrived(block(c, last, 1), across)
        arrived(block(other(far), last, 0), 17)
        arrived(block(other(far), last, 1), 18)
        copy(x_ref.at[1 - core], o_ref.at[shard], 0).wait_send()
        for slot in (2, 3, 6, 7):
            copy(block(chip, first), block(chip, first), slot, pair).wait_send()
        for slot in (1, 4, 5, 8, 9, 19):
            copy(block(chip, first, 0), block(chip, first, 0), slot, pair).wait_send()
        for slot in (10, 12):
            copy(block(chip, last), block(chip, last), slot, pair).wait_send()
        for slot in (11, 13, 14, 15, 16, 17, 18, 20, 21, 22):
            copy(block(chip, last, 0), block(chip, last, 0), slot, pair).wait_send()

    return start, one, two, three, finish


START_SPLIT = 896


def start_kernel(
    x_ref, t_ref, in_hbm, gain_hbm, routes_hbm, logits_hbm, lift_hbm, code_hbm,
    o_ref, p_ref, g_ref, share_o, unit_ref,
    in_ref, gain_ref, routes_ref, logits_ref, lift_ref, code_ref, fetch_sem,
    w_ref, share_ref, local_sem, send_sem, recv_sem, s_part, r_part, s_x, r_x, s_y, r_y,
):
    with_parts = True
    rep, shard = place()
    half = x_ref.shape[0] // 2
    core = lax.rem(shard, 2)
    chip = shard // 2
    y = lax.rem(chip, 2)
    sib = shard + 1 - 2 * core
    pair = shard + 2 - 4 * y
    up = lax.rem(shard + 4, 16)
    down = lax.rem(shard + 12, 16)
    far = lax.rem(shard + 8, 16)
    first, last = pl.ds(0, START_SPLIT), pl.ds(START_SPLIT, D - START_SPLIT)
    rows, top, bottom = pl.ds(0, 2 * half), pl.ds(0, half), pl.ds(half, half)
    peers = [2 * lax.rem(chip + i, 8) + core for i in range(1, 8)]

    def other(block):
        return block + 2 - 4 * y

    greet(
        [(rep, sib)]
        + [(rep, p) for p in peers]
        + [(along_x(rep, 1), shard), (along_x(rep, 3), shard)]
    )
    fetches = [
        pltpu.make_async_copy(src, dst, fetch_sem.at[n])
        for n, (src, dst) in enumerate(
            (
                (in_hbm, in_ref),
                (gain_hbm, gain_ref),
                (routes_hbm, routes_ref),
                (logits_hbm, logits_ref),
                (lift_hbm.at[pl.ds((5 * (rep // 2)) // 2, 3)], lift_ref),
                (code_hbm, code_ref),
            )
        )
    ]
    for fetch in fetches:
        fetch.start()
    x_steps = x_gather(t_ref, g_ref, local_sem.at[2], s_x, r_x)
    y_steps = x_gather(share_ref, share_o, local_sem.at[3], s_y, r_y)
    own = pltpu.make_async_copy(x_ref, o_ref.at[shard], local_sem.at[0])
    own.start()
    sent = []

    def put(src, dst, slot, device):
        sent.append(send(src, dst, send_sem.at[len(sent)], recv_sem.at[slot], (rep, device)))

    def landed(ref, sem):
        landed_on(ref, sem, send_sem.at[0], (rep, sib))

    arrivals = {
        0: (pair, first, rows, ((2, up, rows), (6, down, rows))),
        9: (down, last, rows, ((14, pair, rows), (10, up, top))),
        1: (down, first, rows, ((3, up, top),)),
        11: (up, last, rows, ((15, pair, rows), (12, down, bottom))),
        5: (up, first, rows, ((7, down, bottom),)),
        13: (pair, last, rows, ()),
        2: (other(down), first, rows, ((4, up, top),)),
        6: (other(up), first, rows, ((8, down, bottom),)),
        10: (far, last, top, ((16, pair, top),)),
        12: (far, last, bottom, ((17, pair, bottom),)),
        3: (far, first, top, ()),
        7: (far, first, bottom, ()),
        14: (other(down), last, rows, ()),
        15: (other(up), last, rows, ()),
        4: (other(far), first, top, ()),
        8: (other(far), first, bottom, ()),
        16: (other(far), last, top, ()),
        17: (other(far), last, bottom, ()),
    }

    def arrive(slots):
        for slot in slots:
            block, columns, part, onward = arrivals[slot]
            ref = o_ref.at[block, part, columns]
            landed(ref, recv_sem.at[slot])
            for to_slot, device, rows_on in onward:
                ref_on = o_ref.at[block, rows_on, columns]
                put(ref_on, ref_on, to_slot, device)
            put(ref, ref, 19 + slot, sib)

    for columns, slots in ((first, (0, 1, 5)), (last, (13, 9, 11))):
        for slot, device in zip(slots, (pair, up, down)):
            put(x_ref.at[:, columns], o_ref.at[shard, :, columns], slot, device)
    put(x_ref, o_ref.at[shard], 18, sib)
    x_steps[0]()

    for fetch in fetches:
        fetch.wait()
    row, column = (lax.broadcasted_iota(jnp.int32, (96, 96), d) for d in (0, 1))
    gains = contract(jnp.where(row == column, 1.0, 0.0).astype(bf16), gain_ref[...], ((1,), (1,)))
    gains = jnp.concatenate([gains.astype(bf16), jnp.zeros((96, HEAD - 2), bf16)], 1)
    for c in range(CHIPS):
        w_ref[c] = jnp.concatenate(
            [
                in_ref[:, 192 * c : 192 * (c + 1)],
                gains,
                in_ref[:, 1536 + HEAD * c : 1536 + HEAD * (c + 1)],
                in_ref[:, 2048 + HEAD * c : 2048 + HEAD * (c + 1)],
            ],
            1,
        )
    parts = []
    if with_parts:
        mine = pltpu.make_async_copy(w_ref.at[chip], p_ref.at[shard], local_sem.at[1])
        mine.start()
        parts.append(
            send(w_ref.at[chip], p_ref.at[shard], s_part.at[0], r_part.at[0], (rep, sib))
        )
        for i in range(1, 8):
            c = lax.rem(chip + i, 8)
            parts.append(
                send(
                    w_ref.at[c], p_ref.at[shard], s_part.at[i], r_part.at[i], (rep, 2 * c + core)
                )
            )
    logits = logits_ref[...]
    gates = jnp.exp(logits - jnp.max(logits, 0, keepdims=True))
    gates = gates / jnp.sum(gates, 0, keepdims=True)
    ones = [
        jnp.sum(jnp.where(routes_ref[...] == e, gates, 0.0), 0, keepdims=True)
        for e in range(EXPERTS)
    ]
    shares = jnp.concatenate(ones + [jnp.zeros((128 - EXPERTS, OWN), f32)], 0).T
    lane = lax.broadcasted_iota(jnp.int32, (OWN, 128), 1)
    high = shares.astype(bf16)
    rest = pltpu.roll(shares - high.astype(f32), 16, 1)
    share_ref[...] = jnp.where(lane < 16, high, rest.astype(bf16))
    y_steps[0]()
    choose_units(lift_ref, code_ref, unit_ref)
    arrive((0, 9, 1, 11, 5, 13))
    x_steps[1]()
    y_steps[1]()
    arrive((2, 6, 10, 12))
    x_steps[2]()
    y_steps[2]()
    if with_parts:
        for i in range(1, 8):
            block = 2 * lax.rem(chip + 8 - i, 8) + core
            landed(p_ref.at[block], r_part.at[i])
            parts.append(
                send(
                    p_ref.at[block], p_ref.at[block], s_part.at[7 + i], r_part.at[7 + i], (rep, sib)
                )
            )
    arrive((3, 7, 14, 15, 4, 8, 16, 17))

    def twin(block):
        return block + 1 - 2 * core

    if with_parts:
        landed(p_ref.at[sib], r_part.at[0])
        for i in range(1, 8):
            landed(p_ref.at[twin(2 * lax.rem(chip + 8 - i, 8) + core)], r_part.at[7 + i])
        mine.wait()
    landed(o_ref.at[sib], recv_sem.at[18])
    for slot, (block, columns, part, _) in arrivals.items():
        landed(o_ref.at[twin(block), part, columns], recv_sem.at[19 + slot])
    x_steps[3]()
    y_steps[3]()
    for copy in sent + parts:
        copy.wait_send()
    own.wait()


def start(x, tokens, inward, gains, routes, logits, lifting, codes, collective):
    rows, columns = x.shape
    dma = pltpu.SemaphoreType.DMA
    gathered, parts, tokens, shares, units = pl.pallas_call(
        start_kernel,
        out_shape=(
            jax.ShapeDtypeStruct((SHARDS, rows, columns), bf16),
            jax.ShapeDtypeStruct((SHARDS, 96, 384), bf16),
            jax.ShapeDtypeStruct((PEERS, rows, columns), bf16),
            jax.ShapeDtypeStruct((PEERS, rows, 128), bf16),
            jax.ShapeDtypeStruct((2, 96, EXP), bf16),
        ),
        in_specs=[HBM] * 8,
        out_specs=(ANY,) * 4 + (VMEM,),
        scratch_shapes=[
            pltpu.VMEM(inward.shape, bf16),
            pltpu.VMEM(gains.shape, bf16),
            pltpu.VMEM(routes.shape, jnp.int32),
            pltpu.VMEM(logits.shape, f32),
            pltpu.VMEM((3,) + lifting.shape[1:], bf16),
            pltpu.VMEM(codes.shape, jnp.int32),
            dma((6,)),
            pltpu.VMEM((CHIPS, 96, 384), bf16),
            pltpu.VMEM((rows, 128), bf16),
            dma((4,)),
            dma((37,)),
            dma((37,)),
            dma((15,)),
            dma((15,)),
        ]
        + [dma((9,))] * 4,
        compiler_params=params(collective, 62 * 2**20),
        name="start",
    )(x, tokens, inward, gains, routes, logits, lifting, codes)
    return (
        gathered.reshape(SHARDS * rows, columns),
        parts,
        tokens.reshape(PEERS * rows, columns),
        shares.reshape(PEERS * rows, 128),
        units,
    )


def home_kernel(
    x_ref, half_ref, rows_ref, in_ref, gain_ref,
    mixed_ref, low_ref, down_ref, o_ref, w_ref,
    got, halves, apart, local_sem, s_x, r_x, s_w, r_w,
):
    rep, shard = place()
    core = lax.rem(shard, 2)
    chip = shard // 2
    sib = shard + 1 - 2 * core
    own_half = pltpu.make_async_copy(half_ref, halves.at[core], local_sem.at[0])
    own_half.start()
    fetch = pltpu.make_async_copy(rows_ref, apart, local_sem.at[4])
    fetch.start()
    holder = lax.rem(core + chip, 2)
    greet([(rep, 2 * lax.rem(chip + i, 8) + holder) for i in range(1, 8)] + [(rep, sib)])
    sent = [send(half_ref, halves.at[core], s_w, r_w, (rep, sib))]
    for i in range(1, 8):
        c = lax.rem(chip + i, 8)
        sent.append(
            send(
                x_ref.at[c], got.at[chip], s_x.at[i], r_x.at[i], (rep, 2 * c + lax.rem(c + core, 2))
            )
        )
    same = lax.rem(chip, 2) == 0

    @pl.when(same)
    def _():
        copy = pltpu.make_async_copy(x_ref.at[chip], got.at[chip], local_sem.at[1])
        copy.start()
        copy.wait()

    @pl.when(jnp.logical_not(same))
    def _():
        send(x_ref.at[chip], got.at[chip], s_x.at[0], r_x.at[0], (rep, sib)).wait_send()
        landed_on(got.at[chip], r_x.at[0], s_x.at[0], (rep, sib))

    fetch.wait()
    down_ref[...] = jnp.concatenate([apart[d][:FLAT] for d in range(SHARDS)], 0)
    own_half.wait()
    landed_on(halves.at[1 - core], r_w, s_w, (rep, sib))
    keeps = [pltpu.make_async_copy(halves, w_ref, local_sem.at[2])]
    keeps[0].start()
    for i in range(1, 8):
        landed_on(got.at[lax.rem(chip + 8 - i, 8)], r_x.at[i], s_x.at[0], (rep, sib))
    keeps.append(pltpu.make_async_copy(got, o_ref, local_sem.at[3]))
    keeps[1].start()
    rows = side_by_side(got)
    mixed = in_ref[...].astype(f32) + jnp.concatenate(
        [jnp.dot(rows, halves[k], preferred_element_type=f32) for k in range(2)], 1
    )
    mixed_ref[...] = mixed
    low_ref[...] = (mixed * inverse_root(mixed) * gain_ref[...]).astype(bf16)
    for copy in sent:
        copy.wait_send()
    for keep in keeps:
        keep.wait()


def home(attended, half, rows, x, gain, collective):
    dma = pltpu.SemaphoreType.DMA
    halves = (2, D, D // 2)
    return pl.pallas_call(
        home_kernel,
        out_shape=(
            jax.ShapeDtypeStruct((OWN, D), f32),
            jax.ShapeDtypeStruct((OWN, D), bf16),
            jax.ShapeDtypeStruct((HID, D), bf16),
            jax.ShapeDtypeStruct(attended.shape, bf16),
            jax.ShapeDtypeStruct(halves, bf16),
        ),
        in_specs=[HBM, HBM, HBM, VMEM, VMEM],
        out_specs=(VMEM, VMEM, VMEM, ANY, ANY),
        scratch_shapes=[
            pltpu.VMEM(attended.shape, bf16),
            pltpu.VMEM(halves, bf16),
            pltpu.VMEM(rows.shape, bf16),
            dma((5,)),
            dma((8,)),
            dma((8,)),
            dma,
            dma,
        ],
        compiler_params=params(collective, 62 * 2**20),
        name="attended_home",
    )(attended, half, rows, x, gain)


def away_kernel(
    du_ref, mixed_ref, y_ref, gain_ref, w_ref, a_ref, lift_ref, down_ref,
    dz_ref, part_ref, o_ref, lift_o, down_o,
    x_ref, lift_own, lift_land, down_own, down_land,
    local_sem, s_x, r_x, s_mate, r_mate, s_sib, r_sib,
):
    rep, shard = place()
    core = lax.rem(shard, 2)
    chip = shard // 2
    sib = shard + 1 - 2 * core
    mate = rep + 1 - 2 * lax.rem(rep, 2)
    greet(
        [(rep, 2 * c + lax.rem(c + core, 2)) for c in (lax.rem(chip + i, 8) for i in range(1, 8))]
        + [(rep, sib), (mate, shard)]
    )
    sent = []
    mates, loads = [], []
    for n, (src, own, land) in enumerate(
        ((lift_ref, lift_own, lift_land), (down_ref, down_own, down_land))
    ):
        mates.append(send(src, land, s_mate.at[n], r_mate.at[n], (mate, shard)))
        load = pltpu.make_async_copy(src, own, local_sem.at[n])
        load.start()
        loads.append(load)

    mixed = mixed_ref[...]
    inverse = inverse_root(mixed)
    dz = y_ref[...].astype(f32) + norm_back(du_ref[...] * gain_ref[...], mixed * inverse, inverse)
    dz_ref[...] = dz
    low = dz.astype(bf16)
    back = contract(low[:, : D // 2], w_ref[0], ((1,), (1,)))
    back = (back + contract(low[:, D // 2 :], w_ref[1], ((1,), (1,)))).astype(bf16)
    for c in range(CHIPS):
        x_ref[c] = back[:, c * 192 : (c + 1) * 192]
    for i in range(1, 8):
        c = lax.rem(chip + i, 8)
        sent.append(
            send(
                x_ref.at[c], o_ref.at[chip], s_x.at[i], r_x.at[i],
                (rep, 2 * c + lax.rem(core + chip, 2)),
            )
        )
    part = contract(side_by_side(a_ref), low, ((0,), (0,))).astype(bf16)
    for s in range(SHARDS):
        part_ref[s] = part[s * 96 : (s + 1) * 96]
    same = lax.rem(chip, 2) == 0

    @pl.when(same)
    def _():
        copy = pltpu.make_async_copy(x_ref.at[chip], o_ref.at[chip], local_sem.at[2])
        copy.start()
        copy.wait()

    @pl.when(jnp.logical_not(same))
    def _():
        send(x_ref.at[chip], o_ref.at[chip], s_x.at[0], r_x.at[0], (rep, sib)).wait_send()
        landed_on(o_ref.at[chip], r_x.at[0], s_x.at[0], (rep, sib))

    keeps, halves = [], []
    for n, (own, land, out) in enumerate(
        ((lift_own, lift_land, lift_o), (down_own, down_land, down_o))
    ):
        loads[n].wait()
        mates[n].wait_recv()
        for k in range(2):

            def add(t, _, own=own, land=land, k=k):
                at = pl.ds(pl.multiple_of(t * 16, 16), 16)
                own[k, at] = (own[k, at].astype(f32) + land[k, at].astype(f32)).astype(bf16)
                return 0

            lax.fori_loop(0, own.shape[1] // 16, add, 0)
        halves.append(
            send(own.at[1 - core], out.at[core], s_sib.at[n], r_sib.at[n], (rep, sib))
        )
        keep = pltpu.make_async_copy(own.at[core], out.at[core], local_sem.at[3 + n])
        keep.start()
        keeps.append(keep)
    for i in range(1, 8):
        landed_on(o_ref.at[lax.rem(chip + 8 - i, 8)], r_x.at[i], s_x.at[0], (rep, sib))
    for n, out in enumerate((lift_o, down_o)):
        landed_on(out.at[1 - core], r_sib.at[n], s_x.at[0], (rep, sib))
        keeps[n].wait()
    for copy in sent + mates + halves:
        copy.wait_send()


def grads_away(du, mixed, y, gain, outward_all, attended, lift, down, collective):
    dma = pltpu.SemaphoreType.DMA
    heads = (CHIPS, OWN, 192)
    return pl.pallas_call(
        away_kernel,
        out_shape=(
            jax.ShapeDtypeStruct((OWN, D), f32),
            jax.ShapeDtypeStruct((SHARDS, 96, D), bf16),
            jax.ShapeDtypeStruct(heads, bf16),
            jax.ShapeDtypeStruct(lift.shape, bf16),
            jax.ShapeDtypeStruct(down.shape, bf16),
        ),
        in_specs=[VMEM] * 6 + [ANY] * 2,
        out_specs=(VMEM, VMEM, ANY, ANY, ANY),
        scratch_shapes=[
            pltpu.VMEM(heads, bf16),
            pltpu.VMEM(lift.shape, bf16),
            pltpu.VMEM(lift.shape, bf16),
            pltpu.VMEM(down.shape, bf16),
            pltpu.VMEM(down.shape, bf16),
            dma((5,)),
            dma((8,)),
            dma((8,)),
        ]
        + [dma((2,))] * 4,
        compiler_params=params(collective, 62 * 2**20),
        name="grads_away",
    )(du, mixed, y, gain, outward_all, attended, lift, down)


PART = (48, 384)


def part_of(r):
    rows = pl.ds(pl.multiple_of((r // 4) * PART[0], PART[0]), PART[0])
    return rows, pl.ds(pl.multiple_of(lax.rem(r, 4) * PART[1], PART[1]), PART[1])


def tail_kernel(
    dq_ref, dkv_ref, in_ref, out_ref, w_hbm,
    dh_ref, in_sum, out_sum,
    w_ref, held_k, near_k, held_i, near_i, got_q, got_k, land_i, land_o, own_o, sum_i, sum_o,
    l_sem, s_q, r_q, s_nk, r_nk, s_ni, r_ni, s_k, r_k, s_ri, r_ri, s_ro, r_ro, s_gi, r_gi, s_go, r_go,
):
    rep, shard = place()
    core = lax.rem(shard, 2)
    chip = shard // 2
    sib = shard + 1 - 2 * core
    fetch = pltpu.make_async_copy(w_hbm, w_ref, l_sem.at[20])
    fetch.start()
    own = pltpu.make_async_copy(out_ref.at[part_of(rep)], own_o, l_sem.at[16])
    own.start()
    loads = {}
    for c in range(8):
        for name, src, held, base in (("i", in_ref, held_i, 0), ("k", dkv_ref, held_k, 8)):
            loads[name, c] = pltpu.make_async_copy(
                src.at[2 * c + core], held.at[c], l_sem.at[base + c]
            )
            loads[name, c].start()
    alone = rep == chip
    barrier = pltpu.get_barrier_semaphore()
    for device in [(rep, lax.rem(shard + i, 16)) for i in range(1, 16)] + [
        (lax.rem(rep + i, 8), shard) for i in range(1, 8)
    ]:
        pl.semaphore_signal(barrier, inc=1, device_id=device, device_id_type=MESH)
    for i in range(8):
        device = (chip, 2 * lax.rem(chip + i, 8) + core)
        if i:
            pl.semaphore_signal(barrier, inc=1, device_id=device, device_id_type=MESH)
        else:

            @pl.when(jnp.logical_not(alone))
            def _(device=device):
                pl.semaphore_signal(barrier, inc=1, device_id=device, device_id_type=MESH)

    pl.semaphore_wait(barrier, jnp.where(alone, 29, 30))

    sent = []

    def put(src, dst, s_sem, r_sem, device):
        copy = send(src, dst, s_sem, r_sem, device)
        sent.append(copy)
        return copy

    def landed(ref, sem):
        landed_on(ref, sem, s_q.at[0], (rep, sib))

    nears = {}
    for name, src, near, s_n, r_n in (
        ("i", in_ref, near_i, s_ni, r_ni),
        ("k", dkv_ref, near_k, s_nk, r_nk),
    ):
        for c in range(8):
            nears[name, c] = put(
                src.at[2 * c + 1 - core], near.at[c], s_n.at[c], r_n.at[c], (rep, sib)
            )
    for i in range(1, 8):
        to = lax.rem(rep + i, 8)
        put(out_ref.at[part_of(to)], land_o.at[i - 1], s_ro.at[i], r_ro.at[i], (to, shard))

    def add_near(name, held, near, rows):
        for c in range(8):
            nears[name, c].wait_recv()
            loads[name, c].wait()

        def add(t, _):
            at = pl.ds(pl.multiple_of(t * 32, 32), 32)
            for c in range(8):
                held[c, at] = (held[c, at].astype(f32) + near[c, at].astype(f32)).astype(bf16)
            return 0

        lax.fori_loop(0, rows // 32, add, 0)

    add_near("i", held_i, near_i, 96)
    for i in range(1, 8):
        to = lax.rem(rep + i, 8)
        put(held_i.at[to], land_i.at[i - 1], s_ri.at[i], r_ri.at[i], (to, shard))
    add_near("k", held_k, near_k, OWN)
    for i in range(1, 8):
        c = lax.rem(chip + i, 8)
        put(held_k.at[c], got_k.at[chip], s_k.at[i], r_k.at[i], (rep, 2 * c + core))
        put(
            dq_ref.at[c], got_q.at[chip], s_q.at[i], r_q.at[i],
            (rep, 2 * c + lax.rem(c + core, 2)),
        )
    got_k[chip] = held_k[chip]
    mine = lax.rem(chip, 2) == 0

    @pl.when(mine)
    def _():
        copy = pltpu.make_async_copy(dq_ref.at[chip], got_q.at[chip], l_sem.at[17])
        copy.start()
        copy.wait()

    @pl.when(jnp.logical_not(mine))
    def _():
        send(dq_ref.at[chip], got_q.at[chip], s_q.at[0], r_q.at[0], (rep, sib)).wait_send()

    own.wait()
    for land, total, r_x in ((land_o, sum_o, r_ro), (land_i, sum_i, r_ri)):
        for i in range(1, 8):
            landed(land.at[i - 1], r_x.at[i])

        def add(t, _, land=land, total=total):
            at = pl.ds(pl.multiple_of(t * 16, 16), 16)
            value = own_o[at] if land is land_o else held_i[rep, at]
            value = value.astype(f32)
            for i in range(7):
                value = value + land[i, at].astype(f32)
            total[at] = value.astype(bf16)
            return 0

        lax.fori_loop(0, total.shape[0] // 16, add, 0)
        if land is land_o:
            keep = pltpu.make_async_copy(sum_o, out_sum.at[part_of(rep)], l_sem.at[18])
            keep.start()
            for i in range(1, 8):
                to = lax.rem(rep + i, 8)
                put(sum_o, out_sum.at[part_of(rep)], s_go.at[i], r_go.at[i], (to, shard))
    owner = 2 * rep + core
    for i in range(1, 8):
        put(sum_i, in_sum.at[chip], s_gi.at[i], r_gi.at[chip], (lax.rem(rep + i, 8), owner))

    @pl.when(alone)
    def _():
        copy = pltpu.make_async_copy(sum_i, in_sum.at[chip], l_sem.at[19])
        copy.start()
        copy.wait()

    @pl.when(jnp.logical_not(alone))
    def _():
        send(sum_i, in_sum.at[chip], s_gi.at[0], r_gi.at[chip], (rep, owner)).wait_send()

    @pl.when(jnp.logical_not(mine))
    def _():
        landed(got_q.at[chip], r_q.at[0])

    for i in range(1, 8):
        landed(got_q.at[lax.rem(chip + 8 - i, 8)], r_q.at[i])
        landed(got_k.at[lax.rem(chip + 8 - i, 8)], r_k.at[i])
    joined = jnp.concatenate(
        [got_q[c] for c in range(CHIPS)]
        + [got_k[c][:, :HEAD] for c in range(CHIPS)]
        + [got_k[c][:, HEAD:] for c in range(CHIPS)],
        1,
    )
    fetch.wait()
    dh_ref[...] = contract(joined, w_ref[...], ((1,), (1,)))

    for i in range(1, 8):
        landed(out_sum.at[part_of(lax.rem(rep + 8 - i, 8))], r_go.at[i])
    for j in range(8):

        @pl.when(jnp.logical_not(jnp.logical_and(alone, chip == j)))
        def _(j=j):
            landed(in_sum.at[j], r_gi.at[j])

    keep.wait()
    for copy in sent:
        copy.wait_send()


def tail(dq, dkv, inward_part, outward_own, inward_all, collective):
    dma = pltpu.SemaphoreType.DMA
    return pl.pallas_call(
        tail_kernel,
        out_shape=(
            jax.ShapeDtypeStruct((OWN, D), f32),
            jax.ShapeDtypeStruct((CHIPS, 96, 320), bf16),
            jax.ShapeDtypeStruct((96, D), bf16),
        ),
        in_specs=[ANY, ANY, ANY, ANY, HBM],
        out_specs=(VMEM, ANY, ANY),
        scratch_shapes=[
            pltpu.VMEM(inward_all.shape, bf16),
            pltpu.VMEM((8, OWN, 128), bf16),
            pltpu.VMEM((8, OWN, 128), bf16),
            pltpu.VMEM((8, 96, 320), bf16),
            pltpu.VMEM((8, 96, 320), bf16),
            pltpu.VMEM((8, OWN, 192), bf16),
            pltpu.VMEM((8, OWN, 128), bf16),
            pltpu.VMEM((7, 96, 320), bf16),
            pltpu.VMEM((7,) + PART, bf16),
            pltpu.VMEM(PART, bf16),
            pltpu.VMEM((96, 320), bf16),
            pltpu.VMEM(PART, bf16),
            dma((21,)),
        ]
        + [dma((8,))] * 16,
        compiler_params=params(collective, 62 * 2**20),
        name="tail",
    )(dq, dkv, inward_part, outward_own, inward_all)


def swap_halves(values):
    lanes = values.shape[1]
    lane = lax.broadcasted_iota(jnp.int32, values.shape, 1)
    ahead = pltpu.roll(values, lanes - HEAD // 2, 1)
    behind = pltpu.roll(values, HEAD // 2, 1)
    return jnp.where(lax.rem(lane, HEAD) < HEAD // 2, ahead, behind)


def project_step(i, core, x_ref, w_ref, g_ref, cos_ref, sin_ref, q_ref, k_ref, v_ref, u_ref):
    stream = x_ref[...].astype(f32)
    u_ref[...] = (stream * inverse_root(stream) * g_ref[...]).astype(bf16)
    first = pl.multiple_of(lax.rem(i + core, 2) * OWN, OWN)
    own = pl.ds(first, OWN)
    queries = jnp.dot(u_ref[own, :], w_ref[:, :256], preferred_element_type=f32)
    cos, sin = cos_ref[own, :], sin_ref[own, :]
    cos, sin = jnp.concatenate([cos, cos], 1), jnp.concatenate([sin, sin], 1)
    turned = (queries * cos + swap_halves(queries) * sin).astype(bf16)
    turned = turned * jnp.bfloat16(HEAD**-0.5)
    for r in range(GROUP):
        q_ref[i, r * OWN : (r + 1) * OWN, :] = turned[:, r * HEAD : (r + 1) * HEAD]
    pairs = jnp.dot(u_ref[...], w_ref[:, 256:], preferred_element_type=f32)
    keys = pairs * cos_ref[...] + swap_halves(pairs) * sin_ref[...]
    rows = pl.ds(pl.multiple_of(i * KEYS, KEYS), KEYS)
    k_ref[rows, :] = keys[:, :HEAD].astype(bf16)
    lane = lax.broadcasted_iota(jnp.int32, pairs.shape, 1)
    v_ref[rows, :] = jnp.where(lane < HEAD, pltpu.roll(pairs, HEAD, 1), 1.0).astype(bf16)


def contract(a, b, dims, precision=None):
    return lax.dot_general(
        a, b, ((dims[0], dims[1]), ((), ())), preferred_element_type=f32, precision=precision
    )


def attend_kernel(
    x_ref, w_ref, g_ref, cos_ref, sin_ref, b_ref, d_ref, f_ref,
    q_ref, k_ref, v_ref, u_ref, o_ref, l_ref, bo_ref, do_ref, fo_ref,
    local_sem, s_sem, r_sem, s_low, r_low, s_out, r_out,
):
    i = pl.program_id(0)
    core = lax.rem(lax.axis_index("shard"), 2)
    steps = ring_spread(b_ref, bo_ref, 16, local_sem.at[0], s_sem, r_sem)
    low_steps = ring_spread(d_ref, do_ref, 16, local_sem.at[1], s_low, r_low)
    out_steps = ring_spread(f_ref, fo_ref, 16, local_sem.at[2], s_out, r_out)

    @pl.when(i == 0)
    def _():
        rep, shard = place()
        y = lax.rem(shard // 2, 2)
        greet(
            [(rep, shard + 1 - 2 * core), (rep, shard + 2 - 4 * y)]
            + [(rep + 1 - 2 * lax.rem(rep, 2), shard + 2 - 4 * y)]
            + [(rep, lax.rem(shard + 4, 16)), (rep, lax.rem(shard + 12, 16))]
        )
        out_steps[0]()
        steps[0]()
        low_steps[0]()

    @pl.when(i == 1)
    def _():
        out_steps[1]()
        steps[1]()

    @pl.when(i == 4)
    def _():
        low_steps[1]()

    @pl.when(i == 9)
    def _():
        out_steps[2]()

    @pl.when(i == 11)
    def _():
        steps[2]()

    @pl.when(i == 13)
    def _():
        out_steps[3]()
        low_steps[2]()

    @pl.when(i == 14)
    def _():
        steps[3]()

    @pl.when(i == 15)
    def _():
        low_steps[3]()

    @pl.when(i < BLOCKS)
    def _():
        project_step(i, core, x_ref, w_ref, g_ref, cos_ref, sin_ref, q_ref, k_ref, v_ref, u_ref)

    @pl.when(i >= BLOCKS)
    def _():
        attend_step(i - BLOCKS, core, q_ref, k_ref, v_ref, o_ref, l_ref)

    @pl.when(i == 2 * BLOCKS - 1)
    def _():
        out_steps[4]()
        steps[4]()
        low_steps[4]()


def attend_step(i, core, q_ref, k_ref, v_ref, o_ref, l_ref):
    shift = lax.rem(i + core, 2) * OWN
    q = q_ref[i]

    def step(c, carry, last=False):
        top, total = carry
        at = pl.ds(pl.multiple_of(c * KEYS, KEYS), KEYS)
        scores = contract(q, k_ref[at, :], ((1,), (1,)))
        if last:
            row = lax.broadcasted_iota(jnp.int32, (OWN, KEYS), 0)
            column = lax.broadcasted_iota(jnp.int32, (OWN, KEYS), 1)
            bias = jnp.where(column <= row + shift, 0.0, -1e30)
            scores = scores + jnp.concatenate([bias] * GROUP, 0)
        high = jnp.maximum(top, jnp.max(scores, 1, keepdims=True))
        prob = jnp.exp(scores - high).astype(bf16)
        total = total * jnp.exp(top - high) + jnp.dot(
            prob, v_ref[at, :], preferred_element_type=f32
        )
        return high, total

    carry = (jnp.full((ROWS, 1), -1e30, f32), jnp.zeros((ROWS, 128), f32))
    carry = lax.fori_loop(0, i, step, carry)
    top, total = step(i, carry, True)
    weight = total[:, HEAD : HEAD + 1]
    result = (total[:, :HEAD] / weight).astype(bf16)
    o_ref[0] = jnp.concatenate([result[r * OWN : (r + 1) * OWN] for r in range(GROUP)], 1)
    column = lax.broadcasted_iota(jnp.int32, (8, 8), 1)
    l_ref[0] = contract(
        jnp.where(column == 0, 1.0, 0.0).astype(f32),
        jnp.broadcast_to(top + jnp.log(weight), (ROWS, 8)),
        ((1,), (1,)),
        lax.Precision.HIGHEST,
    )


def attend(x_all, weight, gain, cos, sin, units, low, half, collective):
    dma = pltpu.SemaphoreType.DMA
    whole = lambda i: (0, 0)
    early = lambda i: (jnp.minimum(i, BLOCKS - 1), 0)
    late = lambda i: (jnp.maximum(i - BLOCKS, 0), 0, 0)
    return pl.pallas_call(
        attend_kernel,
        grid=(2 * BLOCKS,),
        in_specs=[
            pl.BlockSpec((KEYS, D), early),
            pl.BlockSpec((D, 384), whole),
            pl.BlockSpec((1, D), whole),
            pl.BlockSpec((KEYS, 128), early),
            pl.BlockSpec((KEYS, 128), early),
            ANY,
            ANY,
            ANY,
        ],
        out_specs=(
            pl.BlockSpec((BLOCKS, ROWS, HEAD), lambda i: (0, 0, 0)),
            pl.BlockSpec((SEQ, HEAD), whole),
            pl.BlockSpec((SEQ, 128), whole),
            pl.BlockSpec((KEYS, D), early),
            pl.BlockSpec((1, OWN, GROUP * HEAD), late),
            pl.BlockSpec((1, 8, ROWS), late),
            ANY,
            ANY,
            ANY,
        ),
        out_shape=(
            jax.ShapeDtypeStruct((BLOCKS, ROWS, HEAD), bf16),
            jax.ShapeDtypeStruct((SEQ, HEAD), bf16),
            jax.ShapeDtypeStruct((SEQ, 128), bf16),
            jax.ShapeDtypeStruct((SEQ, D), bf16),
            jax.ShapeDtypeStruct((BLOCKS, OWN, GROUP * HEAD), bf16),
            jax.ShapeDtypeStruct((BLOCKS, 8, ROWS), f32),
            jax.ShapeDtypeStruct((SHARDS,) + units.shape[1:], bf16),
            jax.ShapeDtypeStruct((SHARDS,) + low.shape[1:], bf16),
            jax.ShapeDtypeStruct((SHARDS,) + half.shape[1:], bf16),
        ),
        scratch_shapes=[dma((3,))] + [dma((23,))] * 6,
        compiler_params=params(collective, 62 * 2**20),
        name="attend",
    )(x_all, weight, gain, cos, sin, units, low, half)


def attend_back_kernel(
    q_ref, k_ref, v_ref, g_ref, a_ref, l_ref, cos_ref, sin_ref, qcos_ref, qsin_ref, u_hbm, part_ref,
    lift_ref, down_ref, dq_ref, dkv_ref, in_ref, part_out, lift_out, down_out,
    u_ref, u_sem, dk, dv, dq, total_q, held, near, landed, local_sem, s_sem, r_sem, h_sem, s_near, r_near, s_far, r_far,
):
    i = pl.program_id(0)
    rep, shard = place()
    core = lax.rem(shard, 2)
    chip = shard // 2
    sib = shard + 1 - 2 * core
    shift = lax.rem(i + core, 2) * OWN
    x = rep // 2
    kept = [
        (n, src, dst)
        for n, (src, dst) in enumerate(((lift_ref, lift_out), (down_ref, down_out)))
    ]

    def copy_same(n, src, dst):
        return pltpu.make_async_copy(src, dst.at[pl.ds(2 * x, 2)], local_sem.at[n])

    x_up, x_down, x_far = (lax.rem(x + d, 4) for d in (1, 3, 2))

    def copy_x(n, src, dst, way):
        return pltpu.make_async_remote_copy(
            src_ref=src,
            dst_ref=dst,
            send_sem=s_sem.at[n, way],
            recv_sem=r_sem.at[n, way],
            device_id=(along_x(rep, 3 if way % 2 else 1), shard),
            device_id_type=MESH,
        )

    def two_of(dst, at):
        return dst.at[pl.ds(2 * at, 2)]

    def copy_near(j):
        return pltpu.make_async_remote_copy(
            src_ref=part_ref.at[2 * lax.rem(chip + j, 8) + 1 - core],
            dst_ref=near.at[j],
            send_sem=s_near.at[j],
            recv_sem=r_near.at[j],
            device_id=(rep, sib),
            device_id_type=MESH,
        )

    def copy_own(j):
        return pltpu.make_async_copy(
            part_ref.at[2 * lax.rem(chip + j, 8) + core], held.at[j], h_sem.at[j]
        )

    def copy_far(j):
        return pltpu.make_async_remote_copy(
            src_ref=held.at[j],
            dst_ref=landed.at[j - 1],
            send_sem=s_far.at[j],
            recv_sem=r_far.at[j],
            device_id=(rep, 2 * lax.rem(chip + j, 8) + core),
            device_id_type=MESH,
        )

    @pl.when(i == 0)
    def _():
        greet(
            [(rep, sib)]
            + [(rep, 2 * lax.rem(chip + n, 8) + core) for n in range(1, 8)]
            + [(along_x(rep, dx), shard) for dx in (1, 3)]
        )
        for j in range(8):
            copy_near(j).start()
            copy_own(j).start()
        for n, src, dst in kept:
            copy_same(n, src, dst).start()
            copy_x(n, src, two_of(dst, x), 0).start()
            copy_x(n, src, two_of(dst, x), 1).start()
        pltpu.make_async_copy(u_hbm, u_ref, u_sem).start()
        total_q[...] = jnp.zeros_like(total_q)
        dk[...] = jnp.zeros_like(dk)
        dv[...] = jnp.zeros_like(dv)

    @pl.when(i == 6)
    def _():
        for n, src, dst in kept:
            ref = two_of(dst, x_down)
            copy_x(n, ref, ref, 0).wait_recv()
            ref = dst.at[2 * x_down]
            copy_x(n, ref, ref, 2).start()
            ref = two_of(dst, x_up)
            copy_x(n, ref, ref, 1).wait_recv()
            ref = dst.at[2 * x_up + 1]
            copy_x(n, ref, ref, 3).start()

    @pl.when(i == 3)
    def _():
        for j in range(8):
            copy_near(j).wait_recv()
            copy_own(j).wait()

            def add(t, _, j=j):
                at = pl.ds(pl.multiple_of(t * 32, 32), 32)
                held[j, at] = (held[j, at].astype(f32) + near[j, at].astype(f32)).astype(bf16)
                return 0

            lax.fori_loop(0, 3, add, 0)
            if j:
                copy_far(j).start()

    q = q_ref[0]
    grad = jnp.concatenate([g_ref[0][:, r * HEAD : (r + 1) * HEAD] for r in range(GROUP)], 0)
    dq[...] = jnp.zeros_like(dq)
    lse = l_ref[0][:1]
    lane = lax.broadcasted_iota(jnp.int32, (8, GROUP * HEAD), 1)
    row = lax.broadcasted_iota(jnp.int32, (8, GROUP * HEAD), 0)
    sums = contract(
        jnp.where(lane // HEAD == row, 1.0, 0.0).astype(f32),
        g_ref[0].astype(f32) * a_ref[0].astype(f32),
        ((1,), (1,)),
        lax.Precision.HIGHEST,
    )
    delta = jnp.concatenate([sums[r : r + 1] for r in range(GROUP)], 1)

    def step(c, _, last=False):
        at = pl.ds(pl.multiple_of(c * KEYS, KEYS), KEYS)
        keys = k_ref[at, :]
        scores = contract(keys, q, ((1,), (1,)))
        if last:
            key = lax.broadcasted_iota(jnp.int32, (KEYS, OWN), 0)
            token = lax.broadcasted_iota(jnp.int32, (KEYS, OWN), 1)
            bias = jnp.where(key <= token + shift, 0.0, -1e30)
            scores = scores + jnp.concatenate([bias] * GROUP, 1)
        prob = jnp.exp(scores - lse)
        back = contract(v_ref[at, :HEAD], grad, ((1,), (1,)))
        slope = (prob * (back - delta)).astype(bf16)
        dv[at, :] += jnp.dot(prob.astype(bf16), grad, preferred_element_type=f32)
        dk[at, :] += jnp.dot(slope, q, preferred_element_type=f32)
        dq[...] += contract(keys, slope, ((0,), (0,)))
        return 0

    def two_steps(c, _):
        step(2 * c, 0)
        return step(2 * c + 1, 0)

    lax.fori_loop(0, i // 2, two_steps, 0)

    @pl.when(lax.rem(i, 2) == 1)
    def _():
        step(i - 1, 0)

    step(i, 0, True)
    turned = dq[...].T
    wide = jnp.concatenate(
        [turned[r * OWN : (r + 1) * OWN, :] for r in range(GROUP)] + [jnp.zeros((OWN, HEAD), f32)], 1
    )
    wide = wide * (HEAD**-0.5)
    cos, sin = qcos_ref[...], qsin_ref[...]
    cos, sin = jnp.concatenate([cos, cos], 1), jnp.concatenate([sin, sin], 1)
    wide = wide * cos - swap_halves(wide) * sin
    wide = wide[:, : GROUP * HEAD].astype(bf16)
    dq_ref[0] = wide

    @pl.when(i == 0)
    def _():
        pltpu.make_async_copy(u_hbm, u_ref, u_sem).wait()

    mine = pl.ds(pl.multiple_of(i * KEYS + shift, OWN), OWN)
    total_q[...] += contract(wide, u_ref[mine, :], ((0,), (0,)))

    @pl.when(i == BLOCKS - 1)
    def _():
        def turn(c, _):
            at = pl.ds(pl.multiple_of(c * OWN, OWN), OWN)
            both = jnp.concatenate([dk[at, :], dv[at, :]], 1)
            lane = lax.broadcasted_iota(jnp.int32, both.shape, 1)
            turned = both * cos_ref[at, :] - swap_halves(both) * sin_ref[at, :]
            dkv_ref[at, :] = jnp.where(lane < HEAD, turned, both).astype(bf16)
            return 0

        lax.fori_loop(0, SHARDS, turn, 0)
        def add_pairs(c, both):
            at = pl.ds(pl.multiple_of(c * 768, 768), 768)
            return both + contract(dkv_ref[at, :], u_ref[at, :], ((0,), (0,)))

        both = lax.fori_loop(0, SEQ // 768, add_pairs, jnp.zeros((128, D), f32))
        both = jnp.concatenate([total_q[...], both], 0).T.astype(bf16)
        for s in range(SHARDS):
            in_ref[s] = both[s * 96 : (s + 1) * 96]

        for j in range(1, 8):
            copy_far(j).wait_recv()

        def add(t, _):
            at = pl.ds(pl.multiple_of(t * 32, 32), 32)
            total = held[0, at].astype(f32)
            for j in range(7):
                total = total + landed[j, at].astype(f32)
            part_out[at] = total.astype(bf16)
            return 0

        lax.fori_loop(0, 3, add, 0)
        for n, src, dst in kept:
            copy_same(n, src, dst).wait()
            for k in range(2):
                ref = dst.at[2 * x_far + k]
                copy_x(n, ref, ref, 2 + k).wait_recv()
            for way in range(4):
                ref = two_of(dst, x) if way < 2 else dst.at[2 * x]
                copy_x(n, ref, ref, way).wait_send()
        for j in range(8):
            copy_near(j).wait_send()
            if j:
                copy_far(j).wait_send()


def attend_back(q, k, v, grad, attended, lse, cos, sin, u_all, part, lift, down, collective):
    def own(i):
        return (2 * i + lax.rem(i + lax.rem(lax.axis_index("shard"), 2), 2), 0)

    whole = lambda i: (0, 0)
    block = lambda i: (i, 0, 0)
    return pl.pallas_call(
        attend_back_kernel,
        grid=(BLOCKS,),
        in_specs=[
            pl.BlockSpec((1, ROWS, HEAD), block),
            pl.BlockSpec((SEQ, HEAD), whole),
            pl.BlockSpec((SEQ, 128), whole),
            pl.BlockSpec((1, OWN, GROUP * HEAD), block),
            pl.BlockSpec((1, OWN, GROUP * HEAD), block),
            pl.BlockSpec((1, 8, ROWS), block),
            pl.BlockSpec((SEQ, 128), whole),
            pl.BlockSpec((SEQ, 128), whole),
            pl.BlockSpec((OWN, 128), own),
            pl.BlockSpec((OWN, 128), own),
            HBM,
            ANY,
            ANY,
            ANY,
        ],
        out_specs=(
            pl.BlockSpec((1, OWN, GROUP * HEAD), block),
            pl.BlockSpec((SEQ, 128), whole),
            pl.BlockSpec((SHARDS, 96, 320), lambda i: (0, 0, 0)),
            pl.BlockSpec(part.shape[1:], whole),
            ANY,
            ANY,
        ),
        out_shape=(
            jax.ShapeDtypeStruct((BLOCKS, OWN, GROUP * HEAD), bf16),
            jax.ShapeDtypeStruct((SEQ, 128), bf16),
            jax.ShapeDtypeStruct((SHARDS, 96, 320), bf16),
            jax.ShapeDtypeStruct(part.shape[1:], bf16),
            jax.ShapeDtypeStruct((PEERS,) + lift.shape[1:], bf16),
            jax.ShapeDtypeStruct((PEERS,) + down.shape[1:], bf16),
        ),
        scratch_shapes=[
            pltpu.VMEM((SEQ, D), bf16),
            pltpu.SemaphoreType.DMA,
            pltpu.VMEM((SEQ, HEAD), f32),
            pltpu.VMEM((SEQ, HEAD), f32),
            pltpu.VMEM((HEAD, ROWS), f32),
            pltpu.VMEM((GROUP * HEAD, D), f32),
            pltpu.VMEM((8,) + part.shape[1:], bf16),
            pltpu.VMEM((8,) + part.shape[1:], bf16),
            pltpu.VMEM((7,) + part.shape[1:], bf16),
            pltpu.SemaphoreType.DMA((2,)),
            pltpu.SemaphoreType.DMA((2, 4)),
            pltpu.SemaphoreType.DMA((2, 4)),
        ]
        + [pltpu.SemaphoreType.DMA((8,))] * 5,
        compiler_params=params(collective, 62 * 2**20),
        name="attend_back",
    )(q, k, v, grad, attended, lse, cos, sin, cos, sin, u_all, part, lift, down)


def distance(i):
    return jnp.where(i == 0, 0, jnp.where(i == 1, 1, jnp.where(i == 2, 3, 2)))


def experts_kernel(
    x_hbm, y_ref, c_ref, wl_hbm, wd_hbm, e_ref,
    du_o, out_o, lift_o, down_o,
    u, wl, wd, gl, acc, down, part, near, land, total,
    la, lb, lc, ld, da, db, dc, dd,
    down_sum, l_sem, s_g, r_g, s_near, r_near, s_land, r_land, s_one, r_one, s_two, r_two,
):
    i = pl.program_id(0)
    rep, shard = place()
    core = lax.rem(shard, 2)
    chip = shard // 2
    y = lax.rem(chip, 2)
    z = chip // 2
    x = rep // 2
    sib = shard + 1 - 2 * core
    pair = shard + 2 - 4 * y

    def remote(src, dst, s_sem, r_sem, device):
        return pltpu.make_async_remote_copy(
            src_ref=src, dst_ref=dst, send_sem=s_sem, recv_sem=r_sem,
            device_id=device, device_id_type=MESH,
        )

    def tokens(dx, k, low=0, size=OWN):
        return u.at[lax.rem(x + dx, 4), pl.ds(pl.multiple_of(OWN * k + low, 96), size)]

    half = OWN // 2
    ups, downs, sibs = (along_x(rep, 1), shard), (along_x(rep, 3), shard), (rep, sib)
    slots = {
        0: (tokens(3, core), None, ups),
        1: (tokens(1, core), None, downs),
        2: (tokens(2, core, 0, half), tokens(3, core, 0, half), ups),
        3: (tokens(2, core, half, half), tokens(1, core, half, half), downs),
        4: (tokens(0, 1 - core), None, sibs),
        5: (tokens(3, 1 - core), tokens(3, core), sibs),
        6: (tokens(1, 1 - core), tokens(1, core), sibs),
        7: (tokens(2, 1 - core, 0, half), tokens(2, core, 0, half), sibs),
        8: (tokens(2, 1 - core, half, half), tokens(2, core, half, half), sibs),
    }

    def gather_send(n):
        _, out, device = slots[n]
        src, dst = (x_hbm, tokens(0, core)) if out is None else (out, out)
        return remote(src, dst, s_g.at[n], r_g.at[n], device)

    def gather_arrival(n):
        ref = slots[n][0]
        remote(ref, ref, s_g.at[n], r_g.at[n], sibs).wait_recv()

    own_tokens = pltpu.make_async_copy(x_hbm, tokens(0, core), l_sem.at[0])
    fetch_wl = pltpu.make_async_copy(wl_hbm, wl, l_sem.at[1])
    fetch_wd = pltpu.make_async_copy(wd_hbm, wd, l_sem.at[2])

    def rows(k):
        return pl.ds(pl.multiple_of(OWN * k, OWN), OWN)

    def near_copy(n, t):
        return remote(
            part.at[t, n, rows(1 - core)], near.at[t, n], s_near.at[t, n], r_near.at[t, n], sibs
        )

    def land_copy(n, t):
        return remote(
            part.at[t, n, rows(core)], land.at[t - 1, n], s_land.at[t, n], r_land.at[t, n],
            (along_x(rep, distance(t)), shard),
        )

    def pass_on(t):
        for n in range(2):
            near_copy(n, t).wait_recv()

            def add(r, _, n=n):
                at = pl.ds(pl.multiple_of(r * 32, 32), 32)
                mine = pl.ds(pl.multiple_of(OWN * core + r * 32, 32), 32)
                part[t, n, mine] = (
                    part[t, n, mine].astype(f32) + near[t, n, at].astype(f32)
                ).astype(bf16)
                return 0

            lax.fori_loop(0, OWN // 32, add, 0)

            @pl.when(t > 0)
            def _(n=n):
                land_copy(n, t).start()

    grads = ((wl, la, lb, lc, ld, lift_o, 192), (wd, da, db, dc, dd, down_sum, 2 * FLAT))

    def piece(m, dz, dy, columns):
        buffer, size = grads[m][0], grads[m][6]
        c = 2 * lax.rem(z + dz, 4) + (1 - y if dy else y)
        return buffer.at[pl.ds(pl.multiple_of(size * c, size), size), columns]

    def columns_of(m):
        width = grads[m][0].shape[1] // 2
        return pl.ds(0, width), pl.ds(width, width)

    def to_z(dz):
        return (rep, 4 * lax.rem(z + dz, 4) + 2 * y + core)

    def one_a(m, dz):
        return remote(
            piece(m, dz, 1, columns_of(m)[0]), grads[m][1].at[dz], s_one.at[m, 0, dz], r_one.at[m, 0, dz],
            (rep, pair),
        )

    def one_b(m, dz, dy):
        j = 2 * dz + dy
        return remote(
            piece(m, dz, dy, columns_of(m)[1]), grads[m][2].at[j - 2], s_one.at[m, 1, j], r_one.at[m, 1, j],
            to_z(dz),
        )

    def two_a(m, dz):
        return remote(
            piece(m, dz, 0, columns_of(m)[0]), grads[m][3].at[dz - 1], s_two.at[m, dz], r_two.at[m, dz],
            to_z(dz),
        )

    def two_b(m):
        return remote(
            piece(m, 0, 1, columns_of(m)[1]), grads[m][4], s_two.at[m, 0], r_two.at[m, 0], (rep, pair)
        )

    def first_sums(m):
        land_a, land_b, size = grads[m][1], grads[m][2], grads[m][6]
        first, last = columns_of(m)
        for dz in (2, 1, 3, 0):
            one_a(m, dz).wait_recv()
            mine = piece(m, dz, 0, first)

            def add(t, _, mine=mine, dz=dz):
                at = pl.ds(pl.multiple_of(t * 16, 16), 16)
                mine[at] = (mine[at].astype(f32) + land_a[dz, at].astype(f32)).astype(bf16)
                return 0

            lax.fori_loop(0, size // 16, add, 0)
            if dz:
                two_a(m, dz).start()
        for dy in (1, 0):
            for dz in (1, 2, 3):
                one_b(m, dz, dy).wait_recv()
            mine = piece(m, 0, dy, last)

            def add(t, _, mine=mine, dy=dy):
                at = pl.ds(pl.multiple_of(t * 16, 16), 16)
                value = mine[at].astype(f32)
                for dz in (1, 2, 3):
                    value = value + land_b[2 * dz + dy - 2, at].astype(f32)
                mine[at] = value.astype(bf16)
                return 0

            lax.fori_loop(0, size // 16, add, 0)
            if dy:
                two_b(m).start()

    def last_sums(m):
        land_c, land_d, out, size = grads[m][3], grads[m][4], grads[m][5], grads[m][6]
        first, last = columns_of(m)
        for dz in (1, 2, 3):
            two_a(m, dz).wait_recv()
        two_b(m).wait_recv()
        mine_a, mine_b = piece(m, 0, 0, first), piece(m, 0, 0, last)

        def add(t, _):
            at = pl.ds(pl.multiple_of(t * 16, 16), 16)
            value = mine_a[at].astype(f32)
            for dz in (1, 2, 3):
                value = value + land_c[dz - 1, at].astype(f32)
            out[at, first] = value.astype(bf16)
            out[at, last] = (mine_b[at].astype(f32) + land_d[at].astype(f32)).astype(bf16)
            return 0

        lax.fori_loop(0, size // 16, add, 0)

    @pl.when(i == 0)
    def _():
        fetch_wl.start()
        fetch_wd.start()
        own_tokens.start()
        greet(
            [(rep, sib), (rep, pair)]
            + [to_z(dz) for dz in (1, 2, 3)]
            + [(along_x(rep, dx), shard) for dx in (1, 2, 3)]
        )
        for n in (4, 0, 1):
            gather_send(n).start()
        down[...] = jnp.zeros_like(down)
        fetch_wl.wait()
        fetch_wd.wait()
        own_tokens.wait()
        gather_arrival(4)

    @pl.when(i == 1)
    def _():
        gather_arrival(1)
        gather_send(6).start()
        gather_send(3).start()
        gather_arrival(0)
        gather_send(5).start()
        gather_send(2).start()
        gather_arrival(6)

    @pl.when(i == 2)
    def _():
        gather_arrival(2)
        gather_send(7).start()
        gather_arrival(3)
        gather_send(8).start()
        gather_arrival(5)

    @pl.when(i == 3)
    def _():
        gather_arrival(7)
        gather_arrival(8)

    @pl.when(i > 0)
    def _():
        pass_on(i - 1)

    @pl.when(i < 4)
    def _():
        h, dy = u[lax.rem(x + distance(i), 4)], y_ref[...]
        lifted = jnp.dot(h, wl[...], preferred_element_type=f32)
        back = contract(dy, wd[...], ((1,), (1,)))
        share = jnp.dot(c_ref[...], e_ref[...], preferred_element_type=f32)
        gate, raised = lifted[:, :HID], lifted[:, HID:]
        s = jax.nn.sigmoid(gate)
        swish = gate * s
        act = (share * swish * raised).astype(bf16)
        back = back * share
        grad_gate = back * raised * s * (1.0 + gate * (1.0 - s))
        gl[i] = jnp.concatenate([grad_gate, back * swish], 1).astype(bf16)
        part[i, 0] = contract(gl[i], wl[...], ((1,), (1,))).astype(bf16)
        near_copy(0, i).start()
        part[i, 1] = jnp.dot(act, wd[...], preferred_element_type=f32).astype(bf16)
        near_copy(1, i).start()
        down[...] += contract(act, dy, ((0,), (0,)))

    @pl.when(i == 4)
    def _():
        wd[...] = down[...].astype(bf16)
        for dz in (2, 1, 3, 0):
            one_a(1, dz).start()
            if dz:
                one_b(1, dz, 1).start()
                one_b(1, dz, 0).start()
        for part_of_lift in range(2):
            columns = slice(HID * part_of_lift, HID * (part_of_lift + 1))
            for t in range(4):
                dx = (0, 1, 3, 2)[t]
                term = contract(u[lax.rem(x + dx, 4)], gl[t][:, columns], ((0,), (0,)))
                if t == 0:
                    acc[...] = term
                elif t < 3:
                    acc[...] += term
                else:
                    wl[:, columns] = (acc[...] + term).astype(bf16)
            if part_of_lift == 0:
                for dz in (2, 1, 3, 0):
                    one_a(0, dz).start()
            else:
                for dz in (2, 1, 3):
                    one_b(0, dz, 1).start()
                    one_b(0, dz, 0).start()
        first_sums(1)
        for n, out in ((0, du_o), (1, out_o)):
            for t in (1, 2, 3):
                land_copy(n, t).wait_recv()

            def add(r, _, n=n):
                at = pl.ds(pl.multiple_of(r * 32, 32), 32)
                mine = pl.ds(pl.multiple_of(OWN * core + r * 32, 32), 32)
                value = part[0, n, mine].astype(f32)
                for t in range(3):
                    value = value + land[t, n, at].astype(f32)
                total[n, at] = value
                return 0

            lax.fori_loop(0, OWN // 32, add, 0)
            pltpu.make_async_copy(total.at[n], out, l_sem.at[3 + n]).start()
        first_sums(0)
        last_sums(1)
        for k in range(2):
            down_o[k] = jnp.concatenate(
                [
                    down_sum[FLAT * k : FLAT * (k + 1)],
                    jnp.zeros((FLAT_PAD - FLAT, D), bf16),
                ],
                0,
            )
        last_sums(0)
        for n, out in ((0, du_o), (1, out_o)):
            pltpu.make_async_copy(total.at[n], out, l_sem.at[3 + n]).wait()
        for n in range(9):
            gather_send(n).wait_send()
        for n in range(2):
            for t in range(4):
                near_copy(n, t).wait_send()
                if t:
                    land_copy(n, t).wait_send()
        for m in range(2):
            for dz in range(4):
                one_a(m, dz).wait_send()
                if dz:
                    one_b(m, dz, 0).wait_send()
                    one_b(m, dz, 1).wait_send()
                    two_a(m, dz).wait_send()
            two_b(m).wait_send()


def experts(h, y_all, shares, wl, wd, table, collective):
    dma = pltpu.SemaphoreType.DMA

    def chip_at(i):
        return (lax.rem(lax.axis_index("rep") // 2 + distance(jnp.minimum(i, 3)), 4), 0)

    whole = lambda i: (0, 0)
    once = pl.Buffered(1)

    def slots(size, width):
        return [
            pltpu.VMEM((4, size, width // 2), bf16),
            pltpu.VMEM((6, size, width // 2), bf16),
            pltpu.VMEM((3, size, width // 2), bf16),
            pltpu.VMEM((size, width // 2), bf16),
        ]

    return pl.pallas_call(
        experts_kernel,
        grid=(5,),
        in_specs=[
            HBM,
            pl.BlockSpec((2 * OWN, D), chip_at),
            pl.BlockSpec((2 * OWN, 128), chip_at),
            HBM,
            HBM,
            pl.BlockSpec((128, HID), whole, pipeline_mode=once),
        ],
        out_specs=(
            ANY,
            ANY,
            pl.BlockSpec((192, EXP), whole),
            pl.BlockSpec((2, FLAT_PAD, D), lambda i: (0, 0, 0)),
        ),
        out_shape=(
            jax.ShapeDtypeStruct((OWN, D), f32),
            jax.ShapeDtypeStruct((OWN, D), f32),
            jax.ShapeDtypeStruct((192, EXP), bf16),
            jax.ShapeDtypeStruct((2, FLAT_PAD, D), bf16),
        ),
        scratch_shapes=[
            pltpu.VMEM((4, 2 * OWN, D), bf16),
            pltpu.VMEM((D, EXP), bf16),
            pltpu.VMEM((HID, D), bf16),
            pltpu.VMEM((4, 2 * OWN, EXP), bf16),
            pltpu.VMEM((D, HID), f32),
            pltpu.VMEM((HID, D), f32),
            pltpu.VMEM((4, 2, 2 * OWN, D), bf16),
            pltpu.VMEM((4, 2, OWN, D), bf16),
            pltpu.VMEM((3, 2, OWN, D), bf16),
            pltpu.VMEM((2, OWN, D), f32),
        ]
        + slots(192, EXP)
        + slots(2 * FLAT, D)
        + [
            pltpu.VMEM((2 * FLAT, D), bf16),
            dma((5,)),
            dma((9,)),
            dma((9,)),
            dma((4, 2)),
            dma((4, 2)),
            dma((4, 2)),
            dma((4, 2)),
            dma((2, 2, 8)),
            dma((2, 2, 8)),
            dma((2, 4)),
            dma((2, 4)),
        ],
        compiler_params=params(collective, 63 * 2**20),
        name="experts",
    )(h, y_all, shares, wl, wd, table)


def choose_units(w_ref, code_ref, out_ref):
    x = lax.axis_index("rep") // 2
    row = lax.broadcasted_iota(jnp.int32, (FF_EXP, HID), 0)
    there = (row // 32) * 1024 + lax.rem(row, 32)
    here = jnp.broadcast_to(code_ref[...], (FF_EXP, HID))
    base = (5 * x) // 2
    for k in range(2):
        for part in range(2):
            total = jnp.zeros((96, HID), f32)
            for i in range(3):
                chosen = there + 32 * (base + i) == here + FLAT * (2 * x + k)
                total = total + jnp.dot(
                    w_ref[i][:, FF_EXP * part : FF_EXP * (part + 1)],
                    jnp.where(chosen, 1.0, 0.0).astype(bf16),
                    preferred_element_type=f32,
                )
            out_ref[k, :, HID * part : HID * (part + 1)] = total.astype(bf16)


def one_step(kernel, arrays, shapes, name):
    return pl.pallas_call(
        kernel,
        in_specs=[VMEM] * len(arrays),
        out_specs=(VMEM,) * len(shapes),
        out_shape=tuple(jax.ShapeDtypeStruct(shape, dtype) for shape, dtype in shapes),
        compiler_params=pltpu.CompilerParams(vmem_limit_bytes=62 * 2**20),
        name=name,
    )(*arrays)


def side_by_side(ref):
    return jnp.concatenate([ref[c] for c in range(CHIPS)], 1)


def adam(weight, old_mean, square, gradient, step_rate, decay_rate):
    values = weight.astype(f32)
    moment = beta_one * old_mean.astype(f32) + (1.0 - beta_one) * gradient
    variance = beta_two * square.astype(f32) + (1.0 - beta_two) * gradient * gradient
    normed_step = (
        moment
        * (1.0 / (1.0 - beta_one**STEP))
        / (jnp.sqrt(variance * (1.0 / (1.0 - beta_two**STEP))) + adam_epsilon)
    )
    return (moment, variance, values - step_rate * (normed_step + decay_rate * values))


def adam_lifting_kernel(w_ref, m_ref, s_ref, g_ref, code_ref, mo_ref, so_ref, wo_ref, dot_ref, grad):
    e = pl.program_id(0)
    first, last = (4 * e) // 5, (4 * e + 3) // 5
    column = lax.broadcasted_iota(jnp.int32, (HID, FF_EXP), 1)
    there = (column // 32) * 1024 + lax.rem(column, 32) + 32 * e
    here = jnp.broadcast_to(code_ref[...], (HID, FF_EXP))
    chosen_first = jnp.where(there == here + FLAT * first, 1.0, 0.0).astype(bf16)
    skip = jnp.where(first == last, 1 << 20, 0)
    chosen_last = jnp.where(there == here + (FLAT * last + skip), 1.0, 0.0).astype(bf16)

    def both(p):
        return jnp.concatenate([g_ref[p][:, :HID], g_ref[p][:, HID:]], 0)

    ordered = jnp.dot(both(first), chosen_first, preferred_element_type=f32) + jnp.dot(
        both(last), chosen_last, preferred_element_type=f32
    )
    grad[:, :FF_EXP] = ordered[:96]
    grad[:, FF_EXP:] = ordered[96:]

    @pl.when(e == 0)
    def _():
        dot_ref[...] = jnp.zeros_like(dot_ref)

    dot = jnp.sum(w_ref[0].astype(f32) * grad[...], 1, keepdims=True)
    dot_ref[...] += jnp.broadcast_to(dot, dot_ref.shape)
    mo_ref[0], so_ref[0], wo_ref[0] = adam(
        w_ref[0], m_ref[0], s_ref[0], grad[...], rate_lifting, weight_decay
    )


def adam_lifting(weight, mean, square, grad, code):
    block = pl.BlockSpec((1, 96, 2 * FF_EXP), lambda e: (e, 0, 0))
    shape = jax.ShapeDtypeStruct(weight.shape, f32)
    return pl.pallas_call(
        adam_lifting_kernel,
        grid=(EXPERTS,),
        in_specs=[
            block,
            block,
            block,
            pl.BlockSpec(grad.shape, lambda e: (0, 0, 0)),
            pl.BlockSpec(code.shape, lambda e: (0, 0)),
        ],
        out_specs=(block, block, block, pl.BlockSpec((96, 128), lambda e: (0, 0))),
        out_shape=(shape, shape, shape, jax.ShapeDtypeStruct((96, 128), f32)),
        scratch_shapes=[pltpu.VMEM((96, 2 * FF_EXP), f32)],
        compiler_params=pltpu.CompilerParams(vmem_limit_bytes=62 * 2**20),
        name="adam_lifting",
    )(weight, mean, square, grad, code)


def last_kernel(
    dh_ref, dz_ref, x_ref, g_ref, mixed_ref, e_ref, w_ref, m_ref, s_ref, gi_ref, wo_ref, mo_ref, so_ref, go_ref,
    grad_ref, out_ref, mi_o, si_o, wi_o, dot_ref, mo_o, so_o, wo_o,
):
    out_ref[...] = mixed_ref[...] + e_ref[...]
    stream = x_ref[...].astype(f32)
    inverse = inverse_root(stream)
    grad_ref[...] = dz_ref[...] + norm_back(dh_ref[...] * g_ref[...], stream * inverse, inverse)
    parts = [gi_ref[c].astype(f32) for c in range(CHIPS)]
    grad = jnp.concatenate(
        [p[:, :192] for p in parts] + [p[:, 192:256] for p in parts] + [p[:, 256:] for p in parts], 1
    )
    dot = jnp.sum(w_ref[...].astype(f32) * grad, 1, keepdims=True)
    dot_ref[...] = jnp.broadcast_to(dot, dot_ref.shape)
    mi_o[...], si_o[...], wi_o[...] = adam(
        w_ref[...], m_ref[...], s_ref[...], grad, rate_inward, weight_decay
    )
    mo_o[...], so_o[...], wo_o[...] = adam(
        wo_ref[...], mo_ref[...], so_ref[...], go_ref[...].astype(f32), rate_outward, weight_decay
    )


def tables():
    half = HEAD // 2
    frequency = np.float32(10000.0) ** (-(2.0 * np.arange(half, dtype=np.float32)) / HEAD)
    phases = np.arange(SEQ, dtype=np.float32)[:, None] * frequency[None, :].astype(np.float32)
    cos, sin = np.cos(phases).astype(np.float32), np.sin(phases).astype(np.float32)
    return (
        np.concatenate([cos, cos, cos, cos], 1),
        np.concatenate([-sin, sin, -sin, sin], 1),
    )


def unit_codes():
    unit = np.arange(HID, dtype=np.int32)
    return (unit // FLAT) * 1024 + unit % FLAT


def inverse_root(stream):
    return lax.rsqrt(jnp.mean(stream * stream, -1, keepdims=True) + norm_epsilon)


def norm_back(scaled, unit, inverse):
    return inverse * (scaled - unit * jnp.mean(scaled * unit, -1, keepdims=True))


def per_device(
    layer_input,
    grad_output,
    routes,
    route_logits,
    norm_gains,
    inward,
    outward,
    lifting,
    lowering,
    mean_gains,
    mean_inward,
    mean_outward,
    mean_lifting,
    mean_lowering,
    square_gains,
    square_inward,
    square_outward,
    square_lifting,
    square_lowering,
):
    gains = norm_gains.astype(f32)
    cos, sin = (jnp.asarray(t) for t in tables())

    lifting_rows = lifting.transpose(1, 0, 2)
    codes = jnp.asarray(unit_codes())
    x = lax.axis_index("rep") // 2
    position = 2 * x + lax.rem(lax.axis_index("shard"), 2)
    low_rows = lowering.transpose(1, 0, 2).reshape(EXPERTS * 32, D)
    low_rows = lax.dynamic_slice(low_rows, (2 * FLAT * x, 0), (2 * FLAT, D)).reshape(2, FLAT, D)
    low_rows = jnp.pad(low_rows, ((0, 0), (0, FLAT_PAD - FLAT), (0, 0)))
    expert = (FLAT * position + lax.rem(jnp.arange(HID), FLAT)) // 32
    row = jnp.arange(128)[:, None]
    share_table = ((row == expert) | (row == expert + 16)).astype(bf16)

    x_all, head_weight, y_all, shares, by_unit = start(
        layer_input, grad_output, inward, norm_gains, routes.T, route_logits.T, lifting_rows, codes[None, :], 2
    )
    head_weight = head_weight.reshape(D, 384)
    gain_rows = head_weight[:, 192:194].T.astype(f32)
    gain_one, gain_two = gain_rows[0:1], gain_rows[1:2]
    by_half = outward.reshape(96, 2, D // 2).transpose(1, 0, 2)

    q, k, v, u_one, attended, lse, unit_weight, down_rows, half = attend(
        x_all, head_weight, gain_one, cos, sin, by_unit, low_rows, by_half, 1
    )
    unit_weight = unit_weight.reshape(D, EXP)
    mixed, low_two, down_weight, own_attended, outward_all = home(
        attended, half.reshape(D, D // 2), down_rows, layer_input, gain_two, 3
    )
    late_inward, low_two = lax.optimization_barrier((inward, low_two))
    inward_all = lax.all_gather(late_inward, "shard", axis=0, tiled=True)
    du, expert_out, lift_sum, down_sum = experts(
        low_two, y_all, shares, unit_weight, down_weight, share_table, 5
    )
    grad_mixed, outward_part, head_grads, lift_pair, down_pair = grads_away(
        du, mixed, grad_output, gain_two, outward_all, own_attended,
        lift_sum.reshape(2, 96, EXP), down_sum, 6,
    )
    dq, dkv, inward_part, outward_own, lift_got, down_got = attend_back(
        q, k, v, head_grads, attended, lse, cos, sin, u_one, outward_part, lift_pair, down_pair, 8
    )
    dh, inward_sum, outward_sum = tail(
        dq, dkv.reshape(SHARDS, OWN, 128), inward_part, outward_own, inward_all, 7
    )
    down_grad = (
        down_got[:, :FLAT].reshape(EXPERTS, 32, D).transpose(1, 0, 2).astype(f32)
    )

    new_lifting = adam_lifting(
        lifting_rows,
        mean_lifting.transpose(1, 0, 2),
        square_lifting.transpose(1, 0, 2),
        lift_got,
        codes[:, None],
    )
    lifting_dot = new_lifting[3]
    new_lifting = tuple(t.transpose(1, 0, 2) for t in new_lifting[:3])
    last = one_step(
        last_kernel,
        (dh, grad_mixed, layer_input, gain_one, mixed, expert_out)
        + (inward, mean_inward, square_inward, inward_sum)
        + (outward, mean_outward, square_outward, outward_sum),
        (((OWN, D), f32),) * 2
        + ((inward.shape, f32),) * 3
        + (((96, 128), f32),)
        + ((outward.shape, f32),) * 3,
        "last",
    )
    input_grad, layer_output, new_inward, new_outward = last[0], last[1], last[2:6], last[6:9]
    gain_grad = jnp.stack([new_inward[3][:, 0], lifting_dot[:, 0]]) / gains
    new_gains = adam(norm_gains, mean_gains, square_gains, gain_grad, rate_gains, 0.0)
    new_lowering = adam(
        lowering, mean_lowering, square_lowering, down_grad, rate_lowering, weight_decay
    )
    return (
        layer_output,
        input_grad,
        new_gains[0],
        new_inward[0],
        new_outward[0],
        new_lifting[0],
        new_lowering[0],
        new_gains[1],
        new_inward[1],
        new_outward[1],
        new_lifting[1],
        new_lowering[1],
        new_gains[2],
        new_inward[2],
        new_outward[2],
        new_lifting[2],
        new_lowering[2],
    )


def solution(mesh):
    tokens = P(("rep", "shard"), None)
    gains, flat, deep = P(None, "shard"), P("shard", None), P("shard", None, None)
    weights = (gains, flat, flat, deep, deep)
    return jax.shard_map(
        per_device,
        mesh=mesh,
        in_specs=(tokens,) * 4 + weights * 3,
        out_specs=(tokens,) * 2 + weights * 3,
        check_vma=False,
    )
```

```python
import functools

import jax
import jax.numpy as jnp
import numpy as np
from jax import lax
from jax.experimental import pallas as pl
from jax.experimental.pallas import tpu as pltpu
from jax.sharding import PartitionSpec as P

HEADS = 24
KV_HEADS = 8
HEAD = 64
GROUP = HEADS // KV_HEADS
FF_EXP = 512
EXPERTS = 10
STEP = 10

norm_epsilon = 1e-06
beta_one = 0.9
beta_two = 0.95
adam_epsilon = 1e-08
weight_decay = 0.1
rate_gains = 0.5
rate_inward = 0.05
rate_outward = 0.3
rate_lifting = 0.05
rate_lowering = 0.3

SHARDS = 16
CHIPS = 8
REPS = 8
OWN = 192
SEQ = OWN * SHARDS
D = 1536
PEERS = 8
FLAT = 40
FLAT_PAD = 48
HID = SHARDS * FLAT
EXP = 2 * HID
BLOCKS = 8
ROWS = GROUP * OWN
KEYS = 2 * OWN

MESH = pl.DeviceIdType.MESH
bf16 = jnp.bfloat16
f32 = jnp.float32


def place():
    rep = lax.axis_index("rep")
    shard = lax.axis_index("shard")
    return rep, shard


def greet(devices):
    barrier = pltpu.get_barrier_semaphore()
    for device in devices:
        pl.semaphore_signal(barrier, inc=1, device_id=device, device_id_type=MESH)
    pl.semaphore_wait(barrier, len(devices))


def send(src, dst, send_sem, recv_sem, device):
    copy = pltpu.make_async_remote_copy(
        src_ref=src,
        dst_ref=dst,
        send_sem=send_sem,
        recv_sem=recv_sem,
        device_id=device,
        device_id_type=MESH,
    )
    copy.start()
    return copy


def params(collective, vmem=None):
    return pltpu.CompilerParams(
        collective_id=collective, has_side_effects=True, vmem_limit_bytes=vmem
    )


ANY = pl.BlockSpec(memory_space=pl.ANY)
VMEM = pl.BlockSpec(memory_space=pltpu.VMEM)
HBM = pl.BlockSpec(memory_space=pltpu.HBM)


def along_x(rep, dx):
    return 2 * lax.rem(rep // 2 + dx, 4) + lax.rem(rep, 2)


def landed_on(ref, recv_sem, any_send_sem, device):
    pltpu.make_async_remote_copy(
        src_ref=ref,
        dst_ref=ref,
        send_sem=any_send_sem,
        recv_sem=recv_sem,
        device_id=device,
        device_id_type=MESH,
    ).wait_recv()


def x_gather(x_ref, o_ref, local_sem, send_sem, recv_sem):
    rep, shard = place()
    core = lax.rem(shard, 2)
    sib = shard + 1 - 2 * core
    half = x_ref.shape[0] // 2
    top, bottom = pl.ds(0, half), pl.ds(half, half)
    up, down, far = (along_x(rep, d) for d in (1, 3, 2))

    def block(r, other=False):
        return 2 * (r // 2) + (1 - core if other else core)

    mine = block(rep)
    own = pltpu.make_async_copy(x_ref, o_ref.at[mine], local_sem)
    sent = []

    def put(ref, dst, slot, device):
        sent.append(send(ref, dst, send_sem.at[len(sent)], recv_sem.at[slot], device))

    def arrived(ref, slot):
        landed_on(ref, recv_sem.at[slot], send_sem.at[0], (rep, sib))

    def start():
        own.start()
        put(x_ref, o_ref.at[mine], 0, (up, shard))
        put(x_ref, o_ref.at[mine], 1, (down, shard))
        put(x_ref, o_ref.at[mine], 4, (rep, sib))

    def relay():
        ref = o_ref.at[block(down)]
        arrived(ref, 0)
        put(o_ref.at[block(down), top], o_ref.at[block(down), top], 2, (up, shard))
        put(ref, ref, 5, (rep, sib))
        ref = o_ref.at[block(up)]
        arrived(ref, 1)
        put(o_ref.at[block(up), bottom], o_ref.at[block(up), bottom], 3, (down, shard))
        put(ref, ref, 6, (rep, sib))

    def relay_far():
        for slot, part in ((2, top), (3, bottom)):
            ref = o_ref.at[block(far), part]
            arrived(ref, slot)
            put(ref, ref, slot + 5, (rep, sib))

    def finish():
        arrived(o_ref.at[block(rep, True)], 4)
        arrived(o_ref.at[block(down, True)], 5)
        arrived(o_ref.at[block(up, True)], 6)
        arrived(o_ref.at[block(far, True), top], 7)
        arrived(o_ref.at[block(far, True), bottom], 8)
        for copy in sent:
            copy.wait_send()
        own.wait()

    return start, relay, relay_far, finish


def ring_spread(x_ref, o_ref, split, local_sem, send_sem, recv_sem):
    rep, shard = place()
    core = lax.rem(shard, 2)
    chip = shard // 2
    y = lax.rem(chip, 2)
    sib = shard + 1 - 2 * core
    pair = chip + 1 - 2 * y
    up, down, far = (lax.rem(chip + d, 8) for d in (2, 6, 4))
    own = pltpu.make_async_copy(x_ref.at[core], o_ref.at[shard], local_sem)
    first, last = pl.ds(0, split), pl.ds(split, x_ref.shape[1] - split)

    mate = rep + 1 - 2 * lax.rem(rep, 2)

    def copy(src, dst, slot, chip_to=None):
        across = slot in (18, 19, 20, 21, 22)
        return pltpu.make_async_remote_copy(
            src_ref=src,
            dst_ref=dst,
            send_sem=send_sem.at[slot],
            recv_sem=recv_sem.at[slot],
            device_id=(mate if across else rep, sib if chip_to is None else 2 * chip_to + core),
            device_id_type=MESH,
        )

    def push_pair(c, rows, slot, across):
        push(block(c, rows, 0), slot, pair)
        push(block(c, rows, 1), across, pair)

    def other(c):
        return c + 1 - 2 * y

    def block(c, rows, part=None):
        if part is None:
            return o_ref.at[pl.ds(2 * c, 2), rows]
        return o_ref.at[2 * c + part, rows]

    def push(ref, slot, to):
        copy(ref, ref, slot, to).start()

    def arrived(ref, slot):
        copy(ref, ref, slot, pair).wait_recv()

    def start():
        own.start()
        copy(x_ref.at[1 - core], o_ref.at[shard], 0).start()

    def one():
        copy(o_ref.at[sib], o_ref.at[sib], 0).wait_recv()
        own.wait()
        push_pair(chip, first, 1, 19)
        push(block(chip, last), 10, up)
        push(block(chip, last), 12, down)
        push(block(chip, first), 2, up)
        push(block(chip, first), 6, down)
        push_pair(chip, last, 14, 20)

    def two():
        arrived(block(pair, first, 0), 1)
        arrived(block(pair, first, 1), 19)
        push(block(pair, first), 3, up)
        push(block(pair, first), 7, down)
        arrived(block(down, last), 10)
        push_pair(down, last, 15, 21)
        push(block(down, last, 0), 11, up)
        arrived(block(up, last), 12)
        push_pair(up, last, 16, 22)
        push(block(up, last, 1), 13, down)

    def three():
        arrived(block(down, first), 2)
        push(block(down, first, 0), 4, up)
        arrived(block(up, first), 6)
        push(block(up, first, 1), 8, down)
        arrived(block(far, last, 0), 11)
        push(block(far, last, 0), 17, pair)
        arrived(block(far, last, 1), 13)
        push(block(far, last, 1), 18, pair)
        arrived(block(other(down), first), 3)
        push(block(other(down), first, 0), 5, up)
        arrived(block(other(up), first), 7)
        push(block(other(up), first, 1), 9, down)

    def finish():
        arrived(block(far, first, 0), 4)
        arrived(block(far, first, 1), 8)
        arrived(block(other(far), first, 0), 5)
        arrived(block(other(far), first, 1), 9)
        for c, slot, across in ((pair, 14, 20), (other(down), 15, 21), (other(up), 16, 22)):
            arrived(block(c, last, 0), slot)
            arrived(block(c, last, 1), across)
        arrived(block(other(far), last, 0), 17)
        arrived(block(other(far), last, 1), 18)
        copy(x_ref.at[1 - core], o_ref.at[shard], 0).wait_send()
        for slot in (2, 3, 6, 7):
            copy(block(chip, first), block(chip, first), slot, pair).wait_send()
        for slot in (1, 4, 5, 8, 9, 19):
            copy(block(chip, first, 0), block(chip, first, 0), slot, pair).wait_send()
        for slot in (10, 12):
            copy(block(chip, last), block(chip, last), slot, pair).wait_send()
        for slot in (11, 13, 14, 15, 16, 17, 18, 20, 21, 22):
            copy(block(chip, last, 0), block(chip, last, 0), slot, pair).wait_send()

    return start, one, two, three, finish


START_SPLIT = 896


def start_kernel(
    x_ref, t_ref, in_hbm, gain_hbm, routes_hbm, logits_hbm, lift_hbm, code_hbm,
    o_ref, p_ref, g_ref, share_o, unit_ref,
    in_ref, gain_ref, routes_ref, logits_ref, lift_ref, code_ref, fetch_sem,
    w_ref, share_ref, local_sem, send_sem, recv_sem, s_part, r_part, s_x, r_x, s_y, r_y,
):
    with_parts = True
    rep, shard = place()
    half = x_ref.shape[0] // 2
    core = lax.rem(shard, 2)
    chip = shard // 2
    y = lax.rem(chip, 2)
    sib = shard + 1 - 2 * core
    pair = shard + 2 - 4 * y
    up = lax.rem(shard + 4, 16)
    down = lax.rem(shard + 12, 16)
    far = lax.rem(shard + 8, 16)
    first, last = pl.ds(0, START_SPLIT), pl.ds(START_SPLIT, D - START_SPLIT)
    rows, top, bottom = pl.ds(0, 2 * half), pl.ds(0, half), pl.ds(half, half)
    peers = [2 * lax.rem(chip + i, 8) + core for i in range(1, 8)]

    def other(block):
        return block + 2 - 4 * y

    greet(
        [(rep, sib)]
        + [(rep, p) for p in peers]
        + [(along_x(rep, 1), shard), (along_x(rep, 3), shard)]
    )
    fetches = [
        pltpu.make_async_copy(src, dst, fetch_sem.at[n])
        for n, (src, dst) in enumerate(
            (
                (in_hbm, in_ref),
                (gain_hbm, gain_ref),
                (routes_hbm, routes_ref),
                (logits_hbm, logits_ref),
                (lift_hbm.at[pl.ds((5 * (rep // 2)) // 2, 3)], lift_ref),
                (code_hbm, code_ref),
            )
        )
    ]
    for fetch in fetches:
        fetch.start()
    x_steps = x_gather(t_ref, g_ref, local_sem.at[2], s_x, r_x)
    y_steps = x_gather(share_ref, share_o, local_sem.at[3], s_y, r_y)
    own = pltpu.make_async_copy(x_ref, o_ref.at[shard], local_sem.at[0])
    own.start()
    sent = []

    def put(src, dst, slot, device):
        sent.append(send(src, dst, send_sem.at[len(sent)], recv_sem.at[slot], (rep, device)))

    def landed(ref, sem):
        landed_on(ref, sem, send_sem.at[0], (rep, sib))

    arrivals = {
        0: (pair, first, rows, ((2, up, rows), (6, down, rows))),
        9: (down, last, rows, ((14, pair, rows), (10, up, top))),
        1: (down, first, rows, ((3, up, top),)),
        11: (up, last, rows, ((15, pair, rows), (12, down, bottom))),
        5: (up, first, rows, ((7, down, bottom),)),
        13: (pair, last, rows, ()),
        2: (other(down), first, rows, ((4, up, top),)),
        6: (other(up), first, rows, ((8, down, bottom),)),
        10: (far, last, top, ((16, pair, top),)),
        12: (far, last, bottom, ((17, pair, bottom),)),
        3: (far, first, top, ()),
        7: (far, first, bottom, ()),
        14: (other(down), last, rows, ()),
        15: (other(up), last, rows, ()),
        4: (other(far), first, top, ()),
        8: (other(far), first, bottom, ()),
        16: (other(far), last, top, ()),
        17: (other(far), last, bottom, ()),
    }

    def arrive(slots):
        for slot in slots:
            block, columns, part, onward = arrivals[slot]
            ref = o_ref.at[block, part, columns]
            landed(ref, recv_sem.at[slot])
            for to_slot, device, rows_on in onward:
                ref_on = o_ref.at[block, rows_on, columns]
                put(ref_on, ref_on, to_slot, device)
            put(ref, ref, 19 + slot, sib)

    for columns, slots in ((first, (0, 1, 5)), (last, (13, 9, 11))):
        for slot, device in zip(slots, (pair, up, down)):
            put(x_ref.at[:, columns], o_ref.at[shard, :, columns], slot, device)
    put(x_ref, o_ref.at[shard], 18, sib)
    x_steps[0]()

    for fetch in fetches:
        fetch.wait()
    row, column = (lax.broadcasted_iota(jnp.int32, (96, 96), d) for d in (0, 1))
    gains = contract(jnp.where(row == column, 1.0, 0.0).astype(bf16), gain_ref[...], ((1,), (1,)))
    gains = jnp.concatenate([gains.astype(bf16), jnp.zeros((96, HEAD - 2), bf16)], 1)
    for c in range(CHIPS):
        w_ref[c] = jnp.concatenate(
            [
                in_ref[:, 192 * c : 192 * (c + 1)],
                gains,
                in_ref[:, 1536 + HEAD * c : 1536 + HEAD * (c + 1)],
                in_ref[:, 2048 + HEAD * c : 2048 + HEAD * (c + 1)],
            ],
            1,
        )
    parts = []
    if with_parts:
        mine = pltpu.make_async_copy(w_ref.at[chip], p_ref.at[shard], local_sem.at[1])
        mine.start()
        parts.append(
            send(w_ref.at[chip], p_ref.at[shard], s_part.at[0], r_part.at[0], (rep, sib))
        )
        for i in range(1, 8):
            c = lax.rem(chip + i, 8)
            parts.append(
                send(
                    w_ref.at[c], p_ref.at[shard], s_part.at[i], r_part.at[i], (rep, 2 * c + core)
                )
            )
    logits = logits_ref[...]
    gates = jnp.exp(logits - jnp.max(logits, 0, keepdims=True))
    gates = gates / jnp.sum(gates, 0, keepdims=True)
    ones = [
        jnp.sum(jnp.where(routes_ref[...] == e, gates, 0.0), 0, keepdims=True)
        for e in range(EXPERTS)
    ]
    shares = jnp.concatenate(ones + [jnp.zeros((128 - EXPERTS, OWN), f32)], 0).T
    lane = lax.broadcasted_iota(jnp.int32, (OWN, 128), 1)
    high = shares.astype(bf16)
    rest = pltpu.roll(shares - high.astype(f32), 16, 1)
    share_ref[...] = jnp.where(lane < 16, high, rest.astype(bf16))
    y_steps[0]()
    choose_units(lift_ref, code_ref, unit_ref)
    arrive((0, 9, 1, 11, 5, 13))
    x_steps[1]()
    y_steps[1]()
    arrive((2, 6, 10, 12))
    x_steps[2]()
    y_steps[2]()
    if with_parts:
        for i in range(1, 8):
            block = 2 * lax.rem(chip + 8 - i, 8) + core
            landed(p_ref.at[block], r_part.at[i])
            parts.append(
                send(
                    p_ref.at[block], p_ref.at[block], s_part.at[7 + i], r_part.at[7 + i], (rep, sib)
                )
            )
    arrive((3, 7, 14, 15, 4, 8, 16, 17))

    def twin(block):
        return block + 1 - 2 * core

    if with_parts:
        landed(p_ref.at[sib], r_part.at[0])
        for i in range(1, 8):
            landed(p_ref.at[twin(2 * lax.rem(chip + 8 - i, 8) + core)], r_part.at[7 + i])
        mine.wait()
    landed(o_ref.at[sib], recv_sem.at[18])
    for slot, (block, columns, part, _) in arrivals.items():
        landed(o_ref.at[twin(block), part, columns], recv_sem.at[19 + slot])
    x_steps[3]()
    y_steps[3]()
    for copy in sent + parts:
        copy.wait_send()
    own.wait()


def start(x, tokens, inward, gains, routes, logits, lifting, codes, collective):
    rows, columns = x.shape
    dma = pltpu.SemaphoreType.DMA
    gathered, parts, tokens, shares, units = pl.pallas_call(
        start_kernel,
        out_shape=(
            jax.ShapeDtypeStruct((SHARDS, rows, columns), bf16),
            jax.ShapeDtypeStruct((SHARDS, 96, 384), bf16),
            jax.ShapeDtypeStruct((PEERS, rows, columns), bf16),
            jax.ShapeDtypeStruct((PEERS, rows, 128), bf16),
            jax.ShapeDtypeStruct((2, 96, EXP), bf16),
        ),
        in_specs=[HBM] * 8,
        out_specs=(ANY,) * 4 + (VMEM,),
        scratch_shapes=[
            pltpu.VMEM(inward.shape, bf16),
            pltpu.VMEM(gains.shape, bf16),
            pltpu.VMEM(routes.shape, jnp.int32),
            pltpu.VMEM(logits.shape, f32),
            pltpu.VMEM((3,) + lifting.shape[1:], bf16),
            pltpu.VMEM(codes.shape, jnp.int32),
            dma((6,)),
            pltpu.VMEM((CHIPS, 96, 384), bf16),
            pltpu.VMEM((rows, 128), bf16),
            dma((4,)),
            dma((37,)),
            dma((37,)),
            dma((15,)),
            dma((15,)),
        ]
        + [dma((9,))] * 4,
        compiler_params=params(collective, 62 * 2**20),
        name="start",
    )(x, tokens, inward, gains, routes, logits, lifting, codes)
    return (
        gathered.reshape(SHARDS * rows, columns),
        parts,
        tokens.reshape(PEERS * rows, columns),
        shares.reshape(PEERS * rows, 128),
        units,
    )


def home_kernel(
    x_ref, half_ref, rows_ref, in_ref, gain_ref,
    mixed_ref, low_ref, down_ref, o_ref, w_ref,
    got, halves, apart, local_sem, s_x, r_x, s_w, r_w,
):
    rep, shard = place()
    core = lax.rem(shard, 2)
    chip = shard // 2
    sib = shard + 1 - 2 * core
    own_half = pltpu.make_async_copy(half_ref, halves.at[core], local_sem.at[0])
    own_half.start()
    fetch = pltpu.make_async_copy(rows_ref, apart, local_sem.at[4])
    fetch.start()
    holder = lax.rem(core + chip, 2)
    greet([(rep, 2 * lax.rem(chip + i, 8) + holder) for i in range(1, 8)] + [(rep, sib)])
    sent = [send(half_ref, halves.at[core], s_w, r_w, (rep, sib))]
    for i in range(1, 8):
        c = lax.rem(chip + i, 8)
        sent.append(
            send(
                x_ref.at[c], got.at[chip], s_x.at[i], r_x.at[i], (rep, 2 * c + lax.rem(c + core, 2))
            )
        )
    same = lax.rem(chip, 2) == 0

    @pl.when(same)
    def _():
        copy = pltpu.make_async_copy(x_ref.at[chip], got.at[chip], local_sem.at[1])
        copy.start()
        copy.wait()

    @pl.when(jnp.logical_not(same))
    def _():
        send(x_ref.at[chip], got.at[chip], s_x.at[0], r_x.at[0], (rep, sib)).wait_send()
        landed_on(got.at[chip], r_x.at[0], s_x.at[0], (rep, sib))

    fetch.wait()
    down_ref[...] = jnp.concatenate([apart[d][:FLAT] for d in range(SHARDS)], 0)
    own_half.wait()
    landed_on(halves.at[1 - core], r_w, s_w, (rep, sib))
    keeps = [pltpu.make_async_copy(halves, w_ref, local_sem.at[2])]
    keeps[0].start()
    for i in range(1, 8):
        landed_on(got.at[lax.rem(chip + 8 - i, 8)], r_x.at[i], s_x.at[0], (rep, sib))
    keeps.append(pltpu.make_async_copy(got, o_ref, local_sem.at[3]))
    keeps[1].start()
    rows = side_by_side(got)
    mixed = in_ref[...].astype(f32) + jnp.concatenate(
        [jnp.dot(rows, halves[k], preferred_element_type=f32) for k in range(2)], 1
    )
    mixed_ref[...] = mixed
    low_ref[...] = (mixed * inverse_root(mixed) * gain_ref[...]).astype(bf16)
    for copy in sent:
        copy.wait_send()
    for keep in keeps:
        keep.wait()


def home(attended, half, rows, x, gain, collective):
    dma = pltpu.SemaphoreType.DMA
    halves = (2, D, D // 2)
    return pl.pallas_call(
        home_kernel,
        out_shape=(
            jax.ShapeDtypeStruct((OWN, D), f32),
            jax.ShapeDtypeStruct((OWN, D), bf16),
            jax.ShapeDtypeStruct((HID, D), bf16),
            jax.ShapeDtypeStruct(attended.shape, bf16),
            jax.ShapeDtypeStruct(halves, bf16),
        ),
        in_specs=[HBM, HBM, HBM, VMEM, VMEM],
        out_specs=(VMEM, VMEM, VMEM, ANY, ANY),
        scratch_shapes=[
            pltpu.VMEM(attended.shape, bf16),
            pltpu.VMEM(halves, bf16),
            pltpu.VMEM(rows.shape, bf16),
            dma((5,)),
            dma((8,)),
            dma((8,)),
            dma,
            dma,
        ],
        compiler_params=params(collective, 62 * 2**20),
        name="attended_home",
    )(attended, half, rows, x, gain)


def away_kernel(
    du_ref, mixed_ref, y_ref, gain_ref, w_ref, a_ref, lift_ref, down_ref,
    dz_ref, part_ref, o_ref, lift_o, down_o,
    x_ref, lift_own, lift_land, down_own, down_land,
    local_sem, s_x, r_x, s_mate, r_mate, s_sib, r_sib,
):
    rep, shard = place()
    core = lax.rem(shard, 2)
    chip = shard // 2
    sib = shard + 1 - 2 * core
    mate = rep + 1 - 2 * lax.rem(rep, 2)
    greet(
        [(rep, 2 * c + lax.rem(c + core, 2)) for c in (lax.rem(chip + i, 8) for i in range(1, 8))]
        + [(rep, sib), (mate, shard)]
    )
    sent = []
    mates, loads = [], []
    for n, (src, own, land) in enumerate(
        ((lift_ref, lift_own, lift_land), (down_ref, down_own, down_land))
    ):
        mates.append(send(src, land, s_mate.at[n], r_mate.at[n], (mate, shard)))
        load = pltpu.make_async_copy(src, own, local_sem.at[n])
        load.start()
        loads.append(load)

    mixed = mixed_ref[...]
    inverse = inverse_root(mixed)
    dz = y_ref[...].astype(f32) + norm_back(du_ref[...] * gain_ref[...], mixed * inverse, inverse)
    dz_ref[...] = dz
    low = dz.astype(bf16)
    back = contract(low[:, : D // 2], w_ref[0], ((1,), (1,)))
    back = (back + contract(low[:, D // 2 :], w_ref[1], ((1,), (1,)))).astype(bf16)
    for c in range(CHIPS):
        x_ref[c] = back[:, c * 192 : (c + 1) * 192]
    for i in range(1, 8):
        c = lax.rem(chip + i, 8)
        sent.append(
            send(
                x_ref.at[c], o_ref.at[chip], s_x.at[i], r_x.at[i],
                (rep, 2 * c + lax.rem(core + chip, 2)),
            )
        )
    part = contract(side_by_side(a_ref), low, ((0,), (0,))).astype(bf16)
    for s in range(SHARDS):
        part_ref[s] = part[s * 96 : (s + 1) * 96]
    same = lax.rem(chip, 2) == 0

    @pl.when(same)
    def _():
        copy = pltpu.make_async_copy(x_ref.at[chip], o_ref.at[chip], local_sem.at[2])
        copy.start()
        copy.wait()

    @pl.when(jnp.logical_not(same))
    def _():
        send(x_ref.at[chip], o_ref.at[chip], s_x.at[0], r_x.at[0], (rep, sib)).wait_send()
        landed_on(o_ref.at[chip], r_x.at[0], s_x.at[0], (rep, sib))

    keeps, halves = [], []
    for n, (own, land, out) in enumerate(
        ((lift_own, lift_land, lift_o), (down_own, down_land, down_o))
    ):
        loads[n].wait()
        mates[n].wait_recv()
        for k in range(2):

            def add(t, _, own=own, land=land, k=k):
                at = pl.ds(pl.multiple_of(t * 16, 16), 16)
                own[k, at] = (own[k, at].astype(f32) + land[k, at].astype(f32)).astype(bf16)
                return 0

            lax.fori_loop(0, own.shape[1] // 16, add, 0)
        halves.append(
            send(own.at[1 - core], out.at[core], s_sib.at[n], r_sib.at[n], (rep, sib))
        )
        keep = pltpu.make_async_copy(own.at[core], out.at[core], local_sem.at[3 + n])
        keep.start()
        keeps.append(keep)
    for i in range(1, 8):
        landed_on(o_ref.at[lax.rem(chip + 8 - i, 8)], r_x.at[i], s_x.at[0], (rep, sib))
    for n, out in enumerate((lift_o, down_o)):
        landed_on(out.at[1 - core], r_sib.at[n], s_x.at[0], (rep, sib))
        keeps[n].wait()
    for copy in sent + mates + halves:
        copy.wait_send()


def grads_away(du, mixed, y, gain, outward_all, attended, lift, down, collective):
    dma = pltpu.SemaphoreType.DMA
    heads = (CHIPS, OWN, 192)
    return pl.pallas_call(
        away_kernel,
        out_shape=(
            jax.ShapeDtypeStruct((OWN, D), f32),
            jax.ShapeDtypeStruct((SHARDS, 96, D), bf16),
            jax.ShapeDtypeStruct(heads, bf16),
            jax.ShapeDtypeStruct(lift.shape, bf16),
            jax.ShapeDtypeStruct(down.shape, bf16),
        ),
        in_specs=[VMEM] * 6 + [ANY] * 2,
        out_specs=(VMEM, VMEM, ANY, ANY, ANY),
        scratch_shapes=[
            pltpu.VMEM(heads, bf16),
            pltpu.VMEM(lift.shape, bf16),
            pltpu.VMEM(lift.shape, bf16),
            pltpu.VMEM(down.shape, bf16),
            pltpu.VMEM(down.shape, bf16),
            dma((5,)),
            dma((8,)),
            dma((8,)),
        ]
        + [dma((2,))] * 4,
        compiler_params=params(collective, 62 * 2**20),
        name="grads_away",
    )(du, mixed, y, gain, outward_all, attended, lift, down)


PART = (48, 384)


def part_of(r):
    rows = pl.ds(pl.multiple_of((r // 4) * PART[0], PART[0]), PART[0])
    return rows, pl.ds(pl.multiple_of(lax.rem(r, 4) * PART[1], PART[1]), PART[1])


def tail_kernel(
    dq_ref, dkv_ref, in_ref, out_ref, w_hbm,
    dh_ref, in_sum, out_sum,
    w_ref, held_k, near_k, held_i, near_i, got_q, got_k, land_i, land_o, own_o, sum_i, sum_o,
    l_sem, s_q, r_q, s_nk, r_nk, s_ni, r_ni, s_k, r_k, s_ri, r_ri, s_ro, r_ro, s_gi, r_gi, s_go, r_go,
):
    rep, shard = place()
    core = lax.rem(shard, 2)
    chip = shard // 2
    sib = shard + 1 - 2 * core
    fetch = pltpu.make_async_copy(w_hbm, w_ref, l_sem.at[20])
    fetch.start()
    own = pltpu.make_async_copy(out_ref.at[part_of(rep)], own_o, l_sem.at[16])
    own.start()
    loads = {}
    for c in range(8):
        for name, src, held, base in (("i", in_ref, held_i, 0), ("k", dkv_ref, held_k, 8)):
            loads[name, c] = pltpu.make_async_copy(
                src.at[2 * c + core], held.at[c], l_sem.at[base + c]
            )
            loads[name, c].start()
    alone = rep == chip
    barrier = pltpu.get_barrier_semaphore()
    for device in [(rep, lax.rem(shard + i, 16)) for i in range(1, 16)] + [
        (lax.rem(rep + i, 8), shard) for i in range(1, 8)
    ]:
        pl.semaphore_signal(barrier, inc=1, device_id=device, device_id_type=MESH)
    for i in range(8):
        device = (chip, 2 * lax.rem(chip + i, 8) + core)
        if i:
            pl.semaphore_signal(barrier, inc=1, device_id=device, device_id_type=MESH)
        else:

            @pl.when(jnp.logical_not(alone))
            def _(device=device):
                pl.semaphore_signal(barrier, inc=1, device_id=device, device_id_type=MESH)

    pl.semaphore_wait(barrier, jnp.where(alone, 29, 30))

    sent = []

    def put(src, dst, s_sem, r_sem, device):
        copy = send(src, dst, s_sem, r_sem, device)
        sent.append(copy)
        return copy

    def landed(ref, sem):
        landed_on(ref, sem, s_q.at[0], (rep, sib))

    nears = {}
    for name, src, near, s_n, r_n in (
        ("i", in_ref, near_i, s_ni, r_ni),
        ("k", dkv_ref, near_k, s_nk, r_nk),
    ):
        for c in range(8):
            nears[name, c] = put(
                src.at[2 * c + 1 - core], near.at[c], s_n.at[c], r_n.at[c], (rep, sib)
            )
    for i in range(1, 8):
        to = lax.rem(rep + i, 8)
        put(out_ref.at[part_of(to)], land_o.at[i - 1], s_ro.at[i], r_ro.at[i], (to, shard))

    def add_near(name, held, near, rows):
        for c in range(8):
            nears[name, c].wait_recv()
            loads[name, c].wait()

        def add(t, _):
            at = pl.ds(pl.multiple_of(t * 32, 32), 32)
            for c in range(8):
                held[c, at] = (held[c, at].astype(f32) + near[c, at].astype(f32)).astype(bf16)
            return 0

        lax.fori_loop(0, rows // 32, add, 0)

    add_near("i", held_i, near_i, 96)
    for i in range(1, 8):
        to = lax.rem(rep + i, 8)
        put(held_i.at[to], land_i.at[i - 1], s_ri.at[i], r_ri.at[i], (to, shard))
    add_near("k", held_k, near_k, OWN)
    for i in range(1, 8):
        c = lax.rem(chip + i, 8)
        put(held_k.at[c], got_k.at[chip], s_k.at[i], r_k.at[i], (rep, 2 * c + core))
        put(
            dq_ref.at[c], got_q.at[chip], s_q.at[i], r_q.at[i],
            (rep, 2 * c + lax.rem(c + core, 2)),
        )
    got_k[chip] = held_k[chip]
    mine = lax.rem(chip, 2) == 0

    @pl.when(mine)
    def _():
        copy = pltpu.make_async_copy(dq_ref.at[chip], got_q.at[chip], l_sem.at[17])
        copy.start()
        copy.wait()

    @pl.when(jnp.logical_not(mine))
    def _():
        send(dq_ref.at[chip], got_q.at[chip], s_q.at[0], r_q.at[0], (rep, sib)).wait_send()

    own.wait()
    for land, total, r_x in ((land_o, sum_o, r_ro), (land_i, sum_i, r_ri)):
        for i in range(1, 8):
            landed(land.at[i - 1], r_x.at[i])

        def add(t, _, land=land, total=total):
            at = pl.ds(pl.multiple_of(t * 16, 16), 16)
            value = own_o[at] if land is land_o else held_i[rep, at]
            value = value.astype(f32)
            for i in range(7):
                value = value + land[i, at].astype(f32)
            total[at] = value.astype(bf16)
            return 0

        lax.fori_loop(0, total.shape[0] // 16, add, 0)
        if land is land_o:
            keep = pltpu.make_async_copy(sum_o, out_sum.at[part_of(rep)], l_sem.at[18])
            keep.start()
            for i in range(1, 8):
                to = lax.rem(rep + i, 8)
                put(sum_o, out_sum.at[part_of(rep)], s_go.at[i], r_go.at[i], (to, shard))
    owner = 2 * rep + core
    for i in range(1, 8):
        put(sum_i, in_sum.at[chip], s_gi.at[i], r_gi.at[chip], (lax.rem(rep + i, 8), owner))

    @pl.when(alone)
    def _():
        copy = pltpu.make_async_copy(sum_i, in_sum.at[chip], l_sem.at[19])
        copy.start()
        copy.wait()

    @pl.when(jnp.logical_not(alone))
    def _():
        send(sum_i, in_sum.at[chip], s_gi.at[0], r_gi.at[chip], (rep, owner)).wait_send()

    @pl.when(jnp.logical_not(mine))
    def _():
        landed(got_q.at[chip], r_q.at[0])

    for i in range(1, 8):
        landed(got_q.at[lax.rem(chip + 8 - i, 8)], r_q.at[i])
        landed(got_k.at[lax.rem(chip + 8 - i, 8)], r_k.at[i])
    joined = jnp.concatenate(
        [got_q[c] for c in range(CHIPS)]
        + [got_k[c][:, :HEAD] for c in range(CHIPS)]
        + [got_k[c][:, HEAD:] for c in range(CHIPS)],
        1,
    )
    fetch.wait()
    dh_ref[...] = contract(joined, w_ref[...], ((1,), (1,)))

    for i in range(1, 8):
        landed(out_sum.at[part_of(lax.rem(rep + 8 - i, 8))], r_go.at[i])
    for j in range(8):

        @pl.when(jnp.logical_not(jnp.logical_and(alone, chip == j)))
        def _(j=j):
            landed(in_sum.at[j], r_gi.at[j])

    keep.wait()
    for copy in sent:
        copy.wait_send()


def tail(dq, dkv, inward_part, outward_own, inward_all, collective):
    dma = pltpu.SemaphoreType.DMA
    return pl.pallas_call(
        tail_kernel,
        out_shape=(
            jax.ShapeDtypeStruct((OWN, D), f32),
            jax.ShapeDtypeStruct((CHIPS, 96, 320), bf16),
            jax.ShapeDtypeStruct((96, D), bf16),
        ),
        in_specs=[ANY, ANY, ANY, ANY, HBM],
        out_specs=(VMEM, ANY, ANY),
        scratch_shapes=[
            pltpu.VMEM(inward_all.shape, bf16),
            pltpu.VMEM((8, OWN, 128), bf16),
            pltpu.VMEM((8, OWN, 128), bf16),
            pltpu.VMEM((8, 96, 320), bf16),
            pltpu.VMEM((8, 96, 320), bf16),
            pltpu.VMEM((8, OWN, 192), bf16),
            pltpu.VMEM((8, OWN, 128), bf16),
            pltpu.VMEM((7, 96, 320), bf16),
            pltpu.VMEM((7,) + PART, bf16),
            pltpu.VMEM(PART, bf16),
            pltpu.VMEM((96, 320), bf16),
            pltpu.VMEM(PART, bf16),
            dma((21,)),
        ]
        + [dma((8,))] * 16,
        compiler_params=params(collective, 62 * 2**20),
        name="tail",
    )(dq, dkv, inward_part, outward_own, inward_all)


def swap_halves(values):
    lanes = values.shape[1]
    lane = lax.broadcasted_iota(jnp.int32, values.shape, 1)
    ahead = pltpu.roll(values, lanes - HEAD // 2, 1)
    behind = pltpu.roll(values, HEAD // 2, 1)
    return jnp.where(lax.rem(lane, HEAD) < HEAD // 2, ahead, behind)


def project_step(i, core, x_ref, w_ref, g_ref, cos_ref, sin_ref, q_ref, k_ref, v_ref, u_ref):
    stream = x_ref[...].astype(f32)
    u_ref[...] = (stream * inverse_root(stream) * g_ref[...]).astype(bf16)
    first = pl.multiple_of(lax.rem(i + core, 2) * OWN, OWN)
    own = pl.ds(first, OWN)
    queries = jnp.dot(u_ref[own, :], w_ref[:, :256], preferred_element_type=f32)
    cos, sin = cos_ref[own, :], sin_ref[own, :]
    cos, sin = jnp.concatenate([cos, cos], 1), jnp.concatenate([sin, sin], 1)
    turned = (queries * cos + swap_halves(queries) * sin).astype(bf16)
    turned = turned * jnp.bfloat16(HEAD**-0.5)
    for r in range(GROUP):
        q_ref[i, r * OWN : (r + 1) * OWN, :] = turned[:, r * HEAD : (r + 1) * HEAD]
    pairs = jnp.dot(u_ref[...], w_ref[:, 256:], preferred_element_type=f32)
    keys = pairs * cos_ref[...] + swap_halves(pairs) * sin_ref[...]
    rows = pl.ds(pl.multiple_of(i * KEYS, KEYS), KEYS)
    k_ref[rows, :] = keys[:, :HEAD].astype(bf16)
    lane = lax.broadcasted_iota(jnp.int32, pairs.shape, 1)
    v_ref[rows, :] = jnp.where(lane < HEAD, pltpu.roll(pairs, HEAD, 1), 1.0).astype(bf16)


def contract(a, b, dims, precision=None):
    return lax.dot_general(
        a, b, ((dims[0], dims[1]), ((), ())), preferred_element_type=f32, precision=precision
    )


def attend_kernel(
    x_ref, w_ref, g_ref, cos_ref, sin_ref, b_ref, d_ref, f_ref,
    q_ref, k_ref, v_ref, u_ref, o_ref, l_ref, bo_ref, do_ref, fo_ref,
    local_sem, s_sem, r_sem, s_low, r_low, s_out, r_out,
):
    i = pl.program_id(0)
    core = lax.rem(lax.axis_index("shard"), 2)
    steps = ring_spread(b_ref, bo_ref, 16, local_sem.at[0], s_sem, r_sem)
    low_steps = ring_spread(d_ref, do_ref, 16, local_sem.at[1], s_low, r_low)
    out_steps = ring_spread(f_ref, fo_ref, 16, local_sem.at[2], s_out, r_out)

    @pl.when(i == 0)
    def _():
        rep, shard = place()
        y = lax.rem(shard // 2, 2)
        greet(
            [(rep, shard + 1 - 2 * core), (rep, shard + 2 - 4 * y)]
            + [(rep + 1 - 2 * lax.rem(rep, 2), shard + 2 - 4 * y)]
            + [(rep, lax.rem(shard + 4, 16)), (rep, lax.rem(shard + 12, 16))]
        )
        out_steps[0]()
        steps[0]()
        low_steps[0]()

    @pl.when(i == 1)
    def _():
        out_steps[1]()
        steps[1]()

    @pl.when(i == 4)
    def _():
        low_steps[1]()

    @pl.when(i == 9)
    def _():
        out_steps[2]()

    @pl.when(i == 11)
    def _():
        steps[2]()

    @pl.when(i == 13)
    def _():
        out_steps[3]()
        low_steps[2]()

    @pl.when(i == 14)
    def _():
        steps[3]()

    @pl.when(i == 15)
    def _():
        low_steps[3]()

    @pl.when(i < BLOCKS)
    def _():
        project_step(i, core, x_ref, w_ref, g_ref, cos_ref, sin_ref, q_ref, k_ref, v_ref, u_ref)

    @pl.when(i >= BLOCKS)
    def _():
        attend_step(i - BLOCKS, core, q_ref, k_ref, v_ref, o_ref, l_ref)

    @pl.when(i == 2 * BLOCKS - 1)
    def _():
        out_steps[4]()
        steps[4]()
        low_steps[4]()


def attend_step(i, core, q_ref, k_ref, v_ref, o_ref, l_ref):
    shift = lax.rem(i + core, 2) * OWN
    q = q_ref[i]

    def step(c, carry, last=False):
        top, total = carry
        at = pl.ds(pl.multiple_of(c * KEYS, KEYS), KEYS)
        scores = contract(q, k_ref[at, :], ((1,), (1,)))
        if last:
            row = lax.broadcasted_iota(jnp.int32, (OWN, KEYS), 0)
            column = lax.broadcasted_iota(jnp.int32, (OWN, KEYS), 1)
            bias = jnp.where(column <= row + shift, 0.0, -1e30)
            scores = scores + jnp.concatenate([bias] * GROUP, 0)
        high = jnp.maximum(top, jnp.max(scores, 1, keepdims=True))
        prob = jnp.exp(scores - high).astype(bf16)
        total = total * jnp.exp(top - high) + jnp.dot(
            prob, v_ref[at, :], preferred_element_type=f32
        )
        return high, total

    carry = (jnp.full((ROWS, 1), -1e30, f32), jnp.zeros((ROWS, 128), f32))
    carry = lax.fori_loop(0, i, step, carry)
    top, total = step(i, carry, True)
    weight = total[:, HEAD : HEAD + 1]
    result = (total[:, :HEAD] / weight).astype(bf16)
    o_ref[0] = jnp.concatenate([result[r * OWN : (r + 1) * OWN] for r in range(GROUP)], 1)
    column = lax.broadcasted_iota(jnp.int32, (8, 8), 1)
    l_ref[0] = contract(
        jnp.where(column == 0, 1.0, 0.0).astype(f32),
        jnp.broadcast_to(top + jnp.log(weight), (ROWS, 8)),
        ((1,), (1,)),
        lax.Precision.HIGHEST,
    )


def attend(x_all, weight, gain, cos, sin, units, low, half, collective):
    dma = pltpu.SemaphoreType.DMA
    whole = lambda i: (0, 0)
    early = lambda i: (jnp.minimum(i, BLOCKS - 1), 0)
    late = lambda i: (jnp.maximum(i - BLOCKS, 0), 0, 0)
    return pl.pallas_call(
        attend_kernel,
        grid=(2 * BLOCKS,),
        in_specs=[
            pl.BlockSpec((KEYS, D), early),
            pl.BlockSpec((D, 384), whole),
            pl.BlockSpec((1, D), whole),
            pl.BlockSpec((KEYS, 128), early),
            pl.BlockSpec((KEYS, 128), early),
            ANY,
            ANY,
            ANY,
        ],
        out_specs=(
            pl.BlockSpec((BLOCKS, ROWS, HEAD), lambda i: (0, 0, 0)),
            pl.BlockSpec((SEQ, HEAD), whole),
            pl.BlockSpec((SEQ, 128), whole),
            pl.BlockSpec((KEYS, D), early),
            pl.BlockSpec((1, OWN, GROUP * HEAD), late),
            pl.BlockSpec((1, 8, ROWS), late),
            ANY,
            ANY,
            ANY,
        ),
        out_shape=(
            jax.ShapeDtypeStruct((BLOCKS, ROWS, HEAD), bf16),
            jax.ShapeDtypeStruct((SEQ, HEAD), bf16),
            jax.ShapeDtypeStruct((SEQ, 128), bf16),
            jax.ShapeDtypeStruct((SEQ, D), bf16),
            jax.ShapeDtypeStruct((BLOCKS, OWN, GROUP * HEAD), bf16),
            jax.ShapeDtypeStruct((BLOCKS, 8, ROWS), f32),
            jax.ShapeDtypeStruct((SHARDS,) + units.shape[1:], bf16),
            jax.ShapeDtypeStruct((SHARDS,) + low.shape[1:], bf16),
            jax.ShapeDtypeStruct((SHARDS,) + half.shape[1:], bf16),
        ),
        scratch_shapes=[dma((3,))] + [dma((23,))] * 6,
        compiler_params=params(collective, 62 * 2**20),
        name="attend",
    )(x_all, weight, gain, cos, sin, units, low, half)


def attend_back_kernel(
    q_ref, k_ref, v_ref, g_ref, a_ref, l_ref, cos_ref, sin_ref, qcos_ref, qsin_ref, u_hbm, part_ref,
    lift_ref, down_ref, dq_ref, dkv_ref, in_ref, part_out, lift_out, down_out,
    u_ref, u_sem, dk, dv, dq, total_q, held, near, landed, local_sem, s_sem, r_sem, h_sem, s_near, r_near, s_far, r_far,
):
    i = pl.program_id(0)
    rep, shard = place()
    core = lax.rem(shard, 2)
    chip = shard // 2
    sib = shard + 1 - 2 * core
    shift = lax.rem(i + core, 2) * OWN
    x = rep // 2
    kept = [
        (n, src, dst)
        for n, (src, dst) in enumerate(((lift_ref, lift_out), (down_ref, down_out)))
    ]

    def copy_same(n, src, dst):
        return pltpu.make_async_copy(src, dst.at[pl.ds(2 * x, 2)], local_sem.at[n])

    x_up, x_down, x_far = (lax.rem(x + d, 4) for d in (1, 3, 2))

    def copy_x(n, src, dst, way):
        return pltpu.make_async_remote_copy(
            src_ref=src,
            dst_ref=dst,
            send_sem=s_sem.at[n, way],
            recv_sem=r_sem.at[n, way],
            device_id=(along_x(rep, 3 if way % 2 else 1), shard),
            device_id_type=MESH,
        )

    def two_of(dst, at):
        return dst.at[pl.ds(2 * at, 2)]

    def copy_near(j):
        return pltpu.make_async_remote_copy(
            src_ref=part_ref.at[2 * lax.rem(chip + j, 8) + 1 - core],
            dst_ref=near.at[j],
            send_sem=s_near.at[j],
            recv_sem=r_near.at[j],
            device_id=(rep, sib),
            device_id_type=MESH,
        )

    def copy_own(j):
        return pltpu.make_async_copy(
            part_ref.at[2 * lax.rem(chip + j, 8) + core], held.at[j], h_sem.at[j]
        )

    def copy_far(j):
        return pltpu.make_async_remote_copy(
            src_ref=held.at[j],
            dst_ref=landed.at[j - 1],
            send_sem=s_far.at[j],
            recv_sem=r_far.at[j],
            device_id=(rep, 2 * lax.rem(chip + j, 8) + core),
            device_id_type=MESH,
        )

    @pl.when(i == 0)
    def _():
        greet(
            [(rep, sib)]
            + [(rep, 2 * lax.rem(chip + n, 8) + core) for n in range(1, 8)]
            + [(along_x(rep, dx), shard) for dx in (1, 3)]
        )
        for j in range(8):
            copy_near(j).start()
            copy_own(j).start()
        for n, src, dst in kept:
            copy_same(n, src, dst).start()
            copy_x(n, src, two_of(dst, x), 0).start()
            copy_x(n, src, two_of(dst, x), 1).start()
        pltpu.make_async_copy(u_hbm, u_ref, u_sem).start()
        total_q[...] = jnp.zeros_like(total_q)
        dk[...] = jnp.zeros_like(dk)
        dv[...] = jnp.zeros_like(dv)

    @pl.when(i == 6)
    def _():
        for n, src, dst in kept:
            ref = two_of(dst, x_down)
            copy_x(n, ref, ref, 0).wait_recv()
            ref = dst.at[2 * x_down]
            copy_x(n, ref, ref, 2).start()
            ref = two_of(dst, x_up)
            copy_x(n, ref, ref, 1).wait_recv()
            ref = dst.at[2 * x_up + 1]
            copy_x(n, ref, ref, 3).start()

    @pl.when(i == 3)
    def _():
        for j in range(8):
            copy_near(j).wait_recv()
            copy_own(j).wait()

            def add(t, _, j=j):
                at = pl.ds(pl.multiple_of(t * 32, 32), 32)
                held[j, at] = (held[j, at].astype(f32) + near[j, at].astype(f32)).astype(bf16)
                return 0

            lax.fori_loop(0, 3, add, 0)
            if j:
                copy_far(j).start()

    q = q_ref[0]
    grad = jnp.concatenate([g_ref[0][:, r * HEAD : (r + 1) * HEAD] for r in range(GROUP)], 0)
    dq[...] = jnp.zeros_like(dq)
    lse = l_ref[0][:1]
    lane = lax.broadcasted_iota(jnp.int32, (8, GROUP * HEAD), 1)
    row = lax.broadcasted_iota(jnp.int32, (8, GROUP * HEAD), 0)
    sums = contract(
        jnp.where(lane // HEAD == row, 1.0, 0.0).astype(f32),
        g_ref[0].astype(f32) * a_ref[0].astype(f32),
        ((1,), (1,)),
        lax.Precision.HIGHEST,
    )
    delta = jnp.concatenate([sums[r : r + 1] for r in range(GROUP)], 1)

    def step(c, _, last=False):
        at = pl.ds(pl.multiple_of(c * KEYS, KEYS), KEYS)
        keys = k_ref[at, :]
        scores = contract(keys, q, ((1,), (1,)))
        if last:
            key = lax.broadcasted_iota(jnp.int32, (KEYS, OWN), 0)
            token = lax.broadcasted_iota(jnp.int32, (KEYS, OWN), 1)
            bias = jnp.where(key <= token + shift, 0.0, -1e30)
            scores = scores + jnp.concatenate([bias] * GROUP, 1)
        prob = jnp.exp(scores - lse)
        back = contract(v_ref[at, :HEAD], grad, ((1,), (1,)))
        slope = (prob * (back - delta)).astype(bf16)
        dv[at, :] += jnp.dot(prob.astype(bf16), grad, preferred_element_type=f32)
        dk[at, :] += jnp.dot(slope, q, preferred_element_type=f32)
        dq[...] += contract(keys, slope, ((0,), (0,)))
        return 0

    def two_steps(c, _):
        step(2 * c, 0)
        return step(2 * c + 1, 0)

    lax.fori_loop(0, i // 2, two_steps, 0)

    @pl.when(lax.rem(i, 2) == 1)
    def _():
        step(i - 1, 0)

    step(i, 0, True)
    turned = dq[...].T
    wide = jnp.concatenate(
        [turned[r * OWN : (r + 1) * OWN, :] for r in range(GROUP)] + [jnp.zeros((OWN, HEAD), f32)], 1
    )
    wide = wide * (HEAD**-0.5)
    cos, sin = qcos_ref[...], qsin_ref[...]
    cos, sin = jnp.concatenate([cos, cos], 1), jnp.concatenate([sin, sin], 1)
    wide = wide * cos - swap_halves(wide) * sin
    wide = wide[:, : GROUP * HEAD].astype(bf16)
    dq_ref[0] = wide

    @pl.when(i == 0)
    def _():
        pltpu.make_async_copy(u_hbm, u_ref, u_sem).wait()

    mine = pl.ds(pl.multiple_of(i * KEYS + shift, OWN), OWN)
    total_q[...] += contract(wide, u_ref[mine, :], ((0,), (0,)))

    @pl.when(i == BLOCKS - 1)
    def _():
        def turn(c, _):
            at = pl.ds(pl.multiple_of(c * OWN, OWN), OWN)
            both = jnp.concatenate([dk[at, :], dv[at, :]], 1)
            lane = lax.broadcasted_iota(jnp.int32, both.shape, 1)
            turned = both * cos_ref[at, :] - swap_halves(both) * sin_ref[at, :]
            dkv_ref[at, :] = jnp.where(lane < HEAD, turned, both).astype(bf16)
            return 0

        lax.fori_loop(0, SHARDS, turn, 0)
        def add_pairs(c, both):
            at = pl.ds(pl.multiple_of(c * 768, 768), 768)
            return both + contract(dkv_ref[at, :], u_ref[at, :], ((0,), (0,)))

        both = lax.fori_loop(0, SEQ // 768, add_pairs, jnp.zeros((128, D), f32))
        both = jnp.concatenate([total_q[...], both], 0).T.astype(bf16)
        for s in range(SHARDS):
            in_ref[s] = both[s * 96 : (s + 1) * 96]

        for j in range(1, 8):
            copy_far(j).wait_recv()

        def add(t, _):
            at = pl.ds(pl.multiple_of(t * 32, 32), 32)
            total = held[0, at].astype(f32)
            for j in range(7):
                total = total + landed[j, at].astype(f32)
            part_out[at] = total.astype(bf16)
            return 0

        lax.fori_loop(0, 3, add, 0)
        for n, src, dst in kept:
            copy_same(n, src, dst).wait()
            for k in range(2):
                ref = dst.at[2 * x_far + k]
                copy_x(n, ref, ref, 2 + k).wait_recv()
            for way in range(4):
                ref = two_of(dst, x) if way < 2 else dst.at[2 * x]
                copy_x(n, ref, ref, way).wait_send()
        for j in range(8):
            copy_near(j).wait_send()
            if j:
                copy_far(j).wait_send()


def attend_back(q, k, v, grad, attended, lse, cos, sin, u_all, part, lift, down, collective):
    def own(i):
        return (2 * i + lax.rem(i + lax.rem(lax.axis_index("shard"), 2), 2), 0)

    whole = lambda i: (0, 0)
    block = lambda i: (i, 0, 0)
    return pl.pallas_call(
        attend_back_kernel,
        grid=(BLOCKS,),
        in_specs=[
            pl.BlockSpec((1, ROWS, HEAD), block),
            pl.BlockSpec((SEQ, HEAD), whole),
            pl.BlockSpec((SEQ, 128), whole),
            pl.BlockSpec((1, OWN, GROUP * HEAD), block),
            pl.BlockSpec((1, OWN, GROUP * HEAD), block),
            pl.BlockSpec((1, 8, ROWS), block),
            pl.BlockSpec((SEQ, 128), whole),
            pl.BlockSpec((SEQ, 128), whole),
            pl.BlockSpec((OWN, 128), own),
            pl.BlockSpec((OWN, 128), own),
            HBM,
            ANY,
            ANY,
            ANY,
        ],
        out_specs=(
            pl.BlockSpec((1, OWN, GROUP * HEAD), block),
            pl.BlockSpec((SEQ, 128), whole),
            pl.BlockSpec((SHARDS, 96, 320), lambda i: (0, 0, 0)),
            pl.BlockSpec(part.shape[1:], whole),
            ANY,
            ANY,
        ),
        out_shape=(
            jax.ShapeDtypeStruct((BLOCKS, OWN, GROUP * HEAD), bf16),
            jax.ShapeDtypeStruct((SEQ, 128), bf16),
            jax.ShapeDtypeStruct((SHARDS, 96, 320), bf16),
            jax.ShapeDtypeStruct(part.shape[1:], bf16),
            jax.ShapeDtypeStruct((PEERS,) + lift.shape[1:], bf16),
            jax.ShapeDtypeStruct((PEERS,) + down.shape[1:], bf16),
        ),
        scratch_shapes=[
            pltpu.VMEM((SEQ, D), bf16),
            pltpu.SemaphoreType.DMA,
            pltpu.VMEM((SEQ, HEAD), f32),
            pltpu.VMEM((SEQ, HEAD), f32),
            pltpu.VMEM((HEAD, ROWS), f32),
            pltpu.VMEM((GROUP * HEAD, D), f32),
            pltpu.VMEM((8,) + part.shape[1:], bf16),
            pltpu.VMEM((8,) + part.shape[1:], bf16),
            pltpu.VMEM((7,) + part.shape[1:], bf16),
            pltpu.SemaphoreType.DMA((2,)),
            pltpu.SemaphoreType.DMA((2, 4)),
            pltpu.SemaphoreType.DMA((2, 4)),
        ]
        + [pltpu.SemaphoreType.DMA((8,))] * 5,
        compiler_params=params(collective, 62 * 2**20),
        name="attend_back",
    )(q, k, v, grad, attended, lse, cos, sin, cos, sin, u_all, part, lift, down)


def distance(i):
    return jnp.where(i == 0, 0, jnp.where(i == 1, 1, jnp.where(i == 2, 3, 2)))


def experts_kernel(
    x_hbm, y_ref, c_ref, wl_hbm, wd_hbm, e_ref,
    du_o, out_o, lift_o, down_o,
    u, wl, wd, gl, acc, down, part, near, land, total,
    la, lb, lc, ld, da, db, dc, dd,
    down_sum, l_sem, s_g, r_g, s_near, r_near, s_land, r_land, s_one, r_one, s_two, r_two,
):
    i = pl.program_id(0)
    rep, shard = place()
    core = lax.rem(shard, 2)
    chip = shard // 2
    y = lax.rem(chip, 2)
    z = chip // 2
    x = rep // 2
    sib = shard + 1 - 2 * core
    pair = shard + 2 - 4 * y

    def remote(src, dst, s_sem, r_sem, device):
        return pltpu.make_async_remote_copy(
            src_ref=src, dst_ref=dst, send_sem=s_sem, recv_sem=r_sem,
            device_id=device, device_id_type=MESH,
        )

    def tokens(dx, k, low=0, size=OWN):
        return u.at[lax.rem(x + dx, 4), pl.ds(pl.multiple_of(OWN * k + low, 96), size)]

    half = OWN // 2
    ups, downs, sibs = (along_x(rep, 1), shard), (along_x(rep, 3), shard), (rep, sib)
    slots = {
        0: (tokens(3, core), None, ups),
        1: (tokens(1, core), None, downs),
        2: (tokens(2, core, 0, half), tokens(3, core, 0, half), ups),
        3: (tokens(2, core, half, half), tokens(1, core, half, half), downs),
        4: (tokens(0, 1 - core), None, sibs),
        5: (tokens(3, 1 - core), tokens(3, core), sibs),
        6: (tokens(1, 1 - core), tokens(1, core), sibs),
        7: (tokens(2, 1 - core, 0, half), tokens(2, core, 0, half), sibs),
        8: (tokens(2, 1 - core, half, half), tokens(2, core, half, half), sibs),
    }

    def gather_send(n):
        _, out, device = slots[n]
        src, dst = (x_hbm, tokens(0, core)) if out is None else (out, out)
        return remote(src, dst, s_g.at[n], r_g.at[n], device)

    def gather_arrival(n):
        ref = slots[n][0]
        remote(ref, ref, s_g.at[n], r_g.at[n], sibs).wait_recv()

    own_tokens = pltpu.make_async_copy(x_hbm, tokens(0, core), l_sem.at[0])
    fetch_wl = pltpu.make_async_copy(wl_hbm, wl, l_sem.at[1])
    fetch_wd = pltpu.make_async_copy(wd_hbm, wd, l_sem.at[2])

    def rows(k):
        return pl.ds(pl.multiple_of(OWN * k, OWN), OWN)

    def near_copy(n, t):
        return remote(
            part.at[t, n, rows(1 - core)], near.at[t, n], s_near.at[t, n], r_near.at[t, n], sibs
        )

    def land_copy(n, t):
        return remote(
            part.at[t, n, rows(core)], land.at[t - 1, n], s_land.at[t, n], r_land.at[t, n],
            (along_x(rep, distance(t)), shard),
        )

    def pass_on(t):
        for n in range(2):
            near_copy(n, t).wait_recv()

            def add(r, _, n=n):
                at = pl.ds(pl.multiple_of(r * 32, 32), 32)
                mine = pl.ds(pl.multiple_of(OWN * core + r * 32, 32), 32)
                part[t, n, mine] = (
                    part[t, n, mine].astype(f32) + near[t, n, at].astype(f32)
                ).astype(bf16)
                return 0

            lax.fori_loop(0, OWN // 32, add, 0)

            @pl.when(t > 0)
            def _(n=n):
                land_copy(n, t).start()

    grads = ((wl, la, lb, lc, ld, lift_o, 192), (wd, da, db, dc, dd, down_sum, 2 * FLAT))

    def piece(m, dz, dy, columns):
        buffer, size = grads[m][0], grads[m][6]
        c = 2 * lax.rem(z + dz, 4) + (1 - y if dy else y)
        return buffer.at[pl.ds(pl.multiple_of(size * c, size), size), columns]

    def columns_of(m):
        width = grads[m][0].shape[1] // 2
        return pl.ds(0, width), pl.ds(width, width)

    def to_z(dz):
        return (rep, 4 * lax.rem(z + dz, 4) + 2 * y + core)

    def one_a(m, dz):
        return remote(
            piece(m, dz, 1, columns_of(m)[0]), grads[m][1].at[dz], s_one.at[m, 0, dz], r_one.at[m, 0, dz],
            (rep, pair),
        )

    def one_b(m, dz, dy):
        j = 2 * dz + dy
        return remote(
            piece(m, dz, dy, columns_of(m)[1]), grads[m][2].at[j - 2], s_one.at[m, 1, j], r_one.at[m, 1, j],
            to_z(dz),
        )

    def two_a(m, dz):
        return remote(
            piece(m, dz, 0, columns_of(m)[0]), grads[m][3].at[dz - 1], s_two.at[m, dz], r_two.at[m, dz],
            to_z(dz),
        )

    def two_b(m):
        return remote(
            piece(m, 0, 1, columns_of(m)[1]), grads[m][4], s_two.at[m, 0], r_two.at[m, 0], (rep, pair)
        )

    def first_sums(m):
        land_a, land_b, size = grads[m][1], grads[m][2], grads[m][6]
        first, last = columns_of(m)
        for dz in (2, 1, 3, 0):
            one_a(m, dz).wait_recv()
            mine = piece(m, dz, 0, first)

            def add(t, _, mine=mine, dz=dz):
                at = pl.ds(pl.multiple_of(t * 16, 16), 16)
                mine[at] = (mine[at].astype(f32) + land_a[dz, at].astype(f32)).astype(bf16)
                return 0

            lax.fori_loop(0, size // 16, add, 0)
            if dz:
                two_a(m, dz).start()
        for dy in (1, 0):
            for dz in (1, 2, 3):
                one_b(m, dz, dy).wait_recv()
            mine = piece(m, 0, dy, last)

            def add(t, _, mine=mine, dy=dy):
                at = pl.ds(pl.multiple_of(t * 16, 16), 16)
                value = mine[at].astype(f32)
                for dz in (1, 2, 3):
                    value = value + land_b[2 * dz + dy - 2, at].astype(f32)
                mine[at] = value.astype(bf16)
                return 0

            lax.fori_loop(0, size // 16, add, 0)
            if dy:
                two_b(m).start()

    def last_sums(m):
        land_c, land_d, out, size = grads[m][3], grads[m][4], grads[m][5], grads[m][6]
        first, last = columns_of(m)
        for dz in (1, 2, 3):
            two_a(m, dz).wait_recv()
        two_b(m).wait_recv()
        mine_a, mine_b = piece(m, 0, 0, first), piece(m, 0, 0, last)

        def add(t, _):
            at = pl.ds(pl.multiple_of(t * 16, 16), 16)
            value = mine_a[at].astype(f32)
            for dz in (1, 2, 3):
                value = value + land_c[dz - 1, at].astype(f32)
            out[at, first] = value.astype(bf16)
            out[at, last] = (mine_b[at].astype(f32) + land_d[at].astype(f32)).astype(bf16)
            return 0

        lax.fori_loop(0, size // 16, add, 0)

    @pl.when(i == 0)
    def _():
        fetch_wl.start()
        fetch_wd.start()
        own_tokens.start()
        greet(
            [(rep, sib), (rep, pair)]
            + [to_z(dz) for dz in (1, 2, 3)]
            + [(along_x(rep, dx), shard) for dx in (1, 2, 3)]
        )
        for n in (4, 0, 1):
            gather_send(n).start()
        down[...] = jnp.zeros_like(down)
        fetch_wl.wait()
        fetch_wd.wait()
        own_tokens.wait()
        gather_arrival(4)

    @pl.when(i == 1)
    def _():
        gather_arrival(1)
        gather_send(6).start()
        gather_send(3).start()
        gather_arrival(0)
        gather_send(5).start()
        gather_send(2).start()
        gather_arrival(6)

    @pl.when(i == 2)
    def _():
        gather_arrival(2)
        gather_send(7).start()
        gather_arrival(3)
        gather_send(8).start()
        gather_arrival(5)

    @pl.when(i == 3)
    def _():
        gather_arrival(7)
        gather_arrival(8)

    @pl.when(i > 0)
    def _():
        pass_on(i - 1)

    @pl.when(i < 4)
    def _():
        h, dy = u[lax.rem(x + distance(i), 4)], y_ref[...]
        lifted = jnp.dot(h, wl[...], preferred_element_type=f32)
        back = contract(dy, wd[...], ((1,), (1,)))
        share = jnp.dot(c_ref[...], e_ref[...], preferred_element_type=f32)
        gate, raised = lifted[:, :HID], lifted[:, HID:]
        s = jax.nn.sigmoid(gate)
        swish = gate * s
        act = (share * swish * raised).astype(bf16)
        back = back * share
        grad_gate = back * raised * s * (1.0 + gate * (1.0 - s))
        gl[i] = jnp.concatenate([grad_gate, back * swish], 1).astype(bf16)
        part[i, 0] = contract(gl[i], wl[...], ((1,), (1,))).astype(bf16)
        near_copy(0, i).start()
        part[i, 1] = jnp.dot(act, wd[...], preferred_element_type=f32).astype(bf16)
        near_copy(1, i).start()
        down[...] += contract(act, dy, ((0,), (0,)))

    @pl.when(i == 4)
    def _():
        wd[...] = down[...].astype(bf16)
        for dz in (2, 1, 3, 0):
            one_a(1, dz).start()
            if dz:
                one_b(1, dz, 1).start()
                one_b(1, dz, 0).start()
        for part_of_lift in range(2):
            columns = slice(HID * part_of_lift, HID * (part_of_lift + 1))
            for t in range(4):
                dx = (0, 1, 3, 2)[t]
                term = contract(u[lax.rem(x + dx, 4)], gl[t][:, columns], ((0,), (0,)))
                if t == 0:
                    acc[...] = term
                elif t < 3:
                    acc[...] += term
                else:
                    wl[:, columns] = (acc[...] + term).astype(bf16)
            if part_of_lift == 0:
                for dz in (2, 1, 3, 0):
                    one_a(0, dz).start()
            else:
                for dz in (2, 1, 3):
                    one_b(0, dz, 1).start()
                    one_b(0, dz, 0).start()
        first_sums(1)
        for n, out in ((0, du_o), (1, out_o)):
            for t in (1, 2, 3):
                land_copy(n, t).wait_recv()

            def add(r, _, n=n):
                at = pl.ds(pl.multiple_of(r * 32, 32), 32)
                mine = pl.ds(pl.multiple_of(OWN * core + r * 32, 32), 32)
                value = part[0, n, mine].astype(f32)
                for t in range(3):
                    value = value + land[t, n, at].astype(f32)
                total[n, at] = value
                return 0

            lax.fori_loop(0, OWN // 32, add, 0)
            pltpu.make_async_copy(total.at[n], out, l_sem.at[3 + n]).start()
        first_sums(0)
        last_sums(1)
        for k in range(2):
            down_o[k] = jnp.concatenate(
                [
                    down_sum[FLAT * k : FLAT * (k + 1)],
                    jnp.zeros((FLAT_PAD - FLAT, D), bf16),
                ],
                0,
            )
        last_sums(0)
        for n, out in ((0, du_o), (1, out_o)):
            pltpu.make_async_copy(total.at[n], out, l_sem.at[3 + n]).wait()
        for n in range(9):
            gather_send(n).wait_send()
        for n in range(2):
            for t in range(4):
                near_copy(n, t).wait_send()
                if t:
                    land_copy(n, t).wait_send()
        for m in range(2):
            for dz in range(4):
                one_a(m, dz).wait_send()
                if dz:
                    one_b(m, dz, 0).wait_send()
                    one_b(m, dz, 1).wait_send()
                    two_a(m, dz).wait_send()
            two_b(m).wait_send()


def experts(h, y_all, shares, wl, wd, table, collective):
    dma = pltpu.SemaphoreType.DMA

    def chip_at(i):
        return (lax.rem(lax.axis_index("rep") // 2 + distance(jnp.minimum(i, 3)), 4), 0)

    whole = lambda i: (0, 0)
    once = pl.Buffered(1)

    def slots(size, width):
        return [
            pltpu.VMEM((4, size, width // 2), bf16),
            pltpu.VMEM((6, size, width // 2), bf16),
            pltpu.VMEM((3, size, width // 2), bf16),
            pltpu.VMEM((size, width // 2), bf16),
        ]

    return pl.pallas_call(
        experts_kernel,
        grid=(5,),
        in_specs=[
            HBM,
            pl.BlockSpec((2 * OWN, D), chip_at),
            pl.BlockSpec((2 * OWN, 128), chip_at),
            HBM,
            HBM,
            pl.BlockSpec((128, HID), whole, pipeline_mode=once),
        ],
        out_specs=(
            ANY,
            ANY,
            pl.BlockSpec((192, EXP), whole),
            pl.BlockSpec((2, FLAT_PAD, D), lambda i: (0, 0, 0)),
        ),
        out_shape=(
            jax.ShapeDtypeStruct((OWN, D), f32),
            jax.ShapeDtypeStruct((OWN, D), f32),
            jax.ShapeDtypeStruct((192, EXP), bf16),
            jax.ShapeDtypeStruct((2, FLAT_PAD, D), bf16),
        ),
        scratch_shapes=[
            pltpu.VMEM((4, 2 * OWN, D), bf16),
            pltpu.VMEM((D, EXP), bf16),
            pltpu.VMEM((HID, D), bf16),
            pltpu.VMEM((4, 2 * OWN, EXP), bf16),
            pltpu.VMEM((D, HID), f32),
            pltpu.VMEM((HID, D), f32),
            pltpu.VMEM((4, 2, 2 * OWN, D), bf16),
            pltpu.VMEM((4, 2, OWN, D), bf16),
            pltpu.VMEM((3, 2, OWN, D), bf16),
            pltpu.VMEM((2, OWN, D), f32),
        ]
        + slots(192, EXP)
        + slots(2 * FLAT, D)
        + [
            pltpu.VMEM((2 * FLAT, D), bf16),
            dma((5,)),
            dma((9,)),
            dma((9,)),
            dma((4, 2)),
            dma((4, 2)),
            dma((4, 2)),
            dma((4, 2)),
            dma((2, 2, 8)),
            dma((2, 2, 8)),
            dma((2, 4)),
            dma((2, 4)),
        ],
        compiler_params=params(collective, 63 * 2**20),
        name="experts",
    )(h, y_all, shares, wl, wd, table)


def choose_units(w_ref, code_ref, out_ref):
    x = lax.axis_index("rep") // 2
    row = lax.broadcasted_iota(jnp.int32, (FF_EXP, HID), 0)
    there = (row // 32) * 1024 + lax.rem(row, 32)
    here = jnp.broadcast_to(code_ref[...], (FF_EXP, HID))
    base = (5 * x) // 2
    for k in range(2):
        for part in range(2):
            total = jnp.zeros((96, HID), f32)
            for i in range(3):
                chosen = there + 32 * (base + i) == here + FLAT * (2 * x + k)
                total = total + jnp.dot(
                    w_ref[i][:, FF_EXP * part : FF_EXP * (part + 1)],
                    jnp.where(chosen, 1.0, 0.0).astype(bf16),
                    preferred_element_type=f32,
                )
            out_ref[k, :, HID * part : HID * (part + 1)] = total.astype(bf16)


def one_step(kernel, arrays, shapes, name):
    return pl.pallas_call(
        kernel,
        in_specs=[VMEM] * len(arrays),
        out_specs=(VMEM,) * len(shapes),
        out_shape=tuple(jax.ShapeDtypeStruct(shape, dtype) for shape, dtype in shapes),
        compiler_params=pltpu.CompilerParams(vmem_limit_bytes=62 * 2**20),
        name=name,
    )(*arrays)


def side_by_side(ref):
    return jnp.concatenate([ref[c] for c in range(CHIPS)], 1)


def adam(weight, old_mean, square, gradient, step_rate, decay_rate):
    values = weight.astype(f32)
    moment = beta_one * old_mean.astype(f32) + (1.0 - beta_one) * gradient
    variance = beta_two * square.astype(f32) + (1.0 - beta_two) * gradient * gradient
    normed_step = (
        moment
        * (1.0 / (1.0 - beta_one**STEP))
        / (jnp.sqrt(variance * (1.0 / (1.0 - beta_two**STEP))) + adam_epsilon)
    )
    return (moment, variance, values - step_rate * (normed_step + decay_rate * values))


def adam_experts_kernel(
    w_ref, m_ref, s_ref, g_ref, code_ref, dw_ref, dm_ref, ds_ref, dg_ref,
    mo_ref, so_ref, wo_ref, dot_ref, dmo_ref, dso_ref, dwo_ref, grad, apart,
):
    e = pl.program_id(0)
    first, last = (4 * e) // 5, (4 * e + 3) // 5

    @pl.when(e == 0)
    def _():
        column = lax.broadcasted_iota(jnp.int32, (HID, FF_EXP), 1)
        there = (column // 32) * 1024 + lax.rem(column, 32)
        apart[...] = there - jnp.broadcast_to(code_ref[...], (HID, FF_EXP))

    distances = apart[...]
    chosen_first = jnp.where(distances == FLAT * first - 32 * e, 1.0, 0.0).astype(bf16)
    other = jnp.where(first == last, 1 << 24, FLAT * last - 32 * e)
    chosen_last = jnp.where(distances == other, 1.0, 0.0).astype(bf16)

    def both(p):
        return jnp.concatenate([g_ref[p][:, :HID], g_ref[p][:, HID:]], 0)

    ordered = jnp.dot(both(first), chosen_first, preferred_element_type=f32) + jnp.dot(
        both(last), chosen_last, preferred_element_type=f32
    )
    grad[:, :FF_EXP] = ordered[:96]
    grad[:, FF_EXP:] = ordered[96:]

    @pl.when(e == 0)
    def _():
        dot_ref[...] = jnp.zeros_like(dot_ref)

    dot = jnp.sum(w_ref[0].astype(f32) * grad[...], 1, keepdims=True)
    dot_ref[...] += jnp.broadcast_to(dot, dot_ref.shape)
    mo_ref[0], so_ref[0], wo_ref[0] = adam(
        w_ref[0], m_ref[0], s_ref[0], grad[...], rate_lifting, weight_decay
    )
    dmo_ref[0], dso_ref[0], dwo_ref[0] = adam(
        dw_ref[0], dm_ref[0], ds_ref[0], dg_ref[0].astype(f32), rate_lowering, weight_decay
    )


def adam_experts(weight, mean, square, grad, code, down, down_mean, down_square, down_grad):
    block = pl.BlockSpec((1, 96, 2 * FF_EXP), lambda e: (e, 0, 0))
    shape = jax.ShapeDtypeStruct(weight.shape, f32)
    down_block = pl.BlockSpec((1, 32, D), lambda e: (e, 0, 0))
    down_shape = jax.ShapeDtypeStruct(down.shape, f32)
    return pl.pallas_call(
        adam_experts_kernel,
        grid=(EXPERTS,),
        in_specs=[
            block,
            block,
            block,
            pl.BlockSpec(grad.shape, lambda e: (0, 0, 0)),
            pl.BlockSpec(code.shape, lambda e: (0, 0)),
            down_block,
            down_block,
            down_block,
            down_block,
        ],
        out_specs=(block, block, block, pl.BlockSpec((96, 128), lambda e: (0, 0)))
        + (down_block,) * 3,
        out_shape=(shape, shape, shape, jax.ShapeDtypeStruct((96, 128), f32)) + (down_shape,) * 3,
        scratch_shapes=[
            pltpu.VMEM((96, 2 * FF_EXP), f32),
            pltpu.VMEM((HID, FF_EXP), jnp.int32),
        ],
        compiler_params=pltpu.CompilerParams(vmem_limit_bytes=62 * 2**20),
        name="adam_experts",
    )(weight, mean, square, grad, code, down, down_mean, down_square, down_grad)


def last_kernel(
    dh_ref, dz_ref, x_ref, g_ref, mixed_ref, e_ref, w_ref, m_ref, s_ref, gi_ref, wo_ref, mo_ref, so_ref, go_ref,
    grad_ref, out_ref, mi_o, si_o, wi_o, dot_ref, mo_o, so_o, wo_o,
):
    out_ref[...] = mixed_ref[...] + e_ref[...]
    stream = x_ref[...].astype(f32)
    inverse = inverse_root(stream)
    grad_ref[...] = dz_ref[...] + norm_back(dh_ref[...] * g_ref[...], stream * inverse, inverse)
    parts = [gi_ref[c].astype(f32) for c in range(CHIPS)]
    grad = jnp.concatenate(
        [p[:, :192] for p in parts] + [p[:, 192:256] for p in parts] + [p[:, 256:] for p in parts], 1
    )
    dot = jnp.sum(w_ref[...].astype(f32) * grad, 1, keepdims=True)
    dot_ref[...] = jnp.broadcast_to(dot, dot_ref.shape)
    mi_o[...], si_o[...], wi_o[...] = adam(
        w_ref[...], m_ref[...], s_ref[...], grad, rate_inward, weight_decay
    )
    mo_o[...], so_o[...], wo_o[...] = adam(
        wo_ref[...], mo_ref[...], so_ref[...], go_ref[...].astype(f32), rate_outward, weight_decay
    )


def tables():
    half = HEAD // 2
    frequency = np.float32(10000.0) ** (-(2.0 * np.arange(half, dtype=np.float32)) / HEAD)
    phases = np.arange(SEQ, dtype=np.float32)[:, None] * frequency[None, :].astype(np.float32)
    cos, sin = np.cos(phases).astype(np.float32), np.sin(phases).astype(np.float32)
    return (
        np.concatenate([cos, cos, cos, cos], 1),
        np.concatenate([-sin, sin, -sin, sin], 1),
    )


def unit_codes():
    unit = np.arange(HID, dtype=np.int32)
    return (unit // FLAT) * 1024 + unit % FLAT


def inverse_root(stream):
    return lax.rsqrt(jnp.mean(stream * stream, -1, keepdims=True) + norm_epsilon)


def norm_back(scaled, unit, inverse):
    return inverse * (scaled - unit * jnp.mean(scaled * unit, -1, keepdims=True))


def per_device(
    layer_input,
    grad_output,
    routes,
    route_logits,
    norm_gains,
    inward,
    outward,
    lifting,
    lowering,
    mean_gains,
    mean_inward,
    mean_outward,
    mean_lifting,
    mean_lowering,
    square_gains,
    square_inward,
    square_outward,
    square_lifting,
    square_lowering,
):
    gains = norm_gains.astype(f32)
    cos, sin = (jnp.asarray(t) for t in tables())

    lifting_rows = lifting.transpose(1, 0, 2)
    codes = jnp.asarray(unit_codes())
    x = lax.axis_index("rep") // 2
    position = 2 * x + lax.rem(lax.axis_index("shard"), 2)
    low_rows = lowering.transpose(1, 0, 2).reshape(EXPERTS * 32, D)
    low_rows = lax.dynamic_slice(low_rows, (2 * FLAT * x, 0), (2 * FLAT, D)).reshape(2, FLAT, D)
    low_rows = jnp.pad(low_rows, ((0, 0), (0, FLAT_PAD - FLAT), (0, 0)))
    expert = (FLAT * position + lax.rem(jnp.arange(HID), FLAT)) // 32
    row = jnp.arange(128)[:, None]
    share_table = ((row == expert) | (row == expert + 16)).astype(bf16)

    x_all, head_weight, y_all, shares, by_unit = start(
        layer_input, grad_output, inward, norm_gains, routes.T, route_logits.T, lifting_rows, codes[None, :], 2
    )
    head_weight = head_weight.reshape(D, 384)
    gain_rows = head_weight[:, 192:194].T.astype(f32)
    gain_one, gain_two = gain_rows[0:1], gain_rows[1:2]
    by_half = outward.reshape(96, 2, D // 2).transpose(1, 0, 2)

    q, k, v, u_one, attended, lse, unit_weight, down_rows, half = attend(
        x_all, head_weight, gain_one, cos, sin, by_unit, low_rows, by_half, 1
    )
    unit_weight = unit_weight.reshape(D, EXP)
    mixed, low_two, down_weight, own_attended, outward_all = home(
        attended, half.reshape(D, D // 2), down_rows, layer_input, gain_two, 3
    )
    late_inward, low_two = lax.optimization_barrier((inward, low_two))
    inward_all = lax.all_gather(late_inward, "shard", axis=0, tiled=True)
    du, expert_out, lift_sum, down_sum = experts(
        low_two, y_all, shares, unit_weight, down_weight, share_table, 5
    )
    grad_mixed, outward_part, head_grads, lift_pair, down_pair = grads_away(
        du, mixed, grad_output, gain_two, outward_all, own_attended,
        lift_sum.reshape(2, 96, EXP), down_sum, 6,
    )
    dq, dkv, inward_part, outward_own, lift_got, down_got = attend_back(
        q, k, v, head_grads, attended, lse, cos, sin, u_one, outward_part, lift_pair, down_pair, 8
    )
    dh, inward_sum, outward_sum = tail(
        dq, dkv.reshape(SHARDS, OWN, 128), inward_part, outward_own, inward_all, 7
    )
    new_lifting = adam_experts(
        lifting_rows,
        mean_lifting.transpose(1, 0, 2),
        square_lifting.transpose(1, 0, 2),
        lift_got,
        codes[:, None],
        lowering.transpose(1, 0, 2),
        mean_lowering.transpose(1, 0, 2),
        square_lowering.transpose(1, 0, 2),
        down_got[:, :FLAT].reshape(EXPERTS, 32, D),
    )
    new_lowering = tuple(t.transpose(1, 0, 2) for t in new_lifting[4:])
    lifting_dot = new_lifting[3]
    new_lifting = tuple(t.transpose(1, 0, 2) for t in new_lifting[:3])
    last = one_step(
        last_kernel,
        (dh, grad_mixed, layer_input, gain_one, mixed, expert_out)
        + (inward, mean_inward, square_inward, inward_sum)
        + (outward, mean_outward, square_outward, outward_sum),
        (((OWN, D), f32),) * 2
        + ((inward.shape, f32),) * 3
        + (((96, 128), f32),)
        + ((outward.shape, f32),) * 3,
        "last",
    )
    input_grad, layer_output, new_inward, new_outward = last[0], last[1], last[2:6], last[6:9]
    gain_grad = jnp.stack([new_inward[3][:, 0], lifting_dot[:, 0]]) / gains
    new_gains = adam(norm_gains, mean_gains, square_gains, gain_grad, rate_gains, 0.0)
    return (
        layer_output,
        input_grad,
        new_gains[0],
        new_inward[0],
        new_outward[0],
        new_lifting[0],
        new_lowering[0],
        new_gains[1],
        new_inward[1],
        new_outward[1],
        new_lifting[1],
        new_lowering[1],
        new_gains[2],
        new_inward[2],
        new_outward[2],
        new_lifting[2],
        new_lowering[2],
    )


def solution(mesh):
    tokens = P(("rep", "shard"), None)
    gains, flat, deep = P(None, "shard"), P("shard", None), P("shard", None, None)
    weights = (gains, flat, flat, deep, deep)
    return jax.shard_map(
        per_device,
        mesh=mesh,
        in_specs=(tokens,) * 4 + weights * 3,
        out_specs=(tokens,) * 2 + weights * 3,
        check_vma=False,
    )
```
